32 devices in a mesh: dp: 8 (over z, y), mp: 4 (over x, core).
Axes of the slice: x: 2, y: 2, z: 4, core: 2. Of those that a mesh axis runs over, the one named last changes fastest.
Arguments:
- inputs: bfloat16 [16384, 1024], P(('dp', 'mp')), may hold values from -6 to 6
- in_proj: bfloat16 [3, 1024, 1024], P(None, None, 'mp'), may hold values from -0.1875 to 0.1875
- qv_bias: float32 [2, 1024], P(None, 'mp'), may hold values from -3 to 3
- out_proj: bfloat16 [1024, 1024], P('mp'), may hold values from -0.5 to 0.5
- out_bias: float32 [1024], replicated, may hold values from -3 to 3
- attn_gain: float32 [1024], replicated, may hold values from 0.25 to 1.75
- attn_shift: float32 [1024], replicated, may hold values from -3 to 3
- up_proj: bfloat16 [1024, 4096], P(None, 'mp'), may hold values from -0.1875 to 0.1875
- up_bias: float32 [4096], P('mp'), may hold values from -3 to 3
- down_proj: bfloat16 [4096, 1024], P('mp'), may hold values from -0.09375 to 0.09375
- down_bias: float32 [1024], replicated, may hold values from -3 to 3
- ffn_gain: float32 [1024], replicated, may hold values from 0.25 to 1.75
- ffn_shift: float32 [1024], replicated, may hold values from -3 to 3
- segments: int32 [8, 2048], P('dp'), may hold values from 0 to 128, as said below
- padding: int32 [8, 2048], P('dp'), may hold values from 0 to 1, as said below
- cotangent: bfloat16 [16384, 1024], P(('dp', 'mp')), may hold values from -6 to 6
Outputs:
- outputs: bfloat16 [16384, 1024], P(('dp', 'mp'))
- inputs_grad: bfloat16 [16384, 1024], P(('dp', 'mp'))
- in_proj_grad: float32 [3, 1024, 1024], P(None, None, 'mp')
- qv_bias_grad: float32 [2, 1024], P(None, 'mp')
- out_proj_grad: float32 [1024, 1024], P('mp')
- out_bias_grad: float32 [1024], replicated
- attn_gain_grad: float32 [1024], replicated
- attn_shift_grad: float32 [1024], replicated
- up_proj_grad: float32 [1024, 4096], P(None, 'mp')
- up_bias_grad: float32 [4096], P('mp')
- down_proj_grad: float32 [4096, 1024], P('mp')
- down_bias_grad: float32 [1024], replicated
- ffn_gain_grad: float32 [1024], replicated
- ffn_shift_grad: float32 [1024], replicated
The draws below stay inside these ranges and needn't reach their ends.
Inputs may be any that keep to these rules, and one draw needn't show every extreme that they name: `segments`: within a row, segment numbers start at 0, never fall, and change only at positions that are multiples of 16, at least once in every 256 positions; the last position of every row alone holds 128. Each row ends in 1 to 128 padding positions; all others are real.
All inputs are finite; a program needn't handle non-finite values.
Results may differ from the reference program's by a relative error of at most 0.02.
Values may be sent and summed in bfloat16 or wider, within the bound.
A program may use at most 192 MiB of HBM per device.

```python
import math
import jax
import jax.numpy as jnp
from jax import lax

D = 1024
HEADS = 16
HEAD = 64
FF = 4096
LEN = 2048
ROWS = 8
TOKENS = 16384


def draw_segments(key, part):
    key = jax.random.fold_in(key, 7)
    places = jnp.arange(LEN, dtype=jnp.int32)[None, :]
    coins = jax.random.randint(key, (ROWS, LEN), 0, 2) == 0
    bounds = (places % 16 == 0) & (places > 0) & (coins | (places % 256 == 0))
    counted = jnp.cumsum(bounds.astype(jnp.int32), axis=1)
    return jnp.where(places == LEN - 1, LEN // 16, counted).astype(jnp.int32)


def draw_padding(key, part):
    key = jax.random.fold_in(key, 13)
    places = jnp.arange(LEN, dtype=jnp.int32)[None, :]
    tails = jax.random.randint(key, (ROWS, 1), 1, LEN // 16 + 1)
    return (places < LEN - tails).astype(jnp.int32)


def level_of(own_key, extent, pieces, least, largest):
    level, own = 1.0, jax.random.fold_in(own_key, 6)
    for axis_at, shards_of in pieces:
        heights = jnp.exp(jax.random.uniform(jax.random.fold_in(own, axis_at), (shards_of,), jnp.float32, least / len(pieces), largest / len(pieces)))
        level = level * jnp.repeat(heights, extent[axis_at] // shards_of).reshape([-1 if axis == axis_at else 1 for axis in range(len(extent))])
    return level


def noise(rng, shape, width, limit, split=(), kind=jnp.bfloat16):
    values = width * jax.random.normal(rng, shape, jnp.float32)
    if split:
        values = values * level_of(rng, shape, split, -0.22, 0.18)
    return jnp.clip(values, -limit, limit).astype(kind)


def setup_inputs(seed: int = 0) -> dict:
    key_of = jax.random.split(jax.random.key(seed), 17)
    return {
        "inputs": noise(key_of[0], (TOKENS, D), 1.0, 6.0, ((0, 32),)),
        "in_proj": noise(key_of[1], (3, D, D), D ** -0.5, 0.1875, ((2, 4),)),
        "qv_bias": noise(key_of[2], (2, D), 0.5, 3.0, ((1, 4),), jnp.float32),
        "out_proj": noise(key_of[3], (D, D), (D // 8) ** -0.5, 0.5, ((0, 4),)),
        "out_bias": noise(key_of[4], (D,), 0.5, 3.0, (), jnp.float32),
        "attn_gain": jnp.clip(1.0 + 0.15 * jax.random.normal(key_of[5], (D,), jnp.float32), 0.25, 1.75),
        "attn_shift": noise(key_of[6], (D,), 0.5, 3.0, (), jnp.float32),
        "up_proj": noise(key_of[7], (D, FF), D ** -0.5, 0.1875, ((1, 4),)),
        "up_bias": noise(key_of[8], (FF,), 0.5, 3.0, ((0, 4),), jnp.float32),
        "down_proj": noise(key_of[9], (FF, D), FF ** -0.5, 0.09375, ((0, 4),)),
        "down_bias": noise(key_of[10], (D,), 0.5, 3.0, (), jnp.float32),
        "ffn_gain": jnp.clip(1.0 + 0.15 * jax.random.normal(key_of[11], (D,), jnp.float32), 0.25, 1.75),
        "ffn_shift": noise(key_of[12], (D,), 0.5, 3.0, (), jnp.float32),
        "segments": draw_segments(jax.random.fold_in(key_of[16], 71), 0),
        "padding": draw_padding(jax.random.fold_in(key_of[16], 71), 0),
        "cotangent": noise(key_of[15], (TOKENS, D), 1.0, 6.0, ((0, 32),)),
    }


EPSILON = 1e-05
HIGH = lax.Precision.HIGHEST

@jax.custom_vjp
def low(v):
    return lax.optimization_barrier(v.astype(jnp.bfloat16)).astype(jnp.float32)

@jax.custom_vjp
def low_back(v):
    return v

def low_keep(v):
    return (low(v), None)

def low_pass(kept, grad):
    return (grad,)

def back_keep(v):
    return (v, None)

def back_low(kept, grad):
    return (low(grad),)
low.defvjp(low_keep, low_pass)
low_back.defvjp(back_keep, back_low)

def rounded(value):
    return low(low_back(value))

def layer_norm(summed, gain, shift):
    center = summed - lax.optimization_barrier(jnp.mean(summed, axis=-1, keepdims=True))
    variance = lax.optimization_barrier(jnp.mean(center * center, axis=-1, keepdims=True))
    return center * lax.rsqrt(variance + EPSILON) * gain + shift

def row_layer(params, tokens, seg_row, real_row):
    in_proj, qv_bias, out_proj, out_bias, attn_gain, attn_shift, up_proj, up_bias, down_proj, down_bias, ffn_gain, ffn_shift = params
    query = rounded(jnp.dot(tokens, in_proj[0], precision=HIGH) + qv_bias[0])
    keys = rounded(jnp.dot(tokens, in_proj[1], precision=HIGH))
    values = rounded(jnp.dot(tokens, in_proj[2], precision=HIGH) + qv_bias[1])
    head_query = query.reshape(LEN, HEADS, HEAD)
    head_keys = keys.reshape(LEN, HEADS, HEAD)
    head_values = values.reshape(LEN, HEADS, HEAD)
    scores = jnp.einsum('qhd,khd->hqk', head_query, head_keys, precision=HIGH) * (1.0 / math.sqrt(HEAD))
    scores = low_back(scores)
    allowed = (seg_row[:, None] == seg_row[None, :]) & ((real_row[None, :] > 0) | (real_row[:, None] == 0))
    scores = jnp.where(allowed[None], scores, -1e+30)
    peak = lax.optimization_barrier(jnp.max(scores, axis=-1, keepdims=True))
    expo = jnp.exp(scores - peak)
    prob = low(expo / lax.optimization_barrier(jnp.sum(expo, axis=-1, keepdims=True)))
    context = jnp.einsum('hqk,khd->qhd', prob, head_values, precision=HIGH).reshape(LEN, D)
    context = rounded(context)
    attended = low_back(jnp.dot(context, out_proj, precision=HIGH))
    normed = layer_norm(tokens + attended + out_bias, attn_gain, attn_shift)
    upper = low_back(jnp.dot(low(normed), up_proj, precision=HIGH) + up_bias)
    active = low(jax.nn.gelu(upper, approximate=False))
    branch = low_back(jnp.dot(active, down_proj, precision=HIGH))
    return layer_norm(normed + branch + down_bias, ffn_gain, ffn_shift)

def reference(inputs, in_proj, qv_bias, out_proj, out_bias, attn_gain, attn_shift, up_proj, up_bias, down_proj, down_bias, ffn_gain, ffn_shift, segments, padding, cotangent):
    params = (in_proj.astype(jnp.float32), qv_bias.astype(jnp.float32), out_proj.astype(jnp.float32), out_bias.astype(jnp.float32), attn_gain.astype(jnp.float32), attn_shift.astype(jnp.float32), up_proj.astype(jnp.float32), up_bias.astype(jnp.float32), down_proj.astype(jnp.float32), down_bias.astype(jnp.float32), ffn_gain.astype(jnp.float32), ffn_shift.astype(jnp.float32))
    tokens = inputs.astype(jnp.float32).reshape(ROWS, LEN, D)

    def forward(token_rows, weights):

        def one_row(item):
            return row_layer(weights, item[0], item[1], item[2])
        return lax.map(jax.checkpoint(one_row), (token_rows, segments, padding))
    result, pullback = jax.vjp(forward, tokens, params)
    token_grad, grads = pullback(cotangent.astype(jnp.float32).reshape(ROWS, LEN, D))
    return (result.reshape(TOKENS, D).astype(jnp.bfloat16), token_grad.reshape(TOKENS, D).astype(jnp.bfloat16), grads[0], grads[1], grads[2], grads[3], grads[4], grads[5], grads[6], grads[7], grads[8], grads[9], grads[10], grads[11])
```

```python
from functools import partial
import math

import jax
import jax.numpy as jnp
from jax import lax
from jax.experimental import pallas as pl
from jax.experimental.pallas import tpu as pltpu
from jax.sharding import PartitionSpec as P

HEAD = 64
BLOCK = 256


EPSILON = 1e-05


NEG = -1e30


def _mask_bias(seg_q, pad_q, seg_k, pad_k):
    allowed = (seg_q == seg_k) & ((pad_k > 0) | (pad_q == 0))
    return jnp.where(allowed, 0.0, NEG).astype(jnp.float32)


def _head_masks(heads, width, value):
    lane = lax.broadcasted_iota(jnp.int32, (1, width), 1) // HEAD
    return [jnp.where(lane == h, value, 0.0).astype(jnp.bfloat16) for h in range(heads)]


def _nt(a, b):
    return lax.dot_general(a, b, (((1,), (1,)), ((), ())), preferred_element_type=jnp.float32)


def _tn(a, b):
    return lax.dot_general(a, b, (((0,), (0,)), ((), ())), preferred_element_type=jnp.float32)


def _nn(a, b):
    return jnp.dot(a, b, preferred_element_type=jnp.float32)


def attention_forward_kernel(
    heads, blocks, ends_ref, query_ref, keys_ref, values_ref, seg_col, pad_col, seg_row, pad_row,
    context_ref, lse_ref, peak_ref, total_ref, acc_ref,
):
    f32, bf16 = jnp.float32, jnp.bfloat16
    i = pl.program_id(0)
    width = query_ref.shape[1]
    scaled = _head_masks(heads, width, 1.0 / math.sqrt(HEAD))
    plain = _head_masks(heads, width, 1.0)
    lane = lax.broadcasted_iota(jnp.int32, (1, width), 1) // HEAD
    column = lax.broadcasted_iota(jnp.int32, (1, 128), 1)
    query = query_ref[...]

    def parts(j):
        rows = pl.ds(pl.multiple_of(j * BLOCK, BLOCK), BLOCK)
        bias = _mask_bias(seg_col[...], pad_col[...], seg_row[:, rows], pad_row[:, rows])
        return keys_ref[rows, :], values_ref[rows, :], bias

    key, value, bias = parts(i)
    acc = jnp.zeros((BLOCK, width), f32)
    for h in range(heads):
        scores = _nt(query * scaled[h], key) + bias
        peak = jnp.max(scores, axis=-1, keepdims=True)
        expo = jnp.exp(scores - peak)
        peak_ref[h] = peak
        total_ref[h] = jnp.sum(expo, axis=-1, keepdims=True)
        acc = acc + _nn(expo.astype(bf16), value * plain[h])
    acc_ref[...] = acc

    def other(j, carry):
        meets = (j != i) & (ends_ref[0, j] <= ends_ref[1, i]) & (ends_ref[1, j] >= ends_ref[0, i])

        @pl.when(meets)
        def _():
            key, value, bias = parts(j)
            shrink = jnp.zeros((BLOCK, width), f32)
            add = jnp.zeros((BLOCK, width), f32)
            for h in range(heads):
                scores = _nt(query * scaled[h], key) + bias
                old = peak_ref[h]
                peak = jnp.maximum(old, jnp.max(scores, axis=-1, keepdims=True))
                expo = jnp.exp(scores - peak)
                ratio = jnp.exp(old - peak)
                peak_ref[h] = peak
                total_ref[h] = total_ref[h] * ratio + jnp.sum(expo, axis=-1, keepdims=True)
                shrink = jnp.where(lane == h, ratio, shrink)
                add = add + _nn(expo.astype(bf16), value * plain[h])
            acc_ref[...] = acc_ref[...] * shrink + add

        return carry

    lax.fori_loop(0, blocks, other, 0)
    inverse = jnp.zeros((BLOCK, width), f32)
    lse = jnp.zeros((BLOCK, 128), f32)
    for h in range(heads):
        total = total_ref[h]
        inverse = jnp.where(lane == h, 1.0 / total, inverse)
        lse = jnp.where(column == h, peak_ref[h] + jnp.log(total), lse)
    context_ref[...] = (acc_ref[...] * inverse).astype(bf16)
    lse_ref[...] = lse


def attention_backward_kernel(
    heads, blocks, ends_ref, query_ref, keys_ref, values_ref, grad_ref, context_ref, lse_ref,
    seg_col, pad_col, seg_row, pad_row, query_grad_ref, keys_grad_ref, values_grad_ref,
    query_acc, keys_acc, values_acc,
):
    f32, bf16 = jnp.float32, jnp.bfloat16
    i = pl.program_id(0)
    width = query_ref.shape[1]
    scaled = _head_masks(heads, width, 1.0 / math.sqrt(HEAD))
    plain = _head_masks(heads, width, 1.0)

    @pl.when(i == 0)
    def _():
        keys_acc[...] = jnp.zeros_like(keys_acc)
        values_acc[...] = jnp.zeros_like(values_acc)

    query, grad = query_ref[...], grad_ref[...]
    product = grad.astype(f32) * context_ref[...].astype(f32)

    def block(j):
        rows = pl.ds(pl.multiple_of(j * BLOCK, BLOCK), BLOCK)
        bias = _mask_bias(seg_col[...], pad_col[...], seg_row[:, rows], pad_row[:, rows])
        key, value = keys_ref[rows, :], values_ref[rows, :]
        query_add = jnp.zeros((BLOCK, width), f32)
        key_add = jnp.zeros((BLOCK, width), f32)
        value_add = jnp.zeros((BLOCK, width), f32)
        for h in range(heads):
            query_h, grad_h = query * scaled[h], grad * plain[h]
            scores = _nt(query_h, key) + bias
            prob = jnp.exp(scores - lse_ref[:, h : h + 1])
            prob_grad = _nt(grad_h, value)
            row_dot = jnp.sum(product * plain[h].astype(f32), axis=-1, keepdims=True)
            score_grad = (prob * (prob_grad - row_dot)).astype(bf16)
            query_add = query_add + _nn(score_grad, key * scaled[h])
            key_add = key_add + _tn(score_grad, query_h)
            value_add = value_add + _tn(prob.astype(bf16), grad_h)
        keys_acc[rows, :] += key_add
        values_acc[rows, :] += value_add
        return query_add

    query_acc[...] = block(i)

    def other(j, carry):
        meets = (j != i) & (ends_ref[0, j] <= ends_ref[1, i]) & (ends_ref[1, j] >= ends_ref[0, i])

        @pl.when(meets)
        def _():
            query_acc[...] += block(j)

        return carry

    lax.fori_loop(0, blocks, other, 0)
    query_grad_ref[...] = query_acc[...].astype(bf16)

    @pl.when(i == blocks - 1)
    def _():
        keys_grad_ref[...] = keys_acc[...].astype(bf16)
        values_grad_ref[...] = values_acc[...].astype(bf16)


def _attention_specs(length, width):
    block = pl.BlockSpec((BLOCK, width), lambda i, ends: (i, 0))
    whole = pl.BlockSpec((length, width), lambda i, ends: (0, 0))
    col = pl.BlockSpec((BLOCK, 1), lambda i, ends: (i, 0))
    row = pl.BlockSpec((1, length), lambda i, ends: (0, 0))
    lse = pl.BlockSpec((BLOCK, 128), lambda i, ends: (i, 0))
    return block, whole, col, row, lse


def attention_forward(query, keys, values, where):
    length, width = query.shape
    heads, blocks = width // HEAD, length // BLOCK
    block, whole, col, row, lse = _attention_specs(length, width)
    return pl.pallas_call(
        partial(attention_forward_kernel, heads, blocks),
        grid_spec=pltpu.PrefetchScalarGridSpec(
            num_scalar_prefetch=1,
            grid=(blocks,),
            in_specs=[block, whole, whole, col, col, row, row],
            out_specs=[block, lse],
            scratch_shapes=[
                pltpu.VMEM((heads, BLOCK, 1), jnp.float32),
                pltpu.VMEM((heads, BLOCK, 1), jnp.float32),
                pltpu.VMEM((BLOCK, width), jnp.float32),
            ],
        ),
        out_shape=[
            jax.ShapeDtypeStruct((length, width), jnp.bfloat16),
            jax.ShapeDtypeStruct((length, 128), jnp.float32),
        ],
        compiler_params=pltpu.CompilerParams(vmem_limit_bytes=32 * 2**20),
        name="attention_forward",
    )(where[0], query, keys, values, *where[1:])


def attention_backward(query, keys, values, grad, context, lse_rows, where):
    length, width = query.shape
    heads, blocks = width // HEAD, length // BLOCK
    block, whole, col, row, lse = _attention_specs(length, width)
    shape = jax.ShapeDtypeStruct((length, width), jnp.bfloat16)
    return pl.pallas_call(
        partial(attention_backward_kernel, heads, blocks),
        grid_spec=pltpu.PrefetchScalarGridSpec(
            num_scalar_prefetch=1,
            grid=(blocks,),
            in_specs=[block, whole, whole, block, block, lse, col, col, row, row],
            out_specs=[block, whole, whole],
            scratch_shapes=[
                pltpu.VMEM((BLOCK, width), jnp.float32),
                pltpu.VMEM((length, width), jnp.float32),
                pltpu.VMEM((length, width), jnp.float32),
            ],
        ),
        out_shape=[shape, shape, shape],
        compiler_params=pltpu.CompilerParams(vmem_limit_bytes=32 * 2**20),
        name="attention_backward",
    )(where[0], query, keys, values, grad, context, lse_rows, *where[1:])


def segment_places(segments, padding):
    row_count, seq_len = segments.shape
    seg = segments + jnp.arange(row_count, dtype=jnp.int32)[:, None] * (seq_len + 1)
    seg, pad = seg.reshape(-1), padding.reshape(-1)
    ends = jnp.stack([seg[::BLOCK], seg[BLOCK - 1 :: BLOCK]])
    return (ends, seg[:, None], pad[:, None], seg[None, :], pad[None, :])


def norm_forward(summed, gain, shift):
    center = summed - jnp.mean(summed, axis=-1, keepdims=True)
    variance = jnp.mean(center * center, axis=-1, keepdims=True)
    inverse = lax.rsqrt(variance + EPSILON)
    unit = center * inverse
    return (unit * gain + shift, unit, inverse)


def norm_backward(incoming, unit, inverse, gain):
    scaled = incoming * gain
    back = inverse * (
        scaled
        - jnp.mean(scaled, axis=-1, keepdims=True)
        - unit * jnp.mean(scaled * unit, axis=-1, keepdims=True)
    )
    return (back, jnp.sum(incoming * unit, axis=0), jnp.sum(incoming, axis=0))


def shards(
    inputs,
    in_proj,
    qv_bias,
    out_proj,
    out_bias,
    attn_gain,
    attn_shift,
    up_proj,
    up_bias,
    down_proj,
    down_bias,
    ffn_gain,
    ffn_shift,
    segments,
    padding,
    cotangent,
):
    f32 = jnp.float32
    bf16 = jnp.bfloat16
    tokens_full = lax.all_gather(inputs, "mp", axis=0, tiled=True)
    length = tokens_full.shape[0]
    where = segment_places(segments, padding)
    query = (
        (jnp.dot(tokens_full, in_proj[0], preferred_element_type=f32) + qv_bias[0])
        .astype(bf16)
    )
    keys = (
        jnp.dot(tokens_full, in_proj[1], preferred_element_type=f32)
        .astype(bf16)
    )
    values = (
        (jnp.dot(tokens_full, in_proj[2], preferred_element_type=f32) + qv_bias[1])
        .astype(bf16)
    )

    context, lse_rows = attention_forward(query, keys, values, where)
    attended = lax.psum_scatter(
        jnp.dot(context, out_proj, preferred_element_type=f32).astype(jnp.bfloat16),
        "mp",
        scatter_dimension=0,
        tiled=True,
    ).astype(jnp.float32)
    normed, unit_low, inverse_low = norm_forward(
        inputs.astype(f32) + attended + out_bias, attn_gain, attn_shift
    )
    normed_full = lax.all_gather(normed.astype(bf16), "mp", axis=0, tiled=True)
    upper = jnp.dot(normed_full, up_proj, preferred_element_type=f32) + up_bias
    active = jax.nn.gelu(upper, approximate=False).astype(bf16)
    branch = lax.psum_scatter(
        jnp.dot(active, down_proj, preferred_element_type=f32).astype(jnp.bfloat16),
        "mp",
        scatter_dimension=0,
        tiled=True,
    ).astype(jnp.float32)
    outputs, unit_high, inverse_high = norm_forward(
        normed + branch + down_bias, ffn_gain, ffn_shift
    )
    upper_grad, ffn_gain_grad, ffn_shift_grad = norm_backward(
        cotangent.astype(f32), unit_high, inverse_high, ffn_gain
    )
    down_bias_grad = jnp.sum(upper_grad, axis=0)
    upper_full = lax.all_gather(upper_grad.astype(bf16), "mp", axis=0, tiled=True)
    down_grad = jnp.einsum("tf,td->fd", active, upper_full, preferred_element_type=f32)
    active_grad = jnp.einsum("td,fd->tf", upper_full, down_proj, preferred_element_type=f32)
    _, gelu_pull = jax.vjp(partial(jax.nn.gelu, approximate=False), upper)
    upper_back = gelu_pull(active_grad)[0].astype(bf16)
    up_bias_grad = jnp.sum(upper_back.astype(f32), axis=0)
    up_grad = jnp.einsum("td,tf->df", normed_full, upper_back, preferred_element_type=f32)
    normed_grad = upper_grad + lax.psum_scatter(
        jnp.einsum("tf,df->td", upper_back, up_proj, preferred_element_type=f32).astype(
            jnp.bfloat16
        ),
        "mp",
        scatter_dimension=0,
        tiled=True,
    ).astype(jnp.float32)
    lower_grad, attn_gain_grad, attn_shift_grad = norm_backward(
        normed_grad, unit_low, inverse_low, attn_gain
    )
    out_bias_grad = jnp.sum(lower_grad, axis=0)
    lower_full = lax.all_gather(lower_grad.astype(bf16), "mp", axis=0, tiled=True)
    out_grad = jnp.einsum("tc,td->cd", context, lower_full, preferred_element_type=f32)
    context_grad = (
        jnp.einsum("td,cd->tc", lower_full, out_proj, preferred_element_type=f32)
        .astype(bf16)
    )

    query_grad, key_grad, value_grad = attention_backward(
        query, keys, values, context_grad, context, lse_rows, where
    )
    stacked = jnp.stack([query_grad, key_grad, value_grad])
    in_grad = jnp.einsum("td,jtc->jdc", tokens_full, stacked, preferred_element_type=f32)
    qv_bias_grad = jnp.stack(
        [jnp.sum(query_grad.astype(f32), axis=0), jnp.sum(value_grad.astype(f32), axis=0)]
    )
    inputs_grad = (
        lower_grad
        + lax.psum_scatter(
            jnp.einsum("jtc,jdc->td", stacked, in_proj, preferred_element_type=f32).astype(
                jnp.bfloat16
            ),
            "mp",
            scatter_dimension=0,
            tiled=True,
        ).astype(jnp.float32)
    ).astype(bf16)
    shared = lax.psum(
        jnp.stack(
            [
                out_bias_grad,
                attn_gain_grad,
                attn_shift_grad,
                down_bias_grad,
                ffn_gain_grad,
                ffn_shift_grad,
            ]
        ),
        "mp",
    )
    shared, up_bias_grad, qv_bias_grad = lax.psum((shared, up_bias_grad, qv_bias_grad), "dp")
    out_bias_grad, attn_gain_grad, attn_shift_grad, down_bias_grad, ffn_gain_grad, ffn_shift_grad = shared
    up_grad, down_grad = lax.psum((up_grad.astype(bf16), down_grad.astype(bf16)), "dp")
    in_grad, out_grad = lax.psum((in_grad.astype(bf16), out_grad.astype(bf16)), "dp")
    in_grad, out_grad, up_grad, down_grad = (
        in_grad.astype(f32), out_grad.astype(f32), up_grad.astype(f32), down_grad.astype(f32)
    )
    return (
        outputs.astype(bf16),
        inputs_grad,
        in_grad,
        qv_bias_grad,
        out_grad,
        out_bias_grad,
        attn_gain_grad,
        attn_shift_grad,
        up_grad,
        up_bias_grad,
        down_grad,
        down_bias_grad,
        ffn_gain_grad,
        ffn_shift_grad,
    )


def solution(mesh):
    return jax.shard_map(
        shards,
        mesh=mesh,
        in_specs=(
            P(("dp", "mp"), None),
            P(None, None, "mp"),
            P(None, "mp"),
            P("mp", None),
            P(),
            P(),
            P(),
            P(None, "mp"),
            P("mp"),
            P("mp", None),
            P(),
            P(),
            P(),
            P("dp", None),
            P("dp", None),
            P(("dp", "mp"), None),
        ),
        out_specs=(
            P(("dp", "mp"), None),
            P(("dp", "mp"), None),
            P(None, None, "mp"),
            P(None, "mp"),
            P("mp", None),
            P(),
            P(),
            P(),
            P(None, "mp"),
            P("mp"),
            P("mp", None),
            P(),
            P(),
            P(),
        ),
        check_vma=False,
    )
```

```python
from functools import partial
import math

import jax
import jax.numpy as jnp
from jax import lax
from jax.experimental import pallas as pl
from jax.experimental.pallas import tpu as pltpu
from jax.sharding import PartitionSpec as P

HEAD = 64
BLOCK = 256
CHUNKS = 4
COLS = 256
MESH = pl.DeviceIdType.MESH


EPSILON = 1e-05


NEG = -1e30


def _mask_bias(seg_q, pad_q, seg_k, pad_k):
    allowed = (seg_q == seg_k) & ((pad_k > 0) | (pad_q == 0))
    return jnp.where(allowed, 0.0, NEG).astype(jnp.float32)


def _head_masks(heads, width, value):
    lane = lax.broadcasted_iota(jnp.int32, (1, width), 1) // HEAD
    return [jnp.where(lane == h, value, 0.0).astype(jnp.bfloat16) for h in range(heads)]


def _nt(a, b):
    return lax.dot_general(a, b, (((1,), (1,)), ((), ())), preferred_element_type=jnp.float32)


def _tn(a, b):
    return lax.dot_general(a, b, (((0,), (0,)), ((), ())), preferred_element_type=jnp.float32)


def _nn(a, b):
    return jnp.dot(a, b, preferred_element_type=jnp.float32)


def attention_forward_kernel(
    heads, blocks, ends_ref, query_ref, keys_ref, values_ref, seg_col, pad_col, seg_row, pad_row,
    context_ref, lse_ref, peak_ref, total_ref, acc_ref,
):
    f32, bf16 = jnp.float32, jnp.bfloat16
    i = pl.program_id(0)
    width = query_ref.shape[1]
    scaled = _head_masks(heads, width, 1.0 / math.sqrt(HEAD))
    plain = _head_masks(heads, width, 1.0)
    lane = lax.broadcasted_iota(jnp.int32, (1, width), 1) // HEAD
    column = lax.broadcasted_iota(jnp.int32, (1, 128), 1)
    query = query_ref[...]

    def parts(j):
        rows = pl.ds(pl.multiple_of(j * BLOCK, BLOCK), BLOCK)
        bias = _mask_bias(seg_col[...], pad_col[...], seg_row[:, rows], pad_row[:, rows])
        return keys_ref[rows, :], values_ref[rows, :], bias

    key, value, bias = parts(i)
    acc = jnp.zeros((BLOCK, width), f32)
    for h in range(heads):
        scores = _nt(query * scaled[h], key) + bias
        peak = jnp.max(scores, axis=-1, keepdims=True)
        expo = jnp.exp(scores - peak)
        peak_ref[h] = peak
        total_ref[h] = jnp.sum(expo, axis=-1, keepdims=True)
        acc = acc + _nn(expo.astype(bf16), value * plain[h])
    acc_ref[...] = acc

    def other(j, carry):
        meets = (j != i) & (ends_ref[0, j] <= ends_ref[1, i]) & (ends_ref[1, j] >= ends_ref[0, i])

        @pl.when(meets)
        def _():
            key, value, bias = parts(j)
            shrink = jnp.zeros((BLOCK, width), f32)
            add = jnp.zeros((BLOCK, width), f32)
            for h in range(heads):
                scores = _nt(query * scaled[h], key) + bias
                old = peak_ref[h]
                peak = jnp.maximum(old, jnp.max(scores, axis=-1, keepdims=True))
                expo = jnp.exp(scores - peak)
                ratio = jnp.exp(old - peak)
                peak_ref[h] = peak
                total_ref[h] = total_ref[h] * ratio + jnp.sum(expo, axis=-1, keepdims=True)
                shrink = jnp.where(lane == h, ratio, shrink)
                add = add + _nn(expo.astype(bf16), value * plain[h])
            acc_ref[...] = acc_ref[...] * shrink + add

        return carry

    lax.fori_loop(0, blocks, other, 0)
    inverse = jnp.zeros((BLOCK, width), f32)
    lse = jnp.zeros((BLOCK, 128), f32)
    for h in range(heads):
        total = total_ref[h]
        inverse = jnp.where(lane == h, 1.0 / total, inverse)
        lse = jnp.where(column == h, peak_ref[h] + jnp.log(total), lse)
    context_ref[...] = (acc_ref[...] * inverse).astype(bf16)
    lse_ref[...] = lse


def attention_backward_kernel(
    heads, blocks, ends_ref, query_ref, keys_ref, values_ref, grad_ref, context_ref, lse_ref,
    seg_col, pad_col, seg_row, pad_row, grads_ref, query_acc, keys_acc, values_acc,
):
    f32, bf16 = jnp.float32, jnp.bfloat16
    i = pl.program_id(0)
    width = query_ref.shape[1]
    scaled = _head_masks(heads, width, 1.0 / math.sqrt(HEAD))
    plain = _head_masks(heads, width, 1.0)

    @pl.when(i == 0)
    def _():
        keys_acc[...] = jnp.zeros_like(keys_acc)
        values_acc[...] = jnp.zeros_like(values_acc)

    query, grad = query_ref[...], grad_ref[...]
    product = grad.astype(f32) * context_ref[...].astype(f32)

    def block(j):
        rows = pl.ds(pl.multiple_of(j * BLOCK, BLOCK), BLOCK)
        bias = _mask_bias(seg_col[...], pad_col[...], seg_row[:, rows], pad_row[:, rows])
        key, value = keys_ref[rows, :], values_ref[rows, :]
        query_add = jnp.zeros((BLOCK, width), f32)
        key_add = jnp.zeros((BLOCK, width), f32)
        value_add = jnp.zeros((BLOCK, width), f32)
        for h in range(heads):
            query_h, grad_h = query * scaled[h], grad * plain[h]
            scores = _nt(query_h, key) + bias
            prob = jnp.exp(scores - lse_ref[:, h : h + 1])
            prob_grad = _nt(grad_h, value)
            row_dot = jnp.sum(product * plain[h].astype(f32), axis=-1, keepdims=True)
            score_grad = (prob * (prob_grad - row_dot)).astype(bf16)
            query_add = query_add + _nn(score_grad, key * scaled[h])
            key_add = key_add + _tn(score_grad, query_h)
            value_add = value_add + _tn(prob.astype(bf16), grad_h)
        keys_acc[rows, :] += key_add
        values_acc[rows, :] += value_add
        return query_add

    query_acc[...] = block(i)

    def other(j, carry):
        meets = (j != i) & (ends_ref[0, j] <= ends_ref[1, i]) & (ends_ref[1, j] >= ends_ref[0, i])

        @pl.when(meets)
        def _():
            query_acc[...] += block(j)

        return carry

    lax.fori_loop(0, blocks, other, 0)
    grads_ref[pl.ds(pl.multiple_of(i * BLOCK, BLOCK), BLOCK), :width] = query_acc[...].astype(bf16)

    @pl.when(i == blocks - 1)
    def _():
        grads_ref[:, width : 2 * width] = keys_acc[...].astype(bf16)
        grads_ref[:, 2 * width :] = values_acc[...].astype(bf16)


def _attention_specs(length, width):
    block = pl.BlockSpec((BLOCK, width), lambda i, ends: (i, 0))
    keys = pl.BlockSpec((length, width), lambda i, ends: (0, 1))
    values = pl.BlockSpec((length, width), lambda i, ends: (0, 2))
    col = pl.BlockSpec((BLOCK, 1), lambda i, ends: (i, 0))
    row = pl.BlockSpec((1, length), lambda i, ends: (0, 0))
    lse = pl.BlockSpec((BLOCK, 128), lambda i, ends: (i, 0))
    return block, keys, values, col, row, lse


def attention_forward(qkv, where):
    length, width = qkv.shape[0], qkv.shape[1] // 3
    heads, blocks = width // HEAD, length // BLOCK
    block, keys, values, col, row, lse = _attention_specs(length, width)
    return pl.pallas_call(
        partial(attention_forward_kernel, heads, blocks),
        grid_spec=pltpu.PrefetchScalarGridSpec(
            num_scalar_prefetch=1,
            grid=(blocks,),
            in_specs=[block, keys, values, col, col, row, row],
            out_specs=[block, lse],
            scratch_shapes=[
                pltpu.VMEM((heads, BLOCK, 1), jnp.float32),
                pltpu.VMEM((heads, BLOCK, 1), jnp.float32),
                pltpu.VMEM((BLOCK, width), jnp.float32),
            ],
        ),
        out_shape=[
            jax.ShapeDtypeStruct((length, width), jnp.bfloat16),
            jax.ShapeDtypeStruct((length, 128), jnp.float32),
        ],
        compiler_params=pltpu.CompilerParams(vmem_limit_bytes=32 * 2**20),
        name="attention_forward",
    )(where[0], qkv, qkv, qkv, *where[1:])


def attention_backward(qkv, grad, context, lse_rows, where):
    length, width = grad.shape
    heads, blocks = width // HEAD, length // BLOCK
    block, keys, values, col, row, lse = _attention_specs(length, width)
    return pl.pallas_call(
        partial(attention_backward_kernel, heads, blocks),
        grid_spec=pltpu.PrefetchScalarGridSpec(
            num_scalar_prefetch=1,
            grid=(blocks,),
            in_specs=[block, keys, values, block, block, lse, col, col, row, row],
            out_specs=pl.BlockSpec((length, 3 * width), lambda i, ends: (0, 0)),
            scratch_shapes=[
                pltpu.VMEM((BLOCK, width), jnp.float32),
                pltpu.VMEM((length, width), jnp.float32),
                pltpu.VMEM((length, width), jnp.float32),
            ],
        ),
        out_shape=jax.ShapeDtypeStruct((length, 3 * width), jnp.bfloat16),
        compiler_params=pltpu.CompilerParams(vmem_limit_bytes=32 * 2**20),
        name="attention_backward",
    )(where[0], qkv, qkv, qkv, grad, context, lse_rows, *where[1:])


def segment_places(segments, padding):
    row_count, seq_len = segments.shape
    seg = segments + jnp.arange(row_count, dtype=jnp.int32)[:, None] * (seq_len + 1)
    seg, pad = seg.reshape(-1), padding.reshape(-1)
    ends = jnp.stack([seg[::BLOCK], seg[BLOCK - 1 :: BLOCK]])
    return (ends, seg[:, None], pad[:, None], seg[None, :], pad[None, :])


def _partners():
    me = lax.axis_index("mp")
    core = lax.rem(me, 2)
    sib = me + 1 - 2 * core
    cnt = lax.rem(me + 2, 4)
    dia = lax.rem(cnt + 1, 2) + cnt - lax.rem(cnt, 2)
    return me, sib, cnt, dia


def _remote(src, dst, send, recv, target):
    return pltpu.make_async_remote_copy(
        src_ref=src, dst_ref=dst, send_sem=send, recv_sem=recv, device_id=target, device_id_type=MESH
    )


def _greet(targets):
    barrier = pltpu.get_barrier_semaphore()
    for target in targets:
        pl.semaphore_signal(barrier, inc=1, device_id=target, device_id_type=MESH)
    pl.semaphore_wait(barrier, len(targets))


def _rows(start, size):
    return pl.ds(pl.multiple_of(start, size), size)


class Gather:
    def __init__(self, buffer, send, recv, stage, size, sib, cnt):
        self.buffer, self.send, self.recv = buffer, send, recv
        self.stage, self.size, self.sib, self.cnt = stage, size, sib, cnt

    def slot(self, r, k):
        return self.buffer.at[_rows((r * 4 + k) * self.size, self.size)]

    def copy(self, r, kind):
        src, dst, target = ((0, 1, self.sib), (0, 2, self.cnt), (2, 3, self.sib))[kind]
        return _remote(
            self.slot(r, src),
            self.slot(r, dst),
            self.send.at[self.stage, kind, r],
            self.recv.at[self.stage, kind, r],
            {"mp": target},
        )

    def start(self, r):
        self.copy(r, 1).start()
        self.copy(r, 0).start()

    def forward(self, r):
        self.copy(r, 1).wait_recv()
        self.copy(r, 2).start()

    def arrive(self, r):
        self.copy(r, 0).wait_recv()
        self.copy(r, 2).wait_recv()

    def sent(self, r):
        for kind in range(3):
            self.copy(r, kind).wait_send()


class Scatter:
    def __init__(self, bufs, send, recv, stage, size, sib, cnt):
        self.own, self.other, self.stage_sib, self.stage_x, self.recv_sib, self.recv_x = bufs
        self.send, self.recv = send, recv
        self.stage, self.size, self.sib, self.cnt = stage, size, sib, cnt

    def copy(self, r, kind):
        rows = _rows(r * self.size, self.size)
        src, dst, target = (
            (self.stage_sib.at[0, rows], self.recv_sib.at[0, rows], self.sib),
            (self.stage_sib.at[1, rows], self.recv_sib.at[1, rows], self.sib),
            (self.stage_x.at[rows], self.recv_x.at[rows], self.cnt),
        )[kind]
        return _remote(
            src, dst, self.send.at[self.stage, kind, r], self.recv.at[self.stage, kind, r], {"mp": target}
        )

    def sent(self, r):
        for kind in range(3):
            self.copy(r, kind).wait_send()

    def project(self, r, tile):
        size = self.size
        rows = _rows(r * size, size)

        def column(n, carry):
            cols = _rows(n * COLS, COLS)
            part = tile(cols)
            self.own[rows, cols] = part[:size]
            self.stage_sib[1, rows, cols] = part[size : 2 * size].astype(jnp.bfloat16)
            self.other[rows, cols] = part[2 * size : 3 * size]
            self.stage_sib[0, rows, cols] = part[3 * size :].astype(jnp.bfloat16)
            return carry

        lax.fori_loop(0, self.own.shape[1] // COLS, column, 0)
        self.copy(r, 0).start()
        self.copy(r, 1).start()

    def finish(self, r):
        rows = _rows(r * self.size, self.size)
        self.copy(r, 0).wait_recv()
        self.stage_x[rows, :] = (
            self.other[rows, :] + self.recv_sib[0, rows, :].astype(jnp.float32)
        ).astype(jnp.bfloat16)
        self.copy(r, 2).start()
        self.copy(r, 1).wait_recv()
        self.own[rows, :] += self.recv_sib[1, rows, :].astype(jnp.float32)

    def result(self, r):
        rows = _rows(r * self.size, self.size)
        self.copy(r, 2).wait_recv()
        return self.own[rows, :] + self.recv_x[rows, :].astype(jnp.float32)


def _scatter_scratch(own, width):
    f32, bf16 = jnp.float32, jnp.bfloat16
    return [
        pltpu.VMEM((own, width), f32),
        pltpu.VMEM((own, width), f32),
        pltpu.VMEM((2, own, width), bf16),
        pltpu.VMEM((own, width), bf16),
        pltpu.VMEM((2, own, width), bf16),
        pltpu.VMEM((own, width), bf16),
    ]


def _norm(summed):
    center = summed - jnp.mean(summed, axis=-1, keepdims=True)
    variance = jnp.mean(center * center, axis=-1, keepdims=True)
    inverse = lax.rsqrt(variance + EPSILON)
    return center * inverse, inverse


def _norm_back(scaled, unit, inverse):
    return inverse * (
        scaled
        - jnp.mean(scaled, axis=-1, keepdims=True)
        - unit * jnp.mean(scaled * unit, axis=-1, keepdims=True)
    )


def project_kernel(
    inputs_ref, in_proj_ref, qv_bias_ref, tokens_ref, qkv_ref, send, recv, local_sem
):
    f32, bf16 = jnp.float32, jnp.bfloat16
    me, sib, cnt, dia = _partners()
    own, width = inputs_ref.shape[0], in_proj_ref.shape[2]
    size = own // CHUNKS
    _greet([{"mp": sib}, {"mp": cnt}])

    def copy(r, kind):
        here = _rows(r * size, size)
        mine, theirs = _rows(me * own + r * size, size), _rows(cnt * own + r * size, size)
        src, place, target = (
            (inputs_ref.at[here], mine, sib),
            (inputs_ref.at[here], mine, cnt),
            (tokens_ref.at[theirs], theirs, sib),
        )[kind]
        return _remote(src, tokens_ref.at[place], send.at[kind, r], recv.at[kind, r], {"mp": target})

    for r in range(CHUNKS):
        copy(r, 1).start()
        copy(r, 0).start()
    keep = pltpu.make_async_copy(inputs_ref, tokens_ref.at[_rows(me * own, own)], local_sem)
    keep.start()

    def compute(block_ref, first, rows):
        place = _rows(first, rows)
        block = block_ref[...]
        for j in range(3):
            part = jnp.dot(block, in_proj_ref[j], preferred_element_type=f32)
            if j != 1:
                part = part + qv_bias_ref[j // 2 : j // 2 + 1, :]
            qkv_ref[place, j * width : (j + 1) * width] = part.astype(bf16)

    def own_part(r, carry):
        compute(inputs_ref.at[_rows(r * size, size)], me * own + r * size, size)
        return carry

    lax.fori_loop(0, CHUNKS, own_part, 0)

    def sib_part(r, carry):
        copy(r, 0).wait_recv()
        first = sib * own + r * size
        compute(tokens_ref.at[_rows(first, size)], first, size)
        return carry

    lax.fori_loop(0, CHUNKS, sib_part, 0)

    def far_part(r, carry):
        copy(r, 1).wait_recv()
        copy(r, 2).start()
        first = cnt * own + r * size
        compute(tokens_ref.at[_rows(first, size)], first, size)
        copy(r, 2).wait_recv()
        first = dia * own + r * size
        compute(tokens_ref.at[_rows(first, size)], first, size)
        return carry

    lax.fori_loop(0, CHUNKS, far_part, 0)
    keep.wait()
    for r in range(CHUNKS):
        for kind in range(3):
            copy(r, kind).wait_send()


def project_tokens(inputs, in_proj, qv_bias):
    own, depth = inputs.shape
    width = in_proj.shape[2]
    vmem = pl.BlockSpec(memory_space=pltpu.VMEM)
    return pl.pallas_call(
        project_kernel,
        out_shape=[
            jax.ShapeDtypeStruct((4 * own, depth), jnp.bfloat16),
            jax.ShapeDtypeStruct((4 * own, 3 * width), jnp.bfloat16),
        ],
        in_specs=[vmem] * 3,
        out_specs=[vmem] * 2,
        scratch_shapes=[
            pltpu.SemaphoreType.DMA((3, CHUNKS)),
            pltpu.SemaphoreType.DMA((3, CHUNKS)),
            pltpu.SemaphoreType.DMA,
        ],
        compiler_params=pltpu.CompilerParams(
            collective_id=0, has_side_effects=True, vmem_limit_bytes=40 * 2**20
        ),
        name="project_tokens",
    )(inputs, in_proj, qv_bias)


def middle_kernel(
    context_ref, inputs_ref, cotangent_ref, out_proj_ref, up_ref, up_bias_ref, down_ref, vectors_ref,
    outputs_ref, grad1_ref, context_grad_ref, down_grad_ref, up_grad_ref, out_grad_ref, sums_ref, up_sum_ref,
    normed_full, grad2_full, grad1_full, active, back, unit1, inverse1, grad2_own, out_acc,
    own_acc, other_acc, stage_sib, stage_x, recv_sib, recv_x,
    gather_send, gather_recv, scatter_send, scatter_recv,
):
    f32, bf16 = jnp.float32, jnp.bfloat16
    me, sib, cnt, dia = _partners()
    own, depth = inputs_ref.shape
    units = up_ref.shape[1]
    size, whole = own // CHUNKS, 4 * own // CHUNKS
    blocks = (me, sib, cnt, dia)
    out_bias, attn_gain, attn_shift, down_bias, ffn_gain, ffn_shift = [
        vectors_ref[k : k + 1, :] for k in range(6)
    ]
    bufs = (own_acc, other_acc, stage_sib, stage_x, recv_sib, recv_x)
    gathers = [
        Gather(buf, gather_send, gather_recv, stage, size, sib, cnt)
        for stage, buf in enumerate((normed_full, grad2_full, grad1_full))
    ]
    scatters = [
        Scatter(bufs, scatter_send, scatter_recv, stage, size, sib, cnt) for stage in range(3)
    ]
    sums_ref[...] = jnp.zeros_like(sums_ref)
    up_sum_ref[...] = jnp.zeros_like(up_sum_ref)
    out_acc[...] = jnp.zeros_like(out_acc)
    _greet([{"mp": sib}, {"mp": cnt}])

    def loop(body):
        def step(r, carry):
            body(r)
            return carry

        lax.fori_loop(0, CHUNKS, step, 0)

    def add_sum(k, value):
        sums_ref[k : k + 1, :] += jnp.sum(value, axis=0, keepdims=True)

    def context_chunk(r):
        return jnp.concatenate(
            [context_ref[_rows(b * own + r * size, size), :] for b in blocks], axis=0
        )

    def attended(r):
        chunk = context_chunk(r)
        scatters[0].project(r, lambda cols: _nn(chunk, out_proj_ref[:, cols]))
        scatters[0].finish(r)

    loop(attended)

    def lower_norm(r):
        rows = _rows(r * size, size)
        unit, inverse = _norm(inputs_ref[rows, :].astype(f32) + scatters[0].result(r) + out_bias)
        unit1[rows, :] = unit
        inverse1[rows, :] = inverse
        gathers[0].slot(r, 0)[...] = (unit * attn_gain + attn_shift).astype(bf16)
        gathers[0].start(r)

    loop(lower_norm)

    def feed_forward(r):
        rows = _rows(r * whole, whole)
        gathers[0].forward(r)
        gathers[0].arrive(r)
        scatters[0].sent(r)

        def column(n, carry):
            cols = _rows(n * COLS, COLS)
            upper = _nn(normed_full[rows, :], up_ref[:, cols]) + up_bias_ref[:, cols]
            cdf = 0.5 + 0.5 * lax.erf(upper * math.sqrt(0.5))
            pdf = jnp.exp(upper * upper * -0.5) * (1.0 / math.sqrt(2.0 * math.pi))
            active[rows, cols] = (upper * cdf).astype(bf16)
            back[rows, cols] = (cdf + upper * pdf).astype(bf16)
            return carry

        lax.fori_loop(0, units // COLS, column, 0)
        scatters[1].project(r, lambda cols: _nn(active[rows, :], down_ref[:, cols]))
        scatters[1].finish(r)

    loop(feed_forward)

    def upper_norm(r):
        rows = _rows(r * size, size)
        normed = unit1[rows, :] * attn_gain + attn_shift
        unit, inverse = _norm(normed + scatters[1].result(r) + down_bias)
        outputs_ref[rows, :] = (unit * ffn_gain + ffn_shift).astype(bf16)
        cotangent = cotangent_ref[rows, :].astype(f32)
        grad = _norm_back(cotangent * ffn_gain, unit, inverse)
        gathers[1].slot(r, 0)[...] = grad.astype(bf16)
        gathers[1].start(r)
        grad2_own[rows, :] = grad
        add_sum(3, grad)
        add_sum(4, cotangent * unit)
        add_sum(5, cotangent)

    loop(upper_norm)

    def feed_back(r):
        rows = _rows(r * whole, whole)
        gathers[1].forward(r)
        gathers[1].arrive(r)
        scatters[1].sent(r)

        def column(n, carry):
            cols = _rows(n * COLS, COLS)
            incoming = _nt(grad2_full[rows, :], down_ref[cols, :])
            upper_back = (back[rows, cols].astype(f32) * incoming).astype(bf16)
            back[rows, cols] = upper_back
            up_sum_ref[:, cols] += jnp.sum(upper_back.astype(f32), axis=0, keepdims=True)
            return carry

        lax.fori_loop(0, units // COLS, column, 0)
        scatters[2].project(r, lambda cols: _nt(back[rows, :], up_ref[cols, :]))
        scatters[2].finish(r)

    loop(feed_back)

    def weights(r):
        cols = _rows(r * (units // CHUNKS), units // CHUNKS)
        down_grad_ref[cols, :] = _tn(active[:, cols], grad2_full[...]).astype(bf16)
        cols = _rows(r * (depth // CHUNKS), depth // CHUNKS)
        up_grad_ref[cols, :] = _tn(normed_full[:, cols], back[...]).astype(bf16)

    def lower_back(r):
        weights(r)
        rows = _rows(r * size, size)
        incoming = grad2_own[rows, :] + scatters[2].result(r)
        unit = unit1[rows, :]
        grad = _norm_back(incoming * attn_gain, unit, inverse1[rows, :])
        gathers[2].slot(r, 0)[...] = grad.astype(bf16)
        gathers[2].start(r)
        grad1_ref[rows, :] = grad
        add_sum(0, grad)
        add_sum(1, incoming * unit)
        add_sum(2, incoming)

    loop(lower_back)

    def context_back(r):
        rows = _rows(r * whole, whole)
        gathers[2].forward(r)
        gathers[2].arrive(r)
        scatters[2].sent(r)
        incoming = grad1_full[rows, :]
        grad = _nt(incoming, out_proj_ref[...]).astype(bf16)
        for k, b in enumerate(blocks):
            context_grad_ref[_rows(b * own + r * size, size), :] = grad[k * size : (k + 1) * size]
        out_acc[...] += _tn(incoming, context_chunk(r))

    loop(context_back)
    out_grad_ref[...] = out_acc[...].astype(bf16)

    def drain(r):
        for gather in gathers:
            gather.sent(r)

    loop(drain)


def middle(context, inputs, cotangent, out_proj, up_proj, up_bias, down_proj, vectors):
    f32, bf16 = jnp.float32, jnp.bfloat16
    own, depth = inputs.shape
    units, width = up_proj.shape[1], out_proj.shape[0]
    whole = 4 * own
    vmem = pl.BlockSpec(memory_space=pltpu.VMEM)
    outs = [
        ((own, depth), bf16),
        ((own, depth), f32),
        ((whole, width), bf16),
        ((units, depth), bf16),
        ((depth, units), bf16),
        ((depth, width), bf16),
        ((8, depth), f32),
        ((1, units), f32),
    ]
    return pl.pallas_call(
        middle_kernel,
        out_shape=[jax.ShapeDtypeStruct(*out) for out in outs],
        in_specs=[vmem] * 8,
        out_specs=[vmem] * 8,
        scratch_shapes=[
            pltpu.VMEM((whole, depth), bf16),
            pltpu.VMEM((whole, depth), bf16),
            pltpu.VMEM((whole, depth), bf16),
            pltpu.VMEM((whole, units), bf16),
            pltpu.VMEM((whole, units), bf16),
            pltpu.VMEM((own, depth), f32),
            pltpu.VMEM((own, 1), f32),
            pltpu.VMEM((own, depth), f32),
            pltpu.VMEM((depth, width), f32),
            *_scatter_scratch(own, depth),
            pltpu.SemaphoreType.DMA((3, 3, CHUNKS)),
            pltpu.SemaphoreType.DMA((3, 3, CHUNKS)),
            pltpu.SemaphoreType.DMA((3, 3, CHUNKS)),
            pltpu.SemaphoreType.DMA((3, 3, CHUNKS)),
        ],
        compiler_params=pltpu.CompilerParams(
            collective_id=1, has_side_effects=True, vmem_limit_bytes=63 * 2**20
        ),
        name="middle_layer",
    )(context, inputs, cotangent, out_proj, up_proj, up_bias, down_proj, vectors)


class Reduce:
    def __init__(self, matrix, rows, source, half_recv, shard_recv, final, sems, place):
        self.matrix, self.rows, self.source = matrix, rows, source
        self.half_recv, self.shard_recv, self.final, self.sems = half_recv, shard_recv, final, sems
        self.y, self.z, self.group = place
        self.half = rows // 2
        self.shard = self.half // self.group

    def peer(self, g):
        return {"dp": lax.rem(self.z + g, self.group) * 2 + self.y}

    def pair(self):
        return {"dp": self.z * 2 + 1 - self.y}

    def sem(self, p, kind):
        return self.sems.at[0, self.matrix, p, kind], self.sems.at[1, self.matrix, p, kind]

    def halves(self, p):
        return self.half_recv.at[self.matrix, _rows(p * self.half, self.half)]

    def first(self, p):
        there = p * self.rows + (1 - self.y) * self.half
        return _remote(
            self.source.at[_rows(there, self.half)], self.halves(p), *self.sem(p, 0), self.pair()
        )

    def shards(self, p):
        return [
            _remote(
                self.half_recv.at[
                    self.matrix,
                    _rows(p * self.half + lax.rem(self.z + g, self.group) * self.shard, self.shard),
                ],
                self.shard_recv.at[self.matrix, p, g - 1],
                *self.sem(p, 1),
                self.peer(g),
            )
            for g in range(1, self.group)
        ]

    def mine(self, p):
        return p * self.rows + self.y * self.half

    def spread(self, p):
        place = _rows(self.mine(p) + self.z * self.shard, self.shard)
        block = self.final.at[self.matrix, place]
        return [_remote(block, block, *self.sem(p, 2), self.peer(g)) for g in range(1, self.group)]

    def last(self, p):
        block = self.final.at[self.matrix, _rows(self.mine(p), self.half)]
        return _remote(block, block, *self.sem(p, 3), self.pair())

    def wait_all(self, p, kind, side):
        block = self.shard_recv.at[self.matrix, p]
        pltpu.make_async_copy(block, block, self.sem(p, kind)[side]).wait()

    def send_half(self, p):
        self.first(p).start()

    def send_shards(self, p):
        self.first(p).wait_recv()
        place = _rows(p * self.half, self.half)
        self.half_recv[self.matrix, place, :] = (
            self.half_recv[self.matrix, place, :].astype(jnp.float32)
            + self.source[_rows(self.mine(p), self.half), :].astype(jnp.float32)
        ).astype(jnp.bfloat16)
        for copy in self.shards(p):
            copy.start()

    def send_sum(self, p):
        self.wait_all(p, 1, 1)
        place = _rows(p * self.half + self.z * self.shard, self.shard)
        total = self.half_recv[self.matrix, place, :].astype(jnp.float32)
        for g in range(1, self.group):
            total = total + self.shard_recv[self.matrix, p, g - 1].astype(jnp.float32)
        self.final[self.matrix, _rows(self.mine(p) + self.z * self.shard, self.shard), :] = (
            total.astype(jnp.bfloat16)
        )
        for copy in self.spread(p):
            copy.start()

    def send_back(self, p):
        self.wait_all(p, 2, 1)
        self.last(p).start()

    def end(self, p):
        self.last(p).wait_recv()
        self.first(p).wait_send()
        self.wait_all(p, 1, 0)
        self.wait_all(p, 2, 0)
        self.last(p).wait_send()


def last_kernel(
    group, pieces, grads_ref, tokens_ref, in_proj_ref, grad1_ref, down_grad_ref, up_grad_ref, out_grad_ref,
    sums_ref, up_sum_ref, inputs_grad_ref, final_ref, small_ref,
    own_acc, other_acc, stage_sib, stage_x, recv_sib, recv_x, attn_grad, half_recv, shard_recv,
    small_recv, small_group, scatter_send, scatter_recv, sems, small_sems,
):
    f32, bf16 = jnp.float32, jnp.bfloat16
    me, sib, cnt, dia = _partners()
    dp = lax.axis_index("dp")
    y, z = lax.rem(dp, 2), dp // 2
    own, depth = grad1_ref.shape
    width = in_proj_ref.shape[2]
    size = own // CHUNKS
    blocks = (me, sib, cnt, dia)
    bufs = (own_acc, other_acc, stage_sib, stage_x, recv_sib, recv_x)
    scatter = Scatter(bufs, scatter_send, scatter_recv, 0, size, sib, cnt)
    reduces = [
        Reduce(k, depth // pieces, source, half_recv, shard_recv, final_ref, sems, (y, z, group))
        for k, source in enumerate((down_grad_ref, up_grad_ref, attn_grad))
    ]
    down, up, attn = reduces

    def loop(body, count):
        def step(r, carry):
            body(r)
            return carry

        lax.fori_loop(0, count, step, 0)

    small_ref[...] = jnp.zeros_like(small_ref)
    small_ref[:8, :] = sums_ref[...]
    small_ref[8:9, :] = up_sum_ref[...]
    _greet([{"mp": sib}, {"mp": cnt}, down.pair(), *[down.peer(g) for g in range(1, group)]])
    for reduce in (down, up):
        for p in range(pieces):
            reduce.send_half(p)

    def partial_rows(r):
        chunk = jnp.concatenate(
            [grads_ref[_rows(b * own + r * size, size), :] for b in blocks], axis=0
        )

        def tile(cols):
            total = _nt(chunk[:, :width], in_proj_ref[0, cols, :])
            total = total + _nt(chunk[:, width : 2 * width], in_proj_ref[1, cols, :])
            return total + _nt(chunk[:, 2 * width :], in_proj_ref[2, cols, :])

        scatter.project(r, tile)
        scatter.finish(r)

    loop(partial_rows, CHUNKS)

    def weights(n):
        cols = _rows(n * COLS, COLS)
        attn_grad[cols, : 3 * width] = _tn(tokens_ref[:, cols], grads_ref[...]).astype(bf16)
        attn_grad[cols, 3 * width :] = out_grad_ref[cols, :]

    loop(weights, depth // COLS)
    for p in range(pieces):
        attn.send_half(p)

    def bias(j):
        return jnp.sum(grads_ref[:, j * width : (j + 1) * width].astype(f32), axis=0, keepdims=True)

    small_ref[9:10, :width] = bias(0)
    small_ref[9:10, width : 2 * width] = bias(2)

    def small_step(k, rows, target):
        copy = _remote(
            small_ref.at[:rows], small_recv.at[k, :rows], small_sems.at[0, k], small_sems.at[1, k], target
        )
        copy.start()
        copy.wait()
        small_ref[:rows, :] += small_recv[k, :rows, :]

    small_step(0, 8, {"mp": sib})
    small_step(1, 8, {"mp": cnt})
    loop(down.send_shards, pieces)
    small_step(2, small_ref.shape[0], down.pair())
    small_copies = [
        _remote(
            small_ref, small_group.at[z], small_sems.at[0, 3], small_sems.at[1, 3], down.peer(g)
        )
        for g in range(1, group)
    ]
    for copy in small_copies:
        copy.start()
    small_group[z] = small_ref[...]
    loop(down.send_sum, pieces)
    loop(up.send_shards, pieces)

    def finish(r):
        rows = _rows(r * size, size)
        inputs_grad_ref[rows, :] = (grad1_ref[rows, :] + scatter.result(r)).astype(bf16)
        scatter.sent(r)

    loop(down.send_back, pieces)
    loop(up.send_sum, pieces)
    loop(finish, CHUNKS)
    loop(attn.send_shards, pieces)
    loop(up.send_back, pieces)
    loop(attn.send_sum, pieces)
    others = small_group.at[1:]
    for side in (1, 0):
        pltpu.make_async_copy(others, others, small_sems.at[side, 3]).wait()
    total = small_group[0]
    for g in range(1, group):
        total = total + small_group[g]
    small_ref[...] = total
    loop(attn.send_back, pieces)
    loop(down.end, pieces)
    loop(up.end, pieces)
    loop(attn.end, pieces)


def last(mesh, grads, tokens, in_proj, grad1, down_grad, up_grad, out_grad, sums, up_sum):
    f32, bf16 = jnp.float32, jnp.bfloat16
    own, depth = grad1.shape
    group = mesh.shape["dp"] // 2
    pieces = max(1, min(4, depth // (32 * group)))
    half = depth // 2
    shard = half // pieces // group
    vmem = pl.BlockSpec(memory_space=pltpu.VMEM)
    return pl.pallas_call(
        partial(last_kernel, group, pieces),
        out_shape=[
            jax.ShapeDtypeStruct((own, depth), bf16),
            jax.ShapeDtypeStruct((3, depth, depth), bf16),
            jax.ShapeDtypeStruct((16, depth), f32),
        ],
        in_specs=[vmem] * 9,
        out_specs=[vmem] * 3,
        scratch_shapes=[
            *_scatter_scratch(own, depth),
            pltpu.VMEM((depth, depth), bf16),
            pltpu.VMEM((3, half, depth), bf16),
            pltpu.VMEM((3, pieces, group - 1, shard, depth), bf16),
            pltpu.VMEM((3, 16, depth), f32),
            pltpu.VMEM((group, 16, depth), f32),
            pltpu.SemaphoreType.DMA((1, 3, CHUNKS)),
            pltpu.SemaphoreType.DMA((1, 3, CHUNKS)),
            pltpu.SemaphoreType.DMA((2, 3, pieces, 4)),
            pltpu.SemaphoreType.DMA((2, 4)),
        ],
        compiler_params=pltpu.CompilerParams(
            collective_id=2, has_side_effects=True, vmem_limit_bytes=60 * 2**20
        ),
        name="last_layer",
    )(grads, tokens, in_proj, grad1, down_grad, up_grad, out_grad, sums, up_sum)


def shards(
    mesh,
    inputs,
    in_proj,
    qv_bias,
    out_proj,
    out_bias,
    attn_gain,
    attn_shift,
    up_proj,
    up_bias,
    down_proj,
    down_bias,
    ffn_gain,
    ffn_shift,
    segments,
    padding,
    cotangent,
):
    f32 = jnp.float32
    width = in_proj.shape[2]
    where = segment_places(segments, padding)
    vectors = jnp.stack([out_bias, attn_gain, attn_shift, down_bias, ffn_gain, ffn_shift])
    tokens, qkv = project_tokens(inputs, in_proj, qv_bias)
    context, lse_rows = attention_forward(qkv, where)
    outputs, grad1, context_grad, down_grad, up_grad, out_grad, sums, up_sum = middle(
        context, inputs, cotangent, out_proj, up_proj, up_bias[None], down_proj, vectors
    )
    grads = attention_backward(qkv, context_grad, context, lse_rows, where)
    inputs_grad, final, small = last(
        mesh, grads, tokens, in_proj, grad1, down_grad, up_grad, out_grad, sums, up_sum
    )
    attn = final[2].astype(f32)
    in_grad = jnp.stack([attn[:, j * width : (j + 1) * width] for j in range(3)])
    return (
        outputs,
        inputs_grad,
        in_grad,
        small[9, : 2 * width].reshape(2, width),
        attn[:, 3 * width :].T,
        small[0],
        small[1],
        small[2],
        final[1].astype(f32),
        small[8],
        final[0].astype(f32),
        small[3],
        small[4],
        small[5],
    )


def solution(mesh):
    return jax.shard_map(
        partial(shards, mesh),
        mesh=mesh,
        in_specs=(
            P(("dp", "mp"), None),
            P(None, None, "mp"),
            P(None, "mp"),
            P("mp", None),
            P(),
            P(),
            P(),
            P(None, "mp"),
            P("mp"),
            P("mp", None),
            P(),
            P(),
            P(),
            P("dp", None),
            P("dp", None),
            P(("dp", "mp"), None),
        ),
        out_specs=(
            P(("dp", "mp"), None),
            P(("dp", "mp"), None),
            P(None, None, "mp"),
            P(None, "mp"),
            P("mp", None),
            P(),
            P(),
            P(),
            P(None, "mp"),
            P("mp"),
            P("mp", None),
            P(),
            P(),
            P(),
        ),
        check_vma=False,
    )
```

```python
from functools import partial
import math

import jax
import jax.numpy as jnp
from jax import lax
from jax.experimental import pallas as pl
from jax.experimental.pallas import tpu as pltpu
from jax.sharding import PartitionSpec as P

HEAD = 64
BLOCK = 256
CHUNKS = 4
EARLY = ((0, 0), (0, 1), (0, 2), (0, 3), (1, 0))
COLS = 256
MESH = pl.DeviceIdType.MESH


EPSILON = 1e-05


NEG = -1e30


def _mask_bias(seg_q, pad_q, seg_k, pad_k):
    allowed = (seg_q == seg_k) & ((pad_k > 0) | (pad_q == 0))
    return jnp.where(allowed, 0.0, NEG).astype(jnp.float32)


def _head_masks(heads, width, value):
    lane = lax.broadcasted_iota(jnp.int32, (1, width), 1) // HEAD
    return [jnp.where(lane == h, value, 0.0).astype(jnp.bfloat16) for h in range(heads)]


def _nt(a, b):
    return lax.dot_general(a, b, (((1,), (1,)), ((), ())), preferred_element_type=jnp.float32)


def _tn(a, b):
    return lax.dot_general(a, b, (((0,), (0,)), ((), ())), preferred_element_type=jnp.float32)


def _nn(a, b):
    return jnp.dot(a, b, preferred_element_type=jnp.float32)


def attention_forward_kernel(
    heads, blocks, ends_ref, query_ref, keys_ref, values_ref, seg_col, pad_col, seg_row, pad_row,
    context_ref, lse_ref, peak_ref, total_ref, acc_ref,
):
    f32, bf16 = jnp.float32, jnp.bfloat16
    i = pl.program_id(0)
    width = query_ref.shape[1]
    scaled = _head_masks(heads, width, 1.0 / math.sqrt(HEAD))
    plain = _head_masks(heads, width, 1.0)
    lane = lax.broadcasted_iota(jnp.int32, (1, width), 1) // HEAD
    column = lax.broadcasted_iota(jnp.int32, (1, 128), 1)
    query = query_ref[...]

    def parts(j):
        rows = pl.ds(pl.multiple_of(j * BLOCK, BLOCK), BLOCK)
        bias = _mask_bias(seg_col[...], pad_col[...], seg_row[:, rows], pad_row[:, rows])
        return keys_ref[rows, :], values_ref[rows, :], bias

    key, value, bias = parts(i)
    acc = jnp.zeros((BLOCK, width), f32)
    for h in range(heads):
        scores = _nt(query * scaled[h], key) + bias
        peak = jnp.max(scores, axis=-1, keepdims=True)
        expo = jnp.exp(scores - peak)
        peak_ref[h] = peak
        total_ref[h] = jnp.sum(expo, axis=-1, keepdims=True)
        acc = acc + _nn(expo.astype(bf16), value * plain[h])
    acc_ref[...] = acc

    def other(j, carry):
        meets = (j != i) & (ends_ref[0, j] <= ends_ref[1, i]) & (ends_ref[1, j] >= ends_ref[0, i])

        @pl.when(meets)
        def _():
            key, value, bias = parts(j)
            shrink = jnp.zeros((BLOCK, width), f32)
            add = jnp.zeros((BLOCK, width), f32)
            for h in range(heads):
                scores = _nt(query * scaled[h], key) + bias
                old = peak_ref[h]
                peak = jnp.maximum(old, jnp.max(scores, axis=-1, keepdims=True))
                expo = jnp.exp(scores - peak)
                ratio = jnp.exp(old - peak)
                peak_ref[h] = peak
                total_ref[h] = total_ref[h] * ratio + jnp.sum(expo, axis=-1, keepdims=True)
                shrink = jnp.where(lane == h, ratio, shrink)
                add = add + _nn(expo.astype(bf16), value * plain[h])
            acc_ref[...] = acc_ref[...] * shrink + add

        return carry

    lax.fori_loop(0, blocks, other, 0)
    inverse = jnp.zeros((BLOCK, width), f32)
    lse = jnp.zeros((BLOCK, 128), f32)
    for h in range(heads):
        total = total_ref[h]
        inverse = jnp.where(lane == h, 1.0 / total, inverse)
        lse = jnp.where(column == h, peak_ref[h] + jnp.log(total), lse)
    context_ref[...] = (acc_ref[...] * inverse).astype(bf16)
    lse_ref[...] = lse


def attention_backward_kernel(
    heads, blocks, ends_ref, query_ref, keys_ref, values_ref, grad_ref, context_ref, lse_ref,
    seg_col, pad_col, seg_row, pad_row, grads_ref, query_acc, keys_acc, values_acc,
):
    f32, bf16 = jnp.float32, jnp.bfloat16
    i = pl.program_id(0)
    width = query_ref.shape[1]
    scaled = _head_masks(heads, width, 1.0 / math.sqrt(HEAD))
    plain = _head_masks(heads, width, 1.0)

    @pl.when(i == 0)
    def _():
        keys_acc[...] = jnp.zeros_like(keys_acc)
        values_acc[...] = jnp.zeros_like(values_acc)

    query, grad = query_ref[...], grad_ref[...]
    product = grad.astype(f32) * context_ref[...].astype(f32)

    def block(j):
        rows = pl.ds(pl.multiple_of(j * BLOCK, BLOCK), BLOCK)
        bias = _mask_bias(seg_col[...], pad_col[...], seg_row[:, rows], pad_row[:, rows])
        key, value = keys_ref[rows, :], values_ref[rows, :]
        query_add = jnp.zeros((BLOCK, width), f32)
        key_add = jnp.zeros((BLOCK, width), f32)
        value_add = jnp.zeros((BLOCK, width), f32)
        for h in range(heads):
            query_h, grad_h = query * scaled[h], grad * plain[h]
            scores = _nt(query_h, key) + bias
            prob = jnp.exp(scores - lse_ref[:, h : h + 1])
            prob_grad = _nt(grad_h, value)
            row_dot = jnp.sum(product * plain[h].astype(f32), axis=-1, keepdims=True)
            score_grad = (prob * (prob_grad - row_dot)).astype(bf16)
            query_add = query_add + _nn(score_grad, key * scaled[h])
            key_add = key_add + _tn(score_grad, query_h)
            value_add = value_add + _tn(prob.astype(bf16), grad_h)
        keys_acc[rows, :] += key_add
        values_acc[rows, :] += value_add
        return query_add

    query_acc[...] = block(i)

    def other(j, carry):
        meets = (j != i) & (ends_ref[0, j] <= ends_ref[1, i]) & (ends_ref[1, j] >= ends_ref[0, i])

        @pl.when(meets)
        def _():
            query_acc[...] += block(j)

        return carry

    lax.fori_loop(0, blocks, other, 0)
    grads_ref[pl.ds(pl.multiple_of(i * BLOCK, BLOCK), BLOCK), :width] = query_acc[...].astype(bf16)

    @pl.when(i == blocks - 1)
    def _():
        grads_ref[:, width : 2 * width] = keys_acc[...].astype(bf16)
        grads_ref[:, 2 * width :] = values_acc[...].astype(bf16)


def _attention_specs(length, width):
    block = pl.BlockSpec((BLOCK, width), lambda i, ends: (i, 0))
    keys = pl.BlockSpec((length, width), lambda i, ends: (0, 1))
    values = pl.BlockSpec((length, width), lambda i, ends: (0, 2))
    col = pl.BlockSpec((BLOCK, 1), lambda i, ends: (i, 0))
    row = pl.BlockSpec((1, length), lambda i, ends: (0, 0))
    lse = pl.BlockSpec((BLOCK, 128), lambda i, ends: (i, 0))
    return block, keys, values, col, row, lse


def attention_forward(qkv, where):
    length, width = qkv.shape[0], qkv.shape[1] // 3
    heads, blocks = width // HEAD, length // BLOCK
    block, keys, values, col, row, lse = _attention_specs(length, width)
    return pl.pallas_call(
        partial(attention_forward_kernel, heads, blocks),
        grid_spec=pltpu.PrefetchScalarGridSpec(
            num_scalar_prefetch=1,
            grid=(blocks,),
            in_specs=[block, keys, values, col, col, row, row],
            out_specs=[block, lse],
            scratch_shapes=[
                pltpu.VMEM((heads, BLOCK, 1), jnp.float32),
                pltpu.VMEM((heads, BLOCK, 1), jnp.float32),
                pltpu.VMEM((BLOCK, width), jnp.float32),
            ],
        ),
        out_shape=[
            jax.ShapeDtypeStruct((length, width), jnp.bfloat16),
            jax.ShapeDtypeStruct((length, 128), jnp.float32),
        ],
        compiler_params=pltpu.CompilerParams(vmem_limit_bytes=32 * 2**20),
        name="attention_forward",
    )(where[0], qkv, qkv, qkv, *where[1:])


def attention_backward(qkv, grad, context, lse_rows, where):
    length, width = grad.shape
    heads, blocks = width // HEAD, length // BLOCK
    block, keys, values, col, row, lse = _attention_specs(length, width)
    return pl.pallas_call(
        partial(attention_backward_kernel, heads, blocks),
        grid_spec=pltpu.PrefetchScalarGridSpec(
            num_scalar_prefetch=1,
            grid=(blocks,),
            in_specs=[block, keys, values, block, block, lse, col, col, row, row],
            out_specs=pl.BlockSpec((length, 3 * width), lambda i, ends: (0, 0)),
            scratch_shapes=[
                pltpu.VMEM((BLOCK, width), jnp.float32),
                pltpu.VMEM((length, width), jnp.float32),
                pltpu.VMEM((length, width), jnp.float32),
            ],
        ),
        out_shape=jax.ShapeDtypeStruct((length, 3 * width), jnp.bfloat16),
        compiler_params=pltpu.CompilerParams(vmem_limit_bytes=32 * 2**20),
        name="attention_backward",
    )(where[0], qkv, qkv, qkv, grad, context, lse_rows, *where[1:])


def segment_places(segments, padding):
    row_count, seq_len = segments.shape
    seg = segments + jnp.arange(row_count, dtype=jnp.int32)[:, None] * (seq_len + 1)
    seg, pad = seg.reshape(-1), padding.reshape(-1)
    ends = jnp.stack([seg[::BLOCK], seg[BLOCK - 1 :: BLOCK]])
    return (ends, seg[:, None], pad[:, None], seg[None, :], pad[None, :])


def _partners():
    me = lax.axis_index("mp")
    core = lax.rem(me, 2)
    sib = me + 1 - 2 * core
    cnt = lax.rem(me + 2, 4)
    dia = lax.rem(cnt + 1, 2) + cnt - lax.rem(cnt, 2)
    return me, sib, cnt, dia


def _remote(src, dst, send, recv, target):
    return pltpu.make_async_remote_copy(
        src_ref=src, dst_ref=dst, send_sem=send, recv_sem=recv, device_id=target, device_id_type=MESH
    )


def _greet(targets):
    barrier = pltpu.get_barrier_semaphore()
    for target in targets:
        pl.semaphore_signal(barrier, inc=1, device_id=target, device_id_type=MESH)
    pl.semaphore_wait(barrier, len(targets))


def _rows(start, size):
    return pl.ds(pl.multiple_of(start, size), size)


class Gather:
    def __init__(self, buffer, send, recv, stage, size, sib, cnt):
        self.buffer, self.send, self.recv = buffer, send, recv
        self.stage, self.size, self.sib, self.cnt = stage, size, sib, cnt

    def slot(self, r, k):
        return self.buffer.at[_rows((r * 4 + k) * self.size, self.size)]

    def copy(self, r, kind):
        src, dst, target = ((0, 1, self.sib), (0, 2, self.cnt), (2, 3, self.sib))[kind]
        return _remote(
            self.slot(r, src),
            self.slot(r, dst),
            self.send.at[self.stage, kind, r],
            self.recv.at[self.stage, kind, r],
            {"mp": target},
        )

    def start(self, r):
        self.copy(r, 1).start()
        self.copy(r, 0).start()

    def forward(self, r):
        self.copy(r, 1).wait_recv()
        self.copy(r, 2).start()

    def arrive(self, r):
        self.copy(r, 0).wait_recv()
        self.copy(r, 2).wait_recv()

    def sent(self, r):
        for kind in range(3):
            self.copy(r, kind).wait_send()


class Scatter:
    def __init__(self, bufs, send, recv, stage, size, sib, cnt):
        self.own, self.other, self.stage_sib, self.stage_x, self.recv_sib, self.recv_x = bufs
        self.send, self.recv = send, recv
        self.stage, self.size, self.sib, self.cnt = stage, size, sib, cnt

    def copy(self, r, kind):
        rows = _rows(r * self.size, self.size)
        src, dst, target = (
            (self.stage_sib.at[0, rows], self.recv_sib.at[0, rows], self.sib),
            (self.stage_sib.at[1, rows], self.recv_sib.at[1, rows], self.sib),
            (self.stage_x.at[rows], self.recv_x.at[rows], self.cnt),
        )[kind]
        return _remote(
            src, dst, self.send.at[self.stage, kind, r], self.recv.at[self.stage, kind, r], {"mp": target}
        )

    def sent(self, r):
        for kind in range(3):
            self.copy(r, kind).wait_send()

    def project(self, r, tile):
        size = self.size
        rows = _rows(r * size, size)

        def column(n, carry):
            cols = _rows(n * COLS, COLS)
            part = tile(cols)
            self.own[rows, cols] = part[:size]
            self.stage_sib[1, rows, cols] = part[size : 2 * size].astype(jnp.bfloat16)
            self.other[rows, cols] = part[2 * size : 3 * size]
            self.stage_sib[0, rows, cols] = part[3 * size :].astype(jnp.bfloat16)
            return carry

        lax.fori_loop(0, self.own.shape[1] // COLS, column, 0)
        self.copy(r, 0).start()
        self.copy(r, 1).start()

    def finish(self, r):
        rows = _rows(r * self.size, self.size)
        self.copy(r, 0).wait_recv()
        self.stage_x[rows, :] = (
            self.other[rows, :] + self.recv_sib[0, rows, :].astype(jnp.float32)
        ).astype(jnp.bfloat16)
        self.copy(r, 2).start()
        self.copy(r, 1).wait_recv()
        self.own[rows, :] += self.recv_sib[1, rows, :].astype(jnp.float32)

    def result(self, r):
        rows = _rows(r * self.size, self.size)
        self.copy(r, 2).wait_recv()
        return self.own[rows, :] + self.recv_x[rows, :].astype(jnp.float32)


def _scatter_scratch(own, width):
    f32, bf16 = jnp.float32, jnp.bfloat16
    return [
        pltpu.VMEM((own, width), f32),
        pltpu.VMEM((own, width), f32),
        pltpu.VMEM((2, own, width), bf16),
        pltpu.VMEM((own, width), bf16),
        pltpu.VMEM((2, own, width), bf16),
        pltpu.VMEM((own, width), bf16),
    ]


def _norm(summed):
    center = summed - jnp.mean(summed, axis=-1, keepdims=True)
    variance = jnp.mean(center * center, axis=-1, keepdims=True)
    inverse = lax.rsqrt(variance + EPSILON)
    return center * inverse, inverse


def _norm_back(scaled, unit, inverse):
    return inverse * (
        scaled
        - jnp.mean(scaled, axis=-1, keepdims=True)
        - unit * jnp.mean(scaled * unit, axis=-1, keepdims=True)
    )


def project_kernel(
    inputs_ref, in_proj_ref, qv_bias_ref, tokens_ref, qkv_ref, send, recv, local_sem
):
    f32, bf16 = jnp.float32, jnp.bfloat16
    me, sib, cnt, dia = _partners()
    own, width = inputs_ref.shape[0], in_proj_ref.shape[2]
    size = own // CHUNKS
    _greet([{"mp": sib}, {"mp": cnt}])

    def copy(r, kind):
        here = _rows(r * size, size)
        mine, theirs = _rows(me * own + r * size, size), _rows(cnt * own + r * size, size)
        src, place, target = (
            (inputs_ref.at[here], mine, sib),
            (inputs_ref.at[here], mine, cnt),
            (tokens_ref.at[theirs], theirs, sib),
        )[kind]
        return _remote(src, tokens_ref.at[place], send.at[kind, r], recv.at[kind, r], {"mp": target})

    for r in range(CHUNKS):
        copy(r, 1).start()
        copy(r, 0).start()
    keep = pltpu.make_async_copy(inputs_ref, tokens_ref.at[_rows(me * own, own)], local_sem)
    keep.start()

    def compute(block_ref, first, rows):
        place = _rows(first, rows)
        block = block_ref[...]
        for j in range(3):
            part = jnp.dot(block, in_proj_ref[j], preferred_element_type=f32)
            if j != 1:
                part = part + qv_bias_ref[j // 2 : j // 2 + 1, :]
            qkv_ref[place, j * width : (j + 1) * width] = part.astype(bf16)

    def own_part(r, carry):
        compute(inputs_ref.at[_rows(r * size, size)], me * own + r * size, size)
        return carry

    lax.fori_loop(0, CHUNKS, own_part, 0)

    def sib_part(r, carry):
        copy(r, 0).wait_recv()
        first = sib * own + r * size
        compute(tokens_ref.at[_rows(first, size)], first, size)
        return carry

    lax.fori_loop(0, CHUNKS, sib_part, 0)

    def far_part(r, carry):
        copy(r, 1).wait_recv()
        copy(r, 2).start()
        first = cnt * own + r * size
        compute(tokens_ref.at[_rows(first, size)], first, size)
        copy(r, 2).wait_recv()
        first = dia * own + r * size
        compute(tokens_ref.at[_rows(first, size)], first, size)
        return carry

    lax.fori_loop(0, CHUNKS, far_part, 0)
    keep.wait()
    for r in range(CHUNKS):
        for kind in range(3):
            copy(r, kind).wait_send()


def project_tokens(inputs, in_proj, qv_bias):
    own, depth = inputs.shape
    width = in_proj.shape[2]
    vmem = pl.BlockSpec(memory_space=pltpu.VMEM)
    return pl.pallas_call(
        project_kernel,
        out_shape=[
            jax.ShapeDtypeStruct((4 * own, depth), jnp.bfloat16),
            jax.ShapeDtypeStruct((4 * own, 3 * width), jnp.bfloat16),
        ],
        in_specs=[vmem] * 3,
        out_specs=[vmem] * 2,
        scratch_shapes=[
            pltpu.SemaphoreType.DMA((3, CHUNKS)),
            pltpu.SemaphoreType.DMA((3, CHUNKS)),
            pltpu.SemaphoreType.DMA,
        ],
        compiler_params=pltpu.CompilerParams(
            collective_id=0, has_side_effects=True, vmem_limit_bytes=40 * 2**20
        ),
        name="project_tokens",
    )(inputs, in_proj, qv_bias)


class Reduce:
    def __init__(self, matrix, rows, place, sems, source=None, halves=None, shards=None, final=None):
        self.matrix, self.rows, self.sems = matrix, rows, sems
        self.source, self.halves, self.shards, self.final = source, halves, shards, final
        self.y, self.z, self.group = place
        self.half = rows // 2
        self.shard = self.half // self.group

    def peer(self, g):
        return {"dp": lax.rem(self.z + g, self.group) * 2 + self.y}

    def pair(self):
        return {"dp": self.z * 2 + 1 - self.y}

    def sem(self, p, kind):
        return self.sems.at[0, self.matrix, p, kind], self.sems.at[1, self.matrix, p, kind]

    def half_rows(self, p, y):
        return _rows(p * self.rows + y * self.half, self.half)

    def first(self, p):
        return _remote(
            self.source.at[self.half_rows(p, 1 - self.y)],
            self.halves.at[_rows(p * self.half, self.half)],
            *self.sem(p, 0),
            self.pair(),
        )

    def wait_all(self, shards, p, kind, side):
        block = shards.at[p]
        pltpu.make_async_copy(block, block, self.sem(p, kind)[side]).wait()

    def send_half(self, p):
        self.first(p).start()

    def add_half(self, p):
        self.first(p).wait_recv()
        place = _rows(p * self.half, self.half)
        self.halves[place, :] = (
            self.halves[place, :].astype(jnp.float32)
            + self.source[self.half_rows(p, self.y), :].astype(jnp.float32)
        ).astype(jnp.bfloat16)

    def send_shards(self, p):
        for g in range(1, self.group):
            place = p * self.half + lax.rem(self.z + g, self.group) * self.shard
            _remote(
                self.halves.at[_rows(place, self.shard)],
                self.shards.at[p, g - 1],
                *self.sem(p, 1),
                self.peer(g),
            ).start()

    def send_sum(self, p, shards, block):
        total = self.halves[_rows(p * self.half + self.z * self.shard, self.shard), :].astype(jnp.float32)
        for g in range(1, self.group):
            total = total + shards[p, g - 1].astype(jnp.float32)
        mine = block.at[_rows(self.z * self.shard, self.shard)]
        mine[...] = total.astype(jnp.bfloat16)
        for g in range(1, self.group):
            _remote(mine, mine, *self.sem(p, 2), self.peer(g)).start()

    def final_half(self, p):
        return self.final.at[self.half_rows(p, self.y)]

    def last(self, p, block=None):
        there = self.final_half(p)
        return _remote(there if block is None else block, there, *self.sem(p, 3), self.pair())


def middle_kernel(
    group, pieces, context_ref, inputs_ref, cotangent_ref, out_proj_ref, up_ref, up_bias_ref, down_ref, vectors_ref,
    outputs_ref, grad1_ref, context_grad_ref, halves_ref, shards_ref, block_ref, out_grad_ref, sums_ref, up_sum_ref,
    down_grad, up_grad, normed_full, grad2_full, grad1_full, active, back, unit1, inverse1, grad2_own, out_acc,
    own_acc, other_acc, stage_sib, stage_x, recv_sib, recv_x,
    gather_send, gather_recv, scatter_send, scatter_recv, sems,
):
    f32, bf16 = jnp.float32, jnp.bfloat16
    me, sib, cnt, dia = _partners()
    place = _place(group)
    own, depth = inputs_ref.shape
    units = up_ref.shape[1]
    size, whole = own // CHUNKS, 4 * own // CHUNKS
    blocks = (me, sib, cnt, dia)
    out_bias, attn_gain, attn_shift, down_bias, ffn_gain, ffn_shift = [
        vectors_ref[k : k + 1, :] for k in range(6)
    ]
    bufs = (own_acc, other_acc, stage_sib, stage_x, recv_sib, recv_x)
    gathers = [
        Gather(buf, gather_send, gather_recv, stage, size, sib, cnt)
        for stage, buf in enumerate((normed_full, grad2_full, grad1_full))
    ]
    scatters = [
        Scatter(bufs, scatter_send, scatter_recv, stage, size, sib, cnt) for stage in range(3)
    ]
    sums_ref[...] = jnp.zeros_like(sums_ref)
    up_sum_ref[...] = jnp.zeros_like(up_sum_ref)
    out_acc[...] = jnp.zeros_like(out_acc)
    early = pieces == CHUNKS
    down, up = [
        Reduce(k, depth // pieces, place, sems, source, halves_ref.at[k], shards_ref.at[k])
        for k, source in enumerate((down_grad, up_grad))
    ]
    _greet([{"mp": sib}, {"mp": cnt}, down.pair(), *[down.peer(g) for g in range(1, group)]])

    def loop(body):
        def step(r, carry):
            body(r)
            return carry

        lax.fori_loop(0, CHUNKS, step, 0)

    def add_sum(k, value):
        sums_ref[k : k + 1, :] += jnp.sum(value, axis=0, keepdims=True)

    def context_chunk(r):
        return jnp.concatenate(
            [context_ref[_rows(b * own + r * size, size), :] for b in blocks], axis=0
        )

    def attended(r):
        chunk = context_chunk(r)
        scatters[0].project(r, lambda cols: _nn(chunk, out_proj_ref[:, cols]))
        scatters[0].finish(r)

    loop(attended)

    def lower_norm(r):
        rows = _rows(r * size, size)
        unit, inverse = _norm(inputs_ref[rows, :].astype(f32) + scatters[0].result(r) + out_bias)
        unit1[rows, :] = unit
        inverse1[rows, :] = inverse
        gathers[0].slot(r, 0)[...] = (unit * attn_gain + attn_shift).astype(bf16)
        gathers[0].start(r)

    loop(lower_norm)

    def feed_forward(r):
        rows = _rows(r * whole, whole)
        gathers[0].forward(r)
        gathers[0].arrive(r)
        scatters[0].sent(r)

        def column(n, carry):
            cols = _rows(n * COLS, COLS)
            upper = _nn(normed_full[rows, :], up_ref[:, cols]) + up_bias_ref[:, cols]
            cdf = 0.5 + 0.5 * lax.erf(upper * math.sqrt(0.5))
            pdf = jnp.exp(upper * upper * -0.5) * (1.0 / math.sqrt(2.0 * math.pi))
            active[rows, cols] = (upper * cdf).astype(bf16)
            back[rows, cols] = (cdf + upper * pdf).astype(bf16)
            return carry

        lax.fori_loop(0, units // COLS, column, 0)
        scatters[1].project(r, lambda cols: _nn(active[rows, :], down_ref[:, cols]))
        scatters[1].finish(r)

    loop(feed_forward)

    def upper_norm(r):
        rows = _rows(r * size, size)
        normed = unit1[rows, :] * attn_gain + attn_shift
        unit, inverse = _norm(normed + scatters[1].result(r) + down_bias)
        outputs_ref[rows, :] = (unit * ffn_gain + ffn_shift).astype(bf16)
        cotangent = cotangent_ref[rows, :].astype(f32)
        grad = _norm_back(cotangent * ffn_gain, unit, inverse)
        gathers[1].slot(r, 0)[...] = grad.astype(bf16)
        gathers[1].start(r)
        grad2_own[rows, :] = grad
        add_sum(3, grad)
        add_sum(4, cotangent * unit)
        add_sum(5, cotangent)

    loop(upper_norm)

    def feed_back(r):
        rows = _rows(r * whole, whole)
        gathers[1].forward(r)
        gathers[1].arrive(r)
        scatters[1].sent(r)

        def column(n, carry):
            cols = _rows(n * COLS, COLS)
            incoming = _nt(grad2_full[rows, :], down_ref[cols, :])
            upper_back = (back[rows, cols].astype(f32) * incoming).astype(bf16)
            back[rows, cols] = upper_back
            up_sum_ref[:, cols] += jnp.sum(upper_back.astype(f32), axis=0, keepdims=True)
            return carry

        lax.fori_loop(0, units // COLS, column, 0)
        scatters[2].project(r, lambda cols: _nt(back[rows, :], up_ref[cols, :]))
        scatters[2].finish(r)

    loop(feed_back)

    def weights(k, r):
        cols = _rows(r * (depth // CHUNKS), depth // CHUNKS)
        if k == 0:
            down_grad[cols, :] = _tn(active[:, cols], grad2_full[...]).astype(bf16)
        else:
            up_grad[cols, :] = _tn(normed_full[:, cols], back[...]).astype(bf16)

    def weights_pair(r):
        for k, reduce in enumerate((down, up)):

            @pl.when(r // 2 == k)
            def _():
                for h in range(2):
                    p = 2 * r - 4 * k + h
                    weights(k, p)
                    if early:
                        reduce.send_half(p)
                if not early:

                    @pl.when(r == 2 * k + 1)
                    def _():
                        reduce.send_half(0)

    def forward_half(reduce, p):
        reduce.add_half(p)
        reduce.send_shards(p)

    def lower_back(r):
        weights_pair(r)
        if early:

            @pl.when(r >= 2)
            def _():
                forward_half(down, r - 2)

        rows = _rows(r * size, size)
        incoming = grad2_own[rows, :] + scatters[2].result(r)
        unit = unit1[rows, :]
        grad = _norm_back(incoming * attn_gain, unit, inverse1[rows, :])
        gathers[2].slot(r, 0)[...] = grad.astype(bf16)
        gathers[2].start(r)
        grad1_ref[rows, :] = grad
        add_sum(0, grad)
        add_sum(1, incoming * unit)
        add_sum(2, incoming)

    loop(lower_back)

    def context_back(r):
        rows = _rows(r * whole, whole)
        if early:

            @pl.when(r < 2)
            def _():
                forward_half(down, r + 2)

            @pl.when(r == 2)
            def _():
                forward_half(up, 0)
                down.wait_all(shards_ref.at[0], 0, 1, 1)
                down.send_sum(0, shards_ref.at[0], block_ref)

        gathers[2].forward(r)
        gathers[2].arrive(r)
        scatters[2].sent(r)
        incoming = grad1_full[rows, :]
        grad = _nt(incoming, out_proj_ref[...]).astype(bf16)
        for k, b in enumerate(blocks):
            context_grad_ref[_rows(b * own + r * size, size), :] = grad[k * size : (k + 1) * size]
        out_acc[...] += _tn(incoming, context_chunk(r))

    loop(context_back)
    out_grad_ref[...] = out_acc[...].astype(bf16)

    def drain(r):
        for gather in gathers:
            gather.sent(r)

    loop(drain)
    for k, reduce in enumerate((down, up)):
        for p in range(pieces):
            reduce.first(p).wait_send()
            if not early or (k, p) not in EARLY:
                reduce.add_half(p)
    if early:
        for k, p in EARLY:
            for side in ((1, 0) if (k, p) != (0, 0) else (0,)):
                (down, up)[k].wait_all(shards_ref.at[k], p, 1, side)
        for side in (1, 0):
            down.wait_all(shards_ref.at[0], 0, 2, side)


def _place(group):
    dp = lax.axis_index("dp")
    return lax.rem(dp, 2), dp // 2, group


def _pieces(mesh, depth):
    group = mesh.shape["dp"] // 2
    return group, CHUNKS if depth // CHUNKS // 2 // group >= 16 else 1


def middle(mesh, context, inputs, cotangent, out_proj, up_proj, up_bias, down_proj, vectors):
    f32, bf16 = jnp.float32, jnp.bfloat16
    own, depth = inputs.shape
    units, width = up_proj.shape[1], out_proj.shape[0]
    whole = 4 * own
    group, pieces = _pieces(mesh, depth)
    half = depth // pieces // 2
    vmem = pl.BlockSpec(memory_space=pltpu.VMEM)
    outs = [
        ((own, depth), bf16),
        ((own, depth), f32),
        ((whole, width), bf16),
        ((2, depth // 2, depth), bf16),
        ((2, pieces, group - 1, half // group, depth), bf16),
        ((half, depth), bf16),
        ((depth, width), bf16),
        ((8, depth), f32),
        ((1, units), f32),
    ]
    return pl.pallas_call(
        partial(middle_kernel, group, pieces),
        out_shape=[jax.ShapeDtypeStruct(*out) for out in outs],
        in_specs=[vmem] * 8,
        out_specs=[vmem] * 9,
        scratch_shapes=[
            pltpu.VMEM((units, depth), bf16),
            pltpu.VMEM((depth, units), bf16),
            pltpu.VMEM((whole, depth), bf16),
            pltpu.VMEM((whole, depth), bf16),
            pltpu.VMEM((whole, depth), bf16),
            pltpu.VMEM((whole, units), bf16),
            pltpu.VMEM((whole, units), bf16),
            pltpu.VMEM((own, depth), f32),
            pltpu.VMEM((own, 1), f32),
            pltpu.VMEM((own, depth), f32),
            pltpu.VMEM((depth, width), f32),
            *_scatter_scratch(own, depth),
            pltpu.SemaphoreType.DMA((3, 3, CHUNKS)),
            pltpu.SemaphoreType.DMA((3, 3, CHUNKS)),
            pltpu.SemaphoreType.DMA((3, 3, CHUNKS)),
            pltpu.SemaphoreType.DMA((3, 3, CHUNKS)),
            pltpu.SemaphoreType.DMA((2, 2, pieces, 3)),
        ],
        compiler_params=pltpu.CompilerParams(
            collective_id=1, has_side_effects=True, vmem_limit_bytes=63 * 2**20
        ),
        name="middle_layer",
    )(context, inputs, cotangent, out_proj, up_proj, up_bias, down_proj, vectors)


def last_kernel(
    group, pieces, grads_ref, tokens_ref, in_proj_ref, grad1_ref, halves_ref, early_shards_ref, block_ref,
    out_grad_ref, sums_ref, up_sum_ref, inputs_grad_ref, final_ref, small_ref,
    own_acc, other_acc, stage_sib, stage_x, recv_sib, recv_x, attn_grad, half_recv, shard_recv,
    small_recv, small_group, scatter_send, scatter_recv, sems, small_sems,
):
    f32, bf16 = jnp.float32, jnp.bfloat16
    me, sib, cnt, dia = _partners()
    place = _place(group)
    own, depth = grad1_ref.shape
    width = in_proj_ref.shape[2]
    size = own // CHUNKS
    blocks = (me, sib, cnt, dia)
    bufs = (own_acc, other_acc, stage_sib, stage_x, recv_sib, recv_x)
    scatter = Scatter(bufs, scatter_send, scatter_recv, 0, size, sib, cnt)
    halves = (halves_ref.at[0], halves_ref.at[1], half_recv)
    reduces = [
        Reduce(
            k, depth // pieces, place, sems, attn_grad, halves[k], shard_recv.at[k], final_ref.at[k]
        )
        for k in range(3)
    ]
    down, up, attn = reduces
    early = pieces == CHUNKS

    def loop(body, count):
        def step(r, carry):
            body(r)
            return carry

        lax.fori_loop(0, count, step, 0)

    small_ref[...] = jnp.zeros_like(small_ref)
    small_ref[:8, :] = sums_ref[...]
    small_ref[8:9, :] = up_sum_ref[...]
    _greet([{"mp": sib}, {"mp": cnt}, down.pair(), *[down.peer(g) for g in range(1, group)]])

    def known(k, p):
        return early and (k, p) in EARLY

    for k in range(2):
        for p in range(pieces):
            if not known(k, p):
                reduces[k].send_shards(p)
    if early:
        down.final_half(0)[...] = block_ref[...]
        down.last(0, block_ref).start()
        for k, p in EARLY[1:]:
            reduces[k].send_sum(p, early_shards_ref.at[k], reduces[k].final_half(p))

    def weights(n):
        cols = _rows(n * COLS, COLS)
        attn_grad[cols, : 3 * width] = _tn(tokens_ref[:, cols], grads_ref[...]).astype(bf16)
        attn_grad[cols, 3 * width :] = out_grad_ref[cols, :]
        if early:
            attn.send_half(n)

    loop(weights, depth // COLS)
    if not early:
        attn.send_half(0)

    def partial_rows(r):
        chunk = jnp.concatenate(
            [grads_ref[_rows(b * own + r * size, size), :] for b in blocks], axis=0
        )

        def tile(cols):
            total = _nt(chunk[:, :width], in_proj_ref[0, cols, :])
            total = total + _nt(chunk[:, width : 2 * width], in_proj_ref[1, cols, :])
            return total + _nt(chunk[:, 2 * width :], in_proj_ref[2, cols, :])

        scatter.project(r, tile)
        scatter.finish(r)

    loop(partial_rows, CHUNKS)

    def bias(j):
        return jnp.sum(grads_ref[:, j * width : (j + 1) * width].astype(f32), axis=0, keepdims=True)

    small_ref[9:10, :width] = bias(0)
    small_ref[9:10, width : 2 * width] = bias(2)

    def small_step(k, rows, target):
        copy = _remote(
            small_ref.at[:rows], small_recv.at[k, :rows], small_sems.at[0, k], small_sems.at[1, k], target
        )
        copy.start()
        copy.wait()
        small_ref[:rows, :] += small_recv[k, :rows, :]

    def send_sum(k, p):
        reduces[k].wait_all(shard_recv.at[k], p, 1, 1)
        reduces[k].send_sum(p, shard_recv.at[k], reduces[k].final_half(p))

    def send_back(k, p):
        reduces[k].wait_all(shard_recv.at[k], p, 2, 1)
        reduces[k].last(p).start()

    small_step(0, 8, {"mp": sib})
    small_step(1, 8, {"mp": cnt})
    for k in range(2):
        for p in range(pieces):
            if not known(k, p):
                send_sum(k, p)

    def attn_half(p):
        attn.add_half(p)
        attn.send_shards(p)

    loop(attn_half, pieces)
    if early:
        for k, p in EARLY[1:]:
            send_back(k, p)
    small_step(2, small_ref.shape[0], down.pair())
    small_copies = [
        _remote(
            small_ref, small_group.at[place[1]], small_sems.at[0, 3], small_sems.at[1, 3], down.peer(g)
        )
        for g in range(1, group)
    ]
    for copy in small_copies:
        copy.start()
    small_group[place[1]] = small_ref[...]
    for k in range(2):
        for p in range(pieces):
            if not known(k, p):
                send_back(k, p)
    loop(partial(send_sum, 2), pieces)

    def finish(r):
        rows = _rows(r * size, size)
        inputs_grad_ref[rows, :] = (grad1_ref[rows, :] + scatter.result(r)).astype(bf16)
        scatter.sent(r)

    loop(finish, CHUNKS)
    others = small_group.at[1:]
    for side in (1, 0):
        pltpu.make_async_copy(others, others, small_sems.at[side, 3]).wait()
    total = small_group[0]
    for g in range(1, group):
        total = total + small_group[g]
    small_ref[...] = total
    loop(partial(send_back, 2), pieces)
    for k, reduce in enumerate(reduces):
        for p in range(pieces):
            if not known(k, p):
                reduce.wait_all(shard_recv.at[k], p, 1, 0)
            if not known(k, p) or p + k > 0:
                reduce.wait_all(shard_recv.at[k], p, 2, 0)
            if k == 2:
                reduce.first(p).wait_send()
            reduce.last(p).wait()


def last(mesh, grads, tokens, in_proj, grad1, halves, shards, block, out_grad, sums, up_sum):
    f32, bf16 = jnp.float32, jnp.bfloat16
    own, depth = grad1.shape
    group, pieces = _pieces(mesh, depth)
    half = depth // 2
    shard = half // pieces // group
    vmem = pl.BlockSpec(memory_space=pltpu.VMEM)
    return pl.pallas_call(
        partial(last_kernel, group, pieces),
        out_shape=[
            jax.ShapeDtypeStruct((own, depth), bf16),
            jax.ShapeDtypeStruct((3, depth, depth), bf16),
            jax.ShapeDtypeStruct((16, depth), f32),
        ],
        in_specs=[vmem] * 10,
        out_specs=[vmem] * 3,
        scratch_shapes=[
            *_scatter_scratch(own, depth),
            pltpu.VMEM((depth, depth), bf16),
            pltpu.VMEM((half, depth), bf16),
            pltpu.VMEM((3, pieces, group - 1, shard, depth), bf16),
            pltpu.VMEM((3, 16, depth), f32),
            pltpu.VMEM((group, 16, depth), f32),
            pltpu.SemaphoreType.DMA((1, 3, CHUNKS)),
            pltpu.SemaphoreType.DMA((1, 3, CHUNKS)),
            pltpu.SemaphoreType.DMA((2, 3, pieces, 4)),
            pltpu.SemaphoreType.DMA((2, 4)),
        ],
        compiler_params=pltpu.CompilerParams(
            collective_id=2, has_side_effects=True, vmem_limit_bytes=60 * 2**20
        ),
        name="last_layer",
    )(grads, tokens, in_proj, grad1, halves, shards, block, out_grad, sums, up_sum)


def shards(
    mesh,
    inputs,
    in_proj,
    qv_bias,
    out_proj,
    out_bias,
    attn_gain,
    attn_shift,
    up_proj,
    up_bias,
    down_proj,
    down_bias,
    ffn_gain,
    ffn_shift,
    segments,
    padding,
    cotangent,
):
    f32 = jnp.float32
    width = in_proj.shape[2]
    where = segment_places(segments, padding)
    vectors = jnp.stack([out_bias, attn_gain, attn_shift, down_bias, ffn_gain, ffn_shift])
    tokens, qkv = project_tokens(inputs, in_proj, qv_bias)
    context, lse_rows = attention_forward(qkv, where)
    outputs, grad1, context_grad, halves, pieces, block, out_grad, sums, up_sum = middle(
        mesh, context, inputs, cotangent, out_proj, up_proj, up_bias[None], down_proj, vectors
    )
    grads = attention_backward(qkv, context_grad, context, lse_rows, where)
    inputs_grad, final, small = last(
        mesh, grads, tokens, in_proj, grad1, halves, pieces, block, out_grad, sums, up_sum
    )
    attn = final[2].astype(f32)
    in_grad = jnp.stack([attn[:, j * width : (j + 1) * width] for j in range(3)])
    return (
        outputs,
        inputs_grad,
        in_grad,
        small[9, : 2 * width].reshape(2, width),
        attn[:, 3 * width :].T,
        small[0],
        small[1],
        small[2],
        final[1].astype(f32),
        small[8],
        final[0].astype(f32),
        small[3],
        small[4],
        small[5],
    )


def solution(mesh):
    return jax.shard_map(
        partial(shards, mesh),
        mesh=mesh,
        in_specs=(
            P(("dp", "mp"), None),
            P(None, None, "mp"),
            P(None, "mp"),
            P("mp", None),
            P(),
            P(),
            P(),
            P(None, "mp"),
            P("mp"),
            P("mp", None),
            P(),
            P(),
            P(),
            P("dp", None),
            P("dp", None),
            P(("dp", "mp"), None),
        ),
        out_specs=(
            P(("dp", "mp"), None),
            P(("dp", "mp"), None),
            P(None, None, "mp"),
            P(None, "mp"),
            P("mp", None),
            P(),
            P(),
            P(),
            P(None, "mp"),
            P("mp"),
            P("mp", None),
            P(),
            P(),
            P(),
        ),
        check_vma=False,
    )
```

```python
from functools import partial
import math

import jax
import jax.numpy as jnp
from jax import lax
from jax.experimental import pallas as pl
from jax.experimental.pallas import tpu as pltpu
from jax.sharding import PartitionSpec as P

HEAD = 64
BLOCK = 256
CHUNKS = 4
EARLY = ((0, 0), (0, 1), (0, 2), (0, 3), (1, 0))
COLS = 256
VMEM = 60 * 2**20
REMOTE = pl.BlockSpec(memory_space=pl.ANY)
LOCAL = pl.BlockSpec(memory_space=pltpu.VMEM)
SCALARS = pl.BlockSpec(memory_space=pltpu.SMEM)
MESH = pl.DeviceIdType.MESH


EPSILON = 1e-05


NEG = -1e30


def _head_masks(heads, width, value):
    lane = lax.broadcasted_iota(jnp.int32, (1, width), 1) // HEAD
    return [jnp.where(lane == h, value, 0.0).astype(jnp.bfloat16) for h in range(heads)]


def _nt(a, b):
    return lax.dot_general(a, b, (((1,), (1,)), ((), ())), preferred_element_type=jnp.float32)


def _tn(a, b):
    return lax.dot_general(a, b, (((0,), (0,)), ((), ())), preferred_element_type=jnp.float32)


def _nn(a, b):
    return jnp.dot(a, b, preferred_element_type=jnp.float32)


def _column(row):
    wide = jnp.broadcast_to(row.astype(jnp.float32), (128, row.shape[1])).T.astype(jnp.int32)
    return jnp.concatenate([wide] * (BLOCK // 128), axis=1)


def _bias(seg_ref, pad_ref, query_rows, key_rows):
    seg_q, pad_q = seg_ref[:, query_rows], pad_ref[:, query_rows]
    seg_k, pad_k = _column(seg_ref[:, key_rows]), _column(pad_ref[:, key_rows])
    allowed = (seg_k == seg_q) & ((pad_k > 0) | (pad_q == 0))
    return jnp.where(allowed, 0.0, NEG).astype(jnp.float32)


def _meets(places_ref, left):
    edge = left * BLOCK + BLOCK - 1
    return places_ref[0, edge] == places_ref[0, edge + 1]


def _neighbours(places_ref, i, blocks, body):
    @pl.when(i > 0)
    def _():
        @pl.when(_meets(places_ref, jnp.maximum(i - 1, 0)))
        def _():
            body(i - 1)

    @pl.when(i < blocks - 1)
    def _():
        @pl.when(_meets(places_ref, jnp.minimum(i, blocks - 2)))
        def _():
            body(i + 1)


def _block_copies(source, target, sems):
    def copy(i):
        rows = _rows(i * BLOCK, BLOCK)
        return pltpu.make_async_copy(source.at[rows], target.at[rows], sems.at[i])

    return copy


def _loop(count, body):
    def step(i, carry):
        body(i)
        return carry

    lax.fori_loop(0, count, step, 0)


def attention_forward_kernel(
    heads, blocks, places_ref, qkv_hbm, seg_ref, pad_ref, context_hbm, lse_ref,
    qkv_ref, context_ref, peak_ref, total_ref, acc_ref, load_sems, store_sems,
):
    bf16 = jnp.bfloat16
    width = context_ref.shape[1]
    load = _block_copies(qkv_hbm, qkv_ref, load_sems)
    store = _block_copies(context_ref, context_hbm, store_sems)
    _loop(blocks, lambda i: load(i).start())
    scaled = _head_masks(heads, width, 1.0 / math.sqrt(HEAD))
    load(0).wait()

    def attend(i):
        @pl.when(i + 1 < blocks)
        def _():
            load(i + 1).wait()

        query_rows = _rows(i * BLOCK, BLOCK)
        query = qkv_ref[query_rows, :width]

        def parts(j):
            rows = _rows(j * BLOCK, BLOCK)
            return (
                qkv_ref[rows, width : 2 * width],
                qkv_ref[rows, 2 * width :].T,
                _bias(seg_ref, pad_ref, query_rows, rows),
            )

        key, value, bias = parts(i)
        for h in range(heads):
            scores = _nt(key, query * scaled[h]) + bias
            peak = jnp.max(scores, axis=0, keepdims=True)
            expo = jnp.exp(scores - peak)
            peak_ref[h] = peak
            total_ref[h] = jnp.sum(expo, axis=0, keepdims=True)
            place = pl.ds(h * HEAD, HEAD)
            acc_ref[place, :] = _nn(value[h * HEAD : (h + 1) * HEAD], expo.astype(bf16))

        def other(j):
            key, value, bias = parts(j)
            for h in range(heads):
                scores = _nt(key, query * scaled[h]) + bias
                old = peak_ref[h]
                peak = jnp.maximum(old, jnp.max(scores, axis=0, keepdims=True))
                expo = jnp.exp(scores - peak)
                ratio = jnp.exp(old - peak)
                peak_ref[h] = peak
                total_ref[h] = total_ref[h] * ratio + jnp.sum(expo, axis=0, keepdims=True)
                place = pl.ds(h * HEAD, HEAD)
                acc_ref[place, :] = acc_ref[place, :] * ratio + _nn(
                    value[h * HEAD : (h + 1) * HEAD], expo.astype(bf16)
                )

        _neighbours(places_ref, i, blocks, other)
        for h in range(heads):
            place = pl.ds(h * HEAD, HEAD)
            acc_ref[place, :] = acc_ref[place, :] / total_ref[h]
            lse_ref[h : h + 1, query_rows] = peak_ref[h] + jnp.log(total_ref[h])
        context_ref[query_rows, :] = acc_ref[...].astype(bf16).T
        store(i).start()

    _loop(blocks, attend)
    _loop(blocks, lambda i: store(i).wait())


def attention_backward_kernel(
    heads, blocks, places_ref, qkv_hbm, grad_hbm, context_hbm, lse_ref, seg_ref, pad_ref, grads_hbm,
    qkv_ref, grad_ref, context_ref, grads_ref, query_acc, keys_acc, values_acc, load_sems, store_sems,
):
    f32, bf16 = jnp.float32, jnp.bfloat16
    width = grad_ref.shape[1]
    loads = [
        _block_copies(*pair, load_sems.at[k])
        for k, pair in enumerate(((qkv_hbm, qkv_ref), (grad_hbm, grad_ref), (context_hbm, context_ref)))
    ]
    store = _block_copies(grads_ref, grads_hbm, store_sems)
    _loop(blocks, lambda i: [load(i).start() for load in loads])
    scaled = _head_masks(heads, width, 1.0 / math.sqrt(HEAD))
    plain = _head_masks(heads, width, 1.0)
    keys_acc[...] = jnp.zeros_like(keys_acc)
    values_acc[...] = jnp.zeros_like(values_acc)
    for load in loads:
        load(0).wait()

    def finish(i):
        rows = _rows(i * BLOCK, BLOCK)
        grads_ref[rows, width : 2 * width] = keys_acc[rows, :].astype(bf16)
        grads_ref[rows, 2 * width :] = values_acc[rows, :].astype(bf16)
        store(i).start()

    def attend(i):
        @pl.when(i + 1 < blocks)
        def _():
            for load in loads:
                load(i + 1).wait()

        query_rows = _rows(i * BLOCK, BLOCK)
        query, grad = qkv_ref[query_rows, :width], grad_ref[query_rows, :]
        product = (grad.astype(f32) * context_ref[query_rows, :].astype(f32)).T
        row_dots = [
            jnp.sum(product[h * HEAD : (h + 1) * HEAD], axis=0, keepdims=True) for h in range(heads)
        ]

        def block(j, add):
            rows = _rows(j * BLOCK, BLOCK)
            bias = _bias(seg_ref, pad_ref, query_rows, rows)
            key, value = qkv_ref[rows, width : 2 * width], qkv_ref[rows, 2 * width :]
            key_rows = (key * (1.0 / math.sqrt(HEAD))).astype(bf16).T
            key_add = jnp.zeros((BLOCK, width), f32)
            value_add = jnp.zeros((BLOCK, width), f32)
            for h in range(heads):
                query_h, grad_h = query * scaled[h], grad * plain[h]
                scores = _nt(key, query_h) + bias
                prob = jnp.exp(scores - lse_ref[h : h + 1, query_rows])
                score_grad = (prob * (_nt(value, grad_h) - row_dots[h])).astype(bf16)
                key_add = key_add + _nn(score_grad, query_h)
                value_add = value_add + _nn(prob.astype(bf16), grad_h)
                place = pl.ds(h * HEAD, HEAD)
                part = _nn(key_rows[h * HEAD : (h + 1) * HEAD], score_grad)
                query_acc[place, :] = query_acc[place, :] + part if add else part
            keys_acc[rows, :] += key_add
            values_acc[rows, :] += value_add

        block(i, False)
        _neighbours(places_ref, i, blocks, lambda j: block(j, True))
        grads_ref[query_rows, :width] = query_acc[...].astype(bf16).T

        @pl.when(i > 0)
        def _():
            finish(i - 1)

    _loop(blocks, attend)
    finish(blocks - 1)
    _loop(blocks, lambda i: store(i).wait())


def attention_forward(qkv, places, padding):
    length, width = qkv.shape[0], qkv.shape[1] // 3
    heads, blocks = width // HEAD, length // BLOCK
    return pl.pallas_call(
        partial(attention_forward_kernel, heads, blocks),
        in_specs=[SCALARS, REMOTE, LOCAL, LOCAL],
        out_specs=[REMOTE, LOCAL],
        scratch_shapes=[
            pltpu.VMEM((length, 3 * width), jnp.bfloat16),
            pltpu.VMEM((length, width), jnp.bfloat16),
            pltpu.VMEM((heads, 1, BLOCK), jnp.float32),
            pltpu.VMEM((heads, 1, BLOCK), jnp.float32),
            pltpu.VMEM((width, BLOCK), jnp.float32),
            pltpu.SemaphoreType.DMA((blocks,)),
            pltpu.SemaphoreType.DMA((blocks,)),
        ],
        out_shape=[
            jax.ShapeDtypeStruct((length, width), jnp.bfloat16),
            jax.ShapeDtypeStruct((8, length), jnp.float32),
        ],
        compiler_params=pltpu.CompilerParams(vmem_limit_bytes=VMEM),
        name="attention_forward",
    )(places, qkv, places, padding)


def attention_backward(qkv, grad, context, lse_rows, places, padding):
    length, width = grad.shape
    heads, blocks = width // HEAD, length // BLOCK
    return pl.pallas_call(
        partial(attention_backward_kernel, heads, blocks),
        in_specs=[SCALARS, REMOTE, REMOTE, REMOTE, LOCAL, LOCAL, LOCAL],
        out_specs=REMOTE,
        scratch_shapes=[
            pltpu.VMEM((length, 3 * width), jnp.bfloat16),
            pltpu.VMEM((length, width), jnp.bfloat16),
            pltpu.VMEM((length, width), jnp.bfloat16),
            pltpu.VMEM((length, 3 * width), jnp.bfloat16),
            pltpu.VMEM((width, BLOCK), jnp.float32),
            pltpu.VMEM((length, width), jnp.float32),
            pltpu.VMEM((length, width), jnp.float32),
            pltpu.SemaphoreType.DMA((3, blocks)),
            pltpu.SemaphoreType.DMA((blocks,)),
        ],
        out_shape=jax.ShapeDtypeStruct((length, 3 * width), jnp.bfloat16),
        compiler_params=pltpu.CompilerParams(vmem_limit_bytes=VMEM),
        name="attention_backward",
    )(places, qkv, grad, context, lse_rows, places, padding)


def segment_places(segments, padding):
    row_count, seq_len = segments.shape
    if row_count > 1:
        segments = segments + jnp.arange(row_count, dtype=jnp.int32)[:, None] * (seq_len + 1)
    return segments.reshape(1, -1), padding.reshape(1, -1)


def _partners():
    me = lax.axis_index("mp")
    core = lax.rem(me, 2)
    sib = me + 1 - 2 * core
    cnt = lax.rem(me + 2, 4)
    dia = lax.rem(cnt + 1, 2) + cnt - lax.rem(cnt, 2)
    return me, sib, cnt, dia


def _remote(src, dst, send, recv, target):
    return pltpu.make_async_remote_copy(
        src_ref=src, dst_ref=dst, send_sem=send, recv_sem=recv, device_id=target, device_id_type=MESH
    )


def _greet(targets):
    barrier = pltpu.get_barrier_semaphore()
    for target in targets:
        pl.semaphore_signal(barrier, inc=1, device_id=target, device_id_type=MESH)
    pl.semaphore_wait(barrier, len(targets))


def _rows(start, size):
    return pl.ds(pl.multiple_of(start, size), size)


class Gather:
    def __init__(self, buffer, send, recv, stage, size, sib, cnt):
        self.buffer, self.send, self.recv = buffer, send, recv
        self.stage, self.size, self.sib, self.cnt = stage, size, sib, cnt

    def slot(self, r, k):
        return self.buffer.at[_rows((r * 4 + k) * self.size, self.size)]

    def copy(self, r, kind):
        src, dst, target = ((0, 1, self.sib), (0, 2, self.cnt), (2, 3, self.sib))[kind]
        return _remote(
            self.slot(r, src),
            self.slot(r, dst),
            self.send.at[self.stage, kind, r],
            self.recv.at[self.stage, kind, r],
            {"mp": target},
        )

    def start(self, r):
        self.copy(r, 1).start()
        self.copy(r, 0).start()

    def forward(self, r):
        self.copy(r, 1).wait_recv()
        self.copy(r, 2).start()

    def arrive(self, r):
        self.copy(r, 0).wait_recv()
        self.copy(r, 2).wait_recv()

    def sent(self, r):
        for kind in range(3):
            self.copy(r, kind).wait_send()


class Scatter:
    def __init__(self, bufs, send, recv, stage, size, sib, cnt):
        self.own, self.other, self.stage_sib, self.stage_x, self.recv_sib, self.recv_x = bufs
        self.send, self.recv = send, recv
        self.stage, self.size, self.sib, self.cnt = stage, size, sib, cnt

    def copy(self, r, kind):
        rows = _rows(r * self.size, self.size)
        src, dst, target = (
            (self.stage_sib.at[0, rows], self.recv_sib.at[0, rows], self.sib),
            (self.stage_sib.at[1, rows], self.recv_sib.at[1, rows], self.sib),
            (self.stage_x.at[rows], self.recv_x.at[rows], self.cnt),
        )[kind]
        return _remote(
            src, dst, self.send.at[self.stage, kind, r], self.recv.at[self.stage, kind, r], {"mp": target}
        )

    def sent(self, r):
        for kind in range(3):
            self.copy(r, kind).wait_send()

    def project(self, r, tile):
        size = self.size
        rows = _rows(r * size, size)

        def column(n, carry):
            cols = _rows(n * COLS, COLS)
            part = tile(cols)
            self.own[rows, cols] = part[:size]
            self.stage_sib[1, rows, cols] = part[size : 2 * size].astype(jnp.bfloat16)
            self.other[rows, cols] = part[2 * size : 3 * size]
            self.stage_sib[0, rows, cols] = part[3 * size :].astype(jnp.bfloat16)
            return carry

        lax.fori_loop(0, self.own.shape[1] // COLS, column, 0)
        self.copy(r, 0).start()
        self.copy(r, 1).start()

    def finish(self, r):
        rows = _rows(r * self.size, self.size)
        self.copy(r, 0).wait_recv()
        self.stage_x[rows, :] = (
            self.other[rows, :] + self.recv_sib[0, rows, :].astype(jnp.float32)
        ).astype(jnp.bfloat16)
        self.copy(r, 2).start()
        self.copy(r, 1).wait_recv()
        self.own[rows, :] += self.recv_sib[1, rows, :].astype(jnp.float32)

    def result(self, r):
        rows = _rows(r * self.size, self.size)
        self.copy(r, 2).wait_recv()
        return self.own[rows, :] + self.recv_x[rows, :].astype(jnp.float32)


def _scatter_scratch(own, width):
    f32, bf16 = jnp.float32, jnp.bfloat16
    return [
        pltpu.VMEM((own, width), f32),
        pltpu.VMEM((own, width), f32),
        pltpu.VMEM((2, own, width), bf16),
        pltpu.VMEM((own, width), bf16),
        pltpu.VMEM((2, own, width), bf16),
        pltpu.VMEM((own, width), bf16),
    ]


def _norm(summed):
    center = summed - jnp.mean(summed, axis=-1, keepdims=True)
    variance = jnp.mean(center * center, axis=-1, keepdims=True)
    inverse = lax.rsqrt(variance + EPSILON)
    return center * inverse, inverse


def _norm_back(scaled, unit, inverse):
    return inverse * (
        scaled
        - jnp.mean(scaled, axis=-1, keepdims=True)
        - unit * jnp.mean(scaled * unit, axis=-1, keepdims=True)
    )


def project_kernel(
    inputs_ref, in_proj_ref, qv_bias_ref, tokens_hbm, qkv_hbm, tokens_ref, qkv_ref, weights,
    send, recv, load_sems, store_sems,
):
    f32, bf16 = jnp.float32, jnp.bfloat16
    me, sib, cnt, dia = _partners()
    own, width = inputs_ref.shape[0], in_proj_ref.shape[2]
    size = own // CHUNKS
    mine = _rows(me * own, own)
    keep = pltpu.make_async_copy(inputs_ref, tokens_ref.at[mine], load_sems.at[0])
    fetch = pltpu.make_async_copy(in_proj_ref, weights, load_sems.at[1])
    fetch.start()
    keep.start()
    _greet([{"mp": sib}, {"mp": cnt}])

    def copy(r, kind):
        here = inputs_ref.at[_rows(r * size, size)]
        place = _rows((cnt if kind == 2 else me) * own + r * size, size)
        src, target = ((here, sib), (here, cnt), (tokens_ref.at[place], sib))[kind]
        return _remote(src, tokens_ref.at[place], send.at[kind, r], recv.at[kind, r], {"mp": target})

    for r in range(CHUNKS):
        copy(r, 1).start()
        copy(r, 0).start()

    def stores(first, rows, k):
        place = _rows(first, rows)
        return [
            pltpu.make_async_copy(tokens_ref.at[place], tokens_hbm.at[place], store_sems.at[0, k]),
            pltpu.make_async_copy(qkv_ref.at[place], qkv_hbm.at[place], store_sems.at[1, k]),
        ]

    def compute(first):
        place = _rows(first, size)
        block = tokens_ref[place, :]
        for j in range(3):
            part = jnp.dot(block, weights[j], preferred_element_type=f32)
            if j != 1:
                part = part + qv_bias_ref[j // 2 : j // 2 + 1, :]
            qkv_ref[place, j * width : (j + 1) * width] = part.astype(bf16)

    fetch.wait()
    keep.wait()
    _loop(CHUNKS, lambda r: compute(me * own + r * size))
    for store in stores(me * own, own, 0):
        store.start()

    def sib_part(r):
        copy(r, 0).wait_recv()
        compute(sib * own + r * size)

    _loop(CHUNKS, sib_part)
    for store in stores(sib * own, own, 1):
        store.start()

    def far_part(r):
        copy(r, 1).wait_recv()
        copy(r, 2).start()
        compute(cnt * own + r * size)
        for store in stores(cnt * own + r * size, size, 2 + 2 * r):
            store.start()
        copy(r, 2).wait_recv()
        compute(dia * own + r * size)
        for store in stores(dia * own + r * size, size, 3 + 2 * r):
            store.start()

    _loop(CHUNKS, far_part)
    for k in range(2):
        for store in stores((me, sib)[k] * own, own, k):
            store.wait()

    def drain(r):
        for kind in range(3):
            copy(r, kind).wait_send()
        for k, block in enumerate((cnt, dia)):
            for store in stores(block * own + r * size, size, 2 + 2 * r + k):
                store.wait()

    _loop(CHUNKS, drain)


def project_tokens(inputs, in_proj, qv_bias):
    own, depth = inputs.shape
    width = in_proj.shape[2]
    shapes = [(4 * own, depth), (4 * own, 3 * width)]
    return pl.pallas_call(
        project_kernel,
        out_shape=[jax.ShapeDtypeStruct(shape, jnp.bfloat16) for shape in shapes],
        in_specs=[REMOTE, REMOTE, LOCAL],
        out_specs=[REMOTE] * 2,
        scratch_shapes=[
            *[pltpu.VMEM(shape, jnp.bfloat16) for shape in shapes],
            pltpu.VMEM(in_proj.shape, jnp.bfloat16),
            pltpu.SemaphoreType.DMA((3, CHUNKS)),
            pltpu.SemaphoreType.DMA((3, CHUNKS)),
            pltpu.SemaphoreType.DMA((2,)),
            pltpu.SemaphoreType.DMA((2, 2 + 2 * CHUNKS)),
        ],
        compiler_params=pltpu.CompilerParams(
            collective_id=0, has_side_effects=True, vmem_limit_bytes=VMEM
        ),
        name="project_tokens",
    )(inputs, in_proj, qv_bias)


class Reduce:
    def __init__(self, matrix, rows, place, sems, source=None, halves=None, shards=None, final=None):
        self.matrix, self.rows, self.sems = matrix, rows, sems
        self.source, self.halves, self.shards, self.final = source, halves, shards, final
        self.y, self.z, self.group = place
        self.half = rows // 2
        self.shard = self.half // self.group

    def peer(self, g):
        return {"dp": lax.rem(self.z + g, self.group) * 2 + self.y}

    def pair(self):
        return {"dp": self.z * 2 + 1 - self.y}

    def sem(self, p, kind):
        return self.sems.at[0, self.matrix, p, kind], self.sems.at[1, self.matrix, p, kind]

    def half_rows(self, p, y):
        return _rows(p * self.rows + y * self.half, self.half)

    def first(self, p):
        return _remote(
            self.source.at[self.half_rows(p, 1 - self.y)],
            self.halves.at[_rows(p * self.half, self.half)],
            *self.sem(p, 0),
            self.pair(),
        )

    def wait_all(self, shards, p, kind, side):
        block = shards.at[p]
        pltpu.make_async_copy(block, block, self.sem(p, kind)[side]).wait()

    def send_half(self, p):
        self.first(p).start()

    def add_half(self, p):
        self.first(p).wait_recv()
        place = _rows(p * self.half, self.half)
        self.halves[place, :] = (
            self.halves[place, :].astype(jnp.float32)
            + self.source[self.half_rows(p, self.y), :].astype(jnp.float32)
        ).astype(jnp.bfloat16)

    def send_shards(self, p):
        for g in range(1, self.group):
            place = p * self.half + lax.rem(self.z + g, self.group) * self.shard
            _remote(
                self.halves.at[_rows(place, self.shard)],
                self.shards.at[p, g - 1],
                *self.sem(p, 1),
                self.peer(g),
            ).start()

    def send_sum(self, p, shards, block):
        total = self.halves[_rows(p * self.half + self.z * self.shard, self.shard), :].astype(jnp.float32)
        for g in range(1, self.group):
            total = total + shards[p, g - 1].astype(jnp.float32)
        mine = block.at[_rows(self.z * self.shard, self.shard)]
        mine[...] = total.astype(jnp.bfloat16)
        for g in range(1, self.group):
            _remote(mine, mine, *self.sem(p, 2), self.peer(g)).start()

    def final_half(self, p):
        return self.final.at[self.half_rows(p, self.y)]

    def last(self, p, block=None):
        there = self.final_half(p)
        return _remote(there if block is None else block, there, *self.sem(p, 3), self.pair())


def middle_kernel(
    group, pieces, context_hbm, out_proj_hbm, inputs_hbm, up_hbm, down_hbm, cotangent_hbm, up_bias_ref, *refs
):
    vectors, refs = refs[:6], refs[6:]
    outputs_hbm, grad1_hbm, context_grad_hbm, *refs = refs
    middle_body(
        group, pieces, (context_hbm, out_proj_hbm, inputs_hbm, up_hbm, down_hbm, cotangent_hbm),
        (outputs_hbm, grad1_hbm, context_grad_hbm), up_bias_ref, [v[...] for v in vectors], *refs
    )


def middle_body(
    group, pieces, sources, targets, up_bias_ref, vectors,
    halves_ref, shards_ref, block_ref, out_grad_ref, sums_ref, up_sum_ref,
    context_ref, out_proj_ref, inputs_ref, up_ref, down_ref, cotangent_ref,
    outputs_ref, grad1_ref, context_grad_ref, load_sems, store_sems, down_grad, up_grad, normed_full, grad2_full, grad1_full, active, back, unit1, inverse1, grad2_own, out_acc,
    own_acc, other_acc, stage_sib, stage_x, recv_sib, recv_x,
    gather_send, gather_recv, scatter_send, scatter_recv, sems,
):
    f32, bf16 = jnp.float32, jnp.bfloat16
    me, sib, cnt, dia = _partners()
    place = _place(group)
    own, depth = inputs_ref.shape
    units = up_ref.shape[1]
    size, whole = own // CHUNKS, 4 * own // CHUNKS
    blocks = (me, sib, cnt, dia)
    out_bias, attn_gain, attn_shift, down_bias, ffn_gain, ffn_shift = vectors
    scratch = (context_ref, out_proj_ref, inputs_ref, up_ref, down_ref, cotangent_ref)
    loads = [
        pltpu.make_async_copy(source, target, load_sems.at[k])
        for k, (source, target) in enumerate(zip(sources, scratch))
    ]
    for load in loads:
        load.start()

    def store(k, r):
        rows = _rows(r * size, size)
        return pltpu.make_async_copy(
            (outputs_ref, grad1_ref)[k].at[rows], targets[k].at[rows], store_sems.at[k, r]
        )

    bufs = (own_acc, other_acc, stage_sib, stage_x, recv_sib, recv_x)
    gathers = [
        Gather(buf, gather_send, gather_recv, stage, size, sib, cnt)
        for stage, buf in enumerate((normed_full, grad2_full, grad1_full))
    ]
    scatters = [
        Scatter(bufs, scatter_send, scatter_recv, stage, size, sib, cnt) for stage in range(3)
    ]
    sums_ref[...] = jnp.zeros_like(sums_ref)
    up_sum_ref[...] = jnp.zeros_like(up_sum_ref)
    out_acc[...] = jnp.zeros_like(out_acc)
    early = pieces == CHUNKS
    down, up = [
        Reduce(k, depth // pieces, place, sems, source, halves_ref.at[k], shards_ref.at[k])
        for k, source in enumerate((down_grad, up_grad))
    ]
    _greet([{"mp": sib}, {"mp": cnt}, down.pair(), *[down.peer(g) for g in range(1, group)]])

    def loop(body):
        def step(r, carry):
            body(r)
            return carry

        lax.fori_loop(0, CHUNKS, step, 0)

    def add_sum(k, value):
        sums_ref[k : k + 1, :] += jnp.sum(value, axis=0, keepdims=True)

    def context_chunk(r):
        return jnp.concatenate(
            [context_ref[_rows(b * own + r * size, size), :] for b in blocks], axis=0
        )

    loads[0].wait()
    loads[1].wait()

    def attended(r):
        chunk = context_chunk(r)
        scatters[0].project(r, lambda cols: _nn(chunk, out_proj_ref[:, cols]))
        scatters[0].finish(r)

    loop(attended)
    loads[2].wait()

    def lower_norm(r):
        rows = _rows(r * size, size)
        unit, inverse = _norm(inputs_ref[rows, :].astype(f32) + scatters[0].result(r) + out_bias)
        unit1[rows, :] = unit
        inverse1[rows, :] = inverse
        gathers[0].slot(r, 0)[...] = (unit * attn_gain + attn_shift).astype(bf16)
        gathers[0].start(r)

    loop(lower_norm)
    loads[3].wait()
    loads[4].wait()

    def feed_forward(r):
        rows = _rows(r * whole, whole)
        gathers[0].forward(r)
        gathers[0].arrive(r)
        scatters[0].sent(r)

        def column(n, carry):
            cols = _rows(n * COLS, COLS)
            upper = _nn(normed_full[rows, :], up_ref[:, cols]) + up_bias_ref[:, cols]
            cdf = 0.5 + 0.5 * lax.erf(upper * math.sqrt(0.5))
            pdf = jnp.exp(upper * upper * -0.5) * (1.0 / math.sqrt(2.0 * math.pi))
            active[rows, cols] = (upper * cdf).astype(bf16)
            back[rows, cols] = (cdf + upper * pdf).astype(bf16)
            return carry

        lax.fori_loop(0, units // COLS, column, 0)
        scatters[1].project(r, lambda cols: _nn(active[rows, :], down_ref[:, cols]))
        scatters[1].finish(r)

    loop(feed_forward)
    loads[5].wait()

    def upper_norm(r):
        rows = _rows(r * size, size)
        normed = unit1[rows, :] * attn_gain + attn_shift
        unit, inverse = _norm(normed + scatters[1].result(r) + down_bias)
        outputs_ref[rows, :] = (unit * ffn_gain + ffn_shift).astype(bf16)
        store(0, r).start()
        cotangent = cotangent_ref[rows, :].astype(f32)
        grad = _norm_back(cotangent * ffn_gain, unit, inverse)
        gathers[1].slot(r, 0)[...] = grad.astype(bf16)
        gathers[1].start(r)
        grad2_own[rows, :] = grad
        add_sum(3, grad)
        add_sum(4, cotangent * unit)
        add_sum(5, cotangent)

    loop(upper_norm)

    def feed_back(r):
        rows = _rows(r * whole, whole)
        gathers[1].forward(r)
        gathers[1].arrive(r)
        scatters[1].sent(r)

        def column(n, carry):
            cols = _rows(n * COLS, COLS)
            incoming = _nt(grad2_full[rows, :], down_ref[cols, :])
            upper_back = (back[rows, cols].astype(f32) * incoming).astype(bf16)
            back[rows, cols] = upper_back
            up_sum_ref[:, cols] += jnp.sum(upper_back.astype(f32), axis=0, keepdims=True)
            return carry

        lax.fori_loop(0, units // COLS, column, 0)
        scatters[2].project(r, lambda cols: _nt(back[rows, :], up_ref[cols, :]))
        scatters[2].finish(r)

    loop(feed_back)

    def weights(k, r):
        cols = _rows(r * (depth // CHUNKS), depth // CHUNKS)
        if k == 0:
            down_grad[cols, :] = _tn(active[:, cols], grad2_full[...]).astype(bf16)
        else:
            up_grad[cols, :] = _tn(normed_full[:, cols], back[...]).astype(bf16)

    def weights_pair(r):
        for k, reduce in enumerate((down, up)):

            @pl.when(r // 2 == k)
            def _():
                for h in range(2):
                    p = 2 * r - 4 * k + h
                    weights(k, p)
                    if early:
                        reduce.send_half(p)
                if not early:

                    @pl.when(r == 2 * k + 1)
                    def _():
                        reduce.send_half(0)

    def forward_half(reduce, p):
        reduce.add_half(p)
        reduce.send_shards(p)

    def lower_back(r):
        weights_pair(r)
        if early:

            @pl.when(r >= 2)
            def _():
                forward_half(down, r - 2)

        rows = _rows(r * size, size)
        incoming = grad2_own[rows, :] + scatters[2].result(r)
        unit = unit1[rows, :]
        grad = _norm_back(incoming * attn_gain, unit, inverse1[rows, :])
        gathers[2].slot(r, 0)[...] = grad.astype(bf16)
        gathers[2].start(r)
        grad1_ref[rows, :] = grad
        store(1, r).start()
        add_sum(0, grad)
        add_sum(1, incoming * unit)
        add_sum(2, incoming)

    loop(lower_back)

    def context_back(r):
        rows = _rows(r * whole, whole)
        if early:

            @pl.when(r < 2)
            def _():
                forward_half(down, r + 2)

            @pl.when(r == 2)
            def _():
                forward_half(up, 0)
                down.wait_all(shards_ref.at[0], 0, 1, 1)
                down.send_sum(0, shards_ref.at[0], block_ref)

        gathers[2].forward(r)
        gathers[2].arrive(r)
        scatters[2].sent(r)
        incoming = grad1_full[rows, :]
        grad = _nt(incoming, out_proj_ref[...]).astype(bf16)
        for k, b in enumerate(blocks):
            part = _rows(b * own + r * size, size)
            context_grad_ref[part, :] = grad[k * size : (k + 1) * size]
        out_acc[...] += _tn(incoming, context_chunk(r))

    loop(context_back)
    out_grad_ref[...] = out_acc[...].astype(bf16)
    save = pltpu.make_async_copy(context_grad_ref, targets[2], load_sems.at[0])
    save.start()

    def drain(r):
        store(0, r).wait()
        store(1, r).wait()
        for gather in gathers:
            gather.sent(r)

    loop(drain)
    for k, reduce in enumerate((down, up)):
        for p in range(pieces):
            reduce.first(p).wait_send()
            if not early or (k, p) not in EARLY:
                reduce.add_half(p)
    if early:
        for k, p in EARLY:
            for side in ((1, 0) if (k, p) != (0, 0) else (0,)):
                (down, up)[k].wait_all(shards_ref.at[k], p, 1, side)
        for side in (1, 0):
            down.wait_all(shards_ref.at[0], 0, 2, side)
    save.wait()


def _place(group):
    dp = lax.axis_index("dp")
    return lax.rem(dp, 2), dp // 2, group


def _pieces(mesh, depth):
    group = mesh.shape["dp"] // 2
    return group, CHUNKS if depth // CHUNKS // 2 // group >= 16 else 1


def middle(mesh, context, out_proj, inputs, up_proj, down_proj, cotangent, up_bias, vectors):
    f32, bf16 = jnp.float32, jnp.bfloat16
    own, depth = inputs.shape
    units, width = up_proj.shape[1], out_proj.shape[0]
    whole = 4 * own
    group, pieces = _pieces(mesh, depth)
    half = depth // pieces // 2
    arrays = (context, out_proj, inputs, up_proj, down_proj, cotangent)
    outs = [
        ((own, depth), bf16),
        ((own, depth), f32),
        ((whole, width), bf16),
        ((2, depth // 2, depth), bf16),
        ((2, pieces, group - 1, half // group, depth), bf16),
        ((half, depth), bf16),
        ((depth, width), bf16),
        ((8, depth), f32),
        ((1, units), f32),
    ]
    return pl.pallas_call(
        partial(middle_kernel, group, pieces),
        out_shape=[jax.ShapeDtypeStruct(*out) for out in outs],
        in_specs=[REMOTE] * 6 + [LOCAL] * 7,
        out_specs=[REMOTE] * 3 + [LOCAL] * 6,
        scratch_shapes=[
            *[pltpu.VMEM(array.shape, array.dtype) for array in arrays],
            *[pltpu.VMEM(*out) for out in outs[:3]],
            pltpu.SemaphoreType.DMA((6,)),
            pltpu.SemaphoreType.DMA((2, CHUNKS)),
            pltpu.VMEM((units, depth), bf16),
            pltpu.VMEM((depth, units), bf16),
            pltpu.VMEM((whole, depth), bf16),
            pltpu.VMEM((whole, depth), bf16),
            pltpu.VMEM((whole, depth), bf16),
            pltpu.VMEM((whole, units), bf16),
            pltpu.VMEM((whole, units), bf16),
            pltpu.VMEM((own, depth), f32),
            pltpu.VMEM((own, 1), f32),
            pltpu.VMEM((own, depth), f32),
            pltpu.VMEM((depth, width), f32),
            *_scatter_scratch(own, depth),
            pltpu.SemaphoreType.DMA((3, 3, CHUNKS)),
            pltpu.SemaphoreType.DMA((3, 3, CHUNKS)),
            pltpu.SemaphoreType.DMA((3, 3, CHUNKS)),
            pltpu.SemaphoreType.DMA((3, 3, CHUNKS)),
            pltpu.SemaphoreType.DMA((2, 2, pieces, 3)),
        ],
        compiler_params=pltpu.CompilerParams(
            collective_id=1, has_side_effects=True, vmem_limit_bytes=VMEM
        ),
        name="middle_layer",
    )(*arrays, up_bias, *vectors)


def last_kernel(
    group, pieces, halves_hbm, early_shards_hbm, block_hbm, grads_hbm, tokens_hbm, out_grad_hbm, in_proj_hbm,
    grad1_hbm, sums_ref, up_sum_ref, inputs_grad_hbm, final_hbm, small_ref,
    halves_ref, early_shards_ref, block_ref, grads_ref, tokens_ref, out_grad_ref, in_proj_ref, grad1_ref,
    inputs_grad_ref, final_ref, load_sems, store_sems, final_sems,
    own_acc, other_acc, stage_sib, stage_x, recv_sib, recv_x, attn_grad, half_recv, shard_recv,
    small_recv, small_group, scatter_send, scatter_recv, sems, small_sems,
):
    f32, bf16 = jnp.float32, jnp.bfloat16
    me, sib, cnt, dia = _partners()
    place = _place(group)
    own, depth = grad1_ref.shape
    width = in_proj_ref.shape[2]
    size = own // CHUNKS
    blocks = (me, sib, cnt, dia)
    bufs = (own_acc, other_acc, stage_sib, stage_x, recv_sib, recv_x)
    scatter = Scatter(bufs, scatter_send, scatter_recv, 0, size, sib, cnt)
    halves = (halves_ref.at[0], halves_ref.at[1], half_recv)
    reduces = [
        Reduce(
            k, depth // pieces, place, sems, attn_grad, halves[k], shard_recv.at[k], final_ref.at[k]
        )
        for k in range(3)
    ]
    down, up, attn = reduces
    early = pieces == CHUNKS

    def loop(body, count):
        def step(r, carry):
            body(r)
            return carry

        lax.fori_loop(0, count, step, 0)

    loads = [
        pltpu.make_async_copy(source, target, load_sems.at[k])
        for k, (source, target) in enumerate(
            (
                (halves_hbm, halves_ref),
                (early_shards_hbm, early_shards_ref),
                (block_hbm, block_ref),
                (grads_hbm, grads_ref),
                (tokens_hbm, tokens_ref),
                (out_grad_hbm, out_grad_ref),
                (in_proj_hbm, in_proj_ref),
                (grad1_hbm, grad1_ref),
            )
        )
    ]
    for load in loads:
        load.start()

    def store(r):
        rows = _rows(r * size, size)
        return pltpu.make_async_copy(inputs_grad_ref.at[rows], inputs_grad_hbm.at[rows], store_sems.at[r])

    def store_final(k, p):
        rows = _rows(p * (depth // pieces), depth // pieces)
        return pltpu.make_async_copy(final_ref.at[k, rows], final_hbm.at[k, rows], final_sems.at[k, p])

    small_ref[...] = jnp.zeros_like(small_ref)
    small_ref[:8, :] = sums_ref[...]
    small_ref[8:9, :] = up_sum_ref[...]
    _greet([{"mp": sib}, {"mp": cnt}, down.pair(), *[down.peer(g) for g in range(1, group)]])

    def known(k, p):
        return early and (k, p) in EARLY

    for load in loads[:3]:
        load.wait()
    for k in range(2):
        for p in range(pieces):
            if not known(k, p):
                reduces[k].send_shards(p)
    if early:
        down.final_half(0)[...] = block_ref[...]
        down.last(0, block_ref).start()
        for k, p in EARLY[1:]:
            reduces[k].send_sum(p, early_shards_ref.at[k], reduces[k].final_half(p))
    for load in loads[3:6]:
        load.wait()

    def weights(n):
        cols = _rows(n * COLS, COLS)
        attn_grad[cols, : 3 * width] = _tn(tokens_ref[:, cols], grads_ref[...]).astype(bf16)
        attn_grad[cols, 3 * width :] = out_grad_ref[cols, :]
        if early:
            attn.send_half(n)

    loop(weights, depth // COLS)
    if not early:
        attn.send_half(0)

    loads[6].wait()

    def partial_rows(r):
        chunk = jnp.concatenate(
            [grads_ref[_rows(b * own + r * size, size), :] for b in blocks], axis=0
        )

        def tile(cols):
            total = _nt(chunk[:, :width], in_proj_ref[0, cols, :])
            total = total + _nt(chunk[:, width : 2 * width], in_proj_ref[1, cols, :])
            return total + _nt(chunk[:, 2 * width :], in_proj_ref[2, cols, :])

        scatter.project(r, tile)
        scatter.finish(r)

    loop(partial_rows, CHUNKS)

    def bias(j):
        return jnp.sum(grads_ref[:, j * width : (j + 1) * width].astype(f32), axis=0, keepdims=True)

    small_ref[9:10, :width] = bias(0)
    small_ref[9:10, width : 2 * width] = bias(2)

    def small_step(k, rows, target):
        copy = _remote(
            small_ref.at[:rows], small_recv.at[k, :rows], small_sems.at[0, k], small_sems.at[1, k], target
        )
        copy.start()
        copy.wait()
        small_ref[:rows, :] += small_recv[k, :rows, :]

    def send_sum(k, p):
        reduces[k].wait_all(shard_recv.at[k], p, 1, 1)
        reduces[k].send_sum(p, shard_recv.at[k], reduces[k].final_half(p))

    def send_back(k, p):
        reduces[k].wait_all(shard_recv.at[k], p, 2, 1)
        reduces[k].last(p).start()

    small_step(0, 8, {"mp": sib})
    small_step(1, 8, {"mp": cnt})
    for k in range(2):
        for p in range(pieces):
            if not known(k, p):
                send_sum(k, p)

    def attn_half(p):
        attn.add_half(p)
        attn.send_shards(p)

    loop(attn_half, pieces)
    if early:
        for k, p in EARLY[1:]:
            send_back(k, p)
    small_step(2, small_ref.shape[0], down.pair())
    small_copies = [
        _remote(
            small_ref, small_group.at[place[1]], small_sems.at[0, 3], small_sems.at[1, 3], down.peer(g)
        )
        for g in range(1, group)
    ]
    for copy in small_copies:
        copy.start()
    small_group[place[1]] = small_ref[...]
    for k in range(2):
        for p in range(pieces):
            if not known(k, p):
                send_back(k, p)
    loop(partial(send_sum, 2), pieces)

    def finish(r):
        rows = _rows(r * size, size)
        inputs_grad_ref[rows, :] = (grad1_ref[rows, :] + scatter.result(r)).astype(bf16)
        store(r).start()
        scatter.sent(r)

    loads[7].wait()
    loop(finish, CHUNKS)
    others = small_group.at[1:]
    for side in (1, 0):
        pltpu.make_async_copy(others, others, small_sems.at[side, 3]).wait()
    total = small_group[0]
    for g in range(1, group):
        total = total + small_group[g]
    small_ref[...] = total
    loop(partial(send_back, 2), pieces)
    for k, reduce in enumerate(reduces):
        for p in range(pieces):
            if not known(k, p):
                reduce.wait_all(shard_recv.at[k], p, 1, 0)
            if not known(k, p) or p + k > 0:
                reduce.wait_all(shard_recv.at[k], p, 2, 0)
            if k == 2:
                reduce.first(p).wait_send()
            reduce.last(p).wait()
            store_final(k, p).start()
    loop(lambda r: store(r).wait(), CHUNKS)
    for k in range(3):
        for p in range(pieces):
            store_final(k, p).wait()


def last(mesh, halves, shards, block, grads, tokens, out_grad, in_proj, grad1, sums, up_sum):
    f32, bf16 = jnp.float32, jnp.bfloat16
    own, depth = grad1.shape
    group, pieces = _pieces(mesh, depth)
    half = depth // 2
    shard = half // pieces // group
    arrays = (halves, shards, block, grads, tokens, out_grad, in_proj, grad1)
    outs = [((own, depth), bf16), ((3, depth, depth), bf16), ((16, depth), f32)]
    return pl.pallas_call(
        partial(last_kernel, group, pieces),
        out_shape=[jax.ShapeDtypeStruct(*out) for out in outs],
        in_specs=[REMOTE] * 8 + [LOCAL] * 2,
        out_specs=[REMOTE] * 2 + [LOCAL],
        scratch_shapes=[
            *[pltpu.VMEM(array.shape, array.dtype) for array in arrays],
            *[pltpu.VMEM(*out) for out in outs[:2]],
            pltpu.SemaphoreType.DMA((8,)),
            pltpu.SemaphoreType.DMA((CHUNKS,)),
            pltpu.SemaphoreType.DMA((3, pieces)),
            *_scatter_scratch(own, depth),
            pltpu.VMEM((depth, depth), bf16),
            pltpu.VMEM((half, depth), bf16),
            pltpu.VMEM((3, pieces, group - 1, shard, depth), bf16),
            pltpu.VMEM((3, 16, depth), f32),
            pltpu.VMEM((group, 16, depth), f32),
            pltpu.SemaphoreType.DMA((1, 3, CHUNKS)),
            pltpu.SemaphoreType.DMA((1, 3, CHUNKS)),
            pltpu.SemaphoreType.DMA((2, 3, pieces, 4)),
            pltpu.SemaphoreType.DMA((2, 4)),
        ],
        compiler_params=pltpu.CompilerParams(
            collective_id=2, has_side_effects=True, vmem_limit_bytes=VMEM
        ),
        name="last_layer",
    )(*arrays, sums, up_sum)


def unpack_kernel(
    width, final_ref, small_ref, outputs_ref, inputs_grad_ref, down_ref, up_ref, in_ref, out_ref,
    qv_ref, up_bias_ref, *refs,
):
    f32 = jnp.float32
    vectors, outputs_out, inputs_grad_out = refs[:6], refs[6], refs[7]
    down_ref[...] = final_ref[0].astype(f32)
    up_ref[...] = final_ref[1].astype(f32)
    for j in range(3):
        in_ref[j] = final_ref[2, :, j * width : (j + 1) * width].astype(f32)
    out_ref[...] = final_ref[2, :, 3 * width :].astype(f32).T
    outputs_out[...] = outputs_ref[...]
    inputs_grad_out[...] = inputs_grad_ref[...]
    for k, vector in enumerate(vectors):
        vector[...] = small_ref[k : k + 1, :]
    up_bias_ref[...] = small_ref[8:9, :]
    for k in range(2):
        qv_ref[k : k + 1, :] = small_ref[9:10, k * width : (k + 1) * width]


def unpack(final, small, outputs, inputs_grad, width):
    f32 = jnp.float32
    own, depth = outputs.shape
    steps = depth // 128
    part = own // steps
    matrix = pl.BlockSpec((128, depth), lambda i: (i, 0))
    tokens = pl.BlockSpec((part, depth), lambda i: (i, 0))
    vector = pl.BlockSpec((1, depth), lambda i: (0, 0))
    shapes = [
        ((depth, depth), f32, matrix),
        ((depth, depth), f32, matrix),
        ((3, depth, width), f32, pl.BlockSpec((3, 128, width), lambda i: (0, i, 0))),
        ((width, depth), f32, pl.BlockSpec((width, 128), lambda i: (0, i))),
        ((2, width), f32, pl.BlockSpec((2, width), lambda i: (0, 0))),
        *[((1, depth), f32, vector)] * 7,
        ((own, depth), jnp.bfloat16, tokens),
        ((own, depth), jnp.bfloat16, tokens),
    ]
    return pl.pallas_call(
        partial(unpack_kernel, width),
        grid=(steps,),
        in_specs=[
            pl.BlockSpec((3, 128, depth), lambda i: (0, i, 0)),
            pl.BlockSpec((16, depth), lambda i: (0, 0)),
            tokens,
            tokens,
        ],
        out_specs=[spec for _, _, spec in shapes],
        out_shape=[jax.ShapeDtypeStruct(shape, dtype) for shape, dtype, _ in shapes],
        compiler_params=pltpu.CompilerParams(vmem_limit_bytes=VMEM),
        name="unpack_gradients",
    )(final, small, outputs, inputs_grad)


def shards(
    mesh,
    inputs,
    in_proj,
    qv_bias,
    out_proj,
    out_bias,
    attn_gain,
    attn_shift,
    up_proj,
    up_bias,
    down_proj,
    down_bias,
    ffn_gain,
    ffn_shift,
    segments,
    padding,
    cotangent,
):
    places, real = segment_places(segments, padding)
    vectors = [v[None] for v in (out_bias, attn_gain, attn_shift, down_bias, ffn_gain, ffn_shift)]
    tokens, qkv = project_tokens(inputs, in_proj, qv_bias)
    context, lse_rows = attention_forward(qkv, places, real)
    outputs, grad1, context_grad, halves, pieces, block, out_grad, sums, up_sum = middle(
        mesh, context, out_proj, inputs, up_proj, down_proj, cotangent, up_bias[None], vectors
    )
    grads = attention_backward(qkv, context_grad, context, lse_rows, places, real)
    inputs_grad, final, small = last(
        mesh, halves, pieces, block, grads, tokens, out_grad, in_proj, grad1, sums, up_sum
    )
    down_grad, up_grad, in_grad, out_grad, qv_grad, up_bias_grad, *vectors, outputs, inputs_grad = unpack(
        final, small, outputs, inputs_grad, in_proj.shape[2]
    )
    vectors = [v[0] for v in vectors]
    return (
        outputs,
        inputs_grad,
        in_grad,
        qv_grad,
        out_grad,
        *vectors[:3],
        up_grad,
        up_bias_grad[0],
        down_grad,
        *vectors[3:],
    )


def solution(mesh):
    return jax.shard_map(
        partial(shards, mesh),
        mesh=mesh,
        in_specs=(
            P(("dp", "mp"), None),
            P(None, None, "mp"),
            P(None, "mp"),
            P("mp", None),
            P(),
            P(),
            P(),
            P(None, "mp"),
            P("mp"),
            P("mp", None),
            P(),
            P(),
            P(),
            P("dp", None),
            P("dp", None),
            P(("dp", "mp"), None),
        ),
        out_specs=(
            P(("dp", "mp"), None),
            P(("dp", "mp"), None),
            P(None, None, "mp"),
            P(None, "mp"),
            P("mp", None),
            P(),
            P(),
            P(),
            P(None, "mp"),
            P("mp"),
            P("mp", None),
            P(),
            P(),
            P(),
        ),
        check_vma=False,
    )
```

```python
from functools import partial
import math

import jax
import jax.numpy as jnp
from jax import lax
from jax.experimental import pallas as pl
from jax.experimental.pallas import tpu as pltpu
from jax.sharding import PartitionSpec as P

HEAD = 64
BLOCK = 256
CHUNKS = 4
COLS = 256
VMEM = 60 * 2**20
REMOTE = pl.BlockSpec(memory_space=pl.ANY)
LOCAL = pl.BlockSpec(memory_space=pltpu.VMEM)
SCALARS = pl.BlockSpec(memory_space=pltpu.SMEM)
MESH = pl.DeviceIdType.MESH


EPSILON = 1e-05


NEG = -1e30


def _head_masks(heads, width, value):
    lane = lax.broadcasted_iota(jnp.int32, (1, width), 1) // HEAD
    return [jnp.where(lane == h, value, 0.0).astype(jnp.bfloat16) for h in range(heads)]


def _nt(a, b):
    return lax.dot_general(a, b, (((1,), (1,)), ((), ())), preferred_element_type=jnp.float32)


def _tn(a, b):
    return lax.dot_general(a, b, (((0,), (0,)), ((), ())), preferred_element_type=jnp.float32)


def _nn(a, b):
    return jnp.dot(a, b, preferred_element_type=jnp.float32)


def _column(row):
    wide = jnp.broadcast_to(row.astype(jnp.float32), (128, row.shape[1])).T.astype(jnp.int32)
    return jnp.concatenate([wide] * (BLOCK // 128), axis=1)


def _bias(seg_ref, pad_ref, query_rows, key_rows):
    seg_q, pad_q = seg_ref[:, query_rows], pad_ref[:, query_rows]
    seg_k, pad_k = _column(seg_ref[:, key_rows]), _column(pad_ref[:, key_rows])
    allowed = (seg_k == seg_q) & ((pad_k > 0) | (pad_q == 0))
    return jnp.where(allowed, 0.0, NEG).astype(jnp.float32)


def _meets(places_ref, left):
    edge = left * BLOCK + BLOCK - 1
    return places_ref[0, edge] == places_ref[0, edge + 1]


def _neighbours(places_ref, i, blocks, body):
    @pl.when(i > 0)
    def _():
        @pl.when(_meets(places_ref, jnp.maximum(i - 1, 0)))
        def _():
            body(i - 1)

    @pl.when(i < blocks - 1)
    def _():
        @pl.when(_meets(places_ref, jnp.minimum(i, blocks - 2)))
        def _():
            body(i + 1)


def _block_copies(source, target, sems):
    def copy(i):
        rows = _rows(i * BLOCK, BLOCK)
        return pltpu.make_async_copy(source.at[rows], target.at[rows], sems.at[i])

    return copy


def _loop(count, body):
    def step(i, carry):
        body(i)
        return carry

    lax.fori_loop(0, count, step, 0)


def attention_forward_kernel(
    heads, blocks, places_ref, qkv_hbm, seg_ref, pad_ref, context_hbm, lse_ref,
    qkv_ref, context_ref, peak_ref, total_ref, acc_ref, load_sems, store_sems,
):
    bf16 = jnp.bfloat16
    width = context_ref.shape[1]
    load = _block_copies(qkv_hbm, qkv_ref, load_sems)
    store = _block_copies(context_ref, context_hbm, store_sems)
    _loop(blocks, lambda i: load(i).start())
    scaled = _head_masks(heads, width, 1.0 / math.sqrt(HEAD))
    load(0).wait()

    def attend(i):
        @pl.when(i + 1 < blocks)
        def _():
            load(i + 1).wait()

        query_rows = _rows(i * BLOCK, BLOCK)
        query = qkv_ref[query_rows, :width]

        def parts(j):
            rows = _rows(j * BLOCK, BLOCK)
            return (
                qkv_ref[rows, width : 2 * width],
                qkv_ref[rows, 2 * width :].T,
                _bias(seg_ref, pad_ref, query_rows, rows),
            )

        key, value, bias = parts(i)
        for h in range(heads):
            scores = _nt(key, query * scaled[h]) + bias
            peak = jnp.max(scores, axis=0, keepdims=True)
            expo = jnp.exp(scores - peak)
            peak_ref[h] = peak
            total_ref[h] = jnp.sum(expo, axis=0, keepdims=True)
            place = pl.ds(h * HEAD, HEAD)
            acc_ref[place, :] = _nn(value[h * HEAD : (h + 1) * HEAD], expo.astype(bf16))

        def other(j):
            key, value, bias = parts(j)
            for h in range(heads):
                scores = _nt(key, query * scaled[h]) + bias
                old = peak_ref[h]
                peak = jnp.maximum(old, jnp.max(scores, axis=0, keepdims=True))
                expo = jnp.exp(scores - peak)
                ratio = jnp.exp(old - peak)
                peak_ref[h] = peak
                total_ref[h] = total_ref[h] * ratio + jnp.sum(expo, axis=0, keepdims=True)
                place = pl.ds(h * HEAD, HEAD)
                acc_ref[place, :] = acc_ref[place, :] * ratio + _nn(
                    value[h * HEAD : (h + 1) * HEAD], expo.astype(bf16)
                )

        _neighbours(places_ref, i, blocks, other)
        for h in range(heads):
            place = pl.ds(h * HEAD, HEAD)
            acc_ref[place, :] = acc_ref[place, :] / total_ref[h]
            lse_ref[h : h + 1, query_rows] = peak_ref[h] + jnp.log(total_ref[h])
        context_ref[query_rows, :] = acc_ref[...].astype(bf16).T
        store(i).start()

    _loop(blocks, attend)
    _loop(blocks, lambda i: store(i).wait())


def attention_forward(qkv, places, padding):
    length, width = qkv.shape[0], qkv.shape[1] // 3
    heads, blocks = width // HEAD, length // BLOCK
    return pl.pallas_call(
        partial(attention_forward_kernel, heads, blocks),
        in_specs=[SCALARS, REMOTE, LOCAL, LOCAL],
        out_specs=[REMOTE, LOCAL],
        scratch_shapes=[
            pltpu.VMEM((length, 3 * width), jnp.bfloat16),
            pltpu.VMEM((length, width), jnp.bfloat16),
            pltpu.VMEM((heads, 1, BLOCK), jnp.float32),
            pltpu.VMEM((heads, 1, BLOCK), jnp.float32),
            pltpu.VMEM((width, BLOCK), jnp.float32),
            pltpu.SemaphoreType.DMA((blocks,)),
            pltpu.SemaphoreType.DMA((blocks,)),
        ],
        out_shape=[
            jax.ShapeDtypeStruct((length, width), jnp.bfloat16),
            jax.ShapeDtypeStruct((8, length), jnp.float32),
        ],
        compiler_params=pltpu.CompilerParams(vmem_limit_bytes=VMEM),
        name="attention_forward",
    )(places, qkv, places, padding)


def segment_places(segments, padding):
    row_count, seq_len = segments.shape
    if row_count > 1:
        segments = segments + jnp.arange(row_count, dtype=jnp.int32)[:, None] * (seq_len + 1)
    return segments.reshape(1, -1), padding.reshape(1, -1)


def _partners():
    me = lax.axis_index("mp")
    core = lax.rem(me, 2)
    sib = me + 1 - 2 * core
    cnt = lax.rem(me + 2, 4)
    dia = lax.rem(cnt + 1, 2) + cnt - lax.rem(cnt, 2)
    return me, sib, cnt, dia


def _remote(src, dst, send, recv, target):
    return pltpu.make_async_remote_copy(
        src_ref=src, dst_ref=dst, send_sem=send, recv_sem=recv, device_id=target, device_id_type=MESH
    )


def _greet(targets):
    barrier = pltpu.get_barrier_semaphore()
    for target in targets:
        pl.semaphore_signal(barrier, inc=1, device_id=target, device_id_type=MESH)
    pl.semaphore_wait(barrier, len(targets))


def _rows(start, size):
    return pl.ds(pl.multiple_of(start, size), size)


class Gather:
    def __init__(self, buffer, send, recv, stage, size, sib, cnt):
        self.buffer, self.send, self.recv = buffer, send, recv
        self.stage, self.size, self.sib, self.cnt = stage, size, sib, cnt

    def slot(self, r, k):
        return self.buffer.at[_rows((r * 4 + k) * self.size, self.size)]

    def copy(self, r, kind):
        src, dst, target = ((0, 1, self.sib), (0, 2, self.cnt), (2, 3, self.sib))[kind]
        return _remote(
            self.slot(r, src),
            self.slot(r, dst),
            self.send.at[self.stage, kind, r],
            self.recv.at[self.stage, kind, r],
            {"mp": target},
        )

    def start(self, r):
        self.copy(r, 1).start()
        self.copy(r, 0).start()

    def forward(self, r):
        self.copy(r, 1).wait_recv()
        self.copy(r, 2).start()

    def arrive(self, r):
        self.copy(r, 0).wait_recv()
        self.copy(r, 2).wait_recv()

    def sent(self, r):
        for kind in range(3):
            self.copy(r, kind).wait_send()


class Scatter:
    def __init__(self, bufs, send, recv, stage, size, sib, cnt):
        self.own, self.other, self.stage_sib, self.stage_x, self.recv_sib, self.recv_x = bufs
        self.send, self.recv = send, recv
        self.stage, self.size, self.sib, self.cnt = stage, size, sib, cnt

    def copy(self, r, kind):
        rows = _rows(r * self.size, self.size)
        src, dst, target = (
            (self.stage_sib.at[0, rows], self.recv_sib.at[0, rows], self.sib),
            (self.stage_sib.at[1, rows], self.recv_sib.at[1, rows], self.sib),
            (self.stage_x.at[rows], self.recv_x.at[rows], self.cnt),
        )[kind]
        return _remote(
            src, dst, self.send.at[self.stage, kind, r], self.recv.at[self.stage, kind, r], {"mp": target}
        )

    def sent(self, r):
        for kind in range(3):
            self.copy(r, kind).wait_send()

    def project(self, r, tile):
        size = self.size
        rows = _rows(r * size, size)

        def column(n, carry):
            cols = _rows(n * COLS, COLS)
            part = tile(cols)
            self.own[rows, cols] = part[:size]
            self.stage_sib[1, rows, cols] = part[size : 2 * size].astype(jnp.bfloat16)
            self.other[rows, cols] = part[2 * size : 3 * size]
            self.stage_sib[0, rows, cols] = part[3 * size :].astype(jnp.bfloat16)
            return carry

        lax.fori_loop(0, self.own.shape[1] // COLS, column, 0)
        self.copy(r, 0).start()
        self.copy(r, 1).start()

    def finish(self, r):
        rows = _rows(r * self.size, self.size)
        self.copy(r, 0).wait_recv()
        self.stage_x[rows, :] = (
            self.other[rows, :] + self.recv_sib[0, rows, :].astype(jnp.float32)
        ).astype(jnp.bfloat16)
        self.copy(r, 2).start()
        self.copy(r, 1).wait_recv()
        self.own[rows, :] += self.recv_sib[1, rows, :].astype(jnp.float32)

    def result(self, r):
        rows = _rows(r * self.size, self.size)
        self.copy(r, 2).wait_recv()
        return self.own[rows, :] + self.recv_x[rows, :].astype(jnp.float32)


def _scatter_scratch(own, width):
    f32, bf16 = jnp.float32, jnp.bfloat16
    return [
        pltpu.VMEM((own, width), f32),
        pltpu.VMEM((own, width), f32),
        pltpu.VMEM((2, own, width), bf16),
        pltpu.VMEM((own, width), bf16),
        pltpu.VMEM((2, own, width), bf16),
        pltpu.VMEM((own, width), bf16),
    ]


def _norm(summed):
    center = summed - jnp.mean(summed, axis=-1, keepdims=True)
    variance = jnp.mean(center * center, axis=-1, keepdims=True)
    inverse = lax.rsqrt(variance + EPSILON)
    return center * inverse, inverse


def _norm_back(scaled, unit, inverse):
    return inverse * (
        scaled
        - jnp.mean(scaled, axis=-1, keepdims=True)
        - unit * jnp.mean(scaled * unit, axis=-1, keepdims=True)
    )


def project_kernel(
    inputs_ref, in_proj_ref, qv_bias_ref, tokens_hbm, qkv_hbm, tokens_ref, qkv_ref, weights,
    send, recv, load_sems, store_sems,
):
    f32, bf16 = jnp.float32, jnp.bfloat16
    me, sib, cnt, dia = _partners()
    own, width = inputs_ref.shape[0], in_proj_ref.shape[2]
    size = own // CHUNKS
    mine = _rows(me * own, own)
    keep = pltpu.make_async_copy(inputs_ref, tokens_ref.at[mine], load_sems.at[0])
    fetch = pltpu.make_async_copy(in_proj_ref, weights, load_sems.at[1])
    fetch.start()
    keep.start()
    _greet([{"mp": sib}, {"mp": cnt}])

    def copy(r, kind):
        here = inputs_ref.at[_rows(r * size, size)]
        place = _rows((cnt if kind == 2 else me) * own + r * size, size)
        src, target = ((here, sib), (here, cnt), (tokens_ref.at[place], sib))[kind]
        return _remote(src, tokens_ref.at[place], send.at[kind, r], recv.at[kind, r], {"mp": target})

    for r in range(CHUNKS):
        copy(r, 1).start()
        copy(r, 0).start()

    def stores(first, rows, k):
        place = _rows(first, rows)
        return [
            pltpu.make_async_copy(tokens_ref.at[place], tokens_hbm.at[place], store_sems.at[0, k]),
            pltpu.make_async_copy(qkv_ref.at[place], qkv_hbm.at[place], store_sems.at[1, k]),
        ]

    def compute(first):
        place = _rows(first, size)
        block = tokens_ref[place, :]
        for j in range(3):
            part = jnp.dot(block, weights[j], preferred_element_type=f32)
            if j != 1:
                part = part + qv_bias_ref[j // 2 : j // 2 + 1, :]
            qkv_ref[place, j * width : (j + 1) * width] = part.astype(bf16)

    fetch.wait()
    keep.wait()
    _loop(CHUNKS, lambda r: compute(me * own + r * size))
    for store in stores(me * own, own, 0):
        store.start()

    def sib_part(r):
        copy(r, 0).wait_recv()
        compute(sib * own + r * size)

    _loop(CHUNKS, sib_part)
    for store in stores(sib * own, own, 1):
        store.start()

    def far_part(r):
        copy(r, 1).wait_recv()
        copy(r, 2).start()
        compute(cnt * own + r * size)
        for store in stores(cnt * own + r * size, size, 2 + 2 * r):
            store.start()
        copy(r, 2).wait_recv()
        compute(dia * own + r * size)
        for store in stores(dia * own + r * size, size, 3 + 2 * r):
            store.start()

    _loop(CHUNKS, far_part)
    for k in range(2):
        for store in stores((me, sib)[k] * own, own, k):
            store.wait()

    def drain(r):
        for kind in range(3):
            copy(r, kind).wait_send()
        for k, block in enumerate((cnt, dia)):
            for store in stores(block * own + r * size, size, 2 + 2 * r + k):
                store.wait()

    _loop(CHUNKS, drain)


def project_tokens(inputs, in_proj, qv_bias):
    own, depth = inputs.shape
    width = in_proj.shape[2]
    shapes = [(4 * own, depth), (4 * own, 3 * width)]
    return pl.pallas_call(
        project_kernel,
        out_shape=[jax.ShapeDtypeStruct(shape, jnp.bfloat16) for shape in shapes],
        in_specs=[REMOTE, REMOTE, LOCAL],
        out_specs=[REMOTE] * 2,
        scratch_shapes=[
            *[pltpu.VMEM(shape, jnp.bfloat16) for shape in shapes],
            pltpu.VMEM(in_proj.shape, jnp.bfloat16),
            pltpu.SemaphoreType.DMA((3, CHUNKS)),
            pltpu.SemaphoreType.DMA((3, CHUNKS)),
            pltpu.SemaphoreType.DMA((2,)),
            pltpu.SemaphoreType.DMA((2, 2 + 2 * CHUNKS)),
        ],
        compiler_params=pltpu.CompilerParams(
            collective_id=0, has_side_effects=True, vmem_limit_bytes=VMEM
        ),
        name="project_tokens",
    )(inputs, in_proj, qv_bias)


class Reduce:
    def __init__(self, rows, bits, order, source, work, final, sems):
        self.rows, self.order, self.source, self.work, self.final, self.sems = (
            rows, order, source, work, final, sems
        )
        self.steps = len(order)
        dp = lax.axis_index("dp")
        self.bit = [lax.rem(dp // (1 << b), 2) for b in order]
        self.peer = [{"dp": dp + (1 << b) * (1 - 2 * bit)} for b, bit in zip(order, self.bit)]

    def size(self, s):
        return self.rows >> s

    def start(self, n, s):
        first = n * self.rows
        for t in range(s):
            first = first + self.bit[t] * self.size(t + 1)
        return first

    def held(self, n, s):
        if s == 0:
            return self.source(n)
        return self.work, n * self.rows + self.rows - 2 * self.size(s)

    def halve(self, n, s):
        ref, first = self.held(n, s)
        half = self.size(s + 1)
        there, place = self.held(n, s + 1)
        return _remote(
            ref.at[_rows(first + (1 - self.bit[s]) * half, half)],
            there.at[_rows(place, half)],
            self.sems.at[0, n, s],
            self.sems.at[1, n, s],
            self.peer[s],
        )

    def double(self, n, s):
        block = self.final.at[_rows(self.start(n, s + 1), self.size(s + 1))]
        k = 2 * self.steps - 1 - s
        return _remote(block, block, self.sems.at[0, n, k], self.sems.at[1, n, k], self.peer[s])

    def step(self, n, k):
        steps = self.steps
        if 0 < k <= steps:
            s = k - 1
            half = self.size(s + 1)
            self.halve(n, s).wait_recv()
            ref, first = self.held(n, s)
            there, place = self.held(n, s + 1)
            total = there[_rows(place, half), :].astype(jnp.float32) + ref[
                _rows(first + self.bit[s] * half, half), :
            ].astype(jnp.float32)
            if k < steps:
                there[_rows(place, half), :] = total.astype(jnp.bfloat16)
            else:
                self.final[_rows(self.start(n, steps), half), :] = total.astype(jnp.bfloat16)
        if k > steps:
            self.double(n, 2 * steps - k).wait_recv()
        if k < steps:
            self.halve(n, k).start()
        elif k < 2 * steps:
            self.double(n, 2 * steps - 1 - k).start()

    def sent(self, n):
        for s in range(self.steps):
            if s:
                self.halve(n, s).wait_send()
            self.double(n, s).wait_send()


def main_kernel(bits, pieces, *refs):
    f32, bf16 = jnp.float32, jnp.bfloat16
    (context_hbm, out_proj_hbm, inputs_hbm, up_hbm, down_hbm, cotangent_hbm, qkv_hbm, tokens_hbm, in_proj_hbm,
     lse_ref, seg_ref, pad_ref, up_bias_ref, *refs) = refs
    vectors, refs = [v[...] for v in refs[:6]], refs[6:]
    out_bias, attn_gain, attn_shift, down_bias, ffn_gain, ffn_shift = vectors
    (outputs_hbm, inputs_grad_hbm, final_hbm, small_ref,
     context_ref, out_proj_ref, inputs_ref, up_ref, down_ref, outputs_ref,
     weight_grads, normed_full, grad2_full, grad1_full, active, back, unit1, inverse1, grad_own, query_acc,
     own_acc, other_acc, stage_sib, stage_x, recv_sib, recv_x, work, final, small_recv,
     load_sems, block_sems, store_sems, final_sems, gather_send, gather_recv, scatter_send, scatter_recv,
     sems, small_sems) = refs
    me, sib, cnt, dia = _partners()
    own, depth = inputs_ref.shape
    units, width = up_ref.shape[1], out_proj_ref.shape[0]
    length = 4 * own
    heads, token_blocks = width // HEAD, length // BLOCK
    size, whole = own // CHUNKS, length // CHUNKS
    blocks = (me, sib, cnt, dia)
    early = pieces == CHUNKS
    loop = partial(_loop, CHUNKS)

    def context_load(r):
        return [
            pltpu.make_async_copy(
                context_hbm.at[_rows(b * own + r * size, size)],
                context_ref.at[_rows((r * 4 + k) * size, size)],
                block_sems.at[k, r],
            )
            for k, b in enumerate(blocks)
        ]

    loads = [
        pltpu.make_async_copy(source, target, load_sems.at[k])
        for k, (source, target) in enumerate(
            (
                (out_proj_hbm, out_proj_ref),
                (inputs_hbm, inputs_ref),
                (up_hbm, up_ref),
                (down_hbm, down_ref),
                (cotangent_hbm, inputs_ref),
                (qkv_hbm, active.at[:, : 3 * width]),
                (tokens_hbm, normed_full),
                (context_hbm, back.at[:, width : 2 * width]),
                *[(in_proj_hbm.at[j], up_ref.at[:, j * width : (j + 1) * width]) for j in range(3)],
            )
        )
    ]
    loads[0].start()
    loop(lambda r: [load.start() for load in context_load(r)])
    for load in loads[1:4]:
        load.start()

    def store(k, r):
        rows = _rows(r * size, size)
        target = (outputs_hbm, inputs_grad_hbm)[k]
        return pltpu.make_async_copy(outputs_ref.at[rows], target.at[rows], store_sems.at[k, r])

    bufs = (own_acc, other_acc, stage_sib, stage_x, recv_sib, recv_x)
    gathers = [
        Gather(buf, gather_send, gather_recv, stage, size, sib, cnt)
        for stage, buf in enumerate((normed_full, grad2_full, grad1_full))
    ]
    scatters = [
        Scatter(bufs, scatter_send, scatter_recv, stage, size, sib, cnt) for stage in range(4)
    ]
    piece = depth // pieces
    first = tuple(range(bits))
    reduce = Reduce(piece, bits, first, lambda n: (weight_grads, n * piece), work, final, sems)

    def attn_source(n):
        return weight_grads, (n - 2 * pieces) * piece

    later = [
        Reduce(piece, bits, order, attn_source, work, final, sems)
        for order in (first, first[1:] + first[:1])
    ]
    small_ref[...] = jnp.zeros_like(small_ref)
    _greet([{"mp": sib}, {"mp": cnt}, *reduce.peer])

    def add_sum(k, value):
        small_ref[k : k + 1, :] += jnp.sum(value, axis=0, keepdims=True)

    loads[0].wait()

    def attended(r):
        for load in context_load(r):
            load.wait()
        chunk = context_ref[_rows(r * whole, whole), :]
        scatters[0].project(r, lambda cols: _nn(chunk, out_proj_ref[:, cols]))
        scatters[0].finish(r)

    loop(attended)
    loads[1].wait()

    def lower_norm(r):
        rows = _rows(r * size, size)
        unit, inverse = _norm(inputs_ref[rows, :].astype(f32) + scatters[0].result(r) + out_bias)
        unit1[rows, :] = unit
        inverse1[rows, :] = inverse
        gathers[0].slot(r, 0)[...] = (unit * attn_gain + attn_shift).astype(bf16)
        gathers[0].start(r)

    loop(lower_norm)
    loads[4].start()
    loads[2].wait()
    loads[3].wait()

    def feed_forward(r):
        rows = _rows(r * whole, whole)
        gathers[0].forward(r)
        gathers[0].arrive(r)
        scatters[0].sent(r)

        def column(n, carry):
            cols = _rows(n * COLS, COLS)
            upper = _nn(normed_full[rows, :], up_ref[:, cols]) + up_bias_ref[:, cols]
            cdf = 0.5 + 0.5 * lax.erf(upper * math.sqrt(0.5))
            pdf = jnp.exp(upper * upper * -0.5) * (1.0 / math.sqrt(2.0 * math.pi))
            active[rows, cols] = (upper * cdf).astype(bf16)
            back[rows, cols] = (cdf + upper * pdf).astype(bf16)
            return carry

        lax.fori_loop(0, units // COLS, column, 0)
        scatters[1].project(r, lambda cols: _nn(active[rows, :], down_ref[:, cols]))
        scatters[1].finish(r)

    loop(feed_forward)
    loads[4].wait()

    def upper_norm(r):
        rows = _rows(r * size, size)
        normed = unit1[rows, :] * attn_gain + attn_shift
        unit, inverse = _norm(normed + scatters[1].result(r) + down_bias)
        outputs_ref[rows, :] = (unit * ffn_gain + ffn_shift).astype(bf16)
        store(0, r).start()
        cotangent = inputs_ref[rows, :].astype(f32)
        grad = _norm_back(cotangent * ffn_gain, unit, inverse)
        gathers[1].slot(r, 0)[...] = grad.astype(bf16)
        gathers[1].start(r)
        grad_own[rows, :] = grad
        add_sum(3, grad)
        add_sum(4, cotangent * unit)
        add_sum(5, cotangent)

    loop(upper_norm)

    def feed_back(r):
        rows = _rows(r * whole, whole)
        gathers[1].forward(r)
        gathers[1].arrive(r)
        scatters[1].sent(r)

        def column(n, carry):
            cols = _rows(n * COLS, COLS)
            incoming = _nt(grad2_full[rows, :], down_ref[cols, :])
            upper_back = (back[rows, cols].astype(f32) * incoming).astype(bf16)
            back[rows, cols] = upper_back
            small_ref[8:9, cols] += jnp.sum(upper_back.astype(f32), axis=0, keepdims=True)
            return carry

        lax.fori_loop(0, units // COLS, column, 0)
        scatters[2].project(r, lambda cols: _nt(back[rows, :], up_ref[cols, :]))
        scatters[2].finish(r)

    loop(feed_back)
    for load in loads[8:]:
        load.start()

    def weights(k, p):
        cols = _rows(p * (depth // CHUNKS), depth // CHUNKS)
        place = _rows(k * depth + p * (depth // CHUNKS), depth // CHUNKS)
        if k == 0:
            weight_grads[place, :] = _tn(active[:, cols], grad2_full[...]).astype(bf16)
        else:
            weight_grads[place, :] = _tn(normed_full[:, cols], back[...]).astype(bf16)

    def lower_back(r):
        for k in range(2):

            @pl.when(r // 2 == k)
            def _():
                for h in range(2):
                    p = 2 * r - 4 * k + h
                    weights(k, p)
                    if early:
                        reduce.step(k * pieces + p, 0)
                if not early:

                    @pl.when(r == 2 * k + 1)
                    def _():
                        reduce.step(k, 0)

        if early:

            @pl.when(r >= 2)
            def _():
                reduce.step(r - 2, 1)

        rows = _rows(r * size, size)
        incoming = grad_own[rows, :] + scatters[2].result(r)
        unit = unit1[rows, :]
        grad = _norm_back(incoming * attn_gain, unit, inverse1[rows, :])
        gathers[2].slot(r, 0)[...] = grad.astype(bf16)
        gathers[2].start(r)
        grad_own[rows, :] = grad
        add_sum(0, grad)
        add_sum(1, incoming * unit)
        add_sum(2, incoming)

    loop(lower_back)
    gathers_done = lambda r: [gather.sent(r) for gather in gathers[:2]]
    loop(gathers_done)
    for load in loads[5:8]:
        load.start()

    def context_back(r):
        if early:
            reduce.step(r + 2, 1)
            reduce.step(r, 2)

            @pl.when(r >= 2)
            def _():
                reduce.step(r - 2, 3)

        rows = _rows(r * whole, whole)
        gathers[2].forward(r)
        gathers[2].arrive(r)
        scatters[2].sent(r)
        grad = _nt(grad1_full[rows, :], out_proj_ref[...]).astype(bf16)
        for k, b in enumerate(blocks):
            part = _rows(b * own + r * size, size)
            back[part, :width] = grad[k * size : (k + 1) * size]

    loop(context_back)
    loop(lambda r: gathers[2].sent(r))
    for load in loads[5:8]:
        load.wait()

    scaled = _head_masks(heads, width, 1.0 / math.sqrt(HEAD))
    plain = _head_masks(heads, width, 1.0)
    keys_acc, values_acc = unit1, other_acc
    keys_acc[...] = jnp.zeros_like(keys_acc)
    values_acc[...] = jnp.zeros_like(values_acc)
    grads = grad2_full
    per = own // BLOCK

    def spot(j):
        return _rows(lax.rem(j, per) * BLOCK, BLOCK), _rows(j // per * width, width)

    def attend(i):
        if early:

            @pl.when(i < 2)
            def _():
                reduce.step(i + 6, 1)

            @pl.when(i < 4)
            def _():
                reduce.step(i + 4, 2)

            @pl.when(i < 6)
            def _():
                reduce.step(i + 2, 3)

            reduce.step(i, 4)

            @pl.when((i >= 3) & (i < 7))
            def _():
                reduce.step(i - 3, 5)

        query_rows = _rows(i * BLOCK, BLOCK)
        query, grad = active[query_rows, :width], back[query_rows, :width]
        product = (grad.astype(f32) * back[query_rows, width : 2 * width].astype(f32)).T
        row_dots = [
            jnp.sum(product[h * HEAD : (h + 1) * HEAD], axis=0, keepdims=True) for h in range(heads)
        ]
        query_acc[...] = jnp.zeros_like(query_acc)

        def block(j, carry):
            rows = _rows(j * BLOCK, BLOCK)
            bias = _bias(seg_ref, pad_ref, query_rows, rows)
            key, value = active[rows, width : 2 * width], active[rows, 2 * width : 3 * width]
            key_rows = (key * (1.0 / math.sqrt(HEAD))).astype(bf16).T
            key_add = jnp.zeros((BLOCK, width), f32)
            value_add = jnp.zeros((BLOCK, width), f32)
            for h in range(heads):
                query_h, grad_h = query * scaled[h], grad * plain[h]
                scores = _nt(key, query_h) + bias
                prob = jnp.exp(scores - lse_ref[h : h + 1, query_rows])
                score_grad = (prob * (_nt(value, grad_h) - row_dots[h])).astype(bf16)
                key_add = key_add + _nn(score_grad, query_h)
                value_add = value_add + _nn(prob.astype(bf16), grad_h)
                query_acc[pl.ds(h * HEAD, HEAD), :] += _nn(key_rows[h * HEAD : (h + 1) * HEAD], score_grad)
            keys_acc[spot(j)] += key_add
            values_acc[spot(j)] += value_add
            return carry

        lax.fori_loop(jnp.maximum(i - 1, 0), jnp.minimum(i + 2, token_blocks), block, 0)
        grads[query_rows, :width] = query_acc[...].astype(bf16).T

    _loop(token_blocks, attend)

    def keep(j):
        rows = _rows(j * BLOCK, BLOCK)
        grads[rows, width : 2 * width] = keys_acc[spot(j)].astype(bf16)
        grads[rows, 2 * width : 3 * width] = values_acc[spot(j)].astype(bf16)

    _loop(token_blocks, keep)

    for n in range(2 * pieces):
        if not early:
            reduce.step(n, 1)
        reduce.halve(n, 0).wait_send()

    def kind(p):
        return later[1 if early and p % 2 else 0]

    def attn_weights(n):
        cols = _rows(n * COLS, COLS)
        weight_grads[cols, : 3 * width] = _tn(normed_full[:, cols], grads[:, : 3 * width]).astype(bf16)
        weight_grads[cols, 3 * width :] = _tn(grad1_full[:, cols], context_ref[...]).astype(bf16)

    for n in range(depth // COLS):
        attn_weights(n)
        if early:
            kind(n).step(2 * pieces + n, 0)
    if not early:
        kind(0).step(2 * pieces, 0)

    def tasks():
        steps = 2 * bits
        if not early:
            for k in range(1, steps + 1):
                for n in range(2 if k > 1 else 0):
                    yield reduce, n, k
                yield kind(0), 2 * pieces, k
            return
        ffn = [(4, 5), (5, 5), (6, 5), (7, 5), (0, 6), (1, 6), (2, 6), (3, 6)]
        for k in range(1, steps):
            for p in (1, 0, 3, 2):
                yield kind(p), 2 * pieces + p, k
                if ffn:
                    yield reduce, *ffn.pop(0)
        for n in range(4, 8):
            yield reduce, n, 6
        for p in range(pieces):
            yield kind(p), 2 * pieces + p, steps

    todo = list(tasks())

    def store_final(n):
        rows = _rows(n * piece, piece)
        return pltpu.make_async_copy(final.at[rows], final_hbm.at[rows], final_sems.at[n])

    def work_off(count):
        for task in todo[:count]:
            task[0].step(*task[1:])
            if task[2] == 2 * bits:
                store_final(task[1]).start()
        del todo[:count]

    for load in loads[8:]:
        load.wait()

    def partial_rows(r):
        chunk = jnp.concatenate(
            [grads[_rows(b * own + r * size, size), : 3 * width] for b in blocks], axis=0
        )

        def tile(cols):
            return _nt(chunk, up_ref[cols, : 3 * width])

        scatters[3].project(r, tile)
        scatters[3].finish(r)

    loop(partial_rows)

    def bias(j):
        return jnp.sum(grads[:, j * width : (j + 1) * width].astype(f32), axis=0, keepdims=True)

    small_ref[9:10, :width] = bias(0)
    small_ref[9:10, width : 2 * width] = bias(2)
    targets = [{"mp": sib}, {"mp": cnt}, *reduce.peer]

    def small_step(k):
        rows = 8 if k < 2 else small_ref.shape[0]
        copy = _remote(
            small_ref.at[:rows], small_recv.at[k, :rows], small_sems.at[0, k], small_sems.at[1, k], targets[k]
        )
        return copy, rows

    count = len(todo) // (len(targets) + 1)
    for k in range(len(targets)):
        small_step(k)[0].start()
        work_off(count)
        copy, rows = small_step(k)
        copy.wait()
        small_ref[:rows, :] += small_recv[k, :rows, :]

    def finish(r):
        rows = _rows(r * size, size)
        store(0, r).wait()
        outputs_ref[rows, :] = (grad_own[rows, :] + scatters[3].result(r)).astype(bf16)
        store(1, r).start()
        scatters[3].sent(r)

    loop(finish)
    work_off(len(todo))
    for n in range(2 * pieces):
        reduce.sent(n)
    for p in range(pieces):
        kind(p).halve(2 * pieces + p, 0).wait_send()
        kind(p).sent(2 * pieces + p)
    loop(lambda r: store(1, r).wait())
    for n in range(3 * pieces):
        store_final(n).wait()


def main_layer(mesh, arrays, lse_rows, places, real, up_bias, vectors):
    f32, bf16 = jnp.float32, jnp.bfloat16
    context, out_proj, inputs, up_proj, down_proj = arrays[:5]
    own, depth = inputs.shape
    units, width = up_proj.shape[1], out_proj.shape[0]
    whole, half = 4 * own, depth // 2
    bits = mesh.shape["dp"].bit_length() - 1
    pieces = CHUNKS if (depth // CHUNKS >> bits) >= 16 else 1
    outs = [((own, depth), bf16), ((own, depth), bf16), ((3 * depth, depth), bf16), ((16, depth), f32)]
    return pl.pallas_call(
        partial(main_kernel, bits, pieces),
        out_shape=[jax.ShapeDtypeStruct(*out) for out in outs],
        in_specs=[REMOTE] * 9 + [LOCAL] * 10,
        out_specs=[REMOTE] * 3 + [LOCAL],
        scratch_shapes=[
            *[pltpu.VMEM(array.shape, bf16) for array in arrays[:5]],
            pltpu.VMEM((own, depth), bf16),
            pltpu.VMEM((2 * depth, depth), bf16),
            pltpu.VMEM((whole, depth), bf16),
            pltpu.VMEM((whole, depth), bf16),
            pltpu.VMEM((whole, depth), bf16),
            pltpu.VMEM((whole, units), bf16),
            pltpu.VMEM((whole, units), bf16),
            pltpu.VMEM((own, depth), f32),
            pltpu.VMEM((own, 1), f32),
            pltpu.VMEM((own, depth), f32),
            pltpu.VMEM((width, BLOCK), f32),
            *_scatter_scratch(own, depth),
            pltpu.VMEM((3 * depth, depth), bf16),
            pltpu.VMEM((3 * depth, depth), bf16),
            pltpu.VMEM((2 + bits, 16, depth), f32),
            pltpu.SemaphoreType.DMA((11,)),
            pltpu.SemaphoreType.DMA((4, CHUNKS)),
            pltpu.SemaphoreType.DMA((2, CHUNKS)),
            pltpu.SemaphoreType.DMA((3 * pieces,)),
            pltpu.SemaphoreType.DMA((3, 3, CHUNKS)),
            pltpu.SemaphoreType.DMA((3, 3, CHUNKS)),
            pltpu.SemaphoreType.DMA((4, 3, CHUNKS)),
            pltpu.SemaphoreType.DMA((4, 3, CHUNKS)),
            pltpu.SemaphoreType.DMA((2, 3 * pieces, 2 * bits)),
            pltpu.SemaphoreType.DMA((2, 2 + bits)),
        ],
        compiler_params=pltpu.CompilerParams(
            collective_id=1, has_side_effects=True, vmem_limit_bytes=63 * 2**20
        ),
        name="main_layer",
    )(*arrays, lse_rows, places, real, up_bias, *vectors)


def unpack_kernel(
    width, final_ref, small_ref, outputs_ref, inputs_grad_ref, down_ref, up_ref, in_ref, out_ref,
    qv_ref, up_bias_ref, *refs,
):
    f32 = jnp.float32
    vectors, outputs_out, inputs_grad_out = refs[:6], refs[6], refs[7]
    down_ref[...] = final_ref[0].astype(f32)
    up_ref[...] = final_ref[1].astype(f32)
    for j in range(3):
        in_ref[j] = final_ref[2, :, j * width : (j + 1) * width].astype(f32)
    out_ref[...] = final_ref[2, :, 3 * width :].astype(f32).T
    outputs_out[...] = outputs_ref[...]
    inputs_grad_out[...] = inputs_grad_ref[...]
    for k, vector in enumerate(vectors):
        vector[...] = small_ref[k : k + 1, :]
    up_bias_ref[...] = small_ref[8:9, :]
    for k in range(2):
        qv_ref[k : k + 1, :] = small_ref[9:10, k * width : (k + 1) * width]


def unpack(final, small, outputs, inputs_grad, width):
    f32 = jnp.float32
    own, depth = outputs.shape
    steps = depth // 128
    part = own // steps
    matrix = pl.BlockSpec((128, depth), lambda i: (i, 0))
    tokens = pl.BlockSpec((part, depth), lambda i: (i, 0))
    vector = pl.BlockSpec((1, depth), lambda i: (0, 0))
    shapes = [
        ((depth, depth), f32, matrix),
        ((depth, depth), f32, matrix),
        ((3, depth, width), f32, pl.BlockSpec((3, 128, width), lambda i: (0, i, 0))),
        ((width, depth), f32, pl.BlockSpec((width, 128), lambda i: (0, i))),
        ((2, width), f32, pl.BlockSpec((2, width), lambda i: (0, 0))),
        *[((1, depth), f32, vector)] * 7,
        ((own, depth), jnp.bfloat16, tokens),
        ((own, depth), jnp.bfloat16, tokens),
    ]
    return pl.pallas_call(
        partial(unpack_kernel, width),
        grid=(steps,),
        in_specs=[
            pl.BlockSpec((3, 128, depth), lambda i: (0, i, 0)),
            pl.BlockSpec((16, depth), lambda i: (0, 0)),
            tokens,
            tokens,
        ],
        out_specs=[spec for _, _, spec in shapes],
        out_shape=[jax.ShapeDtypeStruct(shape, dtype) for shape, dtype, _ in shapes],
        compiler_params=pltpu.CompilerParams(vmem_limit_bytes=VMEM),
        name="unpack_gradients",
    )(final, small, outputs, inputs_grad)


def shards(
    mesh,
    inputs,
    in_proj,
    qv_bias,
    out_proj,
    out_bias,
    attn_gain,
    attn_shift,
    up_proj,
    up_bias,
    down_proj,
    down_bias,
    ffn_gain,
    ffn_shift,
    segments,
    padding,
    cotangent,
):
    places, real = segment_places(segments, padding)
    vectors = [v[None] for v in (out_bias, attn_gain, attn_shift, down_bias, ffn_gain, ffn_shift)]
    tokens, qkv = project_tokens(inputs, in_proj, qv_bias)
    context, lse_rows = attention_forward(qkv, places, real)
    arrays = (context, out_proj, inputs, up_proj, down_proj, cotangent, qkv, tokens, in_proj)
    outputs, inputs_grad, final, small = main_layer(
        mesh, arrays, lse_rows, places, real, up_bias[None], vectors
    )
    final = final.reshape(3, *out_proj.shape[1:], -1)
    down_grad, up_grad, in_grad, out_grad, qv_grad, up_bias_grad, *vectors, outputs, inputs_grad = unpack(
        final, small, outputs, inputs_grad, in_proj.shape[2]
    )
    vectors = [v[0] for v in vectors]
    return (
        outputs,
        inputs_grad,
        in_grad,
        qv_grad,
        out_grad,
        *vectors[:3],
        up_grad,
        up_bias_grad[0],
        down_grad,
        *vectors[3:],
    )


def solution(mesh):
    return jax.shard_map(
        partial(shards, mesh),
        mesh=mesh,
        in_specs=(
            P(("dp", "mp"), None),
            P(None, None, "mp"),
            P(None, "mp"),
            P("mp", None),
            P(),
            P(),
            P(),
            P(None, "mp"),
            P("mp"),
            P("mp", None),
            P(),
            P(),
            P(),
            P("dp", None),
            P("dp", None),
            P(("dp", "mp"), None),
        ),
        out_specs=(
            P(("dp", "mp"), None),
            P(("dp", "mp"), None),
            P(None, None, "mp"),
            P(None, "mp"),
            P("mp", None),
            P(),
            P(),
            P(),
            P(None, "mp"),
            P("mp"),
            P("mp", None),
            P(),
            P(),
            P(),
        ),
        check_vma=False,
    )
```

```python
from functools import partial
import math

import jax
import jax.numpy as jnp
from jax import lax
from jax.experimental import pallas as pl
from jax.experimental.pallas import tpu as pltpu
from jax.sharding import PartitionSpec as P

HEAD = 64
BLOCK = 256
CHUNKS = 4
SMALL_TURNS = (0, 1, 3, 10, 16, 23, 23, 23, 23)
ORDERS = (
    (1, 2, 0),
    (0, 1, 2),
    (0, 1, 2),
    (0, 1, 2),
    (0, 1, 2),
    (0, 1, 2),
    (0, 1, 2),
    (0, 1, 2),
    (1, 2, 0),
    (0, 1, 2),
    (0, 1, 2),
    (0, 1, 2),
)
PLAN = {
    -1: ((2, 0), (1, 0), (0, 0), (3, 0),),
    0: ((7, 0), (0, 1), (2, 1), (4, 0),),
    1: ((5, 0), (6, 0),),
    3: ((1, 1), (0, 2),),
    4: ((2, 2), (3, 1), (1, 2),),
    5: ((7, 1), (2, 3), (3, 2),),
    6: ((1, 3), (4, 1), (7, 2), (2, 4),),
    7: ((3, 3), (5, 1), (1, 4), (4, 2),),
    8: ((11, 0), (0, 3), (2, 5), (6, 1), (7, 3),),
    10: ((3, 4),),
    12: ((5, 2),),
    14: ((1, 5),),
    15: ((4, 3),),
    16: ((11, 1),),
    17: ((0, 4), (6, 2),),
    18: ((7, 4),),
    19: ((3, 5),),
    20: ((5, 3),),
    21: ((4, 4),),
    23: ((11, 2),),
    25: ((0, 5),),
    26: ((6, 3),),
    28: ((7, 5),),
    29: ((5, 4),),
    32: ((10, 0), (11, 3), (1, 6), (2, 6), (3, 6), (4, 5), (8, 0), (9, 0), (0, 6), (7, 6), (6, 4), (5, 5), (-1, 0), (10, 1), (11, 4), (8, 1), (-1, 1), (4, 6), (6, 5), (10, 2), (9, 1), (11, 5), (-1, 2), (8, 2), (10, 3), (5, 6), (9, 2), (-1, 3), (6, 6), (10, 4), (9, 3), (8, 3), (11, 6), (9, 4), (8, 4), (10, 5), (9, 5), (8, 5), (10, 6), (9, 6), (8, 6),),
}
COLS = 256
VMEM = 60 * 2**20
REMOTE = pl.BlockSpec(memory_space=pl.ANY)
LOCAL = pl.BlockSpec(memory_space=pltpu.VMEM)
SCALARS = pl.BlockSpec(memory_space=pltpu.SMEM)
MESH = pl.DeviceIdType.MESH


EPSILON = 1e-05


NEG = -1e30


def _head_masks(heads, width, value):
    lane = lax.broadcasted_iota(jnp.int32, (1, width), 1) // HEAD
    return [jnp.where(lane == h, value, 0.0).astype(jnp.bfloat16) for h in range(heads)]


def _nt(a, b):
    return lax.dot_general(a, b, (((1,), (1,)), ((), ())), preferred_element_type=jnp.float32)


def _tn(a, b):
    return lax.dot_general(a, b, (((0,), (0,)), ((), ())), preferred_element_type=jnp.float32)


def _nn(a, b):
    return jnp.dot(a, b, preferred_element_type=jnp.float32)


def _column(row):
    wide = jnp.broadcast_to(row.astype(jnp.float32), (128, row.shape[1])).T.astype(jnp.int32)
    return jnp.concatenate([wide] * (BLOCK // 128), axis=1)


def _bias(seg_ref, pad_ref, query_rows, key_rows):
    seg_q, pad_q = seg_ref[:, query_rows], pad_ref[:, query_rows]
    seg_k, pad_k = _column(seg_ref[:, key_rows]), _column(pad_ref[:, key_rows])
    allowed = (seg_k == seg_q) & ((pad_k > 0) | (pad_q == 0))
    return jnp.where(allowed, 0.0, NEG).astype(jnp.float32)


def _meets(places_ref, left):
    edge = left * BLOCK + BLOCK - 1
    return places_ref[0, edge] == places_ref[0, edge + 1]


def _neighbours(places_ref, i, blocks, body):
    @pl.when(i > 0)
    def _():
        @pl.when(_meets(places_ref, jnp.maximum(i - 1, 0)))
        def _():
            body(i - 1)

    @pl.when(i < blocks - 1)
    def _():
        @pl.when(_meets(places_ref, jnp.minimum(i, blocks - 2)))
        def _():
            body(i + 1)


def _block_copies(source, target, sems):
    def copy(i):
        rows = _rows(i * BLOCK, BLOCK)
        return pltpu.make_async_copy(source.at[rows], target.at[rows], sems.at[i])

    return copy


def _loop(count, body):
    def step(i, carry):
        body(i)
        return carry

    lax.fori_loop(0, count, step, 0)


def attention_forward_kernel(
    heads, blocks, places_ref, qkv_hbm, seg_ref, pad_ref, context_hbm, lse_ref,
    qkv_ref, context_ref, peak_ref, total_ref, acc_ref, load_sems, store_sems,
):
    bf16 = jnp.bfloat16
    width = context_ref.shape[1]
    load = _block_copies(qkv_hbm, qkv_ref, load_sems)
    store = _block_copies(context_ref, context_hbm, store_sems)
    _loop(blocks, lambda i: load(i).start())
    scaled = _head_masks(heads, width, 1.0 / math.sqrt(HEAD))
    load(0).wait()

    def attend(i):
        @pl.when(i + 1 < blocks)
        def _():
            load(i + 1).wait()

        query_rows = _rows(i * BLOCK, BLOCK)
        query = qkv_ref[query_rows, :width]

        def parts(j):
            rows = _rows(j * BLOCK, BLOCK)
            return (
                qkv_ref[rows, width : 2 * width],
                qkv_ref[rows, 2 * width :].T,
                _bias(seg_ref, pad_ref, query_rows, rows),
            )

        key, value, bias = parts(i)
        for h in range(heads):
            scores = _nt(key, query * scaled[h]) + bias
            peak = jnp.max(scores, axis=0, keepdims=True)
            expo = jnp.exp(scores - peak)
            peak_ref[h] = peak
            total_ref[h] = jnp.sum(expo, axis=0, keepdims=True)
            place = pl.ds(h * HEAD, HEAD)
            acc_ref[place, :] = _nn(value[h * HEAD : (h + 1) * HEAD], expo.astype(bf16))

        def other(j):
            key, value, bias = parts(j)
            for h in range(heads):
                scores = _nt(key, query * scaled[h]) + bias
                old = peak_ref[h]
                peak = jnp.maximum(old, jnp.max(scores, axis=0, keepdims=True))
                expo = jnp.exp(scores - peak)
                ratio = jnp.exp(old - peak)
                peak_ref[h] = peak
                total_ref[h] = total_ref[h] * ratio + jnp.sum(expo, axis=0, keepdims=True)
                place = pl.ds(h * HEAD, HEAD)
                acc_ref[place, :] = acc_ref[place, :] * ratio + _nn(
                    value[h * HEAD : (h + 1) * HEAD], expo.astype(bf16)
                )

        _neighbours(places_ref, i, blocks, other)
        for h in range(heads):
            place = pl.ds(h * HEAD, HEAD)
            acc_ref[place, :] = acc_ref[place, :] / total_ref[h]
            lse_ref[h : h + 1, query_rows] = peak_ref[h] + jnp.log(total_ref[h])
        context_ref[query_rows, :] = acc_ref[...].astype(bf16).T
        store(i).start()

    _loop(blocks, attend)
    _loop(blocks, lambda i: store(i).wait())


def attention_forward(qkv, places, padding):
    length, width = qkv.shape[0], qkv.shape[1] // 3
    heads, blocks = width // HEAD, length // BLOCK
    return pl.pallas_call(
        partial(attention_forward_kernel, heads, blocks),
        in_specs=[SCALARS, REMOTE, LOCAL, LOCAL],
        out_specs=[REMOTE, LOCAL],
        scratch_shapes=[
            pltpu.VMEM((length, 3 * width), jnp.bfloat16),
            pltpu.VMEM((length, width), jnp.bfloat16),
            pltpu.VMEM((heads, 1, BLOCK), jnp.float32),
            pltpu.VMEM((heads, 1, BLOCK), jnp.float32),
            pltpu.VMEM((width, BLOCK), jnp.float32),
            pltpu.SemaphoreType.DMA((blocks,)),
            pltpu.SemaphoreType.DMA((blocks,)),
        ],
        out_shape=[
            jax.ShapeDtypeStruct((length, width), jnp.bfloat16),
            jax.ShapeDtypeStruct((8, length), jnp.float32),
        ],
        compiler_params=pltpu.CompilerParams(vmem_limit_bytes=VMEM),
        name="attention_forward",
    )(places, qkv, places, padding)


def segment_places(segments, padding):
    row_count, seq_len = segments.shape
    if row_count > 1:
        segments = segments + jnp.arange(row_count, dtype=jnp.int32)[:, None] * (seq_len + 1)
    return segments.reshape(1, -1), padding.reshape(1, -1)


def _partners():
    me = lax.axis_index("mp")
    core = lax.rem(me, 2)
    sib = me + 1 - 2 * core
    cnt = lax.rem(me + 2, 4)
    dia = lax.rem(cnt + 1, 2) + cnt - lax.rem(cnt, 2)
    return me, sib, cnt, dia


def _remote(src, dst, send, recv, target):
    return pltpu.make_async_remote_copy(
        src_ref=src, dst_ref=dst, send_sem=send, recv_sem=recv, device_id=target, device_id_type=MESH
    )


def _greet(targets):
    barrier = pltpu.get_barrier_semaphore()
    for target in targets:
        pl.semaphore_signal(barrier, inc=1, device_id=target, device_id_type=MESH)
    pl.semaphore_wait(barrier, len(targets))


def _rows(start, size):
    return pl.ds(pl.multiple_of(start, size), size)


def _part(start, size):
    return pl.ds(pl.multiple_of(start, 16), size)


class Gather:
    def __init__(self, buffer, send, recv, stage, size, sib, cnt):
        self.buffer, self.send, self.recv = buffer, send, recv
        self.stage, self.size, self.sib, self.cnt = stage, size, sib, cnt

    def slot(self, r, k):
        return self.buffer.at[_rows((r * 4 + k) * self.size, self.size)]

    def copy(self, r, kind):
        src, dst, target = ((0, 1, self.sib), (0, 2, self.cnt), (2, 3, self.sib))[kind]
        return _remote(
            self.slot(r, src),
            self.slot(r, dst),
            self.send.at[self.stage, kind, r],
            self.recv.at[self.stage, kind, r],
            {"mp": target},
        )

    def start(self, r):
        self.copy(r, 1).start()
        self.copy(r, 0).start()

    def forward(self, r):
        self.copy(r, 1).wait_recv()
        self.copy(r, 2).start()

    def arrive(self, r):
        self.copy(r, 0).wait_recv()
        self.copy(r, 2).wait_recv()

    def sent(self, r):
        for kind in range(3):
            self.copy(r, kind).wait_send()


class Scatter:
    def __init__(self, bufs, send, recv, stage, size, sib, cnt):
        self.own, self.other, self.stage_sib, self.stage_x, self.recv_sib, self.recv_x = bufs
        self.send, self.recv = send, recv
        self.stage, self.size, self.sib, self.cnt = stage, size, sib, cnt

    def copy(self, r, kind):
        rows = _rows(r * self.size, self.size)
        src, dst, target = (
            (self.stage_sib.at[0, rows], self.recv_sib.at[0, rows], self.sib),
            (self.stage_sib.at[1, rows], self.recv_sib.at[1, rows], self.sib),
            (self.stage_x.at[rows], self.recv_x.at[rows], self.cnt),
        )[kind]
        return _remote(
            src, dst, self.send.at[self.stage, kind, r], self.recv.at[self.stage, kind, r], {"mp": target}
        )

    def sent(self, r):
        for kind in range(3):
            self.copy(r, kind).wait_send()

    def project(self, r, tile):
        size = self.size
        rows = _rows(r * size, size)

        def column(n, carry):
            cols = _rows(n * COLS, COLS)
            part = tile(cols)
            self.own[rows, cols] = part[:size]
            self.stage_sib[1, rows, cols] = part[size : 2 * size].astype(jnp.bfloat16)
            self.other[rows, cols] = part[2 * size : 3 * size]
            self.stage_sib[0, rows, cols] = part[3 * size :].astype(jnp.bfloat16)
            return carry

        lax.fori_loop(0, self.own.shape[1] // COLS, column, 0)
        self.copy(r, 0).start()
        self.copy(r, 1).start()

    def finish(self, r):
        rows = _rows(r * self.size, self.size)
        self.copy(r, 0).wait_recv()
        self.stage_x[rows, :] = (
            self.other[rows, :] + self.recv_sib[0, rows, :].astype(jnp.float32)
        ).astype(jnp.bfloat16)
        self.copy(r, 2).start()
        self.copy(r, 1).wait_recv()
        self.own[rows, :] += self.recv_sib[1, rows, :].astype(jnp.float32)

    def result(self, r):
        rows = _rows(r * self.size, self.size)
        self.copy(r, 2).wait_recv()
        return self.own[rows, :] + self.recv_x[rows, :].astype(jnp.float32)


def _scatter_scratch(own, width):
    f32, bf16 = jnp.float32, jnp.bfloat16
    return [
        pltpu.VMEM((own, width), f32),
        pltpu.VMEM((own, width), f32),
        pltpu.VMEM((2, own, width), bf16),
        pltpu.VMEM((own, width), bf16),
        pltpu.VMEM((2, own, width), bf16),
        pltpu.VMEM((own, width), bf16),
    ]


def _norm(summed):
    center = summed - jnp.mean(summed, axis=-1, keepdims=True)
    variance = jnp.mean(center * center, axis=-1, keepdims=True)
    inverse = lax.rsqrt(variance + EPSILON)
    return center * inverse, inverse


def _norm_back(scaled, unit, inverse):
    return inverse * (
        scaled
        - jnp.mean(scaled, axis=-1, keepdims=True)
        - unit * jnp.mean(scaled * unit, axis=-1, keepdims=True)
    )


def project_kernel(
    inputs_ref, in_proj_ref, qv_bias_ref, tokens_hbm, qkv_hbm, tokens_ref, qkv_ref, weights,
    send, recv, load_sems, store_sems,
):
    f32, bf16 = jnp.float32, jnp.bfloat16
    me, sib, cnt, dia = _partners()
    own, width = inputs_ref.shape[0], in_proj_ref.shape[2]
    size = own // CHUNKS
    mine = _rows(me * own, own)
    keep = pltpu.make_async_copy(inputs_ref, tokens_ref.at[mine], load_sems.at[0])
    fetch = pltpu.make_async_copy(in_proj_ref, weights, load_sems.at[1])
    fetch.start()
    keep.start()
    _greet([{"mp": sib}, {"mp": cnt}])

    def copy(r, kind):
        here = inputs_ref.at[_rows(r * size, size)]
        place = _rows((cnt if kind == 2 else me) * own + r * size, size)
        src, target = ((here, sib), (here, cnt), (tokens_ref.at[place], sib))[kind]
        return _remote(src, tokens_ref.at[place], send.at[kind, r], recv.at[kind, r], {"mp": target})

    for r in range(CHUNKS):
        copy(r, 1).start()
        copy(r, 0).start()

    def stores(first, rows, k):
        place = _rows(first, rows)
        return [
            pltpu.make_async_copy(tokens_ref.at[place], tokens_hbm.at[place], store_sems.at[0, k]),
            pltpu.make_async_copy(qkv_ref.at[place], qkv_hbm.at[place], store_sems.at[1, k]),
        ]

    def compute(first):
        place = _rows(first, size)
        block = tokens_ref[place, :]
        for j in range(3):
            part = jnp.dot(block, weights[j], preferred_element_type=f32)
            if j != 1:
                part = part + qv_bias_ref[j // 2 : j // 2 + 1, :]
            qkv_ref[place, j * width : (j + 1) * width] = part.astype(bf16)

    fetch.wait()
    keep.wait()
    _loop(CHUNKS, lambda r: compute(me * own + r * size))
    for store in stores(me * own, own, 0):
        store.start()

    def sib_part(r):
        copy(r, 0).wait_recv()
        compute(sib * own + r * size)

    _loop(CHUNKS, sib_part)
    for store in stores(sib * own, own, 1):
        store.start()

    def far_part(r):
        copy(r, 1).wait_recv()
        copy(r, 2).start()
        compute(cnt * own + r * size)
        for store in stores(cnt * own + r * size, size, 2 + 2 * r):
            store.start()
        copy(r, 2).wait_recv()
        compute(dia * own + r * size)
        for store in stores(dia * own + r * size, size, 3 + 2 * r):
            store.start()

    _loop(CHUNKS, far_part)
    for k in range(2):
        for store in stores((me, sib)[k] * own, own, k):
            store.wait()

    def drain(r):
        for kind in range(3):
            copy(r, kind).wait_send()
        for k, block in enumerate((cnt, dia)):
            for store in stores(block * own + r * size, size, 2 + 2 * r + k):
                store.wait()

    _loop(CHUNKS, drain)


def project_tokens(inputs, in_proj, qv_bias):
    own, depth = inputs.shape
    width = in_proj.shape[2]
    shapes = [(4 * own, depth), (4 * own, 3 * width)]
    return pl.pallas_call(
        project_kernel,
        out_shape=[jax.ShapeDtypeStruct(shape, jnp.bfloat16) for shape in shapes],
        in_specs=[REMOTE, REMOTE, LOCAL],
        out_specs=[REMOTE] * 2,
        scratch_shapes=[
            *[pltpu.VMEM(shape, jnp.bfloat16) for shape in shapes],
            pltpu.VMEM(in_proj.shape, jnp.bfloat16),
            pltpu.SemaphoreType.DMA((3, CHUNKS)),
            pltpu.SemaphoreType.DMA((3, CHUNKS)),
            pltpu.SemaphoreType.DMA((2,)),
            pltpu.SemaphoreType.DMA((2, 2 + 2 * CHUNKS)),
        ],
        compiler_params=pltpu.CompilerParams(
            collective_id=0, has_side_effects=True, vmem_limit_bytes=VMEM
        ),
        name="project_tokens",
    )(inputs, in_proj, qv_bias)


class Reduce:
    def __init__(self, n, rows, order, source, work, final, sems):
        self.n, self.rows, self.source, self.work, self.final, self.sems = n, rows, source, work, final, sems
        self.steps = len(order)
        dp = lax.axis_index("dp")
        self.bit = [lax.rem(dp // (1 << b), 2) for b in order]
        self.peer = [{"dp": dp + (1 << b) * (1 - 2 * bit)} for b, bit in zip(order, self.bit)]

    def size(self, s):
        return self.rows >> s

    def start(self, s):
        first = self.n * self.rows
        for t in range(s):
            first = first + self.bit[t] * self.size(t + 1)
        return first

    def held(self, s):
        if s == 0:
            return self.source
        stride = self.rows - self.size(self.steps)
        return self.work, self.n * stride + self.rows - 2 * self.size(s)

    def halve(self, s):
        ref, first = self.held(s)
        half = self.size(s + 1)
        there, place = self.held(s + 1)
        return _remote(
            ref.at[_part(first + (1 - self.bit[s]) * half, half)],
            there.at[_part(place, half)],
            self.sems.at[0, self.n, s],
            self.sems.at[1, self.n, s],
            self.peer[s],
        )

    def double(self, s):
        block = self.final.at[_rows(self.start(s + 1), self.size(s + 1))]
        k = 2 * self.steps - 1 - s
        return _remote(block, block, self.sems.at[0, self.n, k], self.sems.at[1, self.n, k], self.peer[s])

    def step(self, k):
        steps = self.steps
        if 0 < k <= steps:
            s = k - 1
            half = self.size(s + 1)
            self.halve(s).wait_recv()
            ref, first = self.held(s)
            there, place = self.held(s + 1)
            total = there[_part(place, half), :].astype(jnp.float32) + ref[
                _part(first + self.bit[s] * half, half), :
            ].astype(jnp.float32)
            if k < steps:
                there[_part(place, half), :] = total.astype(jnp.bfloat16)
            else:
                self.final[_rows(self.start(steps), half), :] = total.astype(jnp.bfloat16)
        if k > steps:
            self.double(2 * steps - k).wait_recv()
        if k < steps:
            self.halve(k).start()
        elif k < 2 * steps:
            self.double(2 * steps - 1 - k).start()

    def sent(self):
        for s in range(self.steps):
            if s:
                self.halve(s).wait_send()
            self.double(s).wait_send()


def main_kernel(bits, pieces, *refs):
    f32, bf16 = jnp.float32, jnp.bfloat16
    (context_hbm, out_proj_hbm, inputs_hbm, up_hbm, down_hbm, cotangent_hbm, qkv_hbm, tokens_hbm, in_proj_hbm,
     lse_ref, seg_ref, pad_ref, up_bias_ref, *refs) = refs
    vectors, refs = [v[...] for v in refs[:6]], refs[6:]
    out_bias, attn_gain, attn_shift, down_bias, ffn_gain, ffn_shift = vectors
    (outputs_hbm, inputs_grad_hbm, final_hbm, small_ref,
     context_ref, out_proj_ref, inputs_ref, up_ref, down_ref,
     weight_grads, normed_full, grad2_full, grad1_full, active, back, unit1, inverse1, grad_own, dots_ref,
     own_acc, other_acc, stage_sib, stage_x, recv_sib, recv_x, work, final, small_recv, late_ref, late_recv,
     load_sems, block_sems, store_sems, final_sems, gather_send, gather_recv, scatter_send, scatter_recv,
     sems, small_sems) = refs
    outputs_ref = inputs_ref
    me, sib, cnt, dia = _partners()
    own, depth = inputs_ref.shape
    units, width = up_ref.shape[1], out_proj_ref.shape[0]
    length = 4 * own
    heads, token_blocks = width // HEAD, length // BLOCK
    size, whole = own // CHUNKS, length // CHUNKS
    blocks = (me, sib, cnt, dia)
    early = pieces == CHUNKS
    dp = lax.axis_index("dp")
    loop = partial(_loop, CHUNKS)

    def context_load(r):
        return [
            pltpu.make_async_copy(
                context_hbm.at[_rows(b * own + r * size, size)],
                context_ref.at[_rows((r * 4 + k) * size, size)],
                block_sems.at[k, r],
            )
            for k, b in enumerate(blocks)
        ]

    loads = [
        pltpu.make_async_copy(source, target, load_sems.at[k])
        for k, (source, target) in enumerate(
            (
                (out_proj_hbm, out_proj_ref),
                (inputs_hbm, inputs_ref),
                (up_hbm, up_ref),
                (down_hbm, down_ref),
                (cotangent_hbm, inputs_ref),
                (qkv_hbm, active.at[:, : 3 * width]),
                (tokens_hbm, normed_full),
                (context_hbm, back.at[:, width : 2 * width]),
                *[(in_proj_hbm.at[j], up_ref.at[:, j * width : (j + 1) * width]) for j in range(3)],
            )
        )
    ]
    loads[0].start()
    loop(lambda r: [load.start() for load in context_load(r)])
    for load in loads[1:4]:
        load.start()

    def store(k, r):
        rows = _rows(r * size, size)
        target = (outputs_hbm, inputs_grad_hbm)[k]
        return pltpu.make_async_copy(outputs_ref.at[rows], target.at[rows], store_sems.at[k, r])

    bufs = (own_acc, other_acc, stage_sib, stage_x, recv_sib, recv_x)
    gathers = [
        Gather(buf, gather_send, gather_recv, stage, size, sib, cnt)
        for stage, buf in enumerate((normed_full, grad2_full, grad1_full))
    ]
    scatters = [
        Scatter(bufs, scatter_send, scatter_recv, stage, size, sib, cnt) for stage in range(4)
    ]
    piece = depth // pieces
    count = 3 * pieces

    def source(n):
        if early and n == count - 1:
            return outputs_ref, 0
        return weight_grads, (n if n < 2 * pieces else n - 2 * pieces) * piece

    sums = [
        Reduce(
            n, piece, ORDERS[n] if early else tuple(range(bits)), source(n), work, final, sems
        )
        for n in range(count)
    ]
    over = [{"dp": dp + (1 << b) * (1 - 2 * lax.rem(dp // (1 << b), 2))} for b in range(bits)]
    small_ref[...] = jnp.zeros_like(small_ref)
    late_ref[...] = jnp.zeros_like(late_ref)
    _greet([{"mp": sib}, {"mp": cnt}, *over])

    def add_sum(k, value):
        small_ref[k : k + 1, :] += jnp.sum(value, axis=0, keepdims=True)

    loads[0].wait()

    def attended(r):
        for load in context_load(r):
            load.wait()
        chunk = context_ref[_rows(r * whole, whole), :]
        scatters[0].project(r, lambda cols: _nn(chunk, out_proj_ref[:, cols]))
        scatters[0].finish(r)

    loop(attended)
    loads[1].wait()

    def lower_norm(r):
        rows = _rows(r * size, size)
        unit, inverse = _norm(inputs_ref[rows, :].astype(f32) + scatters[0].result(r) + out_bias)
        unit1[rows, :] = unit
        inverse1[rows, :] = inverse
        gathers[0].slot(r, 0)[...] = (unit * attn_gain + attn_shift).astype(bf16)
        gathers[0].start(r)

    loop(lower_norm)
    loads[4].start()
    loads[2].wait()
    loads[3].wait()

    def feed_forward(r):
        rows = _rows(r * whole, whole)
        gathers[0].forward(r)
        gathers[0].arrive(r)
        scatters[0].sent(r)

        def column(n, carry):
            cols = _rows(n * COLS, COLS)
            upper = _nn(normed_full[rows, :], up_ref[:, cols]) + up_bias_ref[:, cols]
            cdf = 0.5 + 0.5 * lax.erf(upper * math.sqrt(0.5))
            pdf = jnp.exp(upper * upper * -0.5) * (1.0 / math.sqrt(2.0 * math.pi))
            active[rows, cols] = (upper * cdf).astype(bf16)
            back[rows, cols] = (cdf + upper * pdf).astype(bf16)
            return carry

        lax.fori_loop(0, units // COLS, column, 0)
        scatters[1].project(r, lambda cols: _nn(active[rows, :], down_ref[:, cols]))
        scatters[1].finish(r)

    loop(feed_forward)
    loads[4].wait()

    def upper_norm(r):
        rows = _rows(r * size, size)
        normed = unit1[rows, :] * attn_gain + attn_shift
        unit, inverse = _norm(normed + scatters[1].result(r) + down_bias)
        cotangent = inputs_ref[rows, :].astype(f32)
        outputs_ref[rows, :] = (unit * ffn_gain + ffn_shift).astype(bf16)
        store(0, r).start()
        grad = _norm_back(cotangent * ffn_gain, unit, inverse)
        gathers[1].slot(r, 0)[...] = grad.astype(bf16)
        gathers[1].start(r)
        grad_own[rows, :] = grad
        add_sum(3, grad)
        add_sum(4, cotangent * unit)
        add_sum(5, cotangent)

    loop(upper_norm)

    def take(r):
        gathers[1].forward(r)
        gathers[1].arrive(r)
        scatters[1].sent(r)

    def feed_back(r):
        rows = _rows(r * whole, whole)

        def column(n, carry):
            cols = _rows(n * COLS, COLS)
            incoming = _nt(grad2_full[rows, :], down_ref[cols, :])
            upper_back = (back[rows, cols].astype(f32) * incoming).astype(bf16)
            back[rows, cols] = upper_back
            late_ref[1:2, cols] += jnp.sum(upper_back.astype(f32), axis=0, keepdims=True)
            return carry

        lax.fori_loop(0, units // COLS, column, 0)
        scatters[2].project(r, lambda cols: _nt(back[rows, :], up_ref[cols, :]))
        scatters[2].finish(r)

    def take_back(r):
        take(r)
        feed_back(r)

    _loop(CHUNKS - 1, take_back)
    take(CHUNKS - 1)

    def weights(k, p):
        cols = _rows(p * (depth // CHUNKS), depth // CHUNKS)
        place = _rows(k * depth + p * (depth // CHUNKS), depth // CHUNKS)
        if k == 0:
            weight_grads[place, :] = _tn(active[:, cols], grad2_full[...]).astype(bf16)
        else:
            weight_grads[place, :] = _tn(normed_full[:, cols], back[...]).astype(bf16)

    def out_weights():
        target = outputs_ref.at[:width] if early else weight_grads.at[3 * width : 4 * width]
        target[...] = _tn(context_ref[...], grad1_full[...]).astype(bf16)

    def in_weights(j):
        weight_grads[_rows(j * width, width), :] = _tn(
            grads[:, j * width : (j + 1) * width], normed_full[...]
        ).astype(bf16)

    def move(n, k):
        if k == 0 and n < 2 * pieces:
            weights(n // pieces, n % pieces)
        elif k == 0 and n == count - 1:
            out_weights()
        elif k == 0:
            in_weights(n - 2 * pieces)
        sums[n].step(k)
        if k == 2 * bits:
            store_final(n).start()

    def store_final(n):
        rows = _rows(n * piece, piece)
        return pltpu.make_async_copy(final.at[rows], final_hbm.at[rows], final_sems.at[n])

    def slot(i, first, number):
        for at in range(first, first + number) if early else ():
            if at in PLAN:

                @pl.when(i == at - first)
                def _():
                    for n, k in PLAN[at]:
                        move(n, k)

    if early:
        for n, k in PLAN[-1]:
            move(n, k)
    feed_back(CHUNKS - 1)
    for load in loads[8:]:
        load.start()

    def lower_back(r):
        slot(r, 0, CHUNKS)
        if not early:
            for k in range(2):

                @pl.when(r // 2 == k)
                def _():
                    for h in range(2):
                        weights(k, 2 * r - 4 * k + h)

                @pl.when(r == 2 * k + 1)
                def _():
                    sums[k].step(0)

        rows = _rows(r * size, size)
        incoming = grad_own[rows, :] + scatters[2].result(r)
        unit = unit1[rows, :]
        grad = _norm_back(incoming * attn_gain, unit, inverse1[rows, :])
        gathers[2].slot(r, 0)[...] = grad.astype(bf16)
        gathers[2].start(r)
        grad_own[rows, :] = grad
        add_sum(0, grad)
        add_sum(1, incoming * unit)
        add_sum(2, incoming)

    loop(lower_back)
    gathers_done = lambda r: [gather.sent(r) for gather in gathers[:2]]
    loop(gathers_done)
    for load in loads[5:8]:
        load.start()

    def context_back(r):
        slot(r, CHUNKS, CHUNKS)
        rows = _rows(r * whole, whole)
        gathers[2].forward(r)
        gathers[2].arrive(r)
        scatters[2].sent(r)
        grad = _nt(grad1_full[rows, :], out_proj_ref[...]).astype(bf16)
        for k, b in enumerate(blocks):
            part = _rows(b * own + r * size, size)
            back[part, :width] = grad[k * size : (k + 1) * size]

    loop(context_back)
    loop(lambda r: gathers[2].sent(r))
    loop(lambda r: store(0, r).wait())
    for load in loads[5:8]:
        load.wait()

    targets = [{"mp": sib}, {"mp": cnt}, *over]

    def small_step(k):
        return _remote(
            small_ref.at[:8], small_recv.at[k], small_sems.at[0, k], small_sems.at[1, k], targets[k]
        )

    def small_end(k):
        small_step(k).wait()
        small_ref[:8, :] += small_recv[k]

    def late_step(k):
        at = len(targets) + k
        return _remote(late_ref, late_recv.at[k], small_sems.at[0, at], small_sems.at[1, at], over[k])

    def late_end(k):
        late_step(k).wait()
        late_ref[...] += late_recv[k]

    def small_turn(k):
        if k:
            small_end(k - 1)
        if k < len(targets):
            small_step(k).start()

    scaled = _head_masks(heads, width, 1.0 / math.sqrt(HEAD))
    plain = _head_masks(heads, width, 1.0)
    keys_acc, values_acc, query_acc = unit1, other_acc, own_acc.at[:width, :BLOCK]
    keys_acc[...] = jnp.zeros_like(keys_acc)
    values_acc[...] = jnp.zeros_like(values_acc)
    grads = grad2_full
    per = own // BLOCK

    def spot(j):
        return _rows(lax.rem(j, per) * BLOCK, BLOCK), _rows(j // per * width, width)

    def attend(t):
        i, turn = t // 3, lax.rem(t, 3)
        for k in range(len(targets) + 1):

            @pl.when(t == SMALL_TURNS[k])
            def _():
                small_turn(k)

        slot(t, 2 * CHUNKS, 3 * token_blocks)
        query_rows = _rows(i * BLOCK, BLOCK)

        @pl.when(turn == 0)
        def _():
            product = (
                back[query_rows, :width].astype(f32) * back[query_rows, width : 2 * width].astype(f32)
            ).T
            for h in range(heads):
                dots_ref[h : h + 1, :] = jnp.sum(
                    product[h * HEAD : (h + 1) * HEAD], axis=0, keepdims=True
                )
            query_acc[...] = jnp.zeros_like(query_acc)

        @pl.when((i + turn >= 1) & (i + turn <= token_blocks))
        def _():
            j = jnp.clip(i + turn - 1, 0, token_blocks - 1)
            query, grad = active[query_rows, :width], back[query_rows, :width]
            rows = _rows(j * BLOCK, BLOCK)
            bias = _bias(seg_ref, pad_ref, query_rows, rows)
            key, value = active[rows, width : 2 * width], active[rows, 2 * width : 3 * width]
            key_rows = (key * (1.0 / math.sqrt(HEAD))).astype(bf16).T
            key_add = jnp.zeros((BLOCK, width), f32)
            value_add = jnp.zeros((BLOCK, width), f32)
            for h in range(heads):
                query_h, grad_h = query * scaled[h], grad * plain[h]
                scores = _nt(key, query_h) + bias
                prob = jnp.exp(scores - lse_ref[h : h + 1, query_rows])
                score_grad = (prob * (_nt(value, grad_h) - dots_ref[h : h + 1, :])).astype(bf16)
                key_add = key_add + _nn(score_grad, query_h)
                value_add = value_add + _nn(prob.astype(bf16), grad_h)
                query_acc[pl.ds(h * HEAD, HEAD), :] += _nn(key_rows[h * HEAD : (h + 1) * HEAD], score_grad)
            keys_acc[spot(j)] += key_add
            values_acc[spot(j)] += value_add

        @pl.when(turn == 2)
        def _():
            grads[query_rows, :width] = query_acc[...].astype(bf16).T

    _loop(3 * token_blocks, attend)

    def keep(j):
        rows = _rows(j * BLOCK, BLOCK)
        grads[rows, width : 2 * width] = keys_acc[spot(j)].astype(bf16)
        grads[rows, 2 * width : 3 * width] = values_acc[spot(j)].astype(bf16)

    _loop(token_blocks, keep)

    if not early:
        for n in range(2):
            sums[n].step(1)
        out_weights()
        in_weights(0)
        in_weights(1)
        in_weights(2)
    for n in range(2 * pieces):
        sums[n].halve(0).wait_send()

    def partial_rows(r):
        chunk = jnp.concatenate(
            [grads[_rows(b * own + r * size, size), : 3 * width] for b in blocks], axis=0
        )

        def tile(cols):
            return _nt(chunk, up_ref[cols, : 3 * width])

        scatters[3].project(r, tile)
        scatters[3].finish(r)

    def finish(r):
        rows = _rows(r * size, size)
        outputs_ref[rows, :] = (grad_own[rows, :] + scatters[3].result(r)).astype(bf16)
        store(1, r).start()
        scatters[3].sent(r)

    def bias(j):
        return jnp.sum(grads[:, j * width : (j + 1) * width].astype(f32), axis=0, keepdims=True)

    for load in loads[8:]:
        load.wait()
    late_ref[:1, :width] = bias(0)
    late_ref[:1, width : 2 * width] = bias(2)
    late_step(0).start()
    if early:
        tail = PLAN[2 * CHUNKS + 3 * token_blocks]
    else:
        tail = [(2, 0)] + [(-1, r) for r in range(CHUNKS)]
        tail += [(n, k) for k in range(1, 2 * bits + 1) for n in range(3) if n == 2 or k > 1]
    last = max(k for k, (n, _) in enumerate(tail) if n < 0)
    turns = [(len(tail) - 1) * (k + 2) // (bits + 1) for k in range(bits)]
    for at, (n, k) in enumerate(tail):
        if n < 0:
            partial_rows(k)
        elif k or early:
            move(n, k)
        else:
            sums[n].step(0)
        for turn in [turn for turn, place in enumerate(turns) if place == at]:
            late_end(turn)
            if turn + 1 < bits:
                late_step(turn + 1).start()
        if at == last + 3 * (len(tail) - 1 - last) // 4:
            if early:
                sums[-1].halve(0).wait_send()
            loop(finish)
    for n in range(count):
        sums[n].sent()
        if n >= 2 * pieces and not (early and n == count - 1):
            sums[n].halve(0).wait_send()
    small_ref[8:10, :] = late_ref[:2, :]
    loop(lambda r: store(1, r).wait())
    for n in range(3 * pieces):
        store_final(n).wait()


def main_layer(mesh, arrays, lse_rows, places, real, up_bias, vectors):
    f32, bf16 = jnp.float32, jnp.bfloat16
    context, out_proj, inputs, up_proj, down_proj = arrays[:5]
    own, depth = inputs.shape
    units, width = up_proj.shape[1], out_proj.shape[0]
    whole, half = 4 * own, depth // 2
    bits = mesh.shape["dp"].bit_length() - 1
    pieces = CHUNKS if (depth // CHUNKS >> bits) >= 16 else 1
    outs = [((own, depth), bf16), ((own, depth), bf16), ((3 * depth, depth), bf16), ((16, depth), f32)]
    return pl.pallas_call(
        partial(main_kernel, bits, pieces),
        out_shape=[jax.ShapeDtypeStruct(*out) for out in outs],
        in_specs=[REMOTE] * 9 + [LOCAL] * 10,
        out_specs=[REMOTE] * 3 + [LOCAL],
        scratch_shapes=[
            *[pltpu.VMEM(array.shape, bf16) for array in arrays[:5]],
            pltpu.VMEM((2 * depth, depth), bf16),
            pltpu.VMEM((whole, depth), bf16),
            pltpu.VMEM((whole, depth), bf16),
            pltpu.VMEM((whole, depth), bf16),
            pltpu.VMEM((whole, units), bf16),
            pltpu.VMEM((whole, units), bf16),
            pltpu.VMEM((own, depth), f32),
            pltpu.VMEM((own, 1), f32),
            pltpu.VMEM((own, depth), f32),
            pltpu.VMEM((8, BLOCK), f32),
            *_scatter_scratch(own, depth),
            pltpu.VMEM((3 * pieces * (depth // pieces - (depth // pieces >> bits)), depth), bf16),
            pltpu.VMEM((3 * depth, depth), bf16),
            pltpu.VMEM((2 + bits, 8, depth), f32),
            pltpu.VMEM((8, depth), f32),
            pltpu.VMEM((bits, 8, depth), f32),
            pltpu.SemaphoreType.DMA((11,)),
            pltpu.SemaphoreType.DMA((4, CHUNKS)),
            pltpu.SemaphoreType.DMA((2, CHUNKS)),
            pltpu.SemaphoreType.DMA((3 * pieces,)),
            pltpu.SemaphoreType.DMA((3, 3, CHUNKS)),
            pltpu.SemaphoreType.DMA((3, 3, CHUNKS)),
            pltpu.SemaphoreType.DMA((4, 3, CHUNKS)),
            pltpu.SemaphoreType.DMA((4, 3, CHUNKS)),
            pltpu.SemaphoreType.DMA((2, 3 * pieces, 2 * bits)),
            pltpu.SemaphoreType.DMA((2, 2 + 2 * bits)),
        ],
        compiler_params=pltpu.CompilerParams(
            collective_id=1, has_side_effects=True, vmem_limit_bytes=63 * 2**20
        ),
        name="main_layer",
    )(*arrays, lse_rows, places, real, up_bias, *vectors)


def unpack_kernel(
    width, final_ref, attn_ref, small_ref, outputs_ref, inputs_grad_ref, down_ref, up_ref, in_ref, out_ref,
    qv_ref, up_bias_ref, *refs,
):
    f32 = jnp.float32
    vectors, outputs_out, inputs_grad_out = refs[:6], refs[6], refs[7]
    down_ref[...] = final_ref[0].astype(f32)
    up_ref[...] = final_ref[1].astype(f32)
    for j in range(3):
        in_ref[j] = attn_ref[j * width : (j + 1) * width, :].astype(f32).T
    out_ref[...] = attn_ref[3 * width :, :].astype(f32)
    outputs_out[...] = outputs_ref[...]
    inputs_grad_out[...] = inputs_grad_ref[...]
    for k, vector in enumerate(vectors):
        vector[...] = small_ref[k : k + 1, :]
    up_bias_ref[...] = small_ref[9:10, :]
    for k in range(2):
        qv_ref[k : k + 1, :] = small_ref[8:9, k * width : (k + 1) * width]


def unpack(final, small, outputs, inputs_grad, width):
    f32 = jnp.float32
    own, depth = outputs.shape
    steps = depth // 128
    part = own // steps
    matrix = pl.BlockSpec((128, depth), lambda i: (i, 0))
    tokens = pl.BlockSpec((part, depth), lambda i: (i, 0))
    vector = pl.BlockSpec((1, depth), lambda i: (0, 0))
    shapes = [
        ((depth, depth), f32, matrix),
        ((depth, depth), f32, matrix),
        ((3, depth, width), f32, pl.BlockSpec((3, 128, width), lambda i: (0, i, 0))),
        ((width, depth), f32, pl.BlockSpec((width, 128), lambda i: (0, i))),
        ((2, width), f32, pl.BlockSpec((2, width), lambda i: (0, 0))),
        *[((1, depth), f32, vector)] * 7,
        ((own, depth), jnp.bfloat16, tokens),
        ((own, depth), jnp.bfloat16, tokens),
    ]
    return pl.pallas_call(
        partial(unpack_kernel, width),
        grid=(steps,),
        in_specs=[
            pl.BlockSpec((2, 128, depth), lambda i: (0, i, 0)),
            pl.BlockSpec((depth, 128), lambda i: (2, i)),
            pl.BlockSpec((16, depth), lambda i: (0, 0)),
            tokens,
            tokens,
        ],
        out_specs=[spec for _, _, spec in shapes],
        out_shape=[jax.ShapeDtypeStruct(shape, dtype) for shape, dtype, _ in shapes],
        compiler_params=pltpu.CompilerParams(vmem_limit_bytes=VMEM),
        name="unpack_gradients",
    )(final.reshape(3, depth, depth), final, small, outputs, inputs_grad)


def shards(
    mesh,
    inputs,
    in_proj,
    qv_bias,
    out_proj,
    out_bias,
    attn_gain,
    attn_shift,
    up_proj,
    up_bias,
    down_proj,
    down_bias,
    ffn_gain,
    ffn_shift,
    segments,
    padding,
    cotangent,
):
    places, real = segment_places(segments, padding)
    vectors = [v[None] for v in (out_bias, attn_gain, attn_shift, down_bias, ffn_gain, ffn_shift)]
    tokens, qkv = project_tokens(inputs, in_proj, qv_bias)
    context, lse_rows = attention_forward(qkv, places, real)
    arrays = (context, out_proj, inputs, up_proj, down_proj, cotangent, qkv, tokens, in_proj)
    outputs, inputs_grad, final, small = main_layer(
        mesh, arrays, lse_rows, places, real, up_bias[None], vectors
    )
    down_grad, up_grad, in_grad, out_grad, qv_grad, up_bias_grad, *vectors, outputs, inputs_grad = unpack(
        final, small, outputs, inputs_grad, in_proj.shape[2]
    )
    vectors = [v[0] for v in vectors]
    return (
        outputs,
        inputs_grad,
        in_grad,
        qv_grad,
        out_grad,
        *vectors[:3],
        up_grad,
        up_bias_grad[0],
        down_grad,
        *vectors[3:],
    )


def solution(mesh):
    return jax.shard_map(
        partial(shards, mesh),
        mesh=mesh,
        in_specs=(
            P(("dp", "mp"), None),
            P(None, None, "mp"),
            P(None, "mp"),
            P("mp", None),
            P(),
            P(),
            P(),
            P(None, "mp"),
            P("mp"),
            P("mp", None),
            P(),
            P(),
            P(),
            P("dp", None),
            P("dp", None),
            P(("dp", "mp"), None),
        ),
        out_specs=(
            P(("dp", "mp"), None),
            P(("dp", "mp"), None),
            P(None, None, "mp"),
            P(None, "mp"),
            P("mp", None),
            P(),
            P(),
            P(),
            P(None, "mp"),
            P("mp"),
            P("mp", None),
            P(),
            P(),
            P(),
        ),
        check_vma=False,
    )
```

```python
from functools import partial
import math

import jax
import jax.numpy as jnp
from jax import lax
from jax.experimental import pallas as pl
from jax.experimental.pallas import tpu as pltpu
from jax.sharding import PartitionSpec as P

HEAD = 64
BLOCK = 256
CHUNKS = 4
SMALL_TURNS = (0, 1, 3, 10, 16, 23, 23, 23, 23)
ORDERS = (
    (1, 2, 0),
    (0, 1, 2),
    (0, 1, 2),
    (0, 1, 2),
    (0, 1, 2),
    (0, 1, 2),
    (0, 1, 2),
    (0, 1, 2),
    (1, 2, 0),
    (0, 1, 2),
    (0, 1, 2),
    (0, 1, 2),
)
PLAN = {
    -1: ((2, 0), (1, 0), (0, 0), (3, 0),),
    0: ((7, 0), (0, 1), (2, 1), (4, 0),),
    1: ((5, 0), (6, 0),),
    3: ((1, 1), (0, 2),),
    4: ((2, 2), (3, 1), (1, 2),),
    5: ((7, 1), (2, 3), (3, 2),),
    6: ((1, 3), (4, 1), (7, 2), (2, 4),),
    7: ((3, 3), (5, 1), (1, 4), (4, 2),),
    8: ((11, 0), (0, 3), (2, 5), (6, 1), (7, 3),),
    10: ((3, 4),),
    12: ((5, 2),),
    14: ((1, 5),),
    15: ((4, 3),),
    16: ((11, 1),),
    17: ((0, 4), (6, 2),),
    18: ((7, 4),),
    19: ((3, 5),),
    20: ((5, 3),),
    21: ((4, 4),),
    23: ((11, 2),),
    25: ((0, 5),),
    26: ((6, 3),),
    28: ((7, 5),),
    29: ((5, 4),),
    32: ((10, 0), (11, 3), (1, 6), (2, 6), (3, 6), (4, 5), (8, 0), (9, 0), (0, 6), (7, 6), (6, 4), (5, 5), (-1, 0), (10, 1), (11, 4), (8, 1), (-1, 1), (4, 6), (6, 5), (10, 2), (9, 1), (11, 5), (-1, 2), (8, 2), (10, 3), (5, 6), (9, 2), (-1, 3), (6, 6), (10, 4), (9, 3), (8, 3), (11, 6), (9, 4), (8, 4), (10, 5), (9, 5), (8, 5), (10, 6), (9, 6), (8, 6),),
}
COLS = 256
UNPACK = 256
VMEM = 60 * 2**20
REMOTE = pl.BlockSpec(memory_space=pl.ANY)
LOCAL = pl.BlockSpec(memory_space=pltpu.VMEM)
SCALARS = pl.BlockSpec(memory_space=pltpu.SMEM)
MESH = pl.DeviceIdType.MESH


EPSILON = 1e-05


NEG = -1e30


def _head_masks(heads, width, value):
    lane = lax.broadcasted_iota(jnp.int32, (1, width), 1) // HEAD
    return [jnp.where(lane == h, value, 0.0).astype(jnp.bfloat16) for h in range(heads)]


def _nt(a, b):
    return lax.dot_general(a, b, (((1,), (1,)), ((), ())), preferred_element_type=jnp.float32)


def _tn(a, b):
    return lax.dot_general(a, b, (((0,), (0,)), ((), ())), preferred_element_type=jnp.float32)


def _nn(a, b):
    return jnp.dot(a, b, preferred_element_type=jnp.float32)


def _column(row):
    wide = jnp.broadcast_to(row.astype(jnp.float32), (128, row.shape[1])).T.astype(jnp.int32)
    return jnp.concatenate([wide] * (BLOCK // 128), axis=1)


def _bias(seg_ref, pad_ref, query_rows, key_rows):
    seg_q, pad_q = seg_ref[:, query_rows], pad_ref[:, query_rows]
    seg_k, pad_k = _column(seg_ref[:, key_rows]), _column(pad_ref[:, key_rows])
    allowed = (seg_k == seg_q) & ((pad_k > 0) | (pad_q == 0))
    return jnp.where(allowed, 0.0, NEG).astype(jnp.float32)


def _meets(places_ref, left):
    edge = left * BLOCK + BLOCK - 1
    return places_ref[0, edge] == places_ref[0, edge + 1]


def _block_copies(source, target, sems):
    def copy(i):
        rows = _rows(i * BLOCK, BLOCK)
        return pltpu.make_async_copy(source.at[rows], target.at[rows], sems.at[i])

    return copy


def _loop(count, body):
    def step(i, carry):
        body(i)
        return carry

    lax.fori_loop(0, count, step, 0)


def attention_forward_kernel(
    heads, blocks, places_ref, qkv_hbm, seg_ref, pad_ref, context_hbm, lse_ref,
    qkv_ref, context_ref, peak_ref, total_ref, acc_ref, load_sems, store_sems,
):
    bf16 = jnp.bfloat16
    width = context_ref.shape[1]
    load = _block_copies(qkv_hbm, qkv_ref, load_sems)
    store = _block_copies(context_ref, context_hbm, store_sems)
    _loop(blocks, lambda i: load(i).start())
    scaled = _head_masks(heads, width, 1.0 / math.sqrt(HEAD))
    load(0).wait()

    def rows_of(i):
        return _rows(i * BLOCK, BLOCK)

    def scores_of(i, j):
        key, bias = qkv_ref[rows_of(j), width : 2 * width], _bias(seg_ref, pad_ref, rows_of(i), rows_of(j))
        query = qkv_ref[rows_of(i), :width]
        return [_nt(key, query * scaled[h]) + bias for h in range(heads)]

    def alone(i):
        @pl.when(i + 1 < blocks)
        def _():
            load(i + 1).wait()

        value = qkv_ref[rows_of(i), 2 * width :].T
        parts = []
        for h, scores in enumerate(scores_of(i, i)):
            peak = jnp.max(scores, axis=0, keepdims=True)
            expo = jnp.exp(scores - peak)
            total = jnp.sum(expo, axis=0, keepdims=True)
            lse_ref[h : h + 1, rows_of(i)] = peak + jnp.log(total)
            parts.append(_nn(value[h * HEAD : (h + 1) * HEAD], expo.astype(bf16)) / total)
        context_ref[rows_of(i), :] = jnp.concatenate(parts, axis=0).astype(bf16).T

    _loop(blocks, alone)

    def among(i):
        def gather(j):
            value = qkv_ref[rows_of(j), 2 * width :].T
            for h, scores in enumerate(scores_of(i, j)):
                old = peak_ref[h]
                peak = jnp.maximum(old, jnp.max(scores, axis=0, keepdims=True))
                expo = jnp.exp(scores - peak)
                ratio = jnp.exp(old - peak)
                peak_ref[h] = peak
                total_ref[h] = total_ref[h] * ratio + jnp.sum(expo, axis=0, keepdims=True)
                place = pl.ds(h * HEAD, HEAD)
                acc_ref[place, :] = acc_ref[place, :] * ratio + _nn(
                    value[h * HEAD : (h + 1) * HEAD], expo.astype(bf16)
                )

        left = (i > 0) & _meets(places_ref, jnp.maximum(i - 1, 0))
        right = (i < blocks - 1) & _meets(places_ref, jnp.minimum(i, blocks - 2))

        @pl.when(left | right)
        def _():
            peak_ref[...] = jnp.full_like(peak_ref, 2 * NEG)
            total_ref[...] = jnp.zeros_like(total_ref)
            acc_ref[...] = jnp.zeros_like(acc_ref)
            gather(i)

            @pl.when(left)
            def _():
                gather(i - 1)

            @pl.when(right)
            def _():
                gather(i + 1)

            for h in range(heads):
                place = pl.ds(h * HEAD, HEAD)
                acc_ref[place, :] = acc_ref[place, :] / total_ref[h]
                lse_ref[h : h + 1, rows_of(i)] = peak_ref[h] + jnp.log(total_ref[h])
            context_ref[rows_of(i), :] = acc_ref[...].astype(bf16).T

        store(i).start()

    _loop(blocks, among)
    _loop(blocks, lambda i: store(i).wait())


def attention_forward(qkv, places, padding):
    length, width = qkv.shape[0], qkv.shape[1] // 3
    heads, blocks = width // HEAD, length // BLOCK
    return pl.pallas_call(
        partial(attention_forward_kernel, heads, blocks),
        in_specs=[SCALARS, REMOTE, LOCAL, LOCAL],
        out_specs=[REMOTE, LOCAL],
        scratch_shapes=[
            pltpu.VMEM((length, 3 * width), jnp.bfloat16),
            pltpu.VMEM((length, width), jnp.bfloat16),
            pltpu.VMEM((heads, 1, BLOCK), jnp.float32),
            pltpu.VMEM((heads, 1, BLOCK), jnp.float32),
            pltpu.VMEM((width, BLOCK), jnp.float32),
            pltpu.SemaphoreType.DMA((blocks,)),
            pltpu.SemaphoreType.DMA((blocks,)),
        ],
        out_shape=[
            jax.ShapeDtypeStruct((length, width), jnp.bfloat16),
            jax.ShapeDtypeStruct((8, length), jnp.float32),
        ],
        compiler_params=pltpu.CompilerParams(vmem_limit_bytes=VMEM),
        name="attention_forward",
    )(places, qkv, places, padding)


def segment_places(segments, padding):
    row_count, seq_len = segments.shape
    if row_count > 1:
        segments = segments + jnp.arange(row_count, dtype=jnp.int32)[:, None] * (seq_len + 1)
    return segments.reshape(1, -1), padding.reshape(1, -1)


def _partners():
    me = lax.axis_index("mp")
    core = lax.rem(me, 2)
    sib = me + 1 - 2 * core
    cnt = lax.rem(me + 2, 4)
    dia = lax.rem(cnt + 1, 2) + cnt - lax.rem(cnt, 2)
    return me, sib, cnt, dia


def _remote(src, dst, send, recv, target):
    return pltpu.make_async_remote_copy(
        src_ref=src, dst_ref=dst, send_sem=send, recv_sem=recv, device_id=target, device_id_type=MESH
    )


def _greet(targets):
    barrier = pltpu.get_barrier_semaphore()
    for target in targets:
        pl.semaphore_signal(barrier, inc=1, device_id=target, device_id_type=MESH)
    pl.semaphore_wait(barrier, len(targets))


def _rows(start, size):
    return pl.ds(pl.multiple_of(start, size), size)


def _part(start, size):
    return pl.ds(pl.multiple_of(start, 16), size)


class Gather:
    def __init__(self, buffer, send, recv, stage, size, sib, cnt):
        self.buffer, self.send, self.recv = buffer, send, recv
        self.stage, self.size, self.sib, self.cnt = stage, size, sib, cnt

    def slot(self, r, k):
        return self.buffer.at[_rows((r * 4 + k) * self.size, self.size)]

    def copy(self, r, kind):
        src, dst, target = ((0, 1, self.sib), (0, 2, self.cnt), (2, 3, self.sib))[kind]
        return _remote(
            self.slot(r, src),
            self.slot(r, dst),
            self.send.at[self.stage, kind, r],
            self.recv.at[self.stage, kind, r],
            {"mp": target},
        )

    def start(self, r):
        self.copy(r, 1).start()
        self.copy(r, 0).start()

    def forward(self, r):
        self.copy(r, 1).wait_recv()
        self.copy(r, 2).start()

    def arrive(self, r):
        self.copy(r, 0).wait_recv()
        self.copy(r, 2).wait_recv()

    def sent(self, r):
        for kind in range(3):
            self.copy(r, kind).wait_send()


class Scatter:
    def __init__(self, bufs, send, recv, stage, size, sib, cnt):
        self.own, self.other, self.stage_sib, self.stage_x, self.recv_sib, self.recv_x = bufs
        self.send, self.recv = send, recv
        self.stage, self.size, self.sib, self.cnt = stage, size, sib, cnt

    def copy(self, r, kind):
        rows = _rows(r * self.size, self.size)
        src, dst, target = (
            (self.stage_sib.at[0, rows], self.recv_sib.at[0, rows], self.sib),
            (self.stage_sib.at[1, rows], self.recv_sib.at[1, rows], self.sib),
            (self.stage_x.at[rows], self.recv_x.at[rows], self.cnt),
        )[kind]
        return _remote(
            src, dst, self.send.at[self.stage, kind, r], self.recv.at[self.stage, kind, r], {"mp": target}
        )

    def sent(self, r):
        for kind in range(3):
            self.copy(r, kind).wait_send()

    def project(self, r, tile):
        size = self.size
        rows = _rows(r * size, size)

        def column(n, carry):
            cols = _rows(n * COLS, COLS)
            part = tile(cols)
            self.own[rows, cols] = part[:size]
            self.stage_sib[1, rows, cols] = part[size : 2 * size].astype(jnp.bfloat16)
            self.other[rows, cols] = part[2 * size : 3 * size]
            self.stage_sib[0, rows, cols] = part[3 * size :].astype(jnp.bfloat16)
            return carry

        lax.fori_loop(0, self.own.shape[1] // COLS, column, 0)
        self.copy(r, 0).start()
        self.copy(r, 1).start()

    def finish(self, r):
        rows = _rows(r * self.size, self.size)
        self.copy(r, 0).wait_recv()
        self.stage_x[rows, :] = (
            self.other[rows, :] + self.recv_sib[0, rows, :].astype(jnp.float32)
        ).astype(jnp.bfloat16)
        self.copy(r, 2).start()
        self.copy(r, 1).wait_recv()
        self.own[rows, :] += self.recv_sib[1, rows, :].astype(jnp.float32)

    def result(self, r):
        rows = _rows(r * self.size, self.size)
        self.copy(r, 2).wait_recv()
        return self.own[rows, :] + self.recv_x[rows, :].astype(jnp.float32)


def _scatter_scratch(own, width):
    f32, bf16 = jnp.float32, jnp.bfloat16
    return [
        pltpu.VMEM((own, width), f32),
        pltpu.VMEM((own, width), f32),
        pltpu.VMEM((2, own, width), bf16),
        pltpu.VMEM((own, width), bf16),
        pltpu.VMEM((2, own, width), bf16),
        pltpu.VMEM((own, width), bf16),
    ]


def _norm(summed):
    center = summed - jnp.mean(summed, axis=-1, keepdims=True)
    variance = jnp.mean(center * center, axis=-1, keepdims=True)
    inverse = lax.rsqrt(variance + EPSILON)
    return center * inverse, inverse


def _norm_back(scaled, unit, inverse):
    return inverse * (
        scaled
        - jnp.mean(scaled, axis=-1, keepdims=True)
        - unit * jnp.mean(scaled * unit, axis=-1, keepdims=True)
    )


def project_kernel(
    bits, inputs_ref, in_proj_ref, out_proj_ref, qv_bias_ref, tokens_hbm, qkv_hbm, full_hbm, tokens_ref, qkv_ref,
    weights, send, recv, load_sems, store_sems, full_sems,
):
    f32, bf16 = jnp.float32, jnp.bfloat16
    me, sib, cnt, dia = _partners()
    own, width = inputs_ref.shape[0], in_proj_ref.shape[2]
    size = own // CHUNKS
    mine = _rows(me * own, own)
    keep = pltpu.make_async_copy(inputs_ref, tokens_ref.at[mine], load_sems.at[0])
    fetch = pltpu.make_async_copy(in_proj_ref, weights, load_sems.at[1])
    fetch.start()
    keep.start()

    quarter = out_proj_ref.shape[0]
    bits = min(bits, (quarter // 16).bit_length() - 1)
    dp = lax.axis_index("dp")
    bit = [lax.rem(dp // (1 << b), 2) for b in range(bits)]
    over = [{"dp": dp + (1 << b) * (1 - 2 * bit[b])} for b in range(bits)]

    def span(block, s):
        first = block * quarter
        for t in range(s):
            first = first + bit[t] * (quarter >> (t + 1))
        return full_hbm.at[_part(first, quarter >> s)]

    def full_copy(k):
        if k < 2:
            mine = span(me, bits if k else 0)
            first = sum(bit[t] * (quarter >> (t + 1)) for t in range(bits)) if k else 0
            source = out_proj_ref.at[_part(first, quarter >> bits)] if k else out_proj_ref
            pair = source, mine, {"mp": cnt if k else sib}
        elif k < 2 + bits:
            block = span(cnt, bits - (k - 2))
            pair = block, block, over[bits - 1 - (k - 2)]
        else:
            block = span(cnt, 0)
            pair = block, block, {"mp": sib}
        return _remote(pair[0], pair[1], full_sems.at[0, k], full_sems.at[1, k], pair[2])

    own_quarter = pltpu.make_async_copy(out_proj_ref, span(me, 0), load_sems.at[2])
    own_quarter.start()

    def full_step(k):
        if k > 0:
            full_copy(k).wait_recv()
        if k <= bits + 1:
            full_copy(k + 1).start()

    _greet([{"mp": sib}, {"mp": cnt}, *over])
    full_copy(1).start()

    def copy(r, kind):
        here = inputs_ref.at[_rows(r * size, size)]
        place = _rows((cnt if kind == 2 else me) * own + r * size, size)
        src, target = ((here, sib), (here, cnt), (tokens_ref.at[place], sib))[kind]
        return _remote(src, tokens_ref.at[place], send.at[kind, r], recv.at[kind, r], {"mp": target})

    for r in range(CHUNKS):
        copy(r, 1).start()
        copy(r, 0).start()

    def stores(first, rows, k):
        place = _rows(first, rows)
        return [
            pltpu.make_async_copy(tokens_ref.at[place], tokens_hbm.at[place], store_sems.at[0, k]),
            pltpu.make_async_copy(qkv_ref.at[place], qkv_hbm.at[place], store_sems.at[1, k]),
        ]

    def compute(first):
        place = _rows(first, size)
        block = tokens_ref[place, :]
        for j in range(3):
            part = jnp.dot(block, weights[j], preferred_element_type=f32)
            if j != 1:
                part = part + qv_bias_ref[j // 2 : j // 2 + 1, :]
            qkv_ref[place, j * width : (j + 1) * width] = part.astype(bf16)

    fetch.wait()
    keep.wait()
    full_copy(0).start()
    _loop(CHUNKS, lambda r: compute(me * own + r * size))
    for store in stores(me * own, own, 0):
        store.start()
    full_step(1)

    def sib_part(r):
        copy(r, 0).wait_recv()
        compute(sib * own + r * size)

    _loop(CHUNKS, sib_part)
    for store in stores(sib * own, own, 1):
        store.start()
    full_step(2)

    def far_part(r):
        @pl.when(r == 0)
        def _():
            full_step(3)

        @pl.when(r == 2)
        def _():
            for k in range(4, bits + 2):
                full_step(k)

        copy(r, 1).wait_recv()
        copy(r, 2).start()
        compute(cnt * own + r * size)
        for store in stores(cnt * own + r * size, size, 2 + 2 * r):
            store.start()
        copy(r, 2).wait_recv()
        compute(dia * own + r * size)
        for store in stores(dia * own + r * size, size, 3 + 2 * r):
            store.start()

    _loop(CHUNKS, far_part)
    full_copy(0).wait_recv()
    full_copy(bits + 2).wait_recv()
    own_quarter.wait()
    for k in range(bits + 3):
        full_copy(k).wait_send()
    for k in range(2):
        for store in stores((me, sib)[k] * own, own, k):
            store.wait()

    def drain(r):
        for kind in range(3):
            copy(r, kind).wait_send()
        for k, block in enumerate((cnt, dia)):
            for store in stores(block * own + r * size, size, 2 + 2 * r + k):
                store.wait()

    _loop(CHUNKS, drain)


def project_tokens(mesh, inputs, in_proj, out_proj, qv_bias):
    own, depth = inputs.shape
    width = in_proj.shape[2]
    shapes = [(4 * own, depth), (4 * own, 3 * width)]
    bits = mesh.shape["dp"].bit_length() - 1
    return pl.pallas_call(
        partial(project_kernel, bits),
        out_shape=[jax.ShapeDtypeStruct(shape, jnp.bfloat16) for shape in (*shapes, (4 * width, depth))],
        in_specs=[REMOTE] * 3 + [LOCAL],
        out_specs=[REMOTE] * 3,
        scratch_shapes=[
            *[pltpu.VMEM(shape, jnp.bfloat16) for shape in shapes],
            pltpu.VMEM(in_proj.shape, jnp.bfloat16),
            pltpu.SemaphoreType.DMA((3, CHUNKS)),
            pltpu.SemaphoreType.DMA((3, CHUNKS)),
            pltpu.SemaphoreType.DMA((3,)),
            pltpu.SemaphoreType.DMA((2, 2 + 2 * CHUNKS)),
            pltpu.SemaphoreType.DMA((2, 3 + bits)),
        ],
        compiler_params=pltpu.CompilerParams(
            collective_id=0, has_side_effects=True, vmem_limit_bytes=VMEM
        ),
        name="project_tokens",
    )(inputs, in_proj, out_proj, qv_bias)


class Reduce:
    def __init__(self, n, rows, order, source, work, final, sems):
        self.n, self.rows, self.source, self.work, self.final, self.sems = n, rows, source, work, final, sems
        self.steps = len(order)
        dp = lax.axis_index("dp")
        self.bit = [lax.rem(dp // (1 << b), 2) for b in order]
        self.peer = [{"dp": dp + (1 << b) * (1 - 2 * bit)} for b, bit in zip(order, self.bit)]

    def size(self, s):
        return self.rows >> s

    def start(self, s):
        first = self.n * self.rows
        for t in range(s):
            first = first + self.bit[t] * self.size(t + 1)
        return first

    def held(self, s):
        if s == 0:
            return self.source
        stride = self.rows - self.size(self.steps)
        return self.work, self.n * stride + self.rows - 2 * self.size(s)

    def halve(self, s):
        ref, first = self.held(s)
        half = self.size(s + 1)
        there, place = self.held(s + 1)
        return _remote(
            ref.at[_part(first + (1 - self.bit[s]) * half, half)],
            there.at[_part(place, half)],
            self.sems.at[0, self.n, s],
            self.sems.at[1, self.n, s],
            self.peer[s],
        )

    def double(self, s):
        block = self.final.at[_rows(self.start(s + 1), self.size(s + 1))]
        k = 2 * self.steps - 1 - s
        return _remote(block, block, self.sems.at[0, self.n, k], self.sems.at[1, self.n, k], self.peer[s])

    def step(self, k):
        steps = self.steps
        if 0 < k <= steps:
            s = k - 1
            half = self.size(s + 1)
            self.halve(s).wait_recv()
            ref, first = self.held(s)
            there, place = self.held(s + 1)
            total = there[_part(place, half), :].astype(jnp.float32) + ref[
                _part(first + self.bit[s] * half, half), :
            ].astype(jnp.float32)
            if k < steps:
                there[_part(place, half), :] = total.astype(jnp.bfloat16)
            else:
                self.final[_rows(self.start(steps), half), :] = total.astype(jnp.bfloat16)
        if k > steps:
            self.double(2 * steps - k).wait_recv()
        if k < steps:
            self.halve(k).start()
        elif k < 2 * steps:
            self.double(2 * steps - 1 - k).start()

    def sent(self):
        for s in range(self.steps):
            if s:
                self.halve(s).wait_send()
            self.double(s).wait_send()


def main_kernel(bits, pieces, *refs):
    f32, bf16 = jnp.float32, jnp.bfloat16
    (context_hbm, out_proj_hbm, inputs_hbm, up_hbm, down_hbm, cotangent_hbm, qkv_hbm, tokens_hbm, in_proj_hbm, full_hbm,
     lse_ref, seg_ref, pad_ref, up_bias_ref, *refs) = refs
    vectors, refs = [v[...] for v in refs[:6]], refs[6:]
    out_bias, attn_gain, attn_shift, down_bias, ffn_gain, ffn_shift = vectors
    (outputs_hbm, inputs_grad_hbm, final_hbm, small_ref,
     context_ref, out_proj_ref, inputs_ref, up_ref, down_ref,
     weight_grads, normed_full, grad2_full, grad1_full, active, back, unit1, inverse1, grad_own, dots_ref,
     own_acc, other_acc, stage_sib, stage_x, recv_sib, recv_x, work, final, small_recv, late_ref, late_recv,
     load_sems, block_sems, trade_sems, store_sems, final_sems, gather_send, gather_recv, scatter_send, scatter_recv,
     sems, small_sems) = refs
    outputs_ref = inputs_ref
    me, sib, cnt, dia = _partners()
    own, depth = inputs_ref.shape
    units, width = up_ref.shape[1], out_proj_ref.shape[0]
    length = 4 * own
    heads, token_blocks = width // HEAD, length // BLOCK
    size, whole = own // CHUNKS, length // CHUNKS
    blocks = (me, sib, cnt, dia)
    early = pieces == CHUNKS
    dp = lax.axis_index("dp")
    loop = partial(_loop, CHUNKS)

    def context_load(r):
        return [
            pltpu.make_async_copy(
                context_hbm.at[_rows(b * own + r * size, size)],
                context_ref.at[_rows((r * 4 + k) * size, size)],
                block_sems.at[k, r],
            )
            for k, b in enumerate(blocks)
        ]

    loads = [
        pltpu.make_async_copy(source, target, load_sems.at[k])
        for k, (source, target) in enumerate(
            (
                (out_proj_hbm, out_proj_ref),
                (inputs_hbm, inputs_ref),
                (up_hbm, up_ref),
                (down_hbm, down_ref),
                (cotangent_hbm, inputs_ref),
                (qkv_hbm, active.at[:, : 3 * width]),
                (tokens_hbm, normed_full),
                (context_hbm, back.at[:, width : 2 * width]),
                (full_hbm, grad1_full.at[:depth]),
                *[(in_proj_hbm.at[j], up_ref.at[:, j * width : (j + 1) * width]) for j in range(3)],
            )
        )
    ]
    loads[1].start()
    loads[8].start()

    own_context = pltpu.make_async_copy(
        context_hbm.at[_rows(me * own, own)], recv_x.at[:, _rows(me * width, width)], load_sems.at[12]
    )
    own_context.start()

    def trade(r, k):
        return _remote(
            context_hbm.at[_rows(blocks[k] * own + r * size, size)],
            recv_x.at[_rows(r * size, size), _rows(me * width, width)],
            trade_sems.at[0, k - 1, r],
            trade_sems.at[1, k - 1, r],
            {"mp": blocks[k]},
        )


    def store(k, r):
        rows = _rows(r * size, size)
        target = (outputs_hbm, inputs_grad_hbm)[k]
        return pltpu.make_async_copy(outputs_ref.at[rows], target.at[rows], store_sems.at[k, r])

    bufs = (own_acc, other_acc, stage_sib, stage_x, recv_sib, recv_x)
    gathers = [
        Gather(buf, gather_send, gather_recv, stage, size, sib, cnt)
        for stage, buf in enumerate((normed_full, grad2_full, grad1_full))
    ]
    scatters = [
        Scatter(bufs, scatter_send, scatter_recv, stage, size, sib, cnt) for stage in range(4)
    ]
    piece = depth // pieces
    count = 3 * pieces

    def source(n):
        if early and n == count - 1:
            return outputs_ref, 0
        return weight_grads, (n if n < 2 * pieces else n - 2 * pieces) * piece

    sums = [
        Reduce(
            n, piece, ORDERS[n] if early else tuple(range(bits)), source(n), work, final, sems
        )
        for n in range(count)
    ]
    over = [{"dp": dp + (1 << b) * (1 - 2 * lax.rem(dp // (1 << b), 2))} for b in range(bits)]
    small_ref[...] = jnp.zeros_like(small_ref)
    late_ref[...] = jnp.zeros_like(late_ref)
    _greet([{"mp": sib}, {"mp": cnt}, {"mp": dia}, *over])
    loop(lambda r: [trade(r, k).start() for k in (2, 3, 1)])
    for load in (loads[2], loads[3], loads[0]):
        load.start()
    loop(lambda r: [load.start() for load in context_load(r)])

    def add_sum(k, value):
        small_ref[k : k + 1, :] += jnp.sum(value, axis=0, keepdims=True)

    own_context.wait()
    loads[1].wait()
    loads[8].wait()

    def lower_norm(r):
        rows = _rows(r * size, size)
        for k in (1, 2, 3):
            trade(r, k).wait_recv()
        attended = _nn(recv_x[rows, :], grad1_full[:depth, :])
        unit, inverse = _norm(inputs_ref[rows, :].astype(f32) + attended + out_bias)
        unit1[rows, :] = unit
        inverse1[rows, :] = inverse
        gathers[0].slot(r, 0)[...] = (unit * attn_gain + attn_shift).astype(bf16)
        gathers[0].start(r)

    loop(lower_norm)
    loads[4].start()
    loads[2].wait()
    loads[3].wait()

    def feed_forward(r):
        rows = _rows(r * whole, whole)
        gathers[0].forward(r)
        gathers[0].arrive(r)
        for k in (1, 2, 3):
            trade(r, k).wait_send()

        def column(n, carry):
            cols = _rows(n * COLS, COLS)
            upper = _nn(normed_full[rows, :], up_ref[:, cols]) + up_bias_ref[:, cols]
            cdf = 0.5 + 0.5 * lax.erf(upper * math.sqrt(0.5))
            pdf = jnp.exp(upper * upper * -0.5) * (1.0 / math.sqrt(2.0 * math.pi))
            active[rows, cols] = (upper * cdf).astype(bf16)
            back[rows, cols] = (cdf + upper * pdf).astype(bf16)
            return carry

        lax.fori_loop(0, units // COLS, column, 0)
        scatters[1].project(r, lambda cols: _nn(active[rows, :], down_ref[:, cols]))
        scatters[1].finish(r)

    loop(feed_forward)
    loads[4].wait()

    def upper_norm(r):
        rows = _rows(r * size, size)
        normed = unit1[rows, :] * attn_gain + attn_shift
        unit, inverse = _norm(normed + scatters[1].result(r) + down_bias)
        cotangent = inputs_ref[rows, :].astype(f32)
        outputs_ref[rows, :] = (unit * ffn_gain + ffn_shift).astype(bf16)
        store(0, r).start()
        grad = _norm_back(cotangent * ffn_gain, unit, inverse)
        gathers[1].slot(r, 0)[...] = grad.astype(bf16)
        gathers[1].start(r)
        grad_own[rows, :] = grad
        add_sum(3, grad)
        add_sum(4, cotangent * unit)
        add_sum(5, cotangent)

    loop(upper_norm)

    def take(r):
        gathers[1].forward(r)
        gathers[1].arrive(r)
        scatters[1].sent(r)

    def feed_back(r):
        rows = _rows(r * whole, whole)

        def column(n, carry):
            cols = _rows(n * COLS, COLS)
            incoming = _nt(grad2_full[rows, :], down_ref[cols, :])
            upper_back = (back[rows, cols].astype(f32) * incoming).astype(bf16)
            back[rows, cols] = upper_back
            late_ref[1:2, cols] += jnp.sum(upper_back.astype(f32), axis=0, keepdims=True)
            return carry

        lax.fori_loop(0, units // COLS, column, 0)
        scatters[2].project(r, lambda cols: _nt(back[rows, :], up_ref[cols, :]))
        scatters[2].finish(r)

    def take_back(r):
        take(r)
        feed_back(r)

    _loop(CHUNKS - 1, take_back)
    take(CHUNKS - 1)

    def weights(k, p):
        cols = _rows(p * (depth // CHUNKS), depth // CHUNKS)
        place = _rows(k * depth + p * (depth // CHUNKS), depth // CHUNKS)
        if k == 0:
            weight_grads[place, :] = _tn(active[:, cols], grad2_full[...]).astype(bf16)
        else:
            weight_grads[place, :] = _tn(normed_full[:, cols], back[...]).astype(bf16)

    def out_weights():
        target = outputs_ref.at[:width] if early else weight_grads.at[3 * width : 4 * width]
        target[...] = _tn(context_ref[...], grad1_full[...]).astype(bf16)

    def in_weights(j):
        weight_grads[_rows(j * width, width), :] = _tn(
            grads[:, j * width : (j + 1) * width], normed_full[...]
        ).astype(bf16)

    def move(n, k):
        if k == 0 and n < 2 * pieces:
            weights(n // pieces, n % pieces)
        elif k == 0 and n == count - 1:
            out_weights()
        elif k == 0:
            in_weights(n - 2 * pieces)
        sums[n].step(k)
        if k == 2 * bits:
            store_final(n).start()

    def store_final(n):
        rows = _rows(n * piece, piece)
        return pltpu.make_async_copy(final.at[rows], final_hbm.at[rows], final_sems.at[n])

    def slot(i, first, number):
        for at in range(first, first + number) if early else ():
            if at in PLAN:

                @pl.when(i == at - first)
                def _():
                    for n, k in PLAN[at]:
                        move(n, k)

    if early:
        for n, k in PLAN[-1]:
            move(n, k)
    feed_back(CHUNKS - 1)
    for load in loads[9:]:
        load.start()

    def lower_back(r):
        slot(r, 0, CHUNKS)
        if not early:
            for k in range(2):

                @pl.when(r // 2 == k)
                def _():
                    for h in range(2):
                        weights(k, 2 * r - 4 * k + h)

                @pl.when(r == 2 * k + 1)
                def _():
                    sums[k].step(0)

        rows = _rows(r * size, size)
        incoming = grad_own[rows, :] + scatters[2].result(r)
        unit = unit1[rows, :]
        grad = _norm_back(incoming * attn_gain, unit, inverse1[rows, :])
        gathers[2].slot(r, 0)[...] = grad.astype(bf16)
        gathers[2].start(r)
        grad_own[rows, :] = grad
        add_sum(0, grad)
        add_sum(1, incoming * unit)
        add_sum(2, incoming)

    loop(lower_back)
    gathers_done = lambda r: [gather.sent(r) for gather in gathers[:2]]
    loop(gathers_done)
    for load in loads[5:8]:
        load.start()

    loads[0].wait()
    loop(lambda r: [load.wait() for load in context_load(r)])

    def context_back(r):
        slot(r, CHUNKS, CHUNKS)
        rows = _rows(r * whole, whole)
        gathers[2].forward(r)
        gathers[2].arrive(r)
        scatters[2].sent(r)
        grad = _nt(grad1_full[rows, :], out_proj_ref[...]).astype(bf16)
        for k, b in enumerate(blocks):
            part = _rows(b * own + r * size, size)
            back[part, :width] = grad[k * size : (k + 1) * size]

    loop(context_back)
    loop(lambda r: gathers[2].sent(r))
    loop(lambda r: store(0, r).wait())
    for load in loads[5:8]:
        load.wait()

    targets = [{"mp": sib}, {"mp": cnt}, *over]

    def small_step(k):
        return _remote(
            small_ref.at[:8], small_recv.at[k], small_sems.at[0, k], small_sems.at[1, k], targets[k]
        )

    def small_end(k):
        small_step(k).wait()
        small_ref[:8, :] += small_recv[k]

    def late_step(k):
        at = len(targets) + k
        return _remote(late_ref, late_recv.at[k], small_sems.at[0, at], small_sems.at[1, at], over[k])

    def late_end(k):
        late_step(k).wait()
        late_ref[...] += late_recv[k]

    def small_turn(k):
        if k:
            small_end(k - 1)
        if k < len(targets):
            small_step(k).start()

    scaled = _head_masks(heads, width, 1.0 / math.sqrt(HEAD))
    plain = _head_masks(heads, width, 1.0)
    keys_acc, values_acc, query_acc = unit1, other_acc, own_acc.at[:width, :BLOCK]
    keys_acc[...] = jnp.zeros_like(keys_acc)
    values_acc[...] = jnp.zeros_like(values_acc)
    grads = grad2_full
    per = own // BLOCK

    def spot(j):
        return _rows(lax.rem(j, per) * BLOCK, BLOCK), _rows(j // per * width, width)

    def attend(t):
        i, turn = t // 3, lax.rem(t, 3)
        for k in range(len(targets) + 1):

            @pl.when(t == SMALL_TURNS[k])
            def _():
                small_turn(k)

        slot(t, 2 * CHUNKS, 3 * token_blocks)
        query_rows = _rows(i * BLOCK, BLOCK)

        @pl.when(turn == 0)
        def _():
            product = (
                back[query_rows, :width].astype(f32) * back[query_rows, width : 2 * width].astype(f32)
            ).T
            for h in range(heads):
                dots_ref[h : h + 1, :] = jnp.sum(
                    product[h * HEAD : (h + 1) * HEAD], axis=0, keepdims=True
                )
            query_acc[...] = jnp.zeros_like(query_acc)

        @pl.when((i + turn >= 1) & (i + turn <= token_blocks))
        def _():
            j = jnp.clip(i + turn - 1, 0, token_blocks - 1)
            query, grad = active[query_rows, :width], back[query_rows, :width]
            rows = _rows(j * BLOCK, BLOCK)
            bias = _bias(seg_ref, pad_ref, query_rows, rows)
            key, value = active[rows, width : 2 * width], active[rows, 2 * width : 3 * width]
            key_rows = (key * (1.0 / math.sqrt(HEAD))).astype(bf16).T
            key_add = jnp.zeros((BLOCK, width), f32)
            value_add = jnp.zeros((BLOCK, width), f32)
            for h in range(heads):
                query_h, grad_h = query * scaled[h], grad * plain[h]
                scores = _nt(key, query_h) + bias
                prob = jnp.exp(scores - lse_ref[h : h + 1, query_rows])
                score_grad = (prob * (_nt(value, grad_h) - dots_ref[h : h + 1, :])).astype(bf16)
                key_add = key_add + _nn(score_grad, query_h)
                value_add = value_add + _nn(prob.astype(bf16), grad_h)
                query_acc[pl.ds(h * HEAD, HEAD), :] += _nn(key_rows[h * HEAD : (h + 1) * HEAD], score_grad)
            keys_acc[spot(j)] += key_add
            values_acc[spot(j)] += value_add

        @pl.when(turn == 2)
        def _():
            grads[query_rows, :width] = query_acc[...].astype(bf16).T

    _loop(3 * token_blocks, attend)

    def keep(j):
        rows = _rows(j * BLOCK, BLOCK)
        grads[rows, width : 2 * width] = keys_acc[spot(j)].astype(bf16)
        grads[rows, 2 * width : 3 * width] = values_acc[spot(j)].astype(bf16)

    _loop(token_blocks, keep)

    if not early:
        for n in range(2):
            sums[n].step(1)
        out_weights()
        in_weights(0)
        in_weights(1)
        in_weights(2)
    for n in range(2 * pieces):
        sums[n].halve(0).wait_send()

    def partial_rows(r):
        chunk = jnp.concatenate(
            [grads[_rows(b * own + r * size, size), : 3 * width] for b in blocks], axis=0
        )

        def tile(cols):
            return _nt(chunk, up_ref[cols, : 3 * width])

        scatters[3].project(r, tile)
        scatters[3].finish(r)

    def finish(r):
        rows = _rows(r * size, size)
        outputs_ref[rows, :] = (grad_own[rows, :] + scatters[3].result(r)).astype(bf16)
        store(1, r).start()
        scatters[3].sent(r)

    def bias(j):
        return jnp.sum(grads[:, j * width : (j + 1) * width].astype(f32), axis=0, keepdims=True)

    for load in loads[9:]:
        load.wait()
    late_ref[:1, :width] = bias(0)
    late_ref[:1, width : 2 * width] = bias(2)
    late_step(0).start()
    if early:
        tail = PLAN[2 * CHUNKS + 3 * token_blocks]
    else:
        tail = [(2, 0)] + [(-1, r) for r in range(CHUNKS)]
        tail += [(n, k) for k in range(1, 2 * bits + 1) for n in range(3) if n == 2 or k > 1]
    last = max(k for k, (n, _) in enumerate(tail) if n < 0)
    turns = [(len(tail) - 1) * (k + 2) // (bits + 1) for k in range(bits)]
    for at, (n, k) in enumerate(tail):
        if n < 0:
            partial_rows(k)
        elif k or early:
            move(n, k)
        else:
            sums[n].step(0)
        for turn in [turn for turn, place in enumerate(turns) if place == at]:
            late_end(turn)
            if turn + 1 < bits:
                late_step(turn + 1).start()
        if at == last + 3 * (len(tail) - 1 - last) // 4:
            if early:
                sums[-1].halve(0).wait_send()
            loop(finish)
    for n in range(count):
        sums[n].sent()
        if n >= 2 * pieces and not (early and n == count - 1):
            sums[n].halve(0).wait_send()
    small_ref[8:10, :] = late_ref[:2, :]
    loop(lambda r: store(1, r).wait())
    for n in range(3 * pieces):
        store_final(n).wait()


def main_layer(mesh, arrays, lse_rows, places, real, up_bias, vectors):
    f32, bf16 = jnp.float32, jnp.bfloat16
    context, out_proj, inputs, up_proj, down_proj = arrays[:5]
    own, depth = inputs.shape
    units, width = up_proj.shape[1], out_proj.shape[0]
    whole, half = 4 * own, depth // 2
    bits = mesh.shape["dp"].bit_length() - 1
    pieces = CHUNKS if (depth // CHUNKS >> bits) >= 16 else 1
    outs = [((own, depth), bf16), ((own, depth), bf16), ((3 * depth, depth), bf16), ((16, depth), f32)]
    return pl.pallas_call(
        partial(main_kernel, bits, pieces),
        out_shape=[jax.ShapeDtypeStruct(*out) for out in outs],
        in_specs=[REMOTE] * 10 + [LOCAL] * 10,
        out_specs=[REMOTE] * 3 + [LOCAL],
        scratch_shapes=[
            *[pltpu.VMEM(array.shape, bf16) for array in arrays[:5]],
            pltpu.VMEM((2 * depth, depth), bf16),
            pltpu.VMEM((whole, depth), bf16),
            pltpu.VMEM((whole, depth), bf16),
            pltpu.VMEM((whole, depth), bf16),
            pltpu.VMEM((whole, units), bf16),
            pltpu.VMEM((whole, units), bf16),
            pltpu.VMEM((own, depth), f32),
            pltpu.VMEM((own, 1), f32),
            pltpu.VMEM((own, depth), f32),
            pltpu.VMEM((8, BLOCK), f32),
            *_scatter_scratch(own, depth),
            pltpu.VMEM((3 * pieces * (depth // pieces - (depth // pieces >> bits)), depth), bf16),
            pltpu.VMEM((3 * depth, depth), bf16),
            pltpu.VMEM((2 + bits, 8, depth), f32),
            pltpu.VMEM((8, depth), f32),
            pltpu.VMEM((bits, 8, depth), f32),
            pltpu.SemaphoreType.DMA((13,)),
            pltpu.SemaphoreType.DMA((4, CHUNKS)),
            pltpu.SemaphoreType.DMA((2, 3, CHUNKS)),
            pltpu.SemaphoreType.DMA((2, CHUNKS)),
            pltpu.SemaphoreType.DMA((3 * pieces,)),
            pltpu.SemaphoreType.DMA((3, 3, CHUNKS)),
            pltpu.SemaphoreType.DMA((3, 3, CHUNKS)),
            pltpu.SemaphoreType.DMA((4, 3, CHUNKS)),
            pltpu.SemaphoreType.DMA((4, 3, CHUNKS)),
            pltpu.SemaphoreType.DMA((2, 3 * pieces, 2 * bits)),
            pltpu.SemaphoreType.DMA((2, 2 + 2 * bits)),
        ],
        compiler_params=pltpu.CompilerParams(
            collective_id=1, has_side_effects=True, vmem_limit_bytes=63 * 2**20
        ),
        name="main_layer",
    )(*arrays, lse_rows, places, real, up_bias, *vectors)


def unpack_kernel(
    width, final_ref, attn_ref, small_ref, outputs_ref, inputs_grad_ref, down_ref, up_ref, in_ref, out_ref,
    qv_ref, up_bias_ref, *refs,
):
    f32 = jnp.float32
    vectors, outputs_out, inputs_grad_out = refs[:6], refs[6], refs[7]
    down_ref[...] = final_ref[0].astype(f32)
    up_ref[...] = final_ref[1].astype(f32)
    for j in range(3):
        in_ref[j] = attn_ref[j * width : (j + 1) * width, :].astype(f32).T
    out_ref[...] = attn_ref[3 * width :, :].astype(f32)
    outputs_out[...] = outputs_ref[...]
    inputs_grad_out[...] = inputs_grad_ref[...]
    for k, vector in enumerate(vectors):
        vector[...] = small_ref[k : k + 1, :]
    up_bias_ref[...] = small_ref[9:10, :]
    for k in range(2):
        qv_ref[k : k + 1, :] = small_ref[8:9, k * width : (k + 1) * width]


def unpack(final, small, outputs, inputs_grad, width):
    f32 = jnp.float32
    own, depth = outputs.shape
    steps = depth // UNPACK
    part = own // steps
    matrix = pl.BlockSpec((UNPACK, depth), lambda i: (i, 0))
    tokens = pl.BlockSpec((part, depth), lambda i: (i, 0))
    vector = pl.BlockSpec((1, depth), lambda i: (0, 0))
    shapes = [
        ((depth, depth), f32, matrix),
        ((depth, depth), f32, matrix),
        ((3, depth, width), f32, pl.BlockSpec((3, UNPACK, width), lambda i: (0, i, 0))),
        ((width, depth), f32, pl.BlockSpec((width, UNPACK), lambda i: (0, i))),
        ((2, width), f32, pl.BlockSpec((2, width), lambda i: (0, 0))),
        *[((1, depth), f32, vector)] * 7,
        ((own, depth), jnp.bfloat16, tokens),
        ((own, depth), jnp.bfloat16, tokens),
    ]
    return pl.pallas_call(
        partial(unpack_kernel, width),
        grid=(steps,),
        in_specs=[
            pl.BlockSpec((2, UNPACK, depth), lambda i: (0, i, 0)),
            pl.BlockSpec((depth, UNPACK), lambda i: (2, i)),
            pl.BlockSpec((16, depth), lambda i: (0, 0)),
            tokens,
            tokens,
        ],
        out_specs=[spec for _, _, spec in shapes],
        out_shape=[jax.ShapeDtypeStruct(shape, dtype) for shape, dtype, _ in shapes],
        compiler_params=pltpu.CompilerParams(vmem_limit_bytes=VMEM),
        name="unpack_gradients",
    )(final.reshape(3, depth, depth), final, small, outputs, inputs_grad)


def shards(
    mesh,
    inputs,
    in_proj,
    qv_bias,
    out_proj,
    out_bias,
    attn_gain,
    attn_shift,
    up_proj,
    up_bias,
    down_proj,
    down_bias,
    ffn_gain,
    ffn_shift,
    segments,
    padding,
    cotangent,
):
    places, real = segment_places(segments, padding)
    vectors = [v[None] for v in (out_bias, attn_gain, attn_shift, down_bias, ffn_gain, ffn_shift)]
    tokens, qkv, full = project_tokens(mesh, inputs, in_proj, out_proj, qv_bias)
    context, lse_rows = attention_forward(qkv, places, real)
    arrays = (context, out_proj, inputs, up_proj, down_proj, cotangent, qkv, tokens, in_proj, full)
    outputs, inputs_grad, final, small = main_layer(
        mesh, arrays, lse_rows, places, real, up_bias[None], vectors
    )
    down_grad, up_grad, in_grad, out_grad, qv_grad, up_bias_grad, *vectors, outputs, inputs_grad = unpack(
        final, small, outputs, inputs_grad, in_proj.shape[2]
    )
    vectors = [v[0] for v in vectors]
    return (
        outputs,
        inputs_grad,
        in_grad,
        qv_grad,
        out_grad,
        *vectors[:3],
        up_grad,
        up_bias_grad[0],
        down_grad,
        *vectors[3:],
    )


def solution(mesh):
    return jax.shard_map(
        partial(shards, mesh),
        mesh=mesh,
        in_specs=(
            P(("dp", "mp"), None),
            P(None, None, "mp"),
            P(None, "mp"),
            P("mp", None),
            P(),
            P(),
            P(),
            P(None, "mp"),
            P("mp"),
            P("mp", None),
            P(),
            P(),
            P(),
            P("dp", None),
            P("dp", None),
            P(("dp", "mp"), None),
        ),
        out_specs=(
            P(("dp", "mp"), None),
            P(("dp", "mp"), None),
            P(None, None, "mp"),
            P(None, "mp"),
            P("mp", None),
            P(),
            P(),
            P(),
            P(None, "mp"),
            P("mp"),
            P("mp", None),
            P(),
            P(),
            P(),
        ),
        check_vma=False,
    )
```

```python
from functools import partial
import math

import jax
import jax.numpy as jnp
from jax import lax
from jax.experimental import pallas as pl
from jax.experimental.pallas import tpu as pltpu
from jax.sharding import PartitionSpec as P

HEAD = 64
BLOCK = 256
CHUNKS = 4
SMALL_TURNS = (0, 1, 3, 10, 16, 23, 23, 23, 23)
ORDERS = (
    (1, 2, 0),
    (0, 1, 2),
    (0, 1, 2),
    (0, 1, 2),
    (0, 1, 2),
    (0, 1, 2),
    (0, 1, 2),
    (0, 1, 2),
    (1, 2, 0),
    (0, 1, 2),
    (0, 1, 2),
    (0, 1, 2),
)
PLAN = {
    -1: ((2, 0), (1, 0), (0, 0), (3, 0),),
    0: ((7, 0), (0, 1), (2, 1), (4, 0),),
    1: ((5, 0), (6, 0),),
    3: ((1, 1), (0, 2),),
    4: ((2, 2), (3, 1), (1, 2),),
    5: ((7, 1), (2, 3), (3, 2),),
    6: ((1, 3), (4, 1), (7, 2), (2, 4),),
    7: ((3, 3), (5, 1), (1, 4), (4, 2),),
    8: ((11, 0), (0, 3), (2, 5), (6, 1), (7, 3),),
    10: ((3, 4),),
    12: ((5, 2),),
    14: ((1, 5),),
    15: ((4, 3),),
    16: ((11, 1),),
    17: ((0, 4), (6, 2),),
    18: ((7, 4),),
    19: ((3, 5),),
    20: ((5, 3),),
    21: ((4, 4),),
    23: ((11, 2),),
    25: ((0, 5),),
    26: ((6, 3),),
    28: ((7, 5),),
    29: ((5, 4),),
    32: ((10, 0), (11, 3), (1, 6), (2, 6), (3, 6), (4, 5), (8, 0), (9, 0), (0, 6), (7, 6), (6, 4), (5, 5), (-1, 0), (10, 1), (11, 4), (8, 1), (-1, 1), (4, 6), (6, 5), (10, 2), (9, 1), (11, 5), (-1, 2), (8, 2), (10, 3), (5, 6), (9, 2), (-1, 3), (6, 6), (10, 4), (9, 3), (8, 3), (11, 6), (9, 4), (8, 4), (10, 5), (9, 5), (8, 5), (10, 6), (9, 6), (8, 6),),
}
COLS = 256
UNPACK = 512
VMEM = 60 * 2**20
REMOTE = pl.BlockSpec(memory_space=pl.ANY)
LOCAL = pl.BlockSpec(memory_space=pltpu.VMEM)
MESH = pl.DeviceIdType.MESH


EPSILON = 1e-05


NEG = -1e30


def _head_masks(heads, width, value):
    lane = lax.broadcasted_iota(jnp.int32, (1, width), 1) // HEAD
    return [jnp.where(lane == h, value, 0.0).astype(jnp.bfloat16) for h in range(heads)]


def _nt(a, b):
    return lax.dot_general(a, b, (((1,), (1,)), ((), ())), preferred_element_type=jnp.float32)


def _tn(a, b):
    return lax.dot_general(a, b, (((0,), (0,)), ((), ())), preferred_element_type=jnp.float32)


def _nn(a, b):
    return jnp.dot(a, b, preferred_element_type=jnp.float32)


def _column(row):
    wide = jnp.broadcast_to(row.astype(jnp.float32), (128, row.shape[1])).T.astype(jnp.int32)
    return jnp.concatenate([wide] * (BLOCK // 128), axis=1)


def _bias(seg_ref, pad_ref, query_rows, key_rows):
    seg_q, pad_q = seg_ref[:, query_rows], pad_ref[:, query_rows]
    seg_k, pad_k = _column(seg_ref[:, key_rows]), _column(pad_ref[:, key_rows])
    allowed = (seg_k == seg_q) & ((pad_k > 0) | (pad_q == 0))
    return jnp.where(allowed, 0.0, NEG).astype(jnp.float32)


def _loop(count, body):
    def step(i, carry):
        body(i)
        return carry

    lax.fori_loop(0, count, step, 0)


def segment_places(segments, padding):
    row_count, seq_len = segments.shape
    if row_count > 1:
        segments = segments + jnp.arange(row_count, dtype=jnp.int32)[:, None] * (seq_len + 1)
    return segments.reshape(1, -1), padding.reshape(1, -1)


def _partners():
    me = lax.axis_index("mp")
    core = lax.rem(me, 2)
    sib = me + 1 - 2 * core
    cnt = lax.rem(me + 2, 4)
    dia = lax.rem(cnt + 1, 2) + cnt - lax.rem(cnt, 2)
    return me, sib, cnt, dia


def _remote(src, dst, send, recv, target):
    return pltpu.make_async_remote_copy(
        src_ref=src, dst_ref=dst, send_sem=send, recv_sem=recv, device_id=target, device_id_type=MESH
    )


def _greet(targets):
    barrier = pltpu.get_barrier_semaphore()
    for target in targets:
        pl.semaphore_signal(barrier, inc=1, device_id=target, device_id_type=MESH)
    pl.semaphore_wait(barrier, len(targets))


def _rows(start, size):
    return pl.ds(pl.multiple_of(start, size), size)


def _part(start, size):
    return pl.ds(pl.multiple_of(start, 16), size)


class Gather:
    def __init__(self, buffer, send, recv, stage, size, sib, cnt):
        self.buffer, self.send, self.recv = buffer, send, recv
        self.stage, self.size, self.sib, self.cnt = stage, size, sib, cnt

    def slot(self, r, k):
        return self.buffer.at[_rows((r * 4 + k) * self.size, self.size)]

    def copy(self, r, kind):
        src, dst, target = ((0, 1, self.sib), (0, 2, self.cnt), (2, 3, self.sib))[kind]
        return _remote(
            self.slot(r, src),
            self.slot(r, dst),
            self.send.at[self.stage, kind, r],
            self.recv.at[self.stage, kind, r],
            {"mp": target},
        )

    def start(self, r):
        self.copy(r, 1).start()
        self.copy(r, 0).start()

    def forward(self, r):
        self.copy(r, 1).wait_recv()
        self.copy(r, 2).start()

    def arrive(self, r):
        self.copy(r, 0).wait_recv()
        self.copy(r, 2).wait_recv()

    def sent(self, r):
        for kind in range(3):
            self.copy(r, kind).wait_send()


class Scatter:
    def __init__(self, bufs, send, recv, stage, size, sib, cnt):
        self.own, self.other, self.stage_sib, self.stage_x, self.recv_sib, self.recv_x = bufs
        self.send, self.recv = send, recv
        self.stage, self.size, self.sib, self.cnt = stage, size, sib, cnt

    def copy(self, r, kind):
        rows = _rows(r * self.size, self.size)
        src, dst, target = (
            (self.stage_sib.at[0, rows], self.recv_sib.at[0, rows], self.sib),
            (self.stage_sib.at[1, rows], self.recv_sib.at[1, rows], self.sib),
            (self.stage_x.at[rows], self.recv_x.at[rows], self.cnt),
        )[kind]
        return _remote(
            src, dst, self.send.at[self.stage, kind, r], self.recv.at[self.stage, kind, r], {"mp": target}
        )

    def sent(self, r):
        for kind in range(3):
            self.copy(r, kind).wait_send()

    def project(self, r, tile):
        size = self.size
        rows = _rows(r * size, size)

        def column(n, carry):
            cols = _rows(n * COLS, COLS)
            part = tile(cols)
            self.own[rows, cols] = part[:size]
            self.stage_sib[1, rows, cols] = part[size : 2 * size].astype(jnp.bfloat16)
            self.other[rows, cols] = part[2 * size : 3 * size]
            self.stage_sib[0, rows, cols] = part[3 * size :].astype(jnp.bfloat16)
            return carry

        lax.fori_loop(0, self.own.shape[1] // COLS, column, 0)
        self.copy(r, 0).start()
        self.copy(r, 1).start()

    def finish(self, r):
        rows = _rows(r * self.size, self.size)
        self.copy(r, 0).wait_recv()
        self.stage_x[rows, :] = (
            self.other[rows, :] + self.recv_sib[0, rows, :].astype(jnp.float32)
        ).astype(jnp.bfloat16)
        self.copy(r, 2).start()
        self.copy(r, 1).wait_recv()
        self.own[rows, :] += self.recv_sib[1, rows, :].astype(jnp.float32)

    def result(self, r):
        rows = _rows(r * self.size, self.size)
        self.copy(r, 2).wait_recv()
        return self.own[rows, :] + self.recv_x[rows, :].astype(jnp.float32)


def _scatter_scratch(own, width):
    f32, bf16 = jnp.float32, jnp.bfloat16
    return [
        pltpu.VMEM((own, width), f32),
        pltpu.VMEM((own, width), f32),
        pltpu.VMEM((2, own, width), bf16),
        pltpu.VMEM((own, width), bf16),
        pltpu.VMEM((2, own, width), bf16),
        pltpu.VMEM((own, width), bf16),
    ]


def _norm(summed):
    center = summed - jnp.mean(summed, axis=-1, keepdims=True)
    variance = jnp.mean(center * center, axis=-1, keepdims=True)
    inverse = lax.rsqrt(variance + EPSILON)
    return center * inverse, inverse


def _norm_back(scaled, unit, inverse):
    return inverse * (
        scaled
        - jnp.mean(scaled, axis=-1, keepdims=True)
        - unit * jnp.mean(scaled * unit, axis=-1, keepdims=True)
    )


class Reduce:
    def __init__(self, n, rows, order, source, work, final, sems):
        self.n, self.rows, self.source, self.work, self.final, self.sems = n, rows, source, work, final, sems
        self.steps = len(order)
        dp = lax.axis_index("dp")
        self.bit = [lax.rem(dp // (1 << b), 2) for b in order]
        self.peer = [{"dp": dp + (1 << b) * (1 - 2 * bit)} for b, bit in zip(order, self.bit)]

    def size(self, s):
        return self.rows >> s

    def start(self, s):
        first = self.n * self.rows
        for t in range(s):
            first = first + self.bit[t] * self.size(t + 1)
        return first

    def held(self, s):
        if s == 0:
            return self.source
        stride = self.rows - self.size(self.steps)
        return self.work, self.n * stride + self.rows - 2 * self.size(s)

    def halve(self, s):
        ref, first = self.held(s)
        half = self.size(s + 1)
        there, place = self.held(s + 1)
        return _remote(
            ref.at[_part(first + (1 - self.bit[s]) * half, half)],
            there.at[_part(place, half)],
            self.sems.at[0, self.n, s],
            self.sems.at[1, self.n, s],
            self.peer[s],
        )

    def double(self, s):
        block = self.final.at[_rows(self.start(s + 1), self.size(s + 1))]
        k = 2 * self.steps - 1 - s
        return _remote(block, block, self.sems.at[0, self.n, k], self.sems.at[1, self.n, k], self.peer[s])

    def step(self, k):
        steps = self.steps
        if 0 < k <= steps:
            s = k - 1
            half = self.size(s + 1)
            self.halve(s).wait_recv()
            ref, first = self.held(s)
            there, place = self.held(s + 1)
            total = there[_part(place, half), :].astype(jnp.float32) + ref[
                _part(first + self.bit[s] * half, half), :
            ].astype(jnp.float32)
            if k < steps:
                there[_part(place, half), :] = total.astype(jnp.bfloat16)
            else:
                self.final[_rows(self.start(steps), half), :] = total.astype(jnp.bfloat16)
        if k > steps:
            self.double(2 * steps - k).wait_recv()
        if k < steps:
            self.halve(k).start()
        elif k < 2 * steps:
            self.double(2 * steps - 1 - k).start()

    def sent(self):
        for s in range(self.steps):
            if s:
                self.halve(s).wait_send()
            self.double(s).wait_send()


def main_kernel(bits, pieces, *refs):
    f32, bf16 = jnp.float32, jnp.bfloat16
    (inputs_hbm, in_proj_hbm, out_proj_hbm, up_hbm, down_hbm, cotangent_hbm,
     qv_bias_ref, seg_ref, pad_ref, up_bias_ref, *refs) = refs
    vectors, refs = [v[...] for v in refs[:6]], refs[6:]
    out_bias, attn_gain, attn_shift, down_bias, ffn_gain, ffn_shift = vectors
    (outputs_hbm, inputs_grad_hbm, final_hbm, tokens_hbm, qkv_hbm, full_hbm, context_hbm, small_ref,
     context_ref, out_proj_ref, inputs_ref, up_ref, down_ref,
     weight_grads, normed_full, grad2_full, grad1_full, active, back, unit1, inverse1, grad_own, dots_ref,
     lse_ref, peak_ref, total_ref,
     own_acc, other_acc, stage_sib, stage_x, recv_sib, recv_x, work, final, small_recv, late_ref, late_recv,
     load_sems, block_sems, trade_sems, store_sems, final_sems, gather_send, gather_recv, scatter_send, scatter_recv,
     sems, small_sems, token_sems, keep_sems, full_sems) = refs
    outputs_ref = inputs_ref
    me, sib, cnt, dia = _partners()
    own, depth = inputs_ref.shape
    units, width = up_ref.shape[1], out_proj_ref.shape[0]
    length = 4 * own
    heads, token_blocks = width // HEAD, length // BLOCK
    size, whole = own // CHUNKS, length // CHUNKS
    blocks = (me, sib, cnt, dia)
    early = pieces == CHUNKS
    loop = partial(_loop, CHUNKS)

    def context_load(r):
        return [
            pltpu.make_async_copy(
                context_hbm.at[_rows(b * own + r * size, size)],
                context_ref.at[_rows((r * 4 + k) * size, size)],
                block_sems.at[k, r],
            )
            for k, b in enumerate(blocks)
        ]

    loads = [
        pltpu.make_async_copy(source, target, load_sems.at[k])
        for k, (source, target) in enumerate(
            (
                (out_proj_hbm, out_proj_ref),
                (inputs_hbm, inputs_ref),
                (up_hbm, up_ref),
                (down_hbm, down_ref),
                (cotangent_hbm, inputs_ref),
                (qkv_hbm, active.at[:, : 3 * width]),
                (tokens_hbm, normed_full),
                (context_hbm, back.at[:, width : 2 * width]),
                (full_hbm, grad1_full.at[:depth]),
                *[(in_proj_hbm.at[j], up_ref.at[:, j * width : (j + 1) * width]) for j in range(3)],
            )
        )
    ]
    own_context = pltpu.make_async_copy(
        back.at[_rows(me * own, own), :width], recv_x.at[:, _rows(me * width, width)], load_sems.at[12]
    )

    def trade(r, k):
        return _remote(
            back.at[_rows(blocks[k] * own + r * size, size), :width],
            recv_x.at[_rows(r * size, size), _rows(me * width, width)],
            trade_sems.at[0, k - 1, r],
            trade_sems.at[1, k - 1, r],
            {"mp": blocks[k]},
        )

    tokens_ref = normed_full

    def token_copy(r, kind):
        here = inputs_hbm.at[_rows(r * size, size)]
        place = _rows((cnt if kind == 2 else me) * own + r * size, size)
        src, target = ((here, sib), (here, cnt), (tokens_ref.at[place], sib))[kind]
        return _remote(
            src, tokens_ref.at[place], token_sems.at[0, kind, r], token_sems.at[1, kind, r], {"mp": target}
        )

    def keeps(k, r):
        place = _rows(blocks[k] * own + r * size, size)
        return [
            pltpu.make_async_copy(tokens_ref.at[place], tokens_hbm.at[place], keep_sems.at[0, k, r]),
            pltpu.make_async_copy(
                active.at[place, : 3 * width], qkv_hbm.at[place], keep_sems.at[1, k, r]
            ),
        ]

    dp = lax.axis_index("dp")
    shares = min(bits, (width // 16).bit_length() - 1)
    bit = [lax.rem(dp // (1 << b), 2) for b in range(bits)]
    over = [{"dp": dp + (1 << b) * (1 - 2 * bit[b])} for b in range(bits)]

    def span(block, s):
        first = block * width
        for t in range(s):
            first = first + bit[t] * (width >> (t + 1))
        return full_hbm.at[_part(first, width >> s)]

    def full_copy(k):
        if k == 0:
            pair = out_proj_hbm, span(me, 0), {"mp": sib}
        elif k == 1:
            first = sum(bit[t] * (width >> (t + 1)) for t in range(shares))
            pair = out_proj_hbm.at[_part(first, width >> shares)], span(me, shares), {"mp": cnt}
        elif k < 2 + shares:
            block = span(cnt, shares - (k - 2))
            pair = block, block, over[shares - 1 - (k - 2)]
        else:
            block = span(cnt, 0)
            pair = block, block, {"mp": sib}
        return _remote(pair[0], pair[1], full_sems.at[0, k], full_sems.at[1, k], pair[2])

    own_quarter = pltpu.make_async_copy(out_proj_hbm, span(me, 0), load_sems.at[13])
    own_tokens = pltpu.make_async_copy(inputs_hbm, tokens_ref.at[_rows(me * own, own)], load_sems.at[14])

    def full_step(k):
        full_copy(k).wait_recv()
        full_copy(k + 1).start()

    def store(k, r):
        rows = _rows(r * size, size)
        target = (outputs_hbm, inputs_grad_hbm)[k]
        return pltpu.make_async_copy(outputs_ref.at[rows], target.at[rows], store_sems.at[k, r])

    bufs = (own_acc, other_acc, stage_sib, stage_x, recv_sib, recv_x)
    gathers = [
        Gather(buf, gather_send, gather_recv, stage, size, sib, cnt)
        for stage, buf in enumerate((normed_full, grad2_full, grad1_full))
    ]
    scatters = [
        Scatter(bufs, scatter_send, scatter_recv, stage, size, sib, cnt) for stage in range(4)
    ]
    piece = depth // pieces
    count = 3 * pieces

    def source(n):
        if early and n == count - 1:
            return outputs_ref, 0
        return weight_grads, (n if n < 2 * pieces else n - 2 * pieces) * piece

    sums = [
        Reduce(
            n, piece, ORDERS[n] if early else tuple(range(bits)), source(n), work, final, sems
        )
        for n in range(count)
    ]
    for load in (*loads[9:], own_tokens, loads[1], own_quarter):
        load.start()
    small_ref[...] = jnp.zeros_like(small_ref)
    late_ref[...] = jnp.zeros_like(late_ref)
    _greet([{"mp": sib}, {"mp": cnt}, {"mp": dia}, *over])
    full_copy(1).start()
    for r in range(CHUNKS):
        token_copy(r, 1).start()
        token_copy(r, 0).start()
    full_copy(0).start()
    for load in (loads[0], loads[3]):
        load.start()

    def project(k, r):
        place = _rows(blocks[k] * own + r * size, size)
        part = _nn(tokens_ref[place, :], up_ref[:, : 3 * width])
        active[place, :width] = (part[:, :width] + qv_bias_ref[:1, :]).astype(bf16)
        active[place, width : 2 * width] = part[:, width : 2 * width].astype(bf16)
        active[place, 2 * width : 3 * width] = (part[:, 2 * width :] + qv_bias_ref[1:, :]).astype(bf16)
        for keep in keeps(k, r):
            keep.start()

    for load in loads[9:]:
        load.wait()
    own_tokens.wait()
    loop(lambda r: project(0, r))
    full_step(1)

    def sib_part(r):
        token_copy(r, 0).wait_recv()
        project(1, r)

    loop(sib_part)
    full_step(2)

    scaled = _head_masks(heads, width, 1.0 / math.sqrt(HEAD))
    plain = _head_masks(heads, width, 1.0)

    def attention(i):
        query_rows = _rows(i * BLOCK, BLOCK)
        acc = own_acc.at[:width, :BLOCK]
        peak_ref[...] = jnp.full_like(peak_ref, 2 * NEG)
        total_ref[...] = jnp.zeros_like(total_ref)
        acc[...] = jnp.zeros_like(acc)

        def meet(j, carry):
            rows = _rows(j * BLOCK, BLOCK)
            bias = _bias(seg_ref, pad_ref, query_rows, rows)
            query, key = active[query_rows, :width], active[rows, width : 2 * width]
            value = active[rows, 2 * width : 3 * width].T
            for h in range(heads):
                scores = _nt(key, query * scaled[h]) + bias
                old = peak_ref[h]
                peak = jnp.maximum(old, jnp.max(scores, axis=0, keepdims=True))
                expo = jnp.exp(scores - peak)
                ratio = jnp.exp(old - peak)
                peak_ref[h] = peak
                total_ref[h] = total_ref[h] * ratio + jnp.sum(expo, axis=0, keepdims=True)
                place = pl.ds(h * HEAD, HEAD)
                acc[place, :] = acc[place, :] * ratio + _nn(
                    value[h * HEAD : (h + 1) * HEAD], expo.astype(bf16)
                )
            return carry

        lax.fori_loop(jnp.maximum(i - 1, 0), jnp.minimum(i + 2, token_blocks), meet, 0)
        for h in range(heads):
            place = pl.ds(h * HEAD, HEAD)
            acc[place, :] = acc[place, :] / total_ref[h]
            lse_ref[h : h + 1, query_rows] = peak_ref[h] + jnp.log(total_ref[h])
        back[query_rows, :width] = acc[...].astype(bf16).T

    half = token_blocks // 2
    chip = me // 2
    per_device = own // BLOCK
    chunks_per = BLOCK // size

    def near(p):
        attention(jnp.where(chip == 0, p, token_blocks - 1 - p))

    _loop(half - 1, near)

    def far_part(r):
        @pl.when(r == 0)
        def _():
            full_step(3)

        @pl.when(r == 2)
        def _():
            for k in range(4, shares + 2):
                full_step(k)

        token_copy(r, 1).wait_recv()
        token_copy(r, 2).start()
        project(2, r)
        token_copy(r, 2).wait_recv()
        project(3, r)

    loop(far_part)
    loads[2].start()
    full_copy(0).wait_recv()
    full_copy(shares + 2).wait_recv()
    own_quarter.wait()
    loads[8].start()

    def tokens_done(r):
        for kind in range(3):
            token_copy(r, kind).wait_send()
        for k in range(4):
            keeps(k, r)[0].wait()

    def far(p):
        k, h = lax.rem(p, 2), p // 2
        attention(jnp.where(k == 0, cnt, dia) * per_device + h)

        @pl.when(p == 0)
        def _():
            loop(tokens_done)

        for c in range(2):

            @pl.when(k == c)
            def _():
                for t in range(chunks_per):
                    trade(h * chunks_per + t, 2 + c).start()

    _loop(2 * per_device, far)
    attention(jnp.where(chip == 0, half - 1, half))
    loop(lambda r: trade(r, 1).start())
    own_context.start()
    save_context = pltpu.make_async_copy(back.at[:, :width], context_hbm, load_sems.at[15])
    save_context.start()

    def add_sum(k, value):
        small_ref[k : k + 1, :] += jnp.sum(value, axis=0, keepdims=True)

    own_context.wait()
    loads[1].wait()
    loads[8].wait()

    def lower_norm(r):
        rows = _rows(r * size, size)
        for k in (1, 2, 3):
            trade(r, k).wait_recv()
        attended = _nn(recv_x[rows, :], grad1_full[:depth, :])
        unit, inverse = _norm(inputs_ref[rows, :].astype(f32) + attended + out_bias)
        unit1[rows, :] = unit
        inverse1[rows, :] = inverse
        gathers[0].slot(r, 0)[...] = (unit * attn_gain + attn_shift).astype(bf16)
        gathers[0].start(r)

    loop(lower_norm)
    loads[4].start()
    save_context.wait()
    for k in range(shares + 3):
        full_copy(k).wait_send()

    def front_done(r):
        for k in range(4):
            keeps(k, r)[1].wait()
        for k in (1, 2, 3):
            trade(r, k).wait_send()
        for load in context_load(r):
            load.start()

    loop(front_done)
    loads[2].wait()
    loads[3].wait()

    def feed_forward(r):
        rows = _rows(r * whole, whole)
        gathers[0].forward(r)
        gathers[0].arrive(r)

        def column(n, carry):
            cols = _rows(n * COLS, COLS)
            upper = _nn(normed_full[rows, :], up_ref[:, cols]) + up_bias_ref[:, cols]
            cdf = 0.5 + 0.5 * lax.erf(upper * math.sqrt(0.5))
            pdf = jnp.exp(upper * upper * -0.5) * (1.0 / math.sqrt(2.0 * math.pi))
            active[rows, cols] = (upper * cdf).astype(bf16)
            back[rows, cols] = (cdf + upper * pdf).astype(bf16)
            return carry

        lax.fori_loop(0, units // COLS, column, 0)
        scatters[1].project(r, lambda cols: _nn(active[rows, :], down_ref[:, cols]))
        scatters[1].finish(r)

    loop(feed_forward)
    loads[4].wait()

    def upper_norm(r):
        rows = _rows(r * size, size)
        normed = unit1[rows, :] * attn_gain + attn_shift
        unit, inverse = _norm(normed + scatters[1].result(r) + down_bias)
        cotangent = inputs_ref[rows, :].astype(f32)
        outputs_ref[rows, :] = (unit * ffn_gain + ffn_shift).astype(bf16)
        store(0, r).start()
        grad = _norm_back(cotangent * ffn_gain, unit, inverse)
        gathers[1].slot(r, 0)[...] = grad.astype(bf16)
        gathers[1].start(r)
        grad_own[rows, :] = grad
        add_sum(3, grad)
        add_sum(4, cotangent * unit)
        add_sum(5, cotangent)

    loop(upper_norm)

    def take(r):
        gathers[1].forward(r)
        gathers[1].arrive(r)
        scatters[1].sent(r)

    def feed_back(r):
        rows = _rows(r * whole, whole)

        def column(n, carry):
            cols = _rows(n * COLS, COLS)
            incoming = _nt(grad2_full[rows, :], down_ref[cols, :])
            upper_back = (back[rows, cols].astype(f32) * incoming).astype(bf16)
            back[rows, cols] = upper_back
            late_ref[1:2, cols] += jnp.sum(upper_back.astype(f32), axis=0, keepdims=True)
            return carry

        lax.fori_loop(0, units // COLS, column, 0)
        scatters[2].project(r, lambda cols: _nt(back[rows, :], up_ref[cols, :]))
        scatters[2].finish(r)

    def take_back(r):
        take(r)
        feed_back(r)

    _loop(CHUNKS - 1, take_back)
    take(CHUNKS - 1)

    def weights(k, p):
        cols = _rows(p * (depth // CHUNKS), depth // CHUNKS)
        place = _rows(k * depth + p * (depth // CHUNKS), depth // CHUNKS)
        if k == 0:
            weight_grads[place, :] = _tn(active[:, cols], grad2_full[...]).astype(bf16)
        else:
            weight_grads[place, :] = _tn(normed_full[:, cols], back[...]).astype(bf16)

    def out_weights():
        target = outputs_ref.at[:width] if early else weight_grads.at[3 * width : 4 * width]
        target[...] = _tn(context_ref[...], grad1_full[...]).astype(bf16)

    def in_weights(j):
        weight_grads[_rows(j * width, width), :] = _tn(
            grads[:, j * width : (j + 1) * width], normed_full[...]
        ).astype(bf16)

    def move(n, k):
        if k == 0 and n < 2 * pieces:
            weights(n // pieces, n % pieces)
        elif k == 0 and n == count - 1:
            out_weights()
        elif k == 0:
            in_weights(n - 2 * pieces)
        sums[n].step(k)
        if k == 2 * bits:
            store_final(n).start()

    def store_final(n):
        rows = _rows(n * piece, piece)
        return pltpu.make_async_copy(final.at[rows], final_hbm.at[rows], final_sems.at[n])

    def slot(i, first, number):
        for at in range(first, first + number) if early else ():
            if at in PLAN:

                @pl.when(i == at - first)
                def _():
                    for n, k in PLAN[at]:
                        move(n, k)

    if early:
        for n, k in PLAN[-1]:
            move(n, k)
    feed_back(CHUNKS - 1)
    for load in loads[9:]:
        load.start()

    def lower_back(r):
        slot(r, 0, CHUNKS)
        if not early:
            for k in range(2):

                @pl.when(r // 2 == k)
                def _():
                    for h in range(2):
                        weights(k, 2 * r - 4 * k + h)

                @pl.when(r == 2 * k + 1)
                def _():
                    sums[k].step(0)

        rows = _rows(r * size, size)
        incoming = grad_own[rows, :] + scatters[2].result(r)
        unit = unit1[rows, :]
        grad = _norm_back(incoming * attn_gain, unit, inverse1[rows, :])
        gathers[2].slot(r, 0)[...] = grad.astype(bf16)
        gathers[2].start(r)
        grad_own[rows, :] = grad
        add_sum(0, grad)
        add_sum(1, incoming * unit)
        add_sum(2, incoming)

    loop(lower_back)
    gathers_done = lambda r: [gather.sent(r) for gather in gathers[:2]]
    loop(gathers_done)
    for load in loads[5:8]:
        load.start()

    loads[0].wait()
    loop(lambda r: [load.wait() for load in context_load(r)])

    def context_back(r):
        slot(r, CHUNKS, CHUNKS)
        rows = _rows(r * whole, whole)
        gathers[2].forward(r)
        gathers[2].arrive(r)
        scatters[2].sent(r)
        grad = _nt(grad1_full[rows, :], out_proj_ref[...]).astype(bf16)
        for k, b in enumerate(blocks):
            part = _rows(b * own + r * size, size)
            back[part, :width] = grad[k * size : (k + 1) * size]

    loop(context_back)
    loop(lambda r: gathers[2].sent(r))
    loop(lambda r: store(0, r).wait())
    for load in loads[5:8]:
        load.wait()

    targets = [{"mp": sib}, {"mp": cnt}, *over]

    def small_step(k):
        return _remote(
            small_ref.at[:8], small_recv.at[k], small_sems.at[0, k], small_sems.at[1, k], targets[k]
        )

    def small_end(k):
        small_step(k).wait()
        small_ref[:8, :] += small_recv[k]

    def late_step(k):
        at = len(targets) + k
        return _remote(late_ref, late_recv.at[k], small_sems.at[0, at], small_sems.at[1, at], over[k])

    def late_end(k):
        late_step(k).wait()
        late_ref[...] += late_recv[k]

    def small_turn(k):
        if k:
            small_end(k - 1)
        if k < len(targets):
            small_step(k).start()

    keys_acc, values_acc, query_acc = unit1, other_acc, own_acc.at[:width, :BLOCK]
    keys_acc[...] = jnp.zeros_like(keys_acc)
    values_acc[...] = jnp.zeros_like(values_acc)
    grads = grad2_full
    per = own // BLOCK

    def spot(j):
        return _rows(lax.rem(j, per) * BLOCK, BLOCK), _rows(j // per * width, width)

    def attend(t):
        i, turn = t // 3, lax.rem(t, 3)
        for k in range(len(targets) + 1):

            @pl.when(t == SMALL_TURNS[k])
            def _():
                small_turn(k)

        slot(t, 2 * CHUNKS, 3 * token_blocks)
        query_rows = _rows(i * BLOCK, BLOCK)

        @pl.when(turn == 0)
        def _():
            product = (
                back[query_rows, :width].astype(f32) * back[query_rows, width : 2 * width].astype(f32)
            ).T
            for h in range(heads):
                dots_ref[h : h + 1, :] = jnp.sum(
                    product[h * HEAD : (h + 1) * HEAD], axis=0, keepdims=True
                )
            query_acc[...] = jnp.zeros_like(query_acc)

        @pl.when((i + turn >= 1) & (i + turn <= token_blocks))
        def _():
            j = jnp.clip(i + turn - 1, 0, token_blocks - 1)
            query, grad = active[query_rows, :width], back[query_rows, :width]
            rows = _rows(j * BLOCK, BLOCK)
            bias = _bias(seg_ref, pad_ref, query_rows, rows)
            key, value = active[rows, width : 2 * width], active[rows, 2 * width : 3 * width]
            key_rows = (key * (1.0 / math.sqrt(HEAD))).astype(bf16).T
            key_add = jnp.zeros((BLOCK, width), f32)
            value_add = jnp.zeros((BLOCK, width), f32)
            for h in range(heads):
                query_h, grad_h = query * scaled[h], grad * plain[h]
                scores = _nt(key, query_h) + bias
                prob = jnp.exp(scores - lse_ref[h : h + 1, query_rows])
                score_grad = (prob * (_nt(value, grad_h) - dots_ref[h : h + 1, :])).astype(bf16)
                key_add = key_add + _nn(score_grad, query_h)
                value_add = value_add + _nn(prob.astype(bf16), grad_h)
                query_acc[pl.ds(h * HEAD, HEAD), :] += _nn(key_rows[h * HEAD : (h + 1) * HEAD], score_grad)
            keys_acc[spot(j)] += key_add
            values_acc[spot(j)] += value_add

        @pl.when(turn == 2)
        def _():
            grads[query_rows, :width] = query_acc[...].astype(bf16).T

    _loop(3 * token_blocks, attend)

    def keep(j):
        rows = _rows(j * BLOCK, BLOCK)
        grads[rows, width : 2 * width] = keys_acc[spot(j)].astype(bf16)
        grads[rows, 2 * width : 3 * width] = values_acc[spot(j)].astype(bf16)

    _loop(token_blocks, keep)

    if not early:
        for n in range(2):
            sums[n].step(1)
        out_weights()
        in_weights(0)
        in_weights(1)
        in_weights(2)
    for n in range(2 * pieces):
        sums[n].halve(0).wait_send()

    def partial_rows(r):
        chunk = jnp.concatenate(
            [grads[_rows(b * own + r * size, size), : 3 * width] for b in blocks], axis=0
        )

        def tile(cols):
            return _nt(chunk, up_ref[cols, : 3 * width])

        scatters[3].project(r, tile)
        scatters[3].finish(r)

    def finish(r):
        rows = _rows(r * size, size)
        outputs_ref[rows, :] = (grad_own[rows, :] + scatters[3].result(r)).astype(bf16)
        store(1, r).start()
        scatters[3].sent(r)

    def bias(j):
        return jnp.sum(grads[:, j * width : (j + 1) * width].astype(f32), axis=0, keepdims=True)

    for load in loads[9:]:
        load.wait()
    late_ref[:1, :width] = bias(0)
    late_ref[:1, width : 2 * width] = bias(2)
    late_step(0).start()
    if early:
        tail = PLAN[2 * CHUNKS + 3 * token_blocks]
    else:
        tail = [(2, 0)] + [(-1, r) for r in range(CHUNKS)]
        tail += [(n, k) for k in range(1, 2 * bits + 1) for n in range(3) if n == 2 or k > 1]
    last = max(k for k, (n, _) in enumerate(tail) if n < 0)
    turns = [(len(tail) - 1) * (k + 2) // (bits + 1) for k in range(bits)]
    for at, (n, k) in enumerate(tail):
        if n < 0:
            partial_rows(k)
        elif k or early:
            move(n, k)
        else:
            sums[n].step(0)
        for turn in [turn for turn, place in enumerate(turns) if place == at]:
            late_end(turn)
            if turn + 1 < bits:
                late_step(turn + 1).start()
        if at == last + 3 * (len(tail) - 1 - last) // 4:
            if early:
                sums[-1].halve(0).wait_send()
            loop(finish)
    for n in range(count):
        sums[n].sent()
        if n >= 2 * pieces and not (early and n == count - 1):
            sums[n].halve(0).wait_send()
    small_ref[8:10, :] = late_ref[:2, :]
    loop(lambda r: store(1, r).wait())
    for n in range(3 * pieces):
        store_final(n).wait()


def main_layer(mesh, arrays, small_arrays):
    f32, bf16 = jnp.float32, jnp.bfloat16
    inputs, in_proj, out_proj, up_proj, down_proj, _ = arrays
    own, depth = inputs.shape
    units, width = up_proj.shape[1], out_proj.shape[0]
    whole, half = 4 * own, depth // 2
    bits = mesh.shape["dp"].bit_length() - 1
    pieces = CHUNKS if (depth // CHUNKS >> bits) >= 16 else 1
    outs = [
        ((own, depth), bf16),
        ((own, depth), bf16),
        ((3 * depth, depth), bf16),
        ((whole, depth), bf16),
        ((whole, 3 * width), bf16),
        ((4 * width, depth), bf16),
        ((whole, width), bf16),
        ((16, depth), f32),
    ]
    return pl.pallas_call(
        partial(main_kernel, bits, pieces),
        out_shape=[jax.ShapeDtypeStruct(*out) for out in outs],
        in_specs=[REMOTE] * 6 + [LOCAL] * 10,
        out_specs=[REMOTE] * 7 + [LOCAL],
        scratch_shapes=[
            pltpu.VMEM((whole, width), bf16),
            *[pltpu.VMEM(array.shape, bf16) for array in (out_proj, inputs, up_proj, down_proj)],
            pltpu.VMEM((2 * depth, depth), bf16),
            pltpu.VMEM((whole, depth), bf16),
            pltpu.VMEM((whole, depth), bf16),
            pltpu.VMEM((whole, depth), bf16),
            pltpu.VMEM((whole, units), bf16),
            pltpu.VMEM((whole, units), bf16),
            pltpu.VMEM((own, depth), f32),
            pltpu.VMEM((own, 1), f32),
            pltpu.VMEM((own, depth), f32),
            pltpu.VMEM((8, BLOCK), f32),
            pltpu.VMEM((8, whole), f32),
            pltpu.VMEM((width // HEAD, 1, BLOCK), f32),
            pltpu.VMEM((width // HEAD, 1, BLOCK), f32),
            *_scatter_scratch(own, depth),
            pltpu.VMEM((3 * pieces * (depth // pieces - (depth // pieces >> bits)), depth), bf16),
            pltpu.VMEM((3 * depth, depth), bf16),
            pltpu.VMEM((2 + bits, 8, depth), f32),
            pltpu.VMEM((8, depth), f32),
            pltpu.VMEM((bits, 8, depth), f32),
            pltpu.SemaphoreType.DMA((16,)),
            pltpu.SemaphoreType.DMA((4, CHUNKS)),
            pltpu.SemaphoreType.DMA((2, 3, CHUNKS)),
            pltpu.SemaphoreType.DMA((2, CHUNKS)),
            pltpu.SemaphoreType.DMA((3 * pieces,)),
            pltpu.SemaphoreType.DMA((3, 3, CHUNKS)),
            pltpu.SemaphoreType.DMA((3, 3, CHUNKS)),
            pltpu.SemaphoreType.DMA((4, 3, CHUNKS)),
            pltpu.SemaphoreType.DMA((4, 3, CHUNKS)),
            pltpu.SemaphoreType.DMA((2, 3 * pieces, 2 * bits)),
            pltpu.SemaphoreType.DMA((2, 2 + 2 * bits)),
            pltpu.SemaphoreType.DMA((2, 3, CHUNKS)),
            pltpu.SemaphoreType.DMA((2, 4, CHUNKS)),
            pltpu.SemaphoreType.DMA((2, 3 + bits)),
        ],
        compiler_params=pltpu.CompilerParams(
            collective_id=1, has_side_effects=True, vmem_limit_bytes=63 * 2**20
        ),
        name="main_layer",
    )(*arrays, *small_arrays)


def unpack_kernel(
    width, final_ref, attn_ref, small_ref, outputs_ref, inputs_grad_ref, down_ref, up_ref, in_ref, out_ref,
    qv_ref, up_bias_ref, *refs,
):
    f32 = jnp.float32
    vectors, outputs_out, inputs_grad_out = refs[:6], refs[6], refs[7]
    down_ref[...] = final_ref[0].astype(f32)
    up_ref[...] = final_ref[1].astype(f32)
    for j in range(3):
        in_ref[j] = attn_ref[j * width : (j + 1) * width, :].astype(f32).T
    out_ref[...] = attn_ref[3 * width :, :].astype(f32)
    outputs_out[...] = outputs_ref[...]
    inputs_grad_out[...] = inputs_grad_ref[...]
    for k, vector in enumerate(vectors):
        vector[...] = small_ref[k : k + 1, :]
    up_bias_ref[...] = small_ref[9:10, :]
    for k in range(2):
        qv_ref[k : k + 1, :] = small_ref[8:9, k * width : (k + 1) * width]


def unpack(final, small, outputs, inputs_grad, width):
    f32 = jnp.float32
    own, depth = outputs.shape
    steps = depth // UNPACK
    part = own // steps
    matrix = pl.BlockSpec((UNPACK, depth), lambda i: (i, 0))
    tokens = pl.BlockSpec((part, depth), lambda i: (i, 0))
    vector = pl.BlockSpec((1, depth), lambda i: (0, 0))
    shapes = [
        ((depth, depth), f32, matrix),
        ((depth, depth), f32, matrix),
        ((3, depth, width), f32, pl.BlockSpec((3, UNPACK, width), lambda i: (0, i, 0))),
        ((width, depth), f32, pl.BlockSpec((width, UNPACK), lambda i: (0, i))),
        ((2, width), f32, pl.BlockSpec((2, width), lambda i: (0, 0))),
        *[((1, depth), f32, vector)] * 7,
        ((own, depth), jnp.bfloat16, tokens),
        ((own, depth), jnp.bfloat16, tokens),
    ]
    return pl.pallas_call(
        partial(unpack_kernel, width),
        grid=(steps,),
        in_specs=[
            pl.BlockSpec((2, UNPACK, depth), lambda i: (0, i, 0)),
            pl.BlockSpec((depth, UNPACK), lambda i: (2, i)),
            pl.BlockSpec((16, depth), lambda i: (0, 0)),
            tokens,
            tokens,
        ],
        out_specs=[spec for _, _, spec in shapes],
        out_shape=[jax.ShapeDtypeStruct(shape, dtype) for shape, dtype, _ in shapes],
        compiler_params=pltpu.CompilerParams(vmem_limit_bytes=VMEM),
        name="unpack_gradients",
    )(final.reshape(3, depth, depth), final, small, outputs, inputs_grad)


def shards(
    mesh,
    inputs,
    in_proj,
    qv_bias,
    out_proj,
    out_bias,
    attn_gain,
    attn_shift,
    up_proj,
    up_bias,
    down_proj,
    down_bias,
    ffn_gain,
    ffn_shift,
    segments,
    padding,
    cotangent,
):
    places, real = segment_places(segments, padding)
    vectors = [v[None] for v in (out_bias, attn_gain, attn_shift, down_bias, ffn_gain, ffn_shift)]
    outputs, inputs_grad, final, _, _, _, _, small = main_layer(
        mesh,
        (inputs, in_proj, out_proj, up_proj, down_proj, cotangent),
        (qv_bias, places, real, up_bias[None], *vectors),
    )
    down_grad, up_grad, in_grad, out_grad, qv_grad, up_bias_grad, *vectors, outputs, inputs_grad = unpack(
        final, small, outputs, inputs_grad, in_proj.shape[2]
    )
    vectors = [v[0] for v in vectors]
    return (
        outputs,
        inputs_grad,
        in_grad,
        qv_grad,
        out_grad,
        *vectors[:3],
        up_grad,
        up_bias_grad[0],
        down_grad,
        *vectors[3:],
    )


def solution(mesh):
    return jax.shard_map(
        partial(shards, mesh),
        mesh=mesh,
        in_specs=(
            P(("dp", "mp"), None),
            P(None, None, "mp"),
            P(None, "mp"),
            P("mp", None),
            P(),
            P(),
            P(),
            P(None, "mp"),
            P("mp"),
            P("mp", None),
            P(),
            P(),
            P(),
            P("dp", None),
            P("dp", None),
            P(("dp", "mp"), None),
        ),
        out_specs=(
            P(("dp", "mp"), None),
            P(("dp", "mp"), None),
            P(None, None, "mp"),
            P(None, "mp"),
            P("mp", None),
            P(),
            P(),
            P(),
            P(None, "mp"),
            P("mp"),
            P("mp", None),
            P(),
            P(),
            P(),
        ),
        check_vma=False,
    )
```

```python
from functools import partial
import math

import jax
import jax.numpy as jnp
from jax import lax
from jax.experimental import pallas as pl
from jax.experimental.pallas import tpu as pltpu
from jax.sharding import PartitionSpec as P

HEAD = 64
BLOCK = 256
CHUNKS = 4
SMALL_TURNS = (0, 1, 3, 10, 16, 23, 23, 23, 23)
ORDERS = (
    (0, 1, 2),
    (1, 0, 2),
    (0, 1, 2),
    (0, 1, 2),
    (0, 1, 2),
    (0, 1, 2),
    (0, 1, 2),
    (0, 1, 2),
    (0, 1, 2),
    (0, 1, 2),
    (1, 0, 2),
    (0, 1, 2),
)
PLAN = {
    -1: ((3, 0), (1, 0), (2, 0), (0, 0),),
    0: ((5, 0), (1, 1), (3, 1), (4, 0),),
    1: ((7, 0), (6, 0), (2, 1),),
    3: ((3, 2),),
    4: ((0, 1), (2, 2), (3, 3),),
    5: ((5, 1), (0, 2), (2, 3), (1, 2),),
    6: ((3, 4), (5, 2), (4, 1), (0, 3),),
    7: ((2, 4), (1, 3), (7, 1), (3, 5),),
    8: ((11, 0), (4, 2), (5, 3),),
    9: ((6, 1),),
    10: ((0, 4),),
    12: ((2, 5),),
    14: ((1, 4),),
    16: ((7, 2),),
    17: ((4, 3),),
    19: ((11, 1), (5, 4),),
    21: ((6, 2),),
    24: ((0, 5),),
    25: ((7, 3),),
    26: ((4, 4),),
    27: ((1, 5),),
    29: ((11, 2),),
    31: ((5, 5),),
    32: ((10, 0), (6, 3), (7, 4), (0, 6), (2, 6), (3, 6), (8, 0), (4, 5), (9, 0), (-1, 0), (1, 6), (5, 6), (-1, 1), (11, 3), (-1, 2), (8, 1), (-1, 3), (10, 1), (6, 4), (4, 6), (7, 5), (11, 4), (8, 2), (9, 1), (6, 5), (10, 2), (11, 5), (8, 3), (7, 6), (9, 2), (10, 3), (8, 4), (6, 6), (9, 3), (11, 6), (10, 4), (8, 5), (9, 4), (9, 5), (10, 5), (8, 6), (10, 6), (9, 6),),
}
COLS = 256
PART = 256
UNPACK = 512
VMEM = 60 * 2**20
REMOTE = pl.BlockSpec(memory_space=pl.ANY)
LOCAL = pl.BlockSpec(memory_space=pltpu.VMEM)
MESH = pl.DeviceIdType.MESH


EPSILON = 1e-05


NEG = -1e30


def _head_masks(heads, width, value):
    lane = lax.broadcasted_iota(jnp.int32, (1, width), 1) // HEAD
    return [jnp.where(lane == h, value, 0.0).astype(jnp.bfloat16) for h in range(heads)]


def _nt(a, b):
    return lax.dot_general(a, b, (((1,), (1,)), ((), ())), preferred_element_type=jnp.float32)


def _tn(a, b):
    return lax.dot_general(a, b, (((0,), (0,)), ((), ())), preferred_element_type=jnp.float32)


def _nn(a, b):
    return jnp.dot(a, b, preferred_element_type=jnp.float32)


def _column(row):
    wide = jnp.broadcast_to(row.astype(jnp.float32), (128, row.shape[1])).T.astype(jnp.int32)
    return jnp.concatenate([wide] * (BLOCK // 128), axis=1)


def _bias(seg_ref, pad_ref, query_rows, key_rows):
    seg_q, pad_q = seg_ref[:, query_rows], pad_ref[:, query_rows]
    seg_k, pad_k = _column(seg_ref[:, key_rows]), _column(pad_ref[:, key_rows])
    allowed = (seg_k == seg_q) & ((pad_k > 0) | (pad_q == 0))
    return jnp.where(allowed, 0.0, NEG).astype(jnp.float32)


def _loop(count, body):
    def step(i, carry):
        body(i)
        return carry

    lax.fori_loop(0, count, step, 0)


def segment_places(segments, padding):
    row_count, seq_len = segments.shape
    if row_count > 1:
        segments = segments + jnp.arange(row_count, dtype=jnp.int32)[:, None] * (seq_len + 1)
    return segments.reshape(1, -1), padding.reshape(1, -1)


def _partners():
    me = lax.axis_index("mp")
    core = lax.rem(me, 2)
    sib = me + 1 - 2 * core
    cnt = lax.rem(me + 2, 4)
    dia = lax.rem(cnt + 1, 2) + cnt - lax.rem(cnt, 2)
    return me, sib, cnt, dia


def _remote(src, dst, send, recv, target):
    return pltpu.make_async_remote_copy(
        src_ref=src, dst_ref=dst, send_sem=send, recv_sem=recv, device_id=target, device_id_type=MESH
    )


def _greet(targets):
    barrier = pltpu.get_barrier_semaphore()
    for target in targets:
        pl.semaphore_signal(barrier, inc=1, device_id=target, device_id_type=MESH)
    pl.semaphore_wait(barrier, len(targets))


def _rows(start, size):
    return pl.ds(pl.multiple_of(start, size), size)


def _part(start, size):
    return pl.ds(pl.multiple_of(start, 16), size)


class Gather:
    def __init__(self, buffer, send, recv, stage, size, sib, cnt):
        self.buffer, self.send, self.recv = buffer, send, recv
        self.stage, self.size, self.sib, self.cnt = stage, size, sib, cnt

    def slot(self, r, k):
        return self.buffer.at[_rows((r * 4 + k) * self.size, self.size)]

    def copy(self, r, kind):
        src, dst, target = ((0, 1, self.sib), (0, 2, self.cnt), (2, 3, self.sib))[kind]
        return _remote(
            self.slot(r, src),
            self.slot(r, dst),
            self.send.at[self.stage, kind, r],
            self.recv.at[self.stage, kind, r],
            {"mp": target},
        )

    def start(self, r):
        self.copy(r, 1).start()
        self.copy(r, 0).start()

    def forward(self, r):
        self.copy(r, 1).wait_recv()
        self.copy(r, 2).start()

    def arrive(self, r):
        self.copy(r, 0).wait_recv()
        self.copy(r, 2).wait_recv()

    def sent(self, r):
        for kind in range(3):
            self.copy(r, kind).wait_send()


class Scatter:
    def __init__(self, bufs, send, recv, stage, size, sib, cnt):
        self.own, self.other, self.stage_sib, self.stage_x, self.recv_sib, self.recv_x = bufs
        self.send, self.recv = send, recv
        self.stage, self.size, self.sib, self.cnt = stage, size, sib, cnt

    def copy(self, r, kind):
        rows = _rows(r * self.size, self.size)
        src, dst, target = (
            (self.stage_sib.at[0, rows], self.recv_sib.at[0, rows], self.sib),
            (self.stage_sib.at[1, rows], self.recv_sib.at[1, rows], self.sib),
            (self.stage_x.at[rows], self.recv_x.at[rows], self.cnt),
        )[kind]
        return _remote(
            src, dst, self.send.at[self.stage, kind, r], self.recv.at[self.stage, kind, r], {"mp": target}
        )

    def sent(self, r):
        for kind in range(3):
            self.copy(r, kind).wait_send()

    def project(self, r, tile):
        size = self.size
        rows = _rows(r * size, size)

        def column(n, carry):
            cols = _rows(n * COLS, COLS)
            part = tile(cols)
            self.own[rows, cols] = part[:size]
            self.stage_sib[1, rows, cols] = part[size : 2 * size].astype(jnp.bfloat16)
            self.other[rows, cols] = part[2 * size : 3 * size]
            self.stage_sib[0, rows, cols] = part[3 * size :].astype(jnp.bfloat16)
            return carry

        lax.fori_loop(0, self.own.shape[1] // COLS, column, 0)
        self.copy(r, 0).start()
        self.copy(r, 1).start()

    def finish(self, r):
        rows = _rows(r * self.size, self.size)
        self.copy(r, 0).wait_recv()
        self.stage_x[rows, :] = (
            self.other[rows, :] + self.recv_sib[0, rows, :].astype(jnp.float32)
        ).astype(jnp.bfloat16)
        self.copy(r, 2).start()
        self.copy(r, 1).wait_recv()
        self.own[rows, :] += self.recv_sib[1, rows, :].astype(jnp.float32)

    def result(self, r):
        rows = _rows(r * self.size, self.size)
        self.copy(r, 2).wait_recv()
        return self.own[rows, :] + self.recv_x[rows, :].astype(jnp.float32)


def _scatter_scratch(own, width):
    f32, bf16 = jnp.float32, jnp.bfloat16
    return [
        pltpu.VMEM((own, width), f32),
        pltpu.VMEM((own, width), f32),
        pltpu.VMEM((2, own, width), bf16),
        pltpu.VMEM((own, width), bf16),
        pltpu.VMEM((2, own, width), bf16),
        pltpu.VMEM((own, width), bf16),
    ]


def _norm(summed):
    center = summed - jnp.mean(summed, axis=-1, keepdims=True)
    variance = jnp.mean(center * center, axis=-1, keepdims=True)
    inverse = lax.rsqrt(variance + EPSILON)
    return center * inverse, inverse


def _norm_back(scaled, unit, inverse):
    return inverse * (
        scaled
        - jnp.mean(scaled, axis=-1, keepdims=True)
        - unit * jnp.mean(scaled * unit, axis=-1, keepdims=True)
    )


class Reduce:
    def __init__(self, n, rows, order, source, work, final, sems):
        self.n, self.rows, self.source, self.work, self.final, self.sems = n, rows, source, work, final, sems
        self.steps = len(order)
        dp = lax.axis_index("dp")
        self.bit = [lax.rem(dp // (1 << b), 2) for b in order]
        self.peer = [{"dp": dp + (1 << b) * (1 - 2 * bit)} for b, bit in zip(order, self.bit)]

    def size(self, s):
        return self.rows >> s

    def start(self, s):
        first = self.n * self.rows
        for t in range(s):
            first = first + self.bit[t] * self.size(t + 1)
        return first

    def held(self, s):
        if s == 0:
            return self.source
        stride = self.rows - self.size(self.steps)
        return self.work, self.n * stride + self.rows - 2 * self.size(s)

    def halve(self, s):
        ref, first = self.held(s)
        half = self.size(s + 1)
        there, place = self.held(s + 1)
        return _remote(
            ref.at[_part(first + (1 - self.bit[s]) * half, half)],
            there.at[_part(place, half)],
            self.sems.at[0, self.n, s],
            self.sems.at[1, self.n, s],
            self.peer[s],
        )

    def double(self, s):
        block = self.final.at[_rows(self.start(s + 1), self.size(s + 1))]
        k = 2 * self.steps - 1 - s
        return _remote(block, block, self.sems.at[0, self.n, k], self.sems.at[1, self.n, k], self.peer[s])

    def step(self, k):
        steps = self.steps
        if 0 < k <= steps:
            s = k - 1
            half = self.size(s + 1)
            self.halve(s).wait_recv()
            ref, first = self.held(s)
            there, place = self.held(s + 1)
            total = there[_part(place, half), :].astype(jnp.float32) + ref[
                _part(first + self.bit[s] * half, half), :
            ].astype(jnp.float32)
            if k < steps:
                there[_part(place, half), :] = total.astype(jnp.bfloat16)
            else:
                self.final[_rows(self.start(steps), half), :] = total.astype(jnp.bfloat16)
        if k > steps:
            self.double(2 * steps - k).wait_recv()
        if k < steps:
            self.halve(k).start()
        elif k < 2 * steps:
            self.double(2 * steps - 1 - k).start()

    def sent(self):
        for s in range(self.steps):
            if s:
                self.halve(s).wait_send()
            self.double(s).wait_send()


def main_kernel(bits, pieces, *refs):
    f32, bf16 = jnp.float32, jnp.bfloat16
    (inputs_hbm, in_proj_hbm, out_proj_hbm, up_hbm, down_hbm, cotangent_hbm,
     *refs) = refs
    small_hbm, refs = refs[:10], refs[10:]
    (outputs_hbm, inputs_grad_hbm, final_hbm, tokens_hbm, qkv_hbm, full_hbm, context_hbm, small_ref,
     context_ref, out_proj_ref, inputs_ref, up_ref, down_ref,
     weight_grads, normed_full, grad2_full, grad1_full, active, back, unit1, inverse1, grad_own, dots_ref,
     lse_ref, peak_ref, total_ref,
     own_acc, other_acc, stage_sib, stage_x, recv_sib, recv_x, work, final, small_recv, late_ref, late_recv,
     load_sems, block_sems, trade_sems, store_sems, final_sems, gather_send, gather_recv, scatter_send, scatter_recv,
     sems, small_sems, token_sems, keep_sems, full_sems, operand_sems, *small_operands) = refs
    qv_bias_ref, seg_ref, pad_ref, up_bias_ref, *vector_refs = small_operands
    small_loads = [
        pltpu.make_async_copy(source, target, operand_sems.at[k])
        for k, (source, target) in enumerate(zip(small_hbm, small_operands))
    ]
    outputs_ref = inputs_ref
    me, sib, cnt, dia = _partners()
    own, depth = inputs_ref.shape
    units, width = up_ref.shape[1], out_proj_ref.shape[0]
    length = 4 * own
    heads, token_blocks = width // HEAD, length // BLOCK
    size, whole = own // CHUNKS, length // CHUNKS
    blocks = (me, sib, cnt, dia)
    early = pieces == CHUNKS
    loop = partial(_loop, CHUNKS)

    def context_load(r):
        return [
            pltpu.make_async_copy(
                context_hbm.at[_rows(b * own + r * size, size)],
                context_ref.at[_rows((r * 4 + k) * size, size)],
                block_sems.at[k, r],
            )
            for k, b in enumerate(blocks)
        ]

    loads = [
        pltpu.make_async_copy(source, target, load_sems.at[k])
        for k, (source, target) in enumerate(
            (
                (out_proj_hbm, out_proj_ref),
                (inputs_hbm, inputs_ref),
                (up_hbm, up_ref),
                (down_hbm, down_ref),
                (cotangent_hbm, inputs_ref),
                (qkv_hbm, active.at[:, : 3 * width]),
                (tokens_hbm, normed_full),
                (context_hbm, back.at[:, width : 2 * width]),
                (full_hbm, grad1_full.at[:depth]),
                *[(in_proj_hbm.at[j], up_ref.at[:, j * width : (j + 1) * width]) for j in range(3)],
            )
        )
    ]
    own_context = pltpu.make_async_copy(
        back.at[_rows(me * own, own), :width], recv_x.at[:, _rows(me * width, width)], load_sems.at[12]
    )

    def trade(r, k):
        return _remote(
            back.at[_rows(blocks[k] * own + r * size, size), :width],
            recv_x.at[_rows(r * size, size), _rows(me * width, width)],
            trade_sems.at[0, k - 1, r],
            trade_sems.at[1, k - 1, r],
            {"mp": blocks[k]},
        )

    tokens_ref = normed_full

    def token_copy(r, kind):
        here = inputs_hbm.at[_rows(r * size, size)]
        place = _rows((cnt if kind == 2 else me) * own + r * size, size)
        src, target = ((here, sib), (here, cnt), (tokens_ref.at[place], sib))[kind]
        return _remote(
            src, tokens_ref.at[place], token_sems.at[0, kind, r], token_sems.at[1, kind, r], {"mp": target}
        )

    def keeps(k, r):
        place = _rows(blocks[k] * own + r * size, size)
        return [
            pltpu.make_async_copy(tokens_ref.at[place], tokens_hbm.at[place], keep_sems.at[0, k, r]),
            pltpu.make_async_copy(
                active.at[place, : 3 * width], qkv_hbm.at[place], keep_sems.at[1, k, r]
            ),
        ]

    dp = lax.axis_index("dp")
    shares = min(bits, (width // 16).bit_length() - 1)
    bit = [lax.rem(dp // (1 << b), 2) for b in range(bits)]
    over = [{"dp": dp + (1 << b) * (1 - 2 * bit[b])} for b in range(bits)]

    def span(block, s):
        first = block * width
        for t in range(s):
            first = first + bit[t] * (width >> (t + 1))
        return full_hbm.at[_part(first, width >> s)]

    def full_copy(k):
        if k == 0:
            pair = out_proj_hbm, span(me, 0), {"mp": sib}
        elif k == 1:
            first = sum(bit[t] * (width >> (t + 1)) for t in range(shares))
            pair = out_proj_hbm.at[_part(first, width >> shares)], span(me, shares), {"mp": cnt}
        elif k < 2 + shares:
            block = span(cnt, shares - (k - 2))
            pair = block, block, over[shares - 1 - (k - 2)]
        else:
            block = span(cnt, 0)
            pair = block, block, {"mp": sib}
        return _remote(pair[0], pair[1], full_sems.at[0, k], full_sems.at[1, k], pair[2])

    own_quarter = pltpu.make_async_copy(out_proj_hbm, span(me, 0), load_sems.at[13])
    own_tokens = pltpu.make_async_copy(inputs_hbm, tokens_ref.at[_rows(me * own, own)], load_sems.at[14])

    def full_step(k):
        full_copy(k).wait_recv()
        full_copy(k + 1).start()

    def store(k, r):
        rows = _rows(r * size, size)
        target = (outputs_hbm, inputs_grad_hbm)[k]
        return pltpu.make_async_copy(outputs_ref.at[rows], target.at[rows], store_sems.at[k, r])

    bufs = (own_acc, other_acc, stage_sib, stage_x, recv_sib, recv_x)
    gathers = [
        Gather(buf, gather_send, gather_recv, stage, size, sib, cnt)
        for stage, buf in enumerate((normed_full, grad2_full, grad1_full))
    ]
    scatters = [
        Scatter(bufs, scatter_send, scatter_recv, stage, size, sib, cnt) for stage in range(4)
    ]
    piece = depth // pieces
    count = 3 * pieces

    def source(n):
        if early and n == count - 1:
            return outputs_ref, 0
        return weight_grads, (n if n < 2 * pieces else n - 2 * pieces) * piece

    sums = [
        Reduce(
            n, piece, ORDERS[n] if early else tuple(range(bits)), source(n), work, final, sems
        )
        for n in range(count)
    ]
    for load in (*loads[9:], own_tokens, *small_loads, loads[1], own_quarter):
        load.start()
    small_ref[...] = jnp.zeros_like(small_ref)
    late_ref[...] = jnp.zeros_like(late_ref)
    _greet([{"mp": sib}, {"mp": cnt}, {"mp": dia}, *over])
    full_copy(1).start()
    for r in range(CHUNKS):
        token_copy(r, 1).start()
        token_copy(r, 0).start()
    full_copy(0).start()
    for load in (loads[0], loads[3]):
        load.start()

    def project(ks, r, number):
        rows = number * size
        places = [_part(blocks[k] * own + r * size, rows) for k in ks]
        chunk = jnp.concatenate([tokens_ref[place, :] for place in places], axis=0)
        for j in range(3):
            part = _nn(chunk, up_ref[:, j * width : (j + 1) * width])
            if j != 1:
                part = part + qv_bias_ref[j // 2 : j // 2 + 1, :]
            for at, place in enumerate(places):
                active[place, j * width : (j + 1) * width] = part[at * rows : (at + 1) * rows].astype(bf16)
        for k in ks:
            for t in range(number):
                for keep in keeps(k, r + t):
                    keep.start()

    for load in loads[9:]:
        load.wait()
    own_tokens.wait()
    for load in small_loads:
        load.wait()
    out_bias, attn_gain, attn_shift, down_bias, ffn_gain, ffn_shift = [v[...] for v in vector_refs]
    project([0], 0, CHUNKS)
    full_step(1)
    loop(lambda r: token_copy(r, 0).wait_recv())
    project([1], 0, CHUNKS)
    full_step(2)

    scaled = _head_masks(heads, width, 1.0 / math.sqrt(HEAD))
    plain = _head_masks(heads, width, 1.0)

    def attention(i):
        query_rows = _rows(i * BLOCK, BLOCK)
        acc = own_acc.at[:width, :BLOCK]
        peak_ref[...] = jnp.full_like(peak_ref, 2 * NEG)
        total_ref[...] = jnp.zeros_like(total_ref)
        acc[...] = jnp.zeros_like(acc)

        def meet(j, carry):
            rows = _rows(j * BLOCK, BLOCK)
            bias = _bias(seg_ref, pad_ref, query_rows, rows)
            query, key = active[query_rows, :width], active[rows, width : 2 * width]
            value = active[rows, 2 * width : 3 * width].T
            for h in range(heads):
                scores = _nt(key, query * scaled[h]) + bias
                old = peak_ref[h]
                peak = jnp.maximum(old, jnp.max(scores, axis=0, keepdims=True))
                expo = jnp.exp(scores - peak)
                ratio = jnp.exp(old - peak)
                peak_ref[h] = peak
                total_ref[h] = total_ref[h] * ratio + jnp.sum(expo, axis=0, keepdims=True)
                place = pl.ds(h * HEAD, HEAD)
                acc[place, :] = acc[place, :] * ratio + _nn(
                    value[h * HEAD : (h + 1) * HEAD], expo.astype(bf16)
                )
            return carry

        lax.fori_loop(jnp.maximum(i - 1, 0), jnp.minimum(i + 2, token_blocks), meet, 0)
        for h in range(heads):
            place = pl.ds(h * HEAD, HEAD)
            acc[place, :] = acc[place, :] / total_ref[h]
            lse_ref[h : h + 1, query_rows] = peak_ref[h] + jnp.log(total_ref[h])
        back[query_rows, :width] = acc[...].astype(bf16).T

    half = token_blocks // 2
    chip = me // 2
    per_device = own // BLOCK
    chunks_per = BLOCK // size

    def near(p):
        attention(jnp.where(chip == 0, p, token_blocks - 1 - p))

    _loop(half - 1, near)

    def far_part(r):
        @pl.when(r == 0)
        def _():
            full_step(3)

        @pl.when(r == 2)
        def _():
            for k in range(4, shares + 2):
                full_step(k)

        token_copy(r, 1).wait_recv()
        token_copy(r, 2).start()
        token_copy(r, 2).wait_recv()
        project([2, 3], r, 1)

    loop(far_part)
    loads[2].start()
    full_copy(0).wait_recv()
    full_copy(shares + 2).wait_recv()
    own_quarter.wait()
    loads[8].start()

    def tokens_done(r):
        for kind in range(3):
            token_copy(r, kind).wait_send()
        for k in range(4):
            keeps(k, r)[0].wait()

    def far(p):
        k, h = lax.rem(p, 2), p // 2
        attention(jnp.where(k == 0, cnt, dia) * per_device + h)

        @pl.when(p == 0)
        def _():
            loop(tokens_done)

        for c in range(2):

            @pl.when(k == c)
            def _():
                for t in range(chunks_per):
                    trade(h * chunks_per + t, 2 + c).start()

    _loop(2 * per_device, far)
    attention(jnp.where(chip == 0, half - 1, half))
    loop(lambda r: trade(r, 1).start())
    own_context.start()
    save_context = pltpu.make_async_copy(back.at[:, :width], context_hbm, load_sems.at[15])
    save_context.start()

    def add_sum(k, value):
        small_ref[k : k + 1, :] += jnp.sum(value, axis=0, keepdims=True)

    own_context.wait()
    loads[1].wait()
    loads[8].wait()

    def lower_norm(r):
        rows = _rows(r * size, size)
        for k in (1, 2, 3):
            trade(r, k).wait_recv()
        attended = _nn(recv_x[rows, :], grad1_full[:depth, :])
        unit, inverse = _norm(inputs_ref[rows, :].astype(f32) + attended + out_bias)
        unit1[rows, :] = unit
        inverse1[rows, :] = inverse
        gathers[0].slot(r, 0)[...] = (unit * attn_gain + attn_shift).astype(bf16)
        gathers[0].start(r)

    loop(lower_norm)
    loads[4].start()
    save_context.wait()
    for k in range(shares + 3):
        full_copy(k).wait_send()

    def front_done(r):
        for k in range(4):
            keeps(k, r)[1].wait()
        for k in (1, 2, 3):
            trade(r, k).wait_send()
        for load in context_load(r):
            load.start()

    loop(front_done)
    loads[2].wait()
    loads[3].wait()

    def feed_forward(r):
        rows = _rows(r * whole, whole)
        gathers[0].forward(r)
        gathers[0].arrive(r)

        def column(n, carry):
            cols = _rows(n * COLS, COLS)
            upper = _nn(normed_full[rows, :], up_ref[:, cols]) + up_bias_ref[:, cols]
            cdf = 0.5 + 0.5 * lax.erf(upper * math.sqrt(0.5))
            pdf = jnp.exp(upper * upper * -0.5) * (1.0 / math.sqrt(2.0 * math.pi))
            active[rows, cols] = (upper * cdf).astype(bf16)
            back[rows, cols] = (cdf + upper * pdf).astype(bf16)
            return carry

        lax.fori_loop(0, units // COLS, column, 0)
        scatters[1].project(r, lambda cols: _nn(active[rows, :], down_ref[:, cols]))
        scatters[1].finish(r)

    loop(feed_forward)
    loads[4].wait()

    def upper_norm(r):
        rows = _rows(r * size, size)
        normed = unit1[rows, :] * attn_gain + attn_shift
        unit, inverse = _norm(normed + scatters[1].result(r) + down_bias)
        cotangent = inputs_ref[rows, :].astype(f32)
        outputs_ref[rows, :] = (unit * ffn_gain + ffn_shift).astype(bf16)
        store(0, r).start()
        grad = _norm_back(cotangent * ffn_gain, unit, inverse)
        gathers[1].slot(r, 0)[...] = grad.astype(bf16)
        gathers[1].start(r)
        grad_own[rows, :] = grad
        add_sum(3, grad)
        add_sum(4, cotangent * unit)
        add_sum(5, cotangent)

    loop(upper_norm)

    def take(r):
        gathers[1].forward(r)
        gathers[1].arrive(r)
        scatters[1].sent(r)

    def feed_back(r):
        rows = _rows(r * whole, whole)

        def column(n, carry):
            cols = _rows(n * COLS, COLS)
            incoming = _nt(grad2_full[rows, :], down_ref[cols, :])
            upper_back = (back[rows, cols].astype(f32) * incoming).astype(bf16)
            back[rows, cols] = upper_back
            late_ref[1:2, cols] += jnp.sum(upper_back.astype(f32), axis=0, keepdims=True)
            return carry

        lax.fori_loop(0, units // COLS, column, 0)
        scatters[2].project(r, lambda cols: _nt(back[rows, :], up_ref[cols, :]))
        scatters[2].finish(r)

    def take_back(r):
        take(r)
        feed_back(r)

    _loop(CHUNKS - 1, take_back)
    take(CHUNKS - 1)

    def weights(k, p):
        cols = _rows(p * (depth // CHUNKS), depth // CHUNKS)
        place = _rows(k * depth + p * (depth // CHUNKS), depth // CHUNKS)
        if k == 0:
            weight_grads[place, :] = _tn(active[:, cols], grad2_full[...]).astype(bf16)
        else:
            weight_grads[place, :] = _tn(normed_full[:, cols], back[...]).astype(bf16)

    def out_weights():
        target = outputs_ref.at[:width] if early else weight_grads.at[3 * width : 4 * width]
        target[...] = _tn(context_ref[...], grad1_full[...]).astype(bf16)

    def in_weights(j):
        weight_grads[_rows(j * width, width), :] = _tn(
            grads[:, j * width : (j + 1) * width], normed_full[...]
        ).astype(bf16)

    def move(n, k):
        if k == 0 and n < 2 * pieces:
            weights(n // pieces, n % pieces)
        elif k == 0 and n == count - 1:
            out_weights()
        elif k == 0:
            in_weights(n - 2 * pieces)
        sums[n].step(k)
        if k == 2 * bits:
            store_final(n).start()

    def store_final(n):
        rows = _rows(n * piece, piece)
        return pltpu.make_async_copy(final.at[rows], final_hbm.at[rows], final_sems.at[n])

    def slot(i, first, number):
        for at in range(first, first + number) if early else ():
            if at in PLAN:

                @pl.when(i == at - first)
                def _():
                    for n, k in PLAN[at]:
                        move(n, k)

    if early:
        for n, k in PLAN[-1]:
            move(n, k)
    feed_back(CHUNKS - 1)
    for load in loads[9:]:
        load.start()

    def lower_back(r):
        slot(r, 0, CHUNKS)
        if not early:
            for k in range(2):

                @pl.when(r // 2 == k)
                def _():
                    for h in range(2):
                        weights(k, 2 * r - 4 * k + h)

                @pl.when(r == 2 * k + 1)
                def _():
                    sums[k].step(0)

        rows = _rows(r * size, size)
        incoming = grad_own[rows, :] + scatters[2].result(r)
        unit = unit1[rows, :]
        grad = _norm_back(incoming * attn_gain, unit, inverse1[rows, :])
        gathers[2].slot(r, 0)[...] = grad.astype(bf16)
        gathers[2].start(r)
        grad_own[rows, :] = grad
        add_sum(0, grad)
        add_sum(1, incoming * unit)
        add_sum(2, incoming)

    loop(lower_back)
    gathers_done = lambda r: [gather.sent(r) for gather in gathers[:2]]
    loop(gathers_done)
    for load in loads[5:8]:
        load.start()

    loads[0].wait()
    loop(lambda r: [load.wait() for load in context_load(r)])

    def context_back(r):
        slot(r, CHUNKS, CHUNKS)
        rows = _rows(r * whole, whole)
        gathers[2].forward(r)
        gathers[2].arrive(r)
        scatters[2].sent(r)
        grad = _nt(grad1_full[rows, :], out_proj_ref[...]).astype(bf16)
        for k, b in enumerate(blocks):
            part = _rows(b * own + r * size, size)
            back[part, :width] = grad[k * size : (k + 1) * size]

    loop(context_back)
    loop(lambda r: gathers[2].sent(r))
    loop(lambda r: store(0, r).wait())
    for load in loads[5:8]:
        load.wait()

    targets = [{"mp": sib}, {"mp": cnt}, *over]

    def small_step(k):
        return _remote(
            small_ref.at[:8], small_recv.at[k], small_sems.at[0, k], small_sems.at[1, k], targets[k]
        )

    def small_end(k):
        small_step(k).wait()
        small_ref[:8, :] += small_recv[k]

    def late_step(k):
        at = len(targets) + k
        return _remote(late_ref, late_recv.at[k], small_sems.at[0, at], small_sems.at[1, at], over[k])

    def late_end(k):
        late_step(k).wait()
        late_ref[...] += late_recv[k]

    def small_turn(k):
        if k:
            small_end(k - 1)
        if k < len(targets):
            small_step(k).start()

    keys_acc, values_acc, query_acc = unit1, other_acc, own_acc.at[:width, :BLOCK]
    keys_acc[...] = jnp.zeros_like(keys_acc)
    values_acc[...] = jnp.zeros_like(values_acc)
    grads = grad2_full
    per = own // BLOCK

    def spot(j):
        return _rows(lax.rem(j, per) * BLOCK, BLOCK), _rows(j // per * width, width)

    def attend(t):
        i, turn = t // 3, lax.rem(t, 3)
        for k in range(len(targets) + 1):

            @pl.when(t == SMALL_TURNS[k])
            def _():
                small_turn(k)

        slot(t, 2 * CHUNKS, 3 * token_blocks)
        query_rows = _rows(i * BLOCK, BLOCK)

        @pl.when(turn == 0)
        def _():
            product = (
                back[query_rows, :width].astype(f32) * back[query_rows, width : 2 * width].astype(f32)
            ).T
            for h in range(heads):
                dots_ref[h : h + 1, :] = jnp.sum(
                    product[h * HEAD : (h + 1) * HEAD], axis=0, keepdims=True
                )
            query_acc[...] = jnp.zeros_like(query_acc)

        @pl.when((i + turn >= 1) & (i + turn <= token_blocks))
        def _():
            j = jnp.clip(i + turn - 1, 0, token_blocks - 1)
            query, grad = active[query_rows, :width], back[query_rows, :width]
            rows = _rows(j * BLOCK, BLOCK)
            bias = _bias(seg_ref, pad_ref, query_rows, rows)
            queries = [query * scaled[h] for h in range(heads)]
            context_grads = [grad * plain[h] for h in range(heads)]
            key_rows = (active[rows, width : 2 * width] * (1.0 / math.sqrt(HEAD))).astype(bf16).T
            parts = []
            for c in range(BLOCK // PART):
                place = pl.ds(pl.multiple_of(j * BLOCK + c * PART, PART), PART)
                key, value = active[place, width : 2 * width], active[place, 2 * width : 3 * width]
                probs, score_grads = [], []
                for h in range(heads):
                    scores = _nt(key, queries[h]) + bias[c * PART : (c + 1) * PART]
                    prob = jnp.exp(scores - lse_ref[h : h + 1, query_rows])
                    probs.append(prob.astype(bf16))
                    score_grads.append(
                        (prob * (_nt(value, context_grads[h]) - dots_ref[h : h + 1, :])).astype(bf16)
                    )
                spot_rows, spot_cols = spot(j)
                spot_part = pl.ds(pl.multiple_of(lax.rem(j, per) * BLOCK + c * PART, PART), PART)
                keys_acc[spot_part, spot_cols] += _nn(
                    jnp.concatenate(score_grads, axis=1), jnp.concatenate(queries, axis=0)
                )
                values_acc[spot_part, spot_cols] += _nn(
                    jnp.concatenate(probs, axis=1), jnp.concatenate(context_grads, axis=0)
                )
                parts.append(score_grads)
            for h in range(heads):
                query_acc[pl.ds(h * HEAD, HEAD), :] += _nn(
                    key_rows[h * HEAD : (h + 1) * HEAD], jnp.concatenate([part[h] for part in parts], axis=0)
                )

        @pl.when(turn == 2)
        def _():
            grads[query_rows, :width] = query_acc[...].astype(bf16).T

    _loop(3 * token_blocks, attend)

    def keep(j):
        rows = _rows(j * BLOCK, BLOCK)
        grads[rows, width : 2 * width] = keys_acc[spot(j)].astype(bf16)
        grads[rows, 2 * width : 3 * width] = values_acc[spot(j)].astype(bf16)

    _loop(token_blocks, keep)

    if not early:
        for n in range(2):
            sums[n].step(1)
        out_weights()
        in_weights(0)
        in_weights(1)
        in_weights(2)
    for n in range(2 * pieces):
        sums[n].halve(0).wait_send()

    def partial_rows(r):
        chunk = jnp.concatenate(
            [grads[_rows(b * own + r * size, size), : 3 * width] for b in blocks], axis=0
        )

        def tile(cols):
            return _nt(chunk, up_ref[cols, : 3 * width])

        scatters[3].project(r, tile)
        scatters[3].finish(r)

    def finish(r):
        rows = _rows(r * size, size)
        outputs_ref[rows, :] = (grad_own[rows, :] + scatters[3].result(r)).astype(bf16)
        store(1, r).start()
        scatters[3].sent(r)

    def bias(j):
        return jnp.sum(grads[:, j * width : (j + 1) * width].astype(f32), axis=0, keepdims=True)

    for load in loads[9:]:
        load.wait()
    late_ref[:1, :width] = bias(0)
    late_ref[:1, width : 2 * width] = bias(2)
    late_step(0).start()
    if early:
        tail = PLAN[2 * CHUNKS + 3 * token_blocks]
    else:
        tail = [(2, 0)] + [(-1, r) for r in range(CHUNKS)]
        tail += [(n, k) for k in range(1, 2 * bits + 1) for n in range(3) if n == 2 or k > 1]
    last = max(k for k, (n, _) in enumerate(tail) if n < 0)
    turns = [(len(tail) - 1) * (k + 2) // (bits + 1) for k in range(bits)]
    for at, (n, k) in enumerate(tail):
        if n < 0:
            partial_rows(k)
        elif k or early:
            move(n, k)
        else:
            sums[n].step(0)
        for turn in [turn for turn, place in enumerate(turns) if place == at]:
            late_end(turn)
            if turn + 1 < bits:
                late_step(turn + 1).start()
        if at == last + 3 * (len(tail) - 1 - last) // 4:
            if early:
                sums[-1].halve(0).wait_send()
            loop(finish)
    for n in range(count):
        sums[n].sent()
        if n >= 2 * pieces and not (early and n == count - 1):
            sums[n].halve(0).wait_send()
    small_ref[8:10, :] = late_ref[:2, :]
    loop(lambda r: store(1, r).wait())
    for n in range(3 * pieces):
        store_final(n).wait()


def main_layer(mesh, arrays, small_arrays):
    f32, bf16 = jnp.float32, jnp.bfloat16
    inputs, in_proj, out_proj, up_proj, down_proj, _ = arrays
    own, depth = inputs.shape
    units, width = up_proj.shape[1], out_proj.shape[0]
    whole, half = 4 * own, depth // 2
    bits = mesh.shape["dp"].bit_length() - 1
    pieces = CHUNKS if (depth // CHUNKS >> bits) >= 16 else 1
    outs = [
        ((own, depth), bf16),
        ((own, depth), bf16),
        ((3 * depth, depth), bf16),
        ((whole, depth), bf16),
        ((whole, 3 * width), bf16),
        ((4 * width, depth), bf16),
        ((whole, width), bf16),
        ((16, depth), f32),
    ]
    return pl.pallas_call(
        partial(main_kernel, bits, pieces),
        out_shape=[jax.ShapeDtypeStruct(*out) for out in outs],
        in_specs=[REMOTE] * 16,
        out_specs=[REMOTE] * 7 + [LOCAL],
        scratch_shapes=[
            pltpu.VMEM((whole, width), bf16),
            *[pltpu.VMEM(array.shape, bf16) for array in (out_proj, inputs, up_proj, down_proj)],
            pltpu.VMEM((2 * depth, depth), bf16),
            pltpu.VMEM((whole, depth), bf16),
            pltpu.VMEM((whole, depth), bf16),
            pltpu.VMEM((whole, depth), bf16),
            pltpu.VMEM((whole, units), bf16),
            pltpu.VMEM((whole, units), bf16),
            pltpu.VMEM((own, depth), f32),
            pltpu.VMEM((own, 1), f32),
            pltpu.VMEM((own, depth), f32),
            pltpu.VMEM((8, BLOCK), f32),
            pltpu.VMEM((8, whole), f32),
            pltpu.VMEM((width // HEAD, 1, BLOCK), f32),
            pltpu.VMEM((width // HEAD, 1, BLOCK), f32),
            *_scatter_scratch(own, depth),
            pltpu.VMEM((3 * pieces * (depth // pieces - (depth // pieces >> bits)), depth), bf16),
            pltpu.VMEM((3 * depth, depth), bf16),
            pltpu.VMEM((2 + bits, 8, depth), f32),
            pltpu.VMEM((8, depth), f32),
            pltpu.VMEM((bits, 8, depth), f32),
            pltpu.SemaphoreType.DMA((16,)),
            pltpu.SemaphoreType.DMA((4, CHUNKS)),
            pltpu.SemaphoreType.DMA((2, 3, CHUNKS)),
            pltpu.SemaphoreType.DMA((2, CHUNKS)),
            pltpu.SemaphoreType.DMA((3 * pieces,)),
            pltpu.SemaphoreType.DMA((3, 3, CHUNKS)),
            pltpu.SemaphoreType.DMA((3, 3, CHUNKS)),
            pltpu.SemaphoreType.DMA((4, 3, CHUNKS)),
            pltpu.SemaphoreType.DMA((4, 3, CHUNKS)),
            pltpu.SemaphoreType.DMA((2, 3 * pieces, 2 * bits)),
            pltpu.SemaphoreType.DMA((2, 2 + 2 * bits)),
            pltpu.SemaphoreType.DMA((2, 3, CHUNKS)),
            pltpu.SemaphoreType.DMA((2, 4, CHUNKS)),
            pltpu.SemaphoreType.DMA((2, 3 + bits)),
            pltpu.SemaphoreType.DMA((10,)),
            *[pltpu.VMEM(array.shape, array.dtype) for array in small_arrays],
        ],
        compiler_params=pltpu.CompilerParams(
            collective_id=1, has_side_effects=True, vmem_limit_bytes=63 * 2**20
        ),
        name="main_layer",
    )(*arrays, *small_arrays)


def unpack_kernel(
    width, final_ref, attn_ref, small_ref, outputs_ref, inputs_grad_ref, down_ref, up_ref, in_ref, out_ref,
    qv_ref, up_bias_ref, *refs,
):
    f32 = jnp.float32
    vectors, outputs_out, inputs_grad_out = refs[:6], refs[6], refs[7]
    down_ref[...] = final_ref[0].astype(f32)
    up_ref[...] = final_ref[1].astype(f32)
    for j in range(3):
        in_ref[j] = attn_ref[j * width : (j + 1) * width, :].astype(f32).T
    out_ref[...] = attn_ref[3 * width :, :].astype(f32)
    outputs_out[...] = outputs_ref[...]
    inputs_grad_out[...] = inputs_grad_ref[...]
    for k, vector in enumerate(vectors):
        vector[...] = small_ref[k : k + 1, :]
    up_bias_ref[...] = small_ref[9:10, :]
    for k in range(2):
        qv_ref[k : k + 1, :] = small_ref[8:9, k * width : (k + 1) * width]


def unpack(final, small, outputs, inputs_grad, width):
    f32 = jnp.float32
    own, depth = outputs.shape
    steps = depth // UNPACK
    part = own // steps
    matrix = pl.BlockSpec((UNPACK, depth), lambda i: (i, 0))
    tokens = pl.BlockSpec((part, depth), lambda i: (i, 0))
    vector = pl.BlockSpec((1, depth), lambda i: (0, 0))
    shapes = [
        ((depth, depth), f32, matrix),
        ((depth, depth), f32, matrix),
        ((3, depth, width), f32, pl.BlockSpec((3, UNPACK, width), lambda i: (0, i, 0))),
        ((width, depth), f32, pl.BlockSpec((width, UNPACK), lambda i: (0, i))),
        ((2, width), f32, pl.BlockSpec((2, width), lambda i: (0, 0))),
        *[((1, depth), f32, vector)] * 7,
        ((own, depth), jnp.bfloat16, tokens),
        ((own, depth), jnp.bfloat16, tokens),
    ]
    return pl.pallas_call(
        partial(unpack_kernel, width),
        grid=(steps,),
        in_specs=[
            pl.BlockSpec((2, UNPACK, depth), lambda i: (0, i, 0)),
            pl.BlockSpec((depth, UNPACK), lambda i: (2, i)),
            pl.BlockSpec((16, depth), lambda i: (0, 0)),
            tokens,
            tokens,
        ],
        out_specs=[spec for _, _, spec in shapes],
        out_shape=[jax.ShapeDtypeStruct(shape, dtype) for shape, dtype, _ in shapes],
        compiler_params=pltpu.CompilerParams(vmem_limit_bytes=VMEM),
        name="unpack_gradients",
    )(final.reshape(3, depth, depth), final, small, outputs, inputs_grad)


def shards(
    mesh,
    inputs,
    in_proj,
    qv_bias,
    out_proj,
    out_bias,
    attn_gain,
    attn_shift,
    up_proj,
    up_bias,
    down_proj,
    down_bias,
    ffn_gain,
    ffn_shift,
    segments,
    padding,
    cotangent,
):
    places, real = segment_places(segments, padding)
    vectors = [v[None] for v in (out_bias, attn_gain, attn_shift, down_bias, ffn_gain, ffn_shift)]
    outputs, inputs_grad, final, _, _, _, _, small = main_layer(
        mesh,
        (inputs, in_proj, out_proj, up_proj, down_proj, cotangent),
        (qv_bias, places, real, up_bias[None], *vectors),
    )
    down_grad, up_grad, in_grad, out_grad, qv_grad, up_bias_grad, *vectors, outputs, inputs_grad = unpack(
        final, small, outputs, inputs_grad, in_proj.shape[2]
    )
    vectors = [v[0] for v in vectors]
    return (
        outputs,
        inputs_grad,
        in_grad,
        qv_grad,
        out_grad,
        *vectors[:3],
        up_grad,
        up_bias_grad[0],
        down_grad,
        *vectors[3:],
    )


def solution(mesh):
    return jax.shard_map(
        partial(shards, mesh),
        mesh=mesh,
        in_specs=(
            P(("dp", "mp"), None),
            P(None, None, "mp"),
            P(None, "mp"),
            P("mp", None),
            P(),
            P(),
            P(),
            P(None, "mp"),
            P("mp"),
            P("mp", None),
            P(),
            P(),
            P(),
            P("dp", None),
            P("dp", None),
            P(("dp", "mp"), None),
        ),
        out_specs=(
            P(("dp", "mp"), None),
            P(("dp", "mp"), None),
            P(None, None, "mp"),
            P(None, "mp"),
            P("mp", None),
            P(),
            P(),
            P(),
            P(None, "mp"),
            P("mp"),
            P("mp", None),
            P(),
            P(),
            P(),
        ),
        check_vma=False,
    )
```

```python
from functools import partial
import math

import jax
import jax.numpy as jnp
from jax import lax
from jax.experimental import pallas as pl
from jax.experimental.pallas import tpu as pltpu
from jax.sharding import PartitionSpec as P

HEAD = 64
BLOCK = 256
CHUNKS = 4
SMALL_TURNS = (0, 1, 3, 10, 16, 23, 23, 23, 23)
ORDERS = (
    (0, 1, 2),
    (1, 0, 2),
    (0, 1, 2),
    (0, 1, 2),
    (0, 1, 2),
    (0, 1, 2),
    (0, 1, 2),
    (0, 1, 2),
    (0, 1, 2),
    (0, 1, 2),
    (1, 0, 2),
    (0, 1, 2),
)
PLAN = {
    -1: ((3, 0), (1, 0), (2, 0), (0, 0),),
    0: ((5, 0), (1, 1), (3, 1), (4, 0),),
    1: ((7, 0), (6, 0), (2, 1),),
    3: ((3, 2),),
    4: ((0, 1), (2, 2), (3, 3),),
    5: ((5, 1), (0, 2), (2, 3), (1, 2),),
    6: ((3, 4), (5, 2), (4, 1), (0, 3),),
    7: ((2, 4), (1, 3), (7, 1), (3, 5),),
    8: ((11, 0), (4, 2), (5, 3),),
    9: ((6, 1),),
    10: ((0, 4),),
    12: ((2, 5),),
    14: ((1, 4),),
    16: ((7, 2),),
    17: ((4, 3),),
    19: ((11, 1), (5, 4),),
    21: ((6, 2),),
    24: ((0, 5),),
    25: ((7, 3),),
    26: ((4, 4),),
    27: ((1, 5),),
    29: ((11, 2),),
    31: ((5, 5),),
    32: ((10, 0), (6, 3), (7, 4), (0, 6), (2, 6), (3, 6), (8, 0), (4, 5), (9, 0), (-1, 0), (1, 6), (5, 6), (-1, 1), (11, 3), (-1, 2), (8, 1), (-1, 3), (10, 1), (6, 4), (4, 6), (7, 5), (11, 4), (8, 2), (9, 1), (6, 5), (10, 2), (11, 5), (8, 3), (7, 6), (9, 2), (10, 3), (8, 4), (6, 6), (9, 3), (11, 6), (10, 4), (8, 5), (9, 4), (9, 5), (10, 5), (8, 6), (10, 6), (9, 6),),
}
COLS = 256
PART = 256
UNPACK = 512
VMEM = 60 * 2**20
REMOTE = pl.BlockSpec(memory_space=pl.ANY)
LOCAL = pl.BlockSpec(memory_space=pltpu.VMEM)
MESH = pl.DeviceIdType.MESH


EPSILON = 1e-05


NEG = -1e30


def _head_masks(heads, width, value):
    lane = lax.broadcasted_iota(jnp.int32, (1, width), 1) // HEAD
    return [jnp.where(lane == h, value, 0.0).astype(jnp.bfloat16) for h in range(heads)]


def _nt(a, b):
    return lax.dot_general(a, b, (((1,), (1,)), ((), ())), preferred_element_type=jnp.float32)


def _tn(a, b):
    return lax.dot_general(a, b, (((0,), (0,)), ((), ())), preferred_element_type=jnp.float32)


def _nn(a, b):
    return jnp.dot(a, b, preferred_element_type=jnp.float32)


def _column(row):
    wide = jnp.broadcast_to(row.astype(jnp.float32), (128, row.shape[1])).T.astype(jnp.int32)
    return jnp.concatenate([wide] * (BLOCK // 128), axis=1)


def _bias(seg_ref, pad_ref, query_rows, key_rows):
    seg_q, pad_q = seg_ref[:, query_rows], pad_ref[:, query_rows]
    seg_k, pad_k = _column(seg_ref[:, key_rows]), _column(pad_ref[:, key_rows])
    allowed = (seg_k == seg_q) & ((pad_k > 0) | (pad_q == 0))
    return jnp.where(allowed, 0.0, NEG).astype(jnp.float32)


def _loop(count, body):
    def step(i, carry):
        body(i)
        return carry

    lax.fori_loop(0, count, step, 0)


def segment_places(segments, padding):
    row_count, seq_len = segments.shape
    if row_count > 1:
        segments = segments + jnp.arange(row_count, dtype=jnp.int32)[:, None] * (seq_len + 1)
    return segments.reshape(1, -1), padding.reshape(1, -1)


def _partners():
    me = lax.axis_index("mp")
    core = lax.rem(me, 2)
    sib = me + 1 - 2 * core
    cnt = lax.rem(me + 2, 4)
    dia = lax.rem(cnt + 1, 2) + cnt - lax.rem(cnt, 2)
    return me, sib, cnt, dia


def _remote(src, dst, send, recv, target):
    return pltpu.make_async_remote_copy(
        src_ref=src, dst_ref=dst, send_sem=send, recv_sem=recv, device_id=target, device_id_type=MESH
    )


def _greet(targets):
    barrier = pltpu.get_barrier_semaphore()
    for target in targets:
        pl.semaphore_signal(barrier, inc=1, device_id=target, device_id_type=MESH)
    pl.semaphore_wait(barrier, len(targets))


def _rows(start, size):
    return pl.ds(pl.multiple_of(start, size), size)


def _part(start, size):
    return pl.ds(pl.multiple_of(start, 16), size)


class Gather:
    def __init__(self, buffer, send, recv, stage, size, sib, cnt):
        self.buffer, self.send, self.recv = buffer, send, recv
        self.stage, self.size, self.sib, self.cnt = stage, size, sib, cnt

    def slot(self, r, k):
        return self.buffer.at[_rows((r * 4 + k) * self.size, self.size)]

    def copy(self, r, kind):
        src, dst, target = ((0, 1, self.sib), (0, 2, self.cnt), (2, 3, self.sib))[kind]
        return _remote(
            self.slot(r, src),
            self.slot(r, dst),
            self.send.at[self.stage, kind, r],
            self.recv.at[self.stage, kind, r],
            {"mp": target},
        )

    def start(self, r):
        self.copy(r, 1).start()
        self.copy(r, 0).start()

    def forward(self, r):
        self.copy(r, 1).wait_recv()
        self.copy(r, 2).start()

    def arrive(self, r):
        self.copy(r, 0).wait_recv()
        self.copy(r, 2).wait_recv()

    def sent(self, r):
        for kind in range(3):
            self.copy(r, kind).wait_send()


class Scatter:
    def __init__(self, bufs, send, recv, stage, size, sib, cnt):
        self.own, self.other, self.stage_sib, self.stage_x, self.recv_sib, self.recv_x = bufs
        self.send, self.recv = send, recv
        self.stage, self.size, self.sib, self.cnt = stage, size, sib, cnt

    def copy(self, r, kind):
        rows = _rows(r * self.size, self.size)
        src, dst, target = (
            (self.stage_sib.at[0, rows], self.recv_sib.at[0, rows], self.sib),
            (self.stage_sib.at[1, rows], self.recv_sib.at[1, rows], self.sib),
            (self.stage_x.at[rows], self.recv_x.at[rows], self.cnt),
        )[kind]
        return _remote(
            src, dst, self.send.at[self.stage, kind, r], self.recv.at[self.stage, kind, r], {"mp": target}
        )

    def sent(self, r):
        for kind in range(3):
            self.copy(r, kind).wait_send()

    def project(self, r, tile):
        size = self.size
        rows = _rows(r * size, size)

        def column(n, carry):
            cols = _rows(n * COLS, COLS)
            part = tile(cols)
            self.own[rows, cols] = part[:size]
            self.stage_sib[1, rows, cols] = part[size : 2 * size].astype(jnp.bfloat16)
            self.other[rows, cols] = part[2 * size : 3 * size]
            self.stage_sib[0, rows, cols] = part[3 * size :].astype(jnp.bfloat16)
            return carry

        lax.fori_loop(0, self.own.shape[1] // COLS, column, 0)
        self.copy(r, 0).start()
        self.copy(r, 1).start()

    def finish(self, r):
        rows = _rows(r * self.size, self.size)
        self.copy(r, 0).wait_recv()
        self.stage_x[rows, :] = (
            self.other[rows, :] + self.recv_sib[0, rows, :].astype(jnp.float32)
        ).astype(jnp.bfloat16)
        self.copy(r, 2).start()
        self.copy(r, 1).wait_recv()
        self.own[rows, :] += self.recv_sib[1, rows, :].astype(jnp.float32)

    def result(self, r):
        rows = _rows(r * self.size, self.size)
        self.copy(r, 2).wait_recv()
        return self.own[rows, :] + self.recv_x[rows, :].astype(jnp.float32)


def _scatter_scratch(own, width):
    f32, bf16 = jnp.float32, jnp.bfloat16
    return [
        pltpu.VMEM((own, width), f32),
        pltpu.VMEM((own, width), f32),
        pltpu.VMEM((2, own, width), bf16),
        pltpu.VMEM((own, width), bf16),
        pltpu.VMEM((2, own, width), bf16),
        pltpu.VMEM((own, width), bf16),
    ]


def _norm(summed):
    center = summed - jnp.mean(summed, axis=-1, keepdims=True)
    variance = jnp.mean(center * center, axis=-1, keepdims=True)
    inverse = lax.rsqrt(variance + EPSILON)
    return center * inverse, inverse


def _norm_back(scaled, unit, inverse):
    return inverse * (
        scaled
        - jnp.mean(scaled, axis=-1, keepdims=True)
        - unit * jnp.mean(scaled * unit, axis=-1, keepdims=True)
    )


class Reduce:
    def __init__(self, n, rows, order, source, work, final, sems):
        self.n, self.rows, self.source, self.work, self.final, self.sems = n, rows, source, work, final, sems
        self.steps = len(order)
        dp = lax.axis_index("dp")
        self.bit = [lax.rem(dp // (1 << b), 2) for b in order]
        self.peer = [{"dp": dp + (1 << b) * (1 - 2 * bit)} for b, bit in zip(order, self.bit)]

    def size(self, s):
        return self.rows >> s

    def start(self, s):
        first = self.n * self.rows
        for t in range(s):
            first = first + self.bit[t] * self.size(t + 1)
        return first

    def held(self, s):
        if s == 0:
            return self.source
        stride = self.rows - self.size(self.steps)
        return self.work, self.n * stride + self.rows - 2 * self.size(s)

    def halve(self, s):
        ref, first = self.held(s)
        half = self.size(s + 1)
        there, place = self.held(s + 1)
        return _remote(
            ref.at[_part(first + (1 - self.bit[s]) * half, half)],
            there.at[_part(place, half)],
            self.sems.at[0, self.n, s],
            self.sems.at[1, self.n, s],
            self.peer[s],
        )

    def double(self, s):
        block = self.final.at[_rows(self.start(s + 1), self.size(s + 1))]
        k = 2 * self.steps - 1 - s
        return _remote(block, block, self.sems.at[0, self.n, k], self.sems.at[1, self.n, k], self.peer[s])

    def step(self, k):
        steps = self.steps
        if 0 < k <= steps:
            s = k - 1
            half = self.size(s + 1)
            self.halve(s).wait_recv()
            ref, first = self.held(s)
            there, place = self.held(s + 1)
            total = there[_part(place, half), :].astype(jnp.float32) + ref[
                _part(first + self.bit[s] * half, half), :
            ].astype(jnp.float32)
            if k < steps:
                there[_part(place, half), :] = total.astype(jnp.bfloat16)
            else:
                self.final[_rows(self.start(steps), half), :] = total.astype(jnp.bfloat16)
        if k > steps:
            self.double(2 * steps - k).wait_recv()
        if k < steps:
            self.halve(k).start()
        elif k < 2 * steps:
            self.double(2 * steps - 1 - k).start()

    def sent(self):
        for s in range(self.steps):
            if s:
                self.halve(s).wait_send()
            self.double(s).wait_send()


def main_kernel(bits, pieces, *refs):
    f32, bf16 = jnp.float32, jnp.bfloat16
    (inputs_hbm, in_proj_hbm, out_proj_hbm, up_hbm, down_hbm, cotangent_hbm,
     *refs) = refs
    small_hbm, refs = refs[:10], refs[10:]
    (outputs_hbm, inputs_grad_hbm, final_hbm, tokens_hbm, qkv_hbm, full_hbm, context_hbm, small_ref,
     context_ref, out_proj_ref, inputs_ref, up_ref, down_ref,
     weight_grads, normed_full, grad2_full, grad1_full, active, back, unit1, inverse1, grad_own, dots_ref,
     lse_ref, peak_ref, total_ref,
     own_acc, other_acc, stage_sib, stage_x, recv_sib, recv_x, work, final, small_recv, late_ref, late_recv,
     load_sems, block_sems, trade_sems, store_sems, final_sems, gather_send, gather_recv, scatter_send, scatter_recv,
     sems, small_sems, token_sems, keep_sems, full_sems, operand_sems, *small_operands) = refs
    qv_bias_ref, seg_ref, pad_ref, up_bias_ref, *vector_refs = small_operands
    small_loads = [
        pltpu.make_async_copy(source, target, operand_sems.at[k])
        for k, (source, target) in enumerate(zip(small_hbm, small_operands))
    ]
    outputs_ref = inputs_ref
    me, sib, cnt, dia = _partners()
    own, depth = inputs_ref.shape
    units, width = up_ref.shape[1], out_proj_ref.shape[0]
    length = 4 * own
    heads, token_blocks = width // HEAD, length // BLOCK
    size, whole = own // CHUNKS, length // CHUNKS
    blocks = (me, sib, cnt, dia)
    early = pieces == CHUNKS
    loop = partial(_loop, CHUNKS)

    def context_load(r):
        return [
            pltpu.make_async_copy(
                context_hbm.at[_rows(b * own + r * size, size)],
                context_ref.at[_rows((r * 4 + k) * size, size)],
                block_sems.at[k, r],
            )
            for k, b in enumerate(blocks)
        ]

    loads = [
        pltpu.make_async_copy(source, target, load_sems.at[k])
        for k, (source, target) in enumerate(
            (
                (out_proj_hbm, out_proj_ref),
                (inputs_hbm, inputs_ref),
                (up_hbm, up_ref),
                (down_hbm, down_ref),
                (cotangent_hbm, inputs_ref),
                (qkv_hbm, active.at[:, : 3 * width]),
                (tokens_hbm, normed_full),
                (context_hbm, back.at[:, width : 2 * width]),
                (full_hbm, grad1_full.at[:depth]),
                *[(in_proj_hbm.at[j], up_ref.at[:, j * width : (j + 1) * width]) for j in range(3)],
            )
        )
    ]
    own_context = pltpu.make_async_copy(
        back.at[_rows(me * own, own), :width], recv_x.at[:, _rows(me * width, width)], load_sems.at[12]
    )

    def trade(r, k):
        return _remote(
            back.at[_rows(blocks[k] * own + r * size, size), :width],
            recv_x.at[_rows(r * size, size), _rows(me * width, width)],
            trade_sems.at[0, k - 1, r],
            trade_sems.at[1, k - 1, r],
            {"mp": blocks[k]},
        )

    tokens_ref = normed_full

    def token_copy(r, kind):
        here = inputs_hbm.at[_rows(r * size, size)]
        place = _rows((cnt if kind == 2 else me) * own + r * size, size)
        src, target = ((here, sib), (here, cnt), (tokens_ref.at[place], sib))[kind]
        return _remote(
            src, tokens_ref.at[place], token_sems.at[0, kind, r], token_sems.at[1, kind, r], {"mp": target}
        )

    def keeps(k, r):
        place = _rows(blocks[k] * own + r * size, size)
        return [
            pltpu.make_async_copy(tokens_ref.at[place], tokens_hbm.at[place], keep_sems.at[0, k, r]),
            pltpu.make_async_copy(
                active.at[place, : 3 * width], qkv_hbm.at[place], keep_sems.at[1, k, r]
            ),
        ]

    dp = lax.axis_index("dp")
    shares = min(bits, (width // 16).bit_length() - 1)
    bit = [lax.rem(dp // (1 << b), 2) for b in range(bits)]
    over = [{"dp": dp + (1 << b) * (1 - 2 * bit[b])} for b in range(bits)]

    def span(block, s):
        first = block * width
        for t in range(s):
            first = first + bit[t] * (width >> (t + 1))
        return full_hbm.at[_part(first, width >> s)]

    def full_copy(k):
        if k == 0:
            pair = out_proj_hbm, span(me, 0), {"mp": sib}
        elif k == 1:
            first = sum(bit[t] * (width >> (t + 1)) for t in range(shares))
            pair = out_proj_hbm.at[_part(first, width >> shares)], span(me, shares), {"mp": cnt}
        elif k < 2 + shares:
            block = span(cnt, shares - (k - 2))
            pair = block, block, over[shares - 1 - (k - 2)]
        else:
            block = span(cnt, 0)
            pair = block, block, {"mp": sib}
        return _remote(pair[0], pair[1], full_sems.at[0, k], full_sems.at[1, k], pair[2])

    own_quarter = pltpu.make_async_copy(out_proj_hbm, span(me, 0), load_sems.at[13])
    own_tokens = pltpu.make_async_copy(inputs_hbm, tokens_ref.at[_rows(me * own, own)], load_sems.at[14])

    def full_step(k):
        full_copy(k).wait_recv()
        full_copy(k + 1).start()

    def store(k, r):
        rows = _rows(r * size, size)
        target = (outputs_hbm, inputs_grad_hbm)[k]
        return pltpu.make_async_copy(outputs_ref.at[rows], target.at[rows], store_sems.at[k, r])

    bufs = (own_acc, other_acc, stage_sib, stage_x, recv_sib, recv_x)
    gathers = [
        Gather(buf, gather_send, gather_recv, stage, size, sib, cnt)
        for stage, buf in enumerate((normed_full, grad2_full, grad1_full))
    ]
    scatters = [
        Scatter(bufs, scatter_send, scatter_recv, stage, size, sib, cnt) for stage in range(4)
    ]
    piece = depth // pieces
    count = 3 * pieces

    def source(n):
        if early and n == count - 1:
            return outputs_ref, 0
        return weight_grads, (n if n < 2 * pieces else n - 2 * pieces) * piece

    sums = [
        Reduce(
            n, piece, ORDERS[n] if early else tuple(range(bits)), source(n), work, final, sems
        )
        for n in range(count)
    ]
    for load in (*loads[9:], own_tokens, *small_loads, loads[1], own_quarter):
        load.start()
    small_ref[...] = jnp.zeros_like(small_ref)
    late_ref[...] = jnp.zeros_like(late_ref)
    _greet([{"mp": sib}, {"mp": cnt}, {"mp": dia}, *over])
    full_copy(1).start()
    for r in range(CHUNKS):
        token_copy(r, 1).start()
        token_copy(r, 0).start()
    full_copy(0).start()
    for load in (loads[0], loads[3]):
        load.start()

    def project(ks, r, number):
        rows = number * size
        places = [_part(blocks[k] * own + r * size, rows) for k in ks]
        chunk = jnp.concatenate([tokens_ref[place, :] for place in places], axis=0)
        for j in range(3):
            part = _nn(chunk, up_ref[:, j * width : (j + 1) * width])
            if j != 1:
                part = part + qv_bias_ref[j // 2 : j // 2 + 1, :]
            for at, place in enumerate(places):
                active[place, j * width : (j + 1) * width] = part[at * rows : (at + 1) * rows].astype(bf16)
        for k in ks:
            for t in range(number):
                for keep in keeps(k, r + t):
                    keep.start()

    for load in loads[9:]:
        load.wait()
    own_tokens.wait()
    for load in small_loads:
        load.wait()
    out_bias, attn_gain, attn_shift, down_bias, ffn_gain, ffn_shift = [v[...] for v in vector_refs]
    project([0], 0, CHUNKS)
    full_step(1)
    loop(lambda r: token_copy(r, 0).wait_recv())
    project([1], 0, CHUNKS)
    full_step(2)

    scaled = _head_masks(heads, width, 1.0 / math.sqrt(HEAD))
    plain = _head_masks(heads, width, 1.0)

    def attention(i, low, high, state=0, begin=True, end=True):
        query_rows = _rows(i * BLOCK, BLOCK)
        acc = own_acc.at[:width, state * BLOCK : (state + 1) * BLOCK]
        peaks, totals = [ref.at[state * heads : (state + 1) * heads] for ref in (peak_ref, total_ref)]
        if begin:
            peaks[...] = jnp.full_like(peaks, 2 * NEG)
            totals[...] = jnp.zeros_like(totals)
            acc[...] = jnp.zeros_like(acc)

        def meet(j, carry):
            rows = _rows(j * BLOCK, BLOCK)
            bias = _bias(seg_ref, pad_ref, query_rows, rows)
            query, key = active[query_rows, :width], active[rows, width : 2 * width]
            value = active[rows, 2 * width : 3 * width].T
            for h in range(heads):
                scores = _nt(key, query * scaled[h]) + bias
                old = peaks[h]
                peak = jnp.maximum(old, jnp.max(scores, axis=0, keepdims=True))
                expo = jnp.exp(scores - peak)
                ratio = jnp.exp(old - peak)
                peaks[h] = peak
                totals[h] = totals[h] * ratio + jnp.sum(expo, axis=0, keepdims=True)
                place = pl.ds(h * HEAD, HEAD)
                acc[place, :] = acc[place, :] * ratio + _nn(
                    value[h * HEAD : (h + 1) * HEAD], expo.astype(bf16)
                )
            return carry

        lax.fori_loop(low, high, meet, 0)
        if not end:
            return
        for h in range(heads):
            place = pl.ds(h * HEAD, HEAD)
            acc[place, :] = acc[place, :] / totals[h]
            lse_ref[h : h + 1, query_rows] = peaks[h] + jnp.log(totals[h])
        back[query_rows, :width] = acc[...].astype(bf16).T

    half = token_blocks // 2
    chip = me // 2
    per_device = own // BLOCK
    chunks_per = BLOCK // size

    def near(p):
        around(jnp.where(chip == 0, p, token_blocks - 1 - p))

    def around(i):
        attention(i, jnp.maximum(i - 1, 0), jnp.minimum(i + 2, token_blocks))

    _loop(half - 1, near)
    edge = half - 1 + chip
    attention(edge, half - 2 + 2 * chip, half + 2 * chip, 1, end=False)

    def far_part(r):
        @pl.when(r == 0)
        def _():
            full_step(3)

        @pl.when(r == 2)
        def _():
            for k in range(4, shares + 2):
                full_step(k)

        token_copy(r, 1).wait_recv()
        token_copy(r, 2).start()
        token_copy(r, 2).wait_recv()
        project([2, 3], r, 1)

    loop(far_part)
    loads[2].start()
    full_copy(0).wait_recv()
    full_copy(shares + 2).wait_recv()
    own_quarter.wait()
    loads[8].start()

    def tokens_done(r):
        for kind in range(3):
            token_copy(r, kind).wait_send()
        for k in range(4):
            keeps(k, r)[0].wait()

    def far(p):
        k, h = lax.rem(p, 2), p // 2
        around(jnp.where(k == 0, cnt, dia) * per_device + h)

        @pl.when(p == 0)
        def _():
            loop(tokens_done)

        for c in range(2):

            @pl.when(k == c)
            def _():
                for t in range(chunks_per):
                    trade(h * chunks_per + t, 2 + c).start()

    _loop(2 * per_device, far)
    attention(edge, half - chip, half - chip + 1, 1, begin=False)
    loop(lambda r: trade(r, 1).start())
    own_context.start()
    save_context = pltpu.make_async_copy(back.at[:, :width], context_hbm, load_sems.at[15])
    save_context.start()

    def add_sum(k, value):
        small_ref[k : k + 1, :] += jnp.sum(value, axis=0, keepdims=True)

    own_context.wait()
    loads[1].wait()
    loads[8].wait()

    def lower_norm(r):
        rows = _rows(r * size, size)
        for k in (1, 2, 3):
            trade(r, k).wait_recv()
        attended = _nn(recv_x[rows, :], grad1_full[:depth, :])
        unit, inverse = _norm(inputs_ref[rows, :].astype(f32) + attended + out_bias)
        unit1[rows, :] = unit
        inverse1[rows, :] = inverse
        gathers[0].slot(r, 0)[...] = (unit * attn_gain + attn_shift).astype(bf16)
        gathers[0].start(r)

    loop(lower_norm)
    loads[4].start()
    save_context.wait()
    for k in range(shares + 3):
        full_copy(k).wait_send()

    def front_done(r):
        for k in range(4):
            keeps(k, r)[1].wait()
        for k in (1, 2, 3):
            trade(r, k).wait_send()
        for load in context_load(r):
            load.start()

    loop(front_done)
    loads[2].wait()
    loads[3].wait()

    def feed_forward(r):
        rows = _rows(r * whole, whole)
        gathers[0].forward(r)
        gathers[0].arrive(r)

        def column(n, carry):
            cols = _rows(n * COLS, COLS)
            upper = _nn(normed_full[rows, :], up_ref[:, cols]) + up_bias_ref[:, cols]
            cdf = 0.5 + 0.5 * lax.erf(upper * math.sqrt(0.5))
            pdf = jnp.exp(upper * upper * -0.5) * (1.0 / math.sqrt(2.0 * math.pi))
            active[rows, cols] = (upper * cdf).astype(bf16)
            back[rows, cols] = (cdf + upper * pdf).astype(bf16)
            return carry

        lax.fori_loop(0, units // COLS, column, 0)
        scatters[1].project(r, lambda cols: _nn(active[rows, :], down_ref[:, cols]))
        scatters[1].finish(r)

    loop(feed_forward)
    loads[4].wait()

    def upper_norm(r):
        rows = _rows(r * size, size)
        normed = unit1[rows, :] * attn_gain + attn_shift
        unit, inverse = _norm(normed + scatters[1].result(r) + down_bias)
        cotangent = inputs_ref[rows, :].astype(f32)
        outputs_ref[rows, :] = (unit * ffn_gain + ffn_shift).astype(bf16)
        store(0, r).start()
        grad = _norm_back(cotangent * ffn_gain, unit, inverse)
        gathers[1].slot(r, 0)[...] = grad.astype(bf16)
        gathers[1].start(r)
        grad_own[rows, :] = grad
        add_sum(3, grad)
        add_sum(4, cotangent * unit)
        add_sum(5, cotangent)

    loop(upper_norm)

    def take(r):
        gathers[1].forward(r)
        gathers[1].arrive(r)
        scatters[1].sent(r)

    def feed_back(r):
        rows = _rows(r * whole, whole)

        def column(n, carry):
            cols = _rows(n * COLS, COLS)
            incoming = _nt(grad2_full[rows, :], down_ref[cols, :])
            upper_back = (back[rows, cols].astype(f32) * incoming).astype(bf16)
            back[rows, cols] = upper_back
            late_ref[1:2, cols] += jnp.sum(upper_back.astype(f32), axis=0, keepdims=True)
            return carry

        lax.fori_loop(0, units // COLS, column, 0)
        scatters[2].project(r, lambda cols: _nt(back[rows, :], up_ref[cols, :]))
        scatters[2].finish(r)

    def take_back(r):
        take(r)
        feed_back(r)

    _loop(CHUNKS - 1, take_back)
    take(CHUNKS - 1)

    def weights(k, p):
        cols = _rows(p * (depth // CHUNKS), depth // CHUNKS)
        place = _rows(k * depth + p * (depth // CHUNKS), depth // CHUNKS)
        if k == 0:
            weight_grads[place, :] = _tn(active[:, cols], grad2_full[...]).astype(bf16)
        else:
            weight_grads[place, :] = _tn(normed_full[:, cols], back[...]).astype(bf16)

    def out_weights():
        target = outputs_ref.at[:width] if early else weight_grads.at[3 * width : 4 * width]
        target[...] = _tn(context_ref[...], grad1_full[...]).astype(bf16)

    def in_weights(j):
        weight_grads[_rows(j * width, width), :] = _tn(
            grads[:, j * width : (j + 1) * width], normed_full[...]
        ).astype(bf16)

    def move(n, k):
        if k == 0 and n < 2 * pieces:
            weights(n // pieces, n % pieces)
        elif k == 0 and n == count - 1:
            out_weights()
        elif k == 0:
            in_weights(n - 2 * pieces)
        sums[n].step(k)
        if k == 2 * bits:
            store_final(n).start()

    def store_final(n):
        rows = _rows(n * piece, piece)
        return pltpu.make_async_copy(final.at[rows], final_hbm.at[rows], final_sems.at[n])

    def slot(i, first, number):
        for at in range(first, first + number) if early else ():
            if at in PLAN:

                @pl.when(i == at - first)
                def _():
                    for n, k in PLAN[at]:
                        move(n, k)

    if early:
        for n, k in PLAN[-1]:
            move(n, k)
    feed_back(CHUNKS - 1)
    for load in loads[9:]:
        load.start()

    def lower_back(r):
        slot(r, 0, CHUNKS)
        if not early:
            for k in range(2):

                @pl.when(r // 2 == k)
                def _():
                    for h in range(2):
                        weights(k, 2 * r - 4 * k + h)

                @pl.when(r == 2 * k + 1)
                def _():
                    sums[k].step(0)

        rows = _rows(r * size, size)
        incoming = grad_own[rows, :] + scatters[2].result(r)
        unit = unit1[rows, :]
        grad = _norm_back(incoming * attn_gain, unit, inverse1[rows, :])
        gathers[2].slot(r, 0)[...] = grad.astype(bf16)
        gathers[2].start(r)
        grad_own[rows, :] = grad
        add_sum(0, grad)
        add_sum(1, incoming * unit)
        add_sum(2, incoming)

    loop(lower_back)
    gathers_done = lambda r: [gather.sent(r) for gather in gathers[:2]]
    loop(gathers_done)
    for load in loads[5:8]:
        load.start()

    loads[0].wait()
    loop(lambda r: [load.wait() for load in context_load(r)])

    def context_back(r):
        slot(r, CHUNKS, CHUNKS)
        rows = _rows(r * whole, whole)
        gathers[2].forward(r)
        gathers[2].arrive(r)
        scatters[2].sent(r)
        grad = _nt(grad1_full[rows, :], out_proj_ref[...]).astype(bf16)
        for k, b in enumerate(blocks):
            part = _rows(b * own + r * size, size)
            back[part, :width] = grad[k * size : (k + 1) * size]

    loop(context_back)
    loop(lambda r: gathers[2].sent(r))
    loop(lambda r: store(0, r).wait())
    for load in loads[5:8]:
        load.wait()

    targets = [{"mp": sib}, {"mp": cnt}, *over]

    def small_step(k):
        return _remote(
            small_ref.at[:8], small_recv.at[k], small_sems.at[0, k], small_sems.at[1, k], targets[k]
        )

    def small_end(k):
        small_step(k).wait()
        small_ref[:8, :] += small_recv[k]

    def late_step(k):
        at = len(targets) + k
        return _remote(late_ref, late_recv.at[k], small_sems.at[0, at], small_sems.at[1, at], over[k])

    def late_end(k):
        late_step(k).wait()
        late_ref[...] += late_recv[k]

    def small_turn(k):
        if k:
            small_end(k - 1)
        if k < len(targets):
            small_step(k).start()

    keys_acc, values_acc, query_acc = unit1, other_acc, own_acc.at[:width, :BLOCK]
    keys_acc[...] = jnp.zeros_like(keys_acc)
    values_acc[...] = jnp.zeros_like(values_acc)
    grads = grad2_full
    per = own // BLOCK

    def spot(j):
        return _rows(lax.rem(j, per) * BLOCK, BLOCK), _rows(j // per * width, width)

    def attend(t):
        i, turn = t // 3, lax.rem(t, 3)
        for k in range(len(targets) + 1):

            @pl.when(t == SMALL_TURNS[k])
            def _():
                small_turn(k)

        slot(t, 2 * CHUNKS, 3 * token_blocks)
        query_rows = _rows(i * BLOCK, BLOCK)

        @pl.when(turn == 0)
        def _():
            product = (
                back[query_rows, :width].astype(f32) * back[query_rows, width : 2 * width].astype(f32)
            ).T
            for h in range(heads):
                dots_ref[h : h + 1, :] = jnp.sum(
                    product[h * HEAD : (h + 1) * HEAD], axis=0, keepdims=True
                )
            query_acc[...] = jnp.zeros_like(query_acc)

        @pl.when((i + turn >= 1) & (i + turn <= token_blocks))
        def _():
            j = jnp.clip(i + turn - 1, 0, token_blocks - 1)
            query, grad = active[query_rows, :width], back[query_rows, :width]
            rows = _rows(j * BLOCK, BLOCK)
            bias = _bias(seg_ref, pad_ref, query_rows, rows)
            queries = [query * scaled[h] for h in range(heads)]
            context_grads = [grad * plain[h] for h in range(heads)]
            key_rows = (active[rows, width : 2 * width] * (1.0 / math.sqrt(HEAD))).astype(bf16).T
            parts = []
            for c in range(BLOCK // PART):
                place = pl.ds(pl.multiple_of(j * BLOCK + c * PART, PART), PART)
                key, value = active[place, width : 2 * width], active[place, 2 * width : 3 * width]
                probs, score_grads = [], []
                for h in range(heads):
                    scores = _nt(key, queries[h]) + bias[c * PART : (c + 1) * PART]
                    prob = jnp.exp(scores - lse_ref[h : h + 1, query_rows])
                    probs.append(prob.astype(bf16))
                    score_grads.append(
                        (prob * (_nt(value, context_grads[h]) - dots_ref[h : h + 1, :])).astype(bf16)
                    )
                spot_rows, spot_cols = spot(j)
                spot_part = pl.ds(pl.multiple_of(lax.rem(j, per) * BLOCK + c * PART, PART), PART)
                keys_acc[spot_part, spot_cols] += _nn(
                    jnp.concatenate(score_grads, axis=1), jnp.concatenate(queries, axis=0)
                )
                values_acc[spot_part, spot_cols] += _nn(
                    jnp.concatenate(probs, axis=1), jnp.concatenate(context_grads, axis=0)
                )
                parts.append(score_grads)
            for h in range(heads):
                query_acc[pl.ds(h * HEAD, HEAD), :] += _nn(
                    key_rows[h * HEAD : (h + 1) * HEAD], jnp.concatenate([part[h] for part in parts], axis=0)
                )

        @pl.when(turn == 2)
        def _():
            grads[query_rows, :width] = query_acc[...].astype(bf16).T

    _loop(3 * token_blocks, attend)

    def keep(j):
        rows = _rows(j * BLOCK, BLOCK)
        grads[rows, width : 2 * width] = keys_acc[spot(j)].astype(bf16)
        grads[rows, 2 * width : 3 * width] = values_acc[spot(j)].astype(bf16)

    _loop(token_blocks, keep)

    if not early:
        for n in range(2):
            sums[n].step(1)
        out_weights()
        in_weights(0)
        in_weights(1)
        in_weights(2)
    for n in range(2 * pieces):
        sums[n].halve(0).wait_send()

    def partial_rows(r):
        chunk = jnp.concatenate(
            [grads[_rows(b * own + r * size, size), : 3 * width] for b in blocks], axis=0
        )

        def tile(cols):
            return _nt(chunk, up_ref[cols, : 3 * width])

        scatters[3].project(r, tile)
        scatters[3].finish(r)

    def finish(r):
        rows = _rows(r * size, size)
        outputs_ref[rows, :] = (grad_own[rows, :] + scatters[3].result(r)).astype(bf16)
        store(1, r).start()
        scatters[3].sent(r)

    def bias(j):
        return jnp.sum(grads[:, j * width : (j + 1) * width].astype(f32), axis=0, keepdims=True)

    for load in loads[9:]:
        load.wait()
    late_ref[:1, :width] = bias(0)
    late_ref[:1, width : 2 * width] = bias(2)
    late_step(0).start()
    if early:
        tail = PLAN[2 * CHUNKS + 3 * token_blocks]
    else:
        tail = [(2, 0)] + [(-1, r) for r in range(CHUNKS)]
        tail += [(n, k) for k in range(1, 2 * bits + 1) for n in range(3) if n == 2 or k > 1]
    last = max(k for k, (n, _) in enumerate(tail) if n < 0)
    turns = [(len(tail) - 1) * (k + 2) // (bits + 1) for k in range(bits)]
    for at, (n, k) in enumerate(tail):
        if n < 0:
            partial_rows(k)
        elif k or early:
            move(n, k)
        else:
            sums[n].step(0)
        for turn in [turn for turn, place in enumerate(turns) if place == at]:
            late_end(turn)
            if turn + 1 < bits:
                late_step(turn + 1).start()
        if at == last + 3 * (len(tail) - 1 - last) // 4:
            if early:
                sums[-1].halve(0).wait_send()
            loop(finish)
    for n in range(count):
        sums[n].sent()
        if n >= 2 * pieces and not (early and n == count - 1):
            sums[n].halve(0).wait_send()
    small_ref[8:10, :] = late_ref[:2, :]
    loop(lambda r: store(1, r).wait())
    for n in range(3 * pieces):
        store_final(n).wait()


def main_layer(mesh, arrays, small_arrays):
    f32, bf16 = jnp.float32, jnp.bfloat16
    inputs, in_proj, out_proj, up_proj, down_proj, _ = arrays
    own, depth = inputs.shape
    units, width = up_proj.shape[1], out_proj.shape[0]
    whole, half = 4 * own, depth // 2
    bits = mesh.shape["dp"].bit_length() - 1
    pieces = CHUNKS if (depth // CHUNKS >> bits) >= 16 else 1
    outs = [
        ((own, depth), bf16),
        ((own, depth), bf16),
        ((3 * depth, depth), bf16),
        ((whole, depth), bf16),
        ((whole, 3 * width), bf16),
        ((4 * width, depth), bf16),
        ((whole, width), bf16),
        ((16, depth), f32),
    ]
    return pl.pallas_call(
        partial(main_kernel, bits, pieces),
        out_shape=[jax.ShapeDtypeStruct(*out) for out in outs],
        in_specs=[REMOTE] * 16,
        out_specs=[REMOTE] * 7 + [LOCAL],
        scratch_shapes=[
            pltpu.VMEM((whole, width), bf16),
            *[pltpu.VMEM(array.shape, bf16) for array in (out_proj, inputs, up_proj, down_proj)],
            pltpu.VMEM((2 * depth, depth), bf16),
            pltpu.VMEM((whole, depth), bf16),
            pltpu.VMEM((whole, depth), bf16),
            pltpu.VMEM((whole, depth), bf16),
            pltpu.VMEM((whole, units), bf16),
            pltpu.VMEM((whole, units), bf16),
            pltpu.VMEM((own, depth), f32),
            pltpu.VMEM((own, 1), f32),
            pltpu.VMEM((own, depth), f32),
            pltpu.VMEM((8, BLOCK), f32),
            pltpu.VMEM((8, whole), f32),
            pltpu.VMEM((2 * (width // HEAD), 1, BLOCK), f32),
            pltpu.VMEM((2 * (width // HEAD), 1, BLOCK), f32),
            *_scatter_scratch(own, depth),
            pltpu.VMEM((3 * pieces * (depth // pieces - (depth // pieces >> bits)), depth), bf16),
            pltpu.VMEM((3 * depth, depth), bf16),
            pltpu.VMEM((2 + bits, 8, depth), f32),
            pltpu.VMEM((8, depth), f32),
            pltpu.VMEM((bits, 8, depth), f32),
            pltpu.SemaphoreType.DMA((16,)),
            pltpu.SemaphoreType.DMA((4, CHUNKS)),
            pltpu.SemaphoreType.DMA((2, 3, CHUNKS)),
            pltpu.SemaphoreType.DMA((2, CHUNKS)),
            pltpu.SemaphoreType.DMA((3 * pieces,)),
            pltpu.SemaphoreType.DMA((3, 3, CHUNKS)),
            pltpu.SemaphoreType.DMA((3, 3, CHUNKS)),
            pltpu.SemaphoreType.DMA((4, 3, CHUNKS)),
            pltpu.SemaphoreType.DMA((4, 3, CHUNKS)),
            pltpu.SemaphoreType.DMA((2, 3 * pieces, 2 * bits)),
            pltpu.SemaphoreType.DMA((2, 2 + 2 * bits)),
            pltpu.SemaphoreType.DMA((2, 3, CHUNKS)),
            pltpu.SemaphoreType.DMA((2, 4, CHUNKS)),
            pltpu.SemaphoreType.DMA((2, 3 + bits)),
            pltpu.SemaphoreType.DMA((10,)),
            *[pltpu.VMEM(array.shape, array.dtype) for array in small_arrays],
        ],
        compiler_params=pltpu.CompilerParams(
            collective_id=1, has_side_effects=True, vmem_limit_bytes=63 * 2**20
        ),
        name="main_layer",
    )(*arrays, *small_arrays)


def unpack_kernel(
    width, final_ref, attn_ref, small_ref, outputs_ref, inputs_grad_ref, down_ref, up_ref, in_ref, out_ref,
    qv_ref, up_bias_ref, *refs,
):
    f32 = jnp.float32
    vectors, outputs_out, inputs_grad_out = refs[:6], refs[6], refs[7]
    down_ref[...] = final_ref[0].astype(f32)
    up_ref[...] = final_ref[1].astype(f32)
    for j in range(3):
        in_ref[j] = attn_ref[j * width : (j + 1) * width, :].astype(f32).T
    out_ref[...] = attn_ref[3 * width :, :].astype(f32)
    outputs_out[...] = outputs_ref[...]
    inputs_grad_out[...] = inputs_grad_ref[...]
    for k, vector in enumerate(vectors):
        vector[...] = small_ref[k : k + 1, :]
    up_bias_ref[...] = small_ref[9:10, :]
    for k in range(2):
        qv_ref[k : k + 1, :] = small_ref[8:9, k * width : (k + 1) * width]


def unpack(final, small, outputs, inputs_grad, width):
    f32 = jnp.float32
    own, depth = outputs.shape
    steps = depth // UNPACK
    part = own // steps
    matrix = pl.BlockSpec((UNPACK, depth), lambda i: (i, 0))
    tokens = pl.BlockSpec((part, depth), lambda i: (i, 0))
    vector = pl.BlockSpec((1, depth), lambda i: (0, 0))
    shapes = [
        ((depth, depth), f32, matrix),
        ((depth, depth), f32, matrix),
        ((3, depth, width), f32, pl.BlockSpec((3, UNPACK, width), lambda i: (0, i, 0))),
        ((width, depth), f32, pl.BlockSpec((width, UNPACK), lambda i: (0, i))),
        ((2, width), f32, pl.BlockSpec((2, width), lambda i: (0, 0))),
        *[((1, depth), f32, vector)] * 7,
        ((own, depth), jnp.bfloat16, tokens),
        ((own, depth), jnp.bfloat16, tokens),
    ]
    return pl.pallas_call(
        partial(unpack_kernel, width),
        grid=(steps,),
        in_specs=[
            pl.BlockSpec((2, UNPACK, depth), lambda i: (0, i, 0)),
            pl.BlockSpec((depth, UNPACK), lambda i: (2, i)),
            pl.BlockSpec((16, depth), lambda i: (0, 0)),
            tokens,
            tokens,
        ],
        out_specs=[spec for _, _, spec in shapes],
        out_shape=[jax.ShapeDtypeStruct(shape, dtype) for shape, dtype, _ in shapes],
        compiler_params=pltpu.CompilerParams(vmem_limit_bytes=VMEM),
        name="unpack_gradients",
    )(final.reshape(3, depth, depth), final, small, outputs, inputs_grad)


def shards(
    mesh,
    inputs,
    in_proj,
    qv_bias,
    out_proj,
    out_bias,
    attn_gain,
    attn_shift,
    up_proj,
    up_bias,
    down_proj,
    down_bias,
    ffn_gain,
    ffn_shift,
    segments,
    padding,
    cotangent,
):
    places, real = segment_places(segments, padding)
    vectors = [v[None] for v in (out_bias, attn_gain, attn_shift, down_bias, ffn_gain, ffn_shift)]
    outputs, inputs_grad, final, _, _, _, _, small = main_layer(
        mesh,
        (inputs, in_proj, out_proj, up_proj, down_proj, cotangent),
        (qv_bias, places, real, up_bias[None], *vectors),
    )
    down_grad, up_grad, in_grad, out_grad, qv_grad, up_bias_grad, *vectors, outputs, inputs_grad = unpack(
        final, small, outputs, inputs_grad, in_proj.shape[2]
    )
    vectors = [v[0] for v in vectors]
    return (
        outputs,
        inputs_grad,
        in_grad,
        qv_grad,
        out_grad,
        *vectors[:3],
        up_grad,
        up_bias_grad[0],
        down_grad,
        *vectors[3:],
    )


def solution(mesh):
    return jax.shard_map(
        partial(shards, mesh),
        mesh=mesh,
        in_specs=(
            P(("dp", "mp"), None),
            P(None, None, "mp"),
            P(None, "mp"),
            P("mp", None),
            P(),
            P(),
            P(),
            P(None, "mp"),
            P("mp"),
            P("mp", None),
            P(),
            P(),
            P(),
            P("dp", None),
            P("dp", None),
            P(("dp", "mp"), None),
        ),
        out_specs=(
            P(("dp", "mp"), None),
            P(("dp", "mp"), None),
            P(None, None, "mp"),
            P(None, "mp"),
            P("mp", None),
            P(),
            P(),
            P(),
            P(None, "mp"),
            P("mp"),
            P("mp", None),
            P(),
            P(),
            P(),
        ),
        check_vma=False,
    )
```
